32 devices in a mesh: batch: 16 (over z, y, core), seq: 2 (over x).
Axes of the slice: x: 2, y: 2, z: 4, core: 2. Of those that a mesh axis runs over, the one named last changes fastest.
Arguments:
- inputs: bfloat16 [96, 1024, 768], P('batch', 'seq'), may hold values from -6 to 6
- lengths: int32 [16, 6], P('batch'), may hold values from 1 to 1024, 3584 in all within a row
- cotangent: bfloat16 [96, 1024, 768], P('batch', 'seq'), may hold values from -6 to 6
- norm_gain: bfloat16 [768], replicated, may hold values from 0.5 to 1.5
- w_query: bfloat16 [768, 768], replicated, may hold values from -0.109375 to 0.109375
- w_key: bfloat16 [768, 768], replicated, may hold values from -0.109375 to 0.109375
- w_value: bfloat16 [768, 768], replicated, may hold values from -0.21875 to 0.21875
- w_out: bfloat16 [768, 768], replicated, may hold values from -0.875 to 0.875
- ff_gain: bfloat16 [768], replicated, may hold values from 0.5 to 1.5
- w_gate: bfloat16 [768, 2048], replicated, may hold values from -0.21875 to 0.21875
- w_up: bfloat16 [768, 2048], replicated, may hold values from -0.21875 to 0.21875
- w_down: bfloat16 [2048, 768], replicated, may hold values from -0.125 to 0.125
- bias_table: bfloat16 [32, 12], replicated, may hold values from -4 to 4
Outputs:
- layer_output: float32 [96, 1024, 768], P('batch', 'seq')
- input_grad: float32 [96, 1024, 768], P('batch', 'seq')
- norm_gain_grad: float32 [768], replicated
- query_grad: float32 [768, 768], replicated
- key_grad: float32 [768, 768], replicated
- value_grad: float32 [768, 768], replicated
- out_grad: float32 [768, 768], replicated
- ff_gain_grad: float32 [768], replicated
- gate_grad: float32 [768, 2048], replicated
- up_grad: float32 [768, 2048], replicated
- down_grad: float32 [2048, 768], replicated
- bias_grad: float32 [32, 12], replicated
The draws below stay inside these ranges and needn't reach their ends.
Inputs may be any that keep to these rules, and one draw needn't show every extreme that they name: Each padded row holds 1 to 1024 real bytes. For each group g, the 6 lengths lengths[g, 0], ..., lengths[g, 5] of that group's rows together add up to 3584, and the largest of them is 1024.
All inputs are finite; a program needn't handle non-finite values.
Results may differ from the reference program's by a relative error of at most 0.018.
Values may be sent and summed in bfloat16 or wider, within the bound.
No kernel may reach another device: no remote copies, remote signals or barrier semaphores. Data moves between devices by JAX's collectives and lax.ppermute only.
A program may use at most 640 MiB of HBM per device.

```python
import math
import jax
import jax.numpy as jnp
import numpy as np
from jax import lax

D = 768
FF = 2048
HEADS = 12
HEAD_DIM = 64
BUCKETS = 32
LEN = 1024
ROWS_DEV = 6
INNER = 768
BATCHES = 16
ROWS = 96


def level_of(stream_key, shape, pieces, low, largest):
    factor_of, own = 1.0, jax.random.fold_in(stream_key, 6)
    for dim, blocks in pieces:
        draws = jnp.exp(jax.random.uniform(jax.random.fold_in(own, dim), (blocks,), jnp.float32, low / len(pieces), largest / len(pieces)))
        factor_of = factor_of * jnp.repeat(draws, shape[dim] // blocks).reshape([-1 if axis == dim else 1 for axis in range(len(shape))])
    return factor_of


def profile(number_of, total, reach, skew):
    loads = [(1 << 20) // math.isqrt(rank ** skew) + 1 for rank in range(2, number_of + 1)]
    spare, holding = total - reach - (number_of - 1), [1] * (number_of - 1)
    while spare > 0:
        free = [i for i in range(number_of - 1) if holding[i] < reach]
        mass, remaining = sum([loads[i] for i in free]), spare
        for i in free:
            addition = min(reach - holding[i], max(1, remaining * loads[i] // mass), spare)
            holding[i] = holding[i] + addition
            spare = spare - addition
    return np.array([reach] + holding)


def ragged(rng, number_of, total, bound, skew):
    if number_of == 2:
        one = jax.random.randint(rng, (), max(1, total - bound), min(bound, total - 1) + 1)
        return jnp.stack([one, total - one])
    sizes = jnp.asarray(profile(number_of, total, bound, skew), jnp.int32)
    couples = (number_of - 1) // 2
    donor, sink = sizes[1:1 + 2 * couples:2], sizes[2:2 + 2 * couples:2]
    margin = jnp.minimum(donor - 1, bound - sink)
    passed = jax.random.randint(jax.random.fold_in(rng, 1), (couples,), 0, 1 << 20) % (margin + 1)
    sizes = sizes.at[1:1 + 2 * couples:2].set(donor - passed).at[2:2 + 2 * couples:2].set(sink + passed)
    return sizes[jax.random.permutation(jax.random.fold_in(rng, 2), number_of)]


def centred(key, shape, width, limit, cuts=(), kind=jnp.bfloat16):
    values = jax.random.normal(key, shape, jnp.float32) * width
    if len(cuts) > 0:
        values = level_of(key, shape, cuts, -0.22, 0.18) * values
    return jnp.clip(values, min=-limit, max=limit).astype(kind)


def setup_inputs(seed: int = 0) -> dict:
    key_of = jax.random.split(jax.random.key(seed), 14)
    return {
        "inputs": centred(key_of[0], (ROWS, LEN, D), 1.0, 6.0, ((0, 16), (1, 2))),
        "lengths": jax.vmap(lambda own: ragged(own, ROWS_DEV, LEN + (ROWS_DEV - 1) * (LEN // 2), LEN, 2))(jax.random.split(key_of[1], BATCHES)).reshape((BATCHES, ROWS_DEV)).astype(jnp.int32),
        "cotangent": centred(key_of[2], (ROWS, LEN, D), 1.0, 6.0, ((0, 16), (1, 2))),
        "norm_gain": jnp.clip(1.0 + 0.1 * jax.random.normal(key_of[3], (D,), jnp.float32), 0.5, 1.5).astype(jnp.bfloat16),
        "w_query": centred(key_of[4], (D, INNER), (4 * D) ** -0.5, 0.109375),
        "w_key": centred(key_of[5], (D, INNER), (4 * D) ** -0.5, 0.109375),
        "w_value": centred(key_of[6], (D, INNER), D ** -0.5, 0.21875),
        "w_out": centred(key_of[7], (INNER, D), (INNER // 16) ** -0.5, 0.875),
        "ff_gain": jnp.clip(1.0 + 0.1 * jax.random.normal(key_of[8], (D,), jnp.float32), 0.5, 1.5).astype(jnp.bfloat16),
        "w_gate": centred(key_of[9], (D, FF), D ** -0.5, 0.21875),
        "w_up": centred(key_of[10], (D, FF), D ** -0.5, 0.21875),
        "w_down": centred(key_of[11], (FF, D), FF ** -0.5, 0.125),
        "bias_table": centred(key_of[12], (BUCKETS, HEADS), 1.0, 4.0),
    }


epsilon = 1e-06
masked_score = -2e+30
bucket_bounds = (12, 16, 23, 32, 46, 64, 91)
highest = lax.Precision.HIGHEST

@jax.custom_vjp
def low(v):
    return lax.optimization_barrier(v.astype(jnp.bfloat16)).astype(jnp.float32)

@jax.custom_vjp
def low_back(v):
    return v

def low_keep(v):
    return (low(v), None)

def low_pass(kept, grad):
    return (grad,)

def back_keep(v):
    return (v, None)

def back_low(kept, grad):
    return (low(grad),)
low.defvjp(low_keep, low_pass)
low_back.defvjp(back_keep, back_low)

def rms_scaled(values, gain):
    mean_square = lax.optimization_barrier(jnp.mean(values * values, axis=-1, keepdims=True))
    return values * lax.rsqrt(mean_square + epsilon) * gain

def bucket_table(extent):
    position = jnp.arange(extent, dtype=jnp.int32)
    offset = position[None, :] - position[:, None]
    distance = jnp.abs(offset)
    far_bucket = jnp.full_like(distance, 8)
    for threshold in bucket_bounds:
        far_bucket = far_bucket + (distance >= threshold).astype(jnp.int32)
    return jnp.where(offset > 0, BUCKETS // 2, 0) + jnp.where(distance < 8, distance, far_bucket)

def project(values, weight):
    return jnp.einsum('gtd,di->gti', values, weight, precision=highest)

def layer(inputs, lengths, norm_gain, w_query, w_key, w_value, w_out, ff_gain, w_gate, w_up, w_down, bias_table):
    group_size = inputs.shape[0]
    normed = low(rms_scaled(inputs, norm_gain))
    queries = low_back(low(project(normed, w_query))).reshape(group_size, LEN, HEADS, HEAD_DIM)
    keys = low_back(low(project(normed, w_key))).reshape(group_size, LEN, HEADS, HEAD_DIM)
    values = low_back(low(project(normed, w_value))).reshape(group_size, LEN, HEADS, HEAD_DIM)
    raw_scores = jnp.einsum('gqhd,gkhd->ghqk', queries, keys, precision=highest)
    bias_full = jnp.transpose(bias_table[bucket_table(LEN)], (2, 0, 1))
    scores = low_back(raw_scores + bias_full[None])
    usable = jnp.arange(LEN, dtype=jnp.int32)[None, :] < lengths[:, None]
    scores = jnp.where(usable[:, None, None, :], scores, masked_score)
    shifted = scores - lax.optimization_barrier(jnp.max(scores, axis=-1, keepdims=True))
    expd = jnp.exp(shifted)
    weights = expd / lax.optimization_barrier(jnp.sum(expd, axis=-1, keepdims=True))
    mixed = jnp.einsum('ghqk,gkhd->gqhd', low(weights), values, precision=highest)
    mixed = low_back(low(mixed.reshape(group_size, LEN, INNER)))
    hidden = inputs + low_back(project(mixed, w_out))
    normed2 = low(rms_scaled(hidden, ff_gain))
    gate = low_back(project(normed2, w_gate))
    up_proj = low_back(project(normed2, w_up))
    activated = low(jax.nn.gelu(gate, approximate=True) * up_proj)
    return hidden + project(activated, w_down)

def reference(inputs, lengths, cotangent, norm_gain, w_query, w_key, w_value, w_out, ff_gain, w_gate, w_up, w_down, bias_table):
    weights_f = tuple((w.astype(jnp.float32) for w in (norm_gain, w_query, w_key, w_value, w_out, ff_gain, w_gate, w_up, w_down, bias_table)))
    group_size = math.gcd(ROWS, 2)
    group_count = ROWS // group_size
    rows_in = inputs.astype(jnp.float32).reshape(group_count, group_size, LEN, D)
    rows_grad = cotangent.astype(jnp.float32).reshape(group_count, group_size, LEN, D)
    rows_len = lengths.reshape(group_count, group_size).astype(jnp.int32)

    def one_group(totals, sample):
        block_in, block_grad, block_len = sample

        def forward(values, *weights):
            return layer(values, block_len, *weights)
        result, pullback = jax.vjp(forward, block_in, *weights_f)
        gradients = pullback(block_grad)
        totals = tuple((a + b for a, b in zip(totals, gradients[1:])))
        return (totals, (result, gradients[0]))
    begin_totals = tuple((jnp.zeros_like(w) for w in weights_f))
    totals, (outputs, input_grads) = lax.scan(one_group, begin_totals, (rows_in, rows_grad, rows_len))
    return (outputs.reshape(ROWS, LEN, D), input_grads.reshape(ROWS, LEN, D), totals[0], totals[1], totals[2], totals[3], totals[4], totals[5], totals[6], totals[7], totals[8], totals[9])
```

```python
import functools
import itertools
import math

import jax
import jax.numpy as jnp
from jax import lax
from jax.experimental import pallas as pl
from jax.experimental.pallas import tpu as pltpu
from jax.sharding import PartitionSpec as P

f32 = jnp.float32
bf16 = jnp.bfloat16
epsilon = 1e-06
masked_score = -2e30
start_max = -1e30
bucket_bounds = (12, 16, 23, 32, 46, 64, 91)
LANE = 128
STEP = 256
NT = (((1,), (1,)), ((), ()))
NN = (((1,), (0,)), ((), ()))
TN = (((0,), (0,)), ((), ()))


def mm(a, b, dims=NN):
    return lax.dot_general(a, b, dims, preferred_element_type=f32)


def params(grid_dims, mib):
    return pltpu.CompilerParams(
        dimension_semantics=("arbitrary",) * grid_dims, vmem_limit_bytes=mib << 20
    )


def bucket_of(offset, bucket_count):
    distance = jnp.abs(offset)
    far = jnp.full_like(distance, 8)
    for bound in bucket_bounds:
        far = far + (distance >= bound).astype(jnp.int32)
    half = bucket_count // 2
    return jnp.where(offset > 0, half, 0) + jnp.where(distance < 8, distance, far)


def near_body(vec_ref, rev_ref, near_ref, near_t_ref):
    wide = jnp.broadcast_to(vec_ref[0], (LANE, 4 * LANE))
    near_ref[0] = pltpu.roll(wide, 0, 1, stride=1, stride_axis=0)[:, : 3 * LANE]
    tall = jnp.broadcast_to(rev_ref[0], (3 * LANE, 4 * LANE))
    near_t_ref[0] = pltpu.roll(tall, 0, 1, stride=1, stride_axis=0)[:, :LANE]


def near_offsets():
    place = jnp.arange(4 * LANE, dtype=jnp.int32)
    signed = jnp.where(place < 3 * LANE, place, place - 4 * LANE)
    forward = signed - LANE
    back = jnp.where(place < LANE, place, place - 4 * LANE)
    reverse = -back - LANE
    return forward, reverse


def bias_pieces(bias_table, tile_count):
    buckets, heads = bias_table.shape
    table = bias_table.astype(f32)
    forward, reverse = near_offsets()

    def spread(offset):
        hot = bucket_of(offset, buckets)[:, None] == jnp.arange(buckets, dtype=jnp.int32)
        picked = jnp.einsum("rb,bh->hr", hot.astype(f32), table, precision=lax.Precision.HIGHEST)
        return picked[:, None, :]

    near, near_t = pl.pallas_call(
        near_body,
        grid=(heads,),
        in_specs=[pl.BlockSpec((1, 1, 4 * LANE), lambda h: (h, 0, 0))] * 2,
        out_specs=[
            pl.BlockSpec((1, LANE, 3 * LANE), lambda h: (h, 0, 0)),
            pl.BlockSpec((1, 3 * LANE, LANE), lambda h: (h, 0, 0)),
        ],
        out_shape=[
            jax.ShapeDtypeStruct((heads, LANE, 3 * LANE), f32),
            jax.ShapeDtypeStruct((heads, 3 * LANE, LANE), f32),
        ],
        name="near_bias",
    )(spread(forward), spread(reverse))
    left = table[buckets // 2 - 1]
    right = table[buckets - 1]
    tile = jnp.arange(tile_count, dtype=jnp.int32)[None, :, None]
    lane = jnp.arange(LANE, dtype=jnp.int32)[None, None, :]
    far = jnp.where(lane == tile, left[:, None, None], 0.0)
    far = far + jnp.where(lane == tile + 8, right[:, None, None], 0.0)
    far = far + jnp.where(lane == 16, masked_score, 0.0)
    return near, near_t, far.astype(bf16)


def key_lanes(extent, length):
    key = lax.broadcasted_iota(jnp.int32, (extent, LANE), 0)
    lane = lax.broadcasted_iota(jnp.int32, (extent, LANE), 1)
    tile = key // LANE
    flag = (lane < 8) & (tile < lane - 1)
    flag = flag | ((lane >= 8) & (lane < 16) & (tile > lane - 8 + 1))
    flag = flag | ((lane == 16) & (key >= length))
    flag = flag | ((lane >= 17) & (lane < 20))
    return jnp.where(flag, 1.0, 0.0).astype(bf16)


def rms_of(values):
    scale = lax.rsqrt(jnp.mean(values * values, axis=-1, keepdims=True) + epsilon)
    return scale


def head_mask(rows, head):
    lane = lax.broadcasted_iota(jnp.int32, (rows, LANE), 1)
    return (lane // (LANE // 2)) == head


def fwd_body(held, scal, xl, xr, gain, wq, wk, wv, near, far, *rest):
    q_out, k_out, v_out, mix_out, tail_out, normt_out, normed, lanes = rest[held:]
    extent = normed.shape[0]
    half = xl.shape[1]
    length = scal[0]
    side = scal[2]
    steps = (length + STEP - 1) // STEP

    @pl.when(pl.program_id(0) == 0)
    def _():
        for ref, own in ((xl, True), (xr, False)):
            values = ref[0].astype(f32)
            out = values * rms_of(values) * gain[...].astype(f32)
            place = side * half if own else (1 - side) * half
            normed[pl.ds(pl.multiple_of(place, half), half), :] = out.astype(bf16)
        lanes[...] = key_lanes(extent, length)
        normt_out[0] = normed[...].T

    q_out[0, 0] = mm(normed[...], wq[...]).astype(bf16)
    for part in range(extent // STEP):
        rows = pl.ds(part * STEP, STEP)

        @pl.when(part < steps)
        def _():
            k_out[0, 0, rows, :] = mm(normed[rows, :], wk[...]).astype(bf16)
            v_out[0, 0, rows, :] = mm(normed[rows, :], wv[...]).astype(bf16)

        @pl.when(part >= steps)
        def _():
            k_out[0, 0, rows, :] = jnp.zeros((STEP, 2 * LANE), bf16)
            v_out[0, 0, rows, :] = jnp.zeros((STEP, 2 * LANE), bf16)

    def attend(width):
        def pair_step(pair, carry):
            cols = pl.ds(pl.multiple_of(pair * LANE, LANE), LANE)
            kext = jnp.concatenate([k_out[0, 0, :width, cols], lanes[:width, :]], axis=1)
            vext = jnp.concatenate(
                [v_out[0, 0, :width, cols], jnp.ones((width, LANE), bf16)], axis=1
            )
            lane = lax.broadcasted_iota(jnp.int32, (STEP, LANE), 1)
            for block in range(extent // STEP):
                rows = slice(block * STEP, (block + 1) * STEP)
                qpair = q_out[0, 0, rows, cols]
                outs = []
                for head in range(2):
                    index = 2 * pair + head
                    tiles = []
                    for sub in range(STEP // LANE):
                        line = far[index, pl.ds(block * (STEP // LANE) + sub, 1), :]
                        tiles.append(jnp.broadcast_to(line, (LANE, LANE)))
                    ext = jnp.concatenate(tiles, axis=0)
                    qm = jnp.where(head_mask(STEP, head), qpair, jnp.zeros_like(qpair))
                    scores = mm(jnp.concatenate([qm, ext], axis=1), kext, NT)
                    probs = []
                    tops = []
                    for sub in range(STEP // LANE):
                        tile = block * (STEP // LANE) + sub
                        own = scores[sub * LANE : (sub + 1) * LANE]
                        base = (tile - 1) * LANE
                        low, high = max(0, base), min(width, base + 3 * LANE)
                        if low < high:
                            add = own[:, low:high] + near[index, :, low - base : high - base]
                            pieces = [own[:, :low]] if low > 0 else []
                            pieces.append(add)
                            if high < width:
                                pieces.append(own[:, high:])
                            own = jnp.concatenate(pieces, axis=1)
                        top = jnp.max(own, axis=1, keepdims=True)
                        probs.append(jnp.exp(own - top).astype(bf16))
                        tops.append(top)
                    both = mm(jnp.concatenate(probs, axis=0), vext)
                    total = both[:, LANE:]
                    outs.append(both[:, :LANE] / total)
                    neg = -(jnp.concatenate(tops, axis=0) + jnp.log(total))
                    first = neg.astype(bf16)
                    rest = neg - first.astype(f32)
                    second = rest.astype(bf16)
                    third = (rest - second.astype(f32)).astype(bf16)
                    line = jnp.where(lane == 17, first, ext)
                    line = jnp.where(lane == 18, second, line)
                    line = jnp.where(lane == 19, third, line)
                    tail_out[0, index, rows, :] = line
                picked = jnp.where(head_mask(STEP, 0), outs[0], outs[1])
                mix_out[0, 0, rows, cols] = picked.astype(bf16)
            return carry

        lax.fori_loop(0, 2, pair_step, 0)

    for count in range(1, extent // STEP + 1):

        @pl.when(steps == count)
        def _():
            attend(count * STEP)


def fwd_row(scal, inputs, remote, which, count, held, gain, wq, wk, wv, near, far, heads):
    rows, half, width = inputs.shape
    extent = 2 * half
    inner = wq.shape[1]
    quads = inner // STEP
    per = heads // quads
    weight = pl.BlockSpec((width, STEP), lambda i, s: (0, i))
    block = pl.BlockSpec((1, 1, extent, STEP), lambda i, s: (which, i, 0, 0))
    grid_spec = pltpu.PrefetchScalarGridSpec(
        num_scalar_prefetch=1,
        grid=(quads,),
        in_specs=[
            pl.BlockSpec((1, half, width), lambda i, s: (s[1], 0, 0)),
            pl.BlockSpec((1, half, width), lambda i, s: (0, 0, 0)),
            pl.BlockSpec((1, width), lambda i, s: (0, 0)),
            weight,
            weight,
            weight,
            pl.BlockSpec((per, LANE, 3 * LANE), lambda i, s: (i, 0, 0)),
            pl.BlockSpec((per, 8, LANE), lambda i, s: (i, 0, 0)),
        ]
        + [pl.BlockSpec(memory_space=pl.ANY)] * len(held),
        out_specs=[block] * 4
        + [
            pl.BlockSpec((1, per, extent, LANE), lambda i, s: (which, i, 0, 0)),
            pl.BlockSpec((1, width, extent), lambda i, s: (which, 0, 0)),
        ],
        scratch_shapes=[pltpu.VMEM((extent, width), bf16), pltpu.VMEM((extent, LANE), bf16)],
    )
    stacked = jax.ShapeDtypeStruct((count, quads, extent, STEP), bf16)
    return pl.pallas_call(
        functools.partial(fwd_body, len(held)),
        grid_spec=grid_spec,
        out_shape=[stacked] * 4
        + [
            jax.ShapeDtypeStruct((count, heads, extent, LANE), bf16),
            jax.ShapeDtypeStruct((count, width, extent), bf16),
        ],
        input_output_aliases={9 + n: n for n in range(len(held))},
        compiler_params=params(1, 56),
        name="attend_row",
    )(scal, inputs, remote, gain, wq, wk, wv, near, far, *held)


def bwd_body(
    scal, q, k, v, mix, dmix, tail, near_t, normt,
    dq_out, dk_out, dv_out, tacc_out, far_out, dwq_out, dwk_out, dwv_out,
    lanes, pl_s, ds_s, do_s, qa_s, dwq, dwk, dwv,
):
    extent = lanes.shape[0]
    row_at = pl.program_id(0)
    length = scal[row_at]
    steps = (length + STEP - 1) // STEP
    lanes[...] = key_lanes(extent, length)

    @pl.when(row_at == 0)
    def _():
        for ref in (tacc_out, far_out, dwq, dwk, dwv):
            ref[...] = jnp.zeros(ref.shape, f32)

    dk_out[...] = jnp.zeros(dk_out.shape, bf16)
    dv_out[...] = jnp.zeros(dv_out.shape, bf16)

    def attend(width):
        def pair_step(pair, carry):
            cols = pl.ds(pl.multiple_of(pair * LANE, LANE), LANE)
            flags = lanes[:width, :]
            kpair = k[0, 0, :width, cols]
            kext = jnp.concatenate([kpair, flags], axis=1)
            vext = jnp.concatenate([v[0, 0, :width, cols], flags], axis=1)
            lane = lax.broadcasted_iota(jnp.int32, (STEP, LANE), 1)
            for block in range(extent // STEP):
                rows = slice(block * STEP, (block + 1) * STEP)
                qpair = q[0, 0, rows, cols]
                dopair = dmix[0, 0, rows, cols]
                product = dopair.astype(f32) * mix[0, 0, rows, cols].astype(f32)
                for head in range(2):
                    index = 2 * pair + head
                    mask = head_mask(STEP, head)
                    qm = jnp.where(mask, qpair, jnp.zeros_like(qpair))
                    dom = jnp.where(mask, dopair, jnp.zeros_like(dopair))
                    neg = -jnp.sum(jnp.where(mask, product, 0.0), axis=1, keepdims=True)
                    neg = jnp.broadcast_to(neg, (STEP, LANE))
                    first = neg.astype(bf16)
                    rest = neg - first.astype(f32)
                    second = rest.astype(bf16)
                    third = (rest - second.astype(f32)).astype(bf16)
                    zero = jnp.zeros((STEP, LANE), bf16)
                    dtail = jnp.where(lane == 17, first, zero)
                    dtail = jnp.where(lane == 18, second, dtail)
                    dtail = jnp.where(lane == 19, third, dtail)
                    st = mm(kext, jnp.concatenate([qm, tail[0, index, rows, :]], axis=1), NT)
                    dp = mm(vext, jnp.concatenate([dom, dtail], axis=1), NT)
                    at = head * extent + block * STEP
                    do_s[at : at + STEP, :] = dom
                    row = lax.broadcasted_iota(jnp.int32, (STEP, LANE), 0)
                    spot = jnp.where(
                        lane == head * 8 + block * (STEP // LANE) + row // LANE, 1.0, 0.0
                    ).astype(bf16)
                    qa_s[at : at + STEP, :] = jnp.concatenate([qm, spot], axis=1)
                    for sub in range(STEP // LANE):
                        tile = block * (STEP // LANE) + sub
                        part = slice(sub * LANE, (sub + 1) * LANE)
                        own = st[:, part]
                        base = (tile - 1) * LANE
                        low, high = max(0, base), min(width, base + 3 * LANE)
                        if low < high:
                            add = own[low:high] + near_t[index, low - base : high - base, :]
                            pieces = [own[:low]] if low > 0 else []
                            pieces.append(add)
                            if high < width:
                                pieces.append(own[high:])
                            own = jnp.concatenate(pieces, axis=0)
                        prob = jnp.exp(own)
                        dst = (prob * dp[:, part]).astype(bf16)
                        spot_at = at + sub * LANE
                        pl_s[:width, spot_at : spot_at + LANE] = prob.astype(bf16)
                        ds_s[:width, spot_at : spot_at + LANE] = dst
                        if low < high:
                            tacc_out[index, low - base : high - base, :] += dst[low:high].astype(
                                f32
                            )
            dv_out[0, :width, cols] = mm(pl_s[:width, :], do_s[...]).astype(bf16)
            dk = mm(ds_s[:width, :], qa_s[...])
            dk_out[0, :width, cols] = dk[:, :LANE].astype(bf16)
            sums = dk[:, LANE:]
            spread = lax.broadcasted_iota(jnp.int32, (width, LANE), 1)
            tile = lax.broadcasted_iota(jnp.int32, (width, LANE), 0) // LANE
            qtile = lax.rem(spread, 8)
            left = jnp.where((tile < qtile - 1) & (spread < 16), sums, 0.0)
            right = jnp.where((tile > qtile + 1) & (spread < 16), sums, 0.0)
            far_out[pl.ds(2 * pair, 1), :] += jnp.sum(left, axis=0, keepdims=True)
            far_out[pl.ds(2 * pair + 1, 1), :] += jnp.sum(right, axis=0, keepdims=True)
            maskk = head_mask(width, 0)
            zerok = jnp.zeros_like(kpair)
            km0 = jnp.where(maskk, kpair, zerok)
            km1 = jnp.where(maskk, zerok, kpair)
            dq = mm(ds_s[:width, :extent], km0, TN) + mm(ds_s[:width, extent:], km1, TN)
            dq_out[0, :, cols] = dq.astype(bf16)
            return carry

        lax.fori_loop(0, 2, pair_step, 0)
        dwk[...] += mm(normt[0, :, :width], dk_out[0, :width, :])
        dwv[...] += mm(normt[0, :, :width], dv_out[0, :width, :])

    for count in range(1, extent // STEP + 1):

        @pl.when(steps == count)
        def _():
            attend(count * STEP)

    dwq[...] += mm(normt[0], dq_out[0])

    @pl.when(row_at == pl.num_programs(0) - 1)
    def _():
        dwq_out[...] = dwq[...].astype(bf16)
        dwk_out[...] = dwk[...].astype(bf16)
        dwv_out[...] = dwv[...].astype(bf16)


def bwd_quad(lengths, quad, q, k, v, mix, dmix, tail, near_t, normt):
    count, quads, extent, _ = q.shape
    heads = tail.shape[1]
    width = normt.shape[1]
    per = heads // quads
    block = pl.BlockSpec((1, 1, extent, STEP), lambda i, s: (i, quad, 0, 0))
    given = pl.BlockSpec((1, extent, STEP), lambda i, s: (i, 0, 0))
    whole = pl.BlockSpec((width, STEP), lambda i, s: (0, 0))
    grid_spec = pltpu.PrefetchScalarGridSpec(
        num_scalar_prefetch=1,
        grid=(count,),
        in_specs=[block] * 5
        + [
            pl.BlockSpec((1, per, extent, LANE), lambda i, s: (i, quad, 0, 0)),
            pl.BlockSpec((per, 3 * LANE, LANE), lambda i, s: (quad, 0, 0)),
            pl.BlockSpec((1, width, extent), lambda i, s: (i, 0, 0)),
        ],
        out_specs=[given] * 3
        + [
            pl.BlockSpec((per, 3 * LANE, LANE), lambda i, s: (0, 0, 0)),
            pl.BlockSpec((8, LANE), lambda i, s: (0, 0)),
        ]
        + [whole] * 3,
        scratch_shapes=[
            pltpu.VMEM((extent, LANE), bf16),
            pltpu.VMEM((extent, 2 * extent), bf16),
            pltpu.VMEM((extent, 2 * extent), bf16),
            pltpu.VMEM((2 * extent, LANE), bf16),
            pltpu.VMEM((2 * extent, 2 * LANE), bf16),
        ]
        + [pltpu.VMEM((width, STEP), f32)] * 3,
    )
    out = jax.ShapeDtypeStruct((count, extent, STEP), bf16)
    return pl.pallas_call(
        bwd_body,
        grid_spec=grid_spec,
        out_shape=[out] * 3
        + [
            jax.ShapeDtypeStruct((per, 3 * LANE, LANE), f32),
            jax.ShapeDtypeStruct((8, LANE), f32),
        ]
        + [jax.ShapeDtypeStruct((width, STEP), bf16)] * 3,
        compiler_params=params(1, 60),
        name="attend_back",
    )(lengths, q, k, v, mix, dmix, tail, near_t, normt)


def table_body(tacc, out):
    total = jnp.zeros((8, 4 * LANE), f32)
    for group in range(3 * LANE // 8):
        part = tacc[0, group * 8 : (group + 1) * 8, :]
        wide = jnp.concatenate([part, jnp.zeros((8, 3 * LANE), f32)], axis=1)
        total = total + (pltpu.roll(wide, 4 * LANE - 8 * group, 1) if group else wide)
    line = total[0:1]
    for row in range(1, 8):
        line = line + pltpu.roll(total[row : row + 1], 4 * LANE - row, 1)
    out[0] = line


def table_sums(tacc, far_sum, buckets):
    heads = tacc.shape[0]
    diagonals = pl.pallas_call(
        table_body,
        grid=(heads,),
        in_specs=[pl.BlockSpec((1, 3 * LANE, LANE), lambda h: (h, 0, 0))],
        out_specs=pl.BlockSpec((1, 1, 4 * LANE), lambda h: (h, 0, 0)),
        out_shape=jax.ShapeDtypeStruct((heads, 1, 4 * LANE), f32),
        name="table_diagonals",
    )(tacc)
    place = jnp.arange(4 * LANE, dtype=jnp.int32)
    back = jnp.where(place < LANE, place, place - 4 * LANE)
    hot = bucket_of(-back - LANE, buckets)[:, None] == jnp.arange(buckets, dtype=jnp.int32)
    near = jnp.einsum(
        "rb,hr->bh", hot.astype(f32), diagonals[:, 0, :], precision=lax.Precision.HIGHEST
    )
    quads = far_sum.shape[0]
    pairs = far_sum[:, :4, :16].reshape(quads, 2, 2, 2, 8).sum(axis=-1)
    sides = jnp.transpose(pairs, (2, 0, 1, 3)).reshape(2, heads)
    half = buckets // 2
    near = near.at[half - 1].add(sides[0])
    return near.at[buckets - 1].add(sides[1])


CHUNK = 512
GELU_K = math.sqrt(2.0 / math.pi)


def ff_body(
    scal, xl, xr, gl, gr, mix, w_out, gain, w_gate, w_up, w_down,
    lo_out, lo_send, dh_out, dmix_out, dw_out, dgain_out,
    dwo, dwg, dwu, dwd, stage, sems,
):
    step = pl.program_id(0)
    last = pl.num_programs(0) - 1
    own = lax.rem(step, 2) == 0
    width = gain.shape[1]
    hidden_units = w_gate.shape[1]

    @pl.when(step == 0)
    def _():
        dwo[...] = jnp.zeros(dwo.shape, f32)
        dwg[...] = jnp.zeros(dwg.shape, f32)
        dwu[...] = jnp.zeros(dwu.shape, f32)
        dwd[...] = jnp.zeros(dwd.shape, f32)
        dgain_out[...] = jnp.zeros(dgain_out.shape, f32)

    g = jnp.where(own, gl[0], gr[0])
    x = jnp.where(own, xl[0], xr[0]).astype(f32)
    quads = mix.shape[1]
    mixed = jnp.concatenate([mix[0, i] for i in range(quads)], axis=1)
    hidden = x + mm(mixed, w_out[...])
    gain_f = gain[...].astype(f32)
    scale = rms_of(hidden)
    unit = hidden * scale
    normed = (unit * gain_f).astype(bf16)
    normed_t = normed.T
    g_t = g.T
    out = hidden
    dn = jnp.zeros_like(hidden)
    for c in range(hidden_units // CHUNK):
        cols = slice(c * CHUNK, (c + 1) * CHUNK)
        gate = mm(normed, w_gate[:, cols])
        up = mm(normed, w_up[:, cols])
        d_act = mm(g, w_down[cols, :], NT)
        square = gate * gate
        th = jnp.tanh(gate * (GELU_K + (GELU_K * 0.044715) * square))
        half = 0.5 + 0.5 * th
        gelu = gate * half
        slope = half + (0.5 * gate) * (1.0 - th * th) * (
            GELU_K + (3.0 * 0.044715 * GELU_K) * square
        )
        act = (gelu * up).astype(bf16)
        d_gate = (d_act * up * slope).astype(bf16)
        d_up = (d_act * gelu).astype(bf16)
        out = out + mm(act, w_down[cols, :])
        dn = dn + mm(d_gate, w_gate[:, cols], NT) + mm(d_up, w_up[:, cols], NT)
        dwd[:, cols] += mm(g_t, act)
        dwg[:, cols] += mm(normed_t, d_gate)
        dwu[:, cols] += mm(normed_t, d_up)

    @pl.when(own)
    def _():
        lo_out[0] = out

    @pl.when(jnp.logical_not(own))
    def _():
        lo_send[0] = out.astype(bf16)

    dgain_out[...] += jnp.sum(dn * unit, axis=0, keepdims=True)
    e = dn * gain_f
    d_hidden = (
        g.astype(f32) + scale * e - unit * (scale * jnp.mean(unit * e, axis=-1, keepdims=True))
    )
    dh_out[0] = d_hidden
    low = d_hidden.astype(bf16)
    dwo[...] += mm(mixed.T, low)
    d_mixed = mm(low, w_out[...], NT).astype(bf16)
    for i in range(quads):
        dmix_out[0, i] = d_mixed[:, i * STEP : (i + 1) * STEP]

    @pl.when(step == last)
    def _():
        rows = stage.shape[1]
        jobs = []
        place = 0
        for acc in (dwg, dwu, dwd, dwo):
            for part in range(acc.shape[0] // rows):
                jobs.append((acc, place, part))
            place += acc.shape[1]
        pending = [None, None]
        for n, (acc, place, part) in enumerate(jobs):
            slot = n % 2
            if pending[slot] is not None:
                pending[slot].wait()
            cols = acc.shape[1]
            span = slice(part * rows, (part + 1) * rows)
            stage[slot, :, :cols] = acc[span, :].astype(bf16)
            copy = pltpu.make_async_copy(
                stage.at[slot, :, pl.ds(0, cols)],
                dw_out.at[pl.ds(part * rows, rows), pl.ds(place, cols)],
                sems.at[slot],
            )
            copy.start()
            pending[slot] = copy
        for copy in pending:
            copy.wait()


def feed_forward(scal, inputs, x_remote, cot, cot_remote, mix, w_out, gain, w_gate, w_up, w_down):
    rows, half, width = inputs.shape
    mine = x_remote.shape[0]
    _, quads, extent, _ = mix.shape
    units = w_gate.shape[1]
    inner = w_out.shape[0]

    def keep(shape):
        return pl.BlockSpec(shape, lambda i, s: (0,) * len(shape), pipeline_mode=pl.Buffered(1))

    local = pl.BlockSpec((1, half, width), lambda i, s: (s[1 + i // 2], 0, 0))
    far = pl.BlockSpec((1, half, width), lambda i, s: (i // 2, 0, 0))
    far_one = pl.BlockSpec(
        (1, half, width), lambda i, s: (i // 2, 0, 0), pipeline_mode=pl.Buffered(1)
    )
    spot = pl.BlockSpec(
        (1, quads, half, STEP),
        lambda i, s: (i // 2, 0, jnp.where(i % 2 == 0, s[0], 1 - s[0]), 0),
    )
    anywhere = pl.BlockSpec(memory_space=pl.ANY)
    grid_spec = pltpu.PrefetchScalarGridSpec(
        num_scalar_prefetch=1,
        grid=(2 * mine,),
        in_specs=[local, far_one, local, far_one, spot, keep((inner, width)), keep((1, width)),
                  keep((width, units)), keep((width, units)), keep((units, width))],
        out_specs=[
            local,
            far,
            pl.BlockSpec((1, half, width), lambda i, s: (i, 0, 0)),
            spot,
            anywhere,
            pl.BlockSpec((1, width), lambda i, s: (0, 0)),
        ],
        scratch_shapes=[
            pltpu.VMEM((inner, width), f32),
            pltpu.VMEM((width, units), f32),
            pltpu.VMEM((width, units), f32),
            pltpu.VMEM((width, units), f32),
            pltpu.VMEM((2, 32, units), bf16),
            pltpu.SemaphoreType.DMA((2,)),
        ],
    )
    return pl.pallas_call(
        ff_body,
        grid_spec=grid_spec,
        out_shape=[
            jax.ShapeDtypeStruct((rows, half, width), f32),
            jax.ShapeDtypeStruct((mine, half, width), bf16),
            jax.ShapeDtypeStruct((2 * mine, half, width), f32),
            jax.ShapeDtypeStruct((mine, quads, extent, STEP), bf16),
            jax.ShapeDtypeStruct((width, 3 * units + width), bf16),
            jax.ShapeDtypeStruct((1, width), f32),
        ],
        compiler_params=params(1, 63),
        name="feed_forward",
    )(scal, inputs, x_remote, cot, cot_remote, mix, w_out, gain, w_gate, w_up, w_down)


def back_body(scal, xl, xr, dh, *rest):
    quads = (len(rest) - 4 - 3) // 3
    grads = rest[: 3 * quads]
    gain, wq, wk, wv, ig_out, ig_send, dgain_out = rest[3 * quads :]
    step = pl.program_id(0)
    own = lax.rem(step, 2) == 0

    @pl.when(step == 0)
    def _():
        dgain_out[...] = jnp.zeros(dgain_out.shape, f32)

    x = jnp.where(own, xl[0], xr[0]).astype(f32)
    dn = jnp.zeros_like(x)
    for n, weight in enumerate((wq, wk, wv)):
        part = jnp.concatenate([ref[0] for ref in grads[n * quads : (n + 1) * quads]], axis=1)
        dn = dn + mm(part, weight[...], NT)
    scale = rms_of(x)
    unit = x * scale
    dgain_out[...] += jnp.sum(dn * unit, axis=0, keepdims=True)
    e = dn * gain[...].astype(f32)
    out = dh[0] + scale * e - unit * (scale * jnp.mean(unit * e, axis=-1, keepdims=True))

    @pl.when(own)
    def _():
        ig_out[0] = out

    @pl.when(jnp.logical_not(own))
    def _():
        ig_send[0] = out.astype(bf16)


def input_back(scal, inputs, x_remote, dh, dq, dk, dv, gain, wq, wk, wv):
    rows, half, width = inputs.shape
    mine = x_remote.shape[0]
    local = pl.BlockSpec((1, half, width), lambda i, s: (s[1 + i // 2], 0, 0))
    far = pl.BlockSpec((1, half, width), lambda i, s: (i // 2, 0, 0))
    tile = pl.BlockSpec((1, half, width), lambda i, s: (i, 0, 0))
    spot = pl.BlockSpec(
        (1, half, STEP), lambda i, s: (i // 2, jnp.where(i % 2 == 0, s[0], 1 - s[0]), 0)
    )
    weight = pl.BlockSpec(wq.shape, lambda i, s: (0, 0), pipeline_mode=pl.Buffered(1))
    line = pl.BlockSpec((1, width), lambda i, s: (0, 0))
    grads = [*dq, *dk, *dv]
    grid_spec = pltpu.PrefetchScalarGridSpec(
        num_scalar_prefetch=1,
        grid=(2 * mine,),
        in_specs=[local, far, tile] + [spot] * len(grads) + [line, weight, weight, weight],
        out_specs=[local, far, line],
    )
    return pl.pallas_call(
        back_body,
        grid_spec=grid_spec,
        out_shape=[
            jax.ShapeDtypeStruct((rows, half, width), f32),
            jax.ShapeDtypeStruct((mine, half, width), bf16),
            jax.ShapeDtypeStruct((1, width), f32),
        ],
        compiler_params=params(1, 56),
        name="input_back",
    )(scal, inputs, x_remote, dh, *grads, gain, wq, wk, wv)


def place_body(scal, arrived, held, out):
    out[0] = arrived[0].astype(f32)


def place_rows(theirs, arrived, held):
    count, half, width = arrived.shape
    grid_spec = pltpu.PrefetchScalarGridSpec(
        num_scalar_prefetch=1,
        grid=(count,),
        in_specs=[
            pl.BlockSpec((1, half, width), lambda i, s: (i, 0, 0)),
            pl.BlockSpec(memory_space=pl.ANY),
        ],
        out_specs=pl.BlockSpec((1, half, width), lambda i, s: (s[i], 0, 0)),
    )
    return pl.pallas_call(
        place_body,
        grid_spec=grid_spec,
        out_shape=jax.ShapeDtypeStruct(held.shape, f32),
        input_output_aliases={2: 0},
        compiler_params=params(1, 32),
        name="place_rows",
    )(theirs, arrived, held)


highest = lax.Precision.HIGHEST


def rms_scaled(values, gain):
    mean_square = jnp.mean(values * values, axis=-1, keepdims=True)
    return values * lax.rsqrt(mean_square + epsilon) * gain


def gated_unit(gate, up_proj):
    return jax.nn.gelu(gate, approximate=True) * up_proj


def relative_one_hot(query_anchor, query_extent, key_extent, bucket_count):
    query_place = query_anchor + jnp.arange(query_extent, dtype=jnp.int32)
    key_place = jnp.arange(key_extent, dtype=jnp.int32)
    offset = key_place[None, :] - query_place[:, None]
    distance = jnp.abs(offset)
    far_bucket = jnp.full_like(distance, 8)
    for threshold in bucket_bounds:
        far_bucket = far_bucket + (distance >= threshold).astype(jnp.int32)
    bucket = jnp.where(offset > 0, bucket_count // 2, 0) + jnp.where(
        distance < 8, distance, far_bucket
    )
    return (bucket[:, :, None] == jnp.arange(bucket_count, dtype=jnp.int32)).astype(jnp.float32)


def block_scores(query_heads, key_heads, query_anchor, lengths, bias_f):
    key_extent = key_heads.shape[1]
    one_hot = relative_one_hot(query_anchor, query_heads.shape[1], key_extent, bias_f.shape[0])
    bias_block = jnp.einsum("qkb,bh->hqk", one_hot, bias_f, precision=highest)
    raw_scores = jnp.einsum(
        "rqhd,rkhd->rhqk", query_heads, key_heads, preferred_element_type=jnp.float32
    )
    usable = jnp.arange(key_extent, dtype=jnp.int32)[None, :] < lengths[:, None]
    return (
        jnp.where(usable[:, None, None, :], raw_scores + bias_block[None], masked_score),
        one_hot,
    )


def score_grads(scores, log_total, row_dot, grad_heads, value_heads):
    weights_hp = jnp.exp(scores - log_total[..., None])
    d_weights = jnp.einsum(
        "rqhd,rkhd->rhqk", grad_heads, value_heads, preferred_element_type=jnp.float32
    )
    d_scores = (weights_hp * (d_weights - row_dot[..., None])).astype(jnp.bfloat16)
    return (weights_hp.astype(jnp.bfloat16), d_scores)


def table_term(one_hot, d_scores):
    summed = jnp.sum(d_scores, axis=0, dtype=jnp.float32)
    return jnp.einsum("qkb,hqk->bh", one_hot, summed, precision=highest)


def gathered_device(
    inputs,
    lengths,
    cotangent,
    norm_gain,
    w_query,
    w_key,
    w_value,
    w_out,
    ff_gain,
    w_gate,
    w_up,
    w_down,
    bias_table,
):
    row_count, block_len, model_width = inputs.shape
    head_count = bias_table.shape[1]
    inner_width = w_query.shape[1]
    head_width = inner_width // head_count
    tokens_here = row_count * block_len
    lengths = lengths.reshape(-1)
    bias_f = bias_table.astype(jnp.float32)
    own_anchor = lax.axis_index("seq") * block_len

    def split_heads(block_array):
        return block_array.reshape(row_count, block_array.shape[1], head_count, head_width)

    tokens_f = inputs.astype(jnp.float32).reshape(tokens_here, model_width)
    normed_f, norm_pull = jax.vjp(rms_scaled, tokens_f, norm_gain.astype(jnp.float32))
    normed = normed_f.astype(jnp.bfloat16)
    queries = (
        jnp.dot(normed, w_query, preferred_element_type=jnp.float32)
        .astype(jnp.bfloat16)
        .reshape(row_count, block_len, inner_width)
    )
    keys = (
        jnp.dot(normed, w_key, preferred_element_type=jnp.float32)
        .astype(jnp.bfloat16)
        .reshape(row_count, block_len, inner_width)
    )
    values = (
        jnp.dot(normed, w_value, preferred_element_type=jnp.float32)
        .astype(jnp.bfloat16)
        .reshape(row_count, block_len, inner_width)
    )
    query_heads = split_heads(queries)
    stat_shape = (row_count, head_count, block_len)
    pieces = (
        lax.all_gather(keys, "seq", axis=1, tiled=True),
        lax.all_gather(values, "seq", axis=1, tiled=True),
    )
    row_max = jnp.full(stat_shape, start_max, jnp.float32)
    key_heads = split_heads(pieces[0])
    value_heads = split_heads(pieces[1])
    scores, one_hot = block_scores(query_heads, key_heads, own_anchor, lengths, bias_f)
    new_max = jnp.maximum(row_max, jnp.max(scores, axis=-1))
    weights_hp = jnp.exp(scores - new_max[..., None])
    row_sum = jnp.sum(weights_hp, axis=-1)
    weighted = jnp.einsum(
        "rhqk,rkhd->rhqd",
        weights_hp.astype(jnp.bfloat16),
        value_heads,
        preferred_element_type=jnp.float32,
    )
    row_max, row_sum, weighted = (new_max, row_sum, weighted)
    log_total = row_max + jnp.log(row_sum)
    mixed_heads = jnp.transpose(weighted / row_sum[..., None], (0, 2, 1, 3))
    mixed_low = mixed_heads.reshape(tokens_here, inner_width).astype(jnp.bfloat16)
    hidden = tokens_f + jnp.dot(mixed_low, w_out, preferred_element_type=jnp.float32)
    normed2_f, ff_pull = jax.vjp(rms_scaled, hidden, ff_gain.astype(jnp.float32))
    normed2 = normed2_f.astype(jnp.bfloat16)
    gate = jnp.dot(normed2, w_gate, preferred_element_type=jnp.float32)
    up_proj = jnp.dot(normed2, w_up, preferred_element_type=jnp.float32)
    activated, gated_pull = jax.vjp(gated_unit, gate, up_proj)
    act_low = activated.astype(jnp.bfloat16)
    layer_output = (hidden + jnp.dot(act_low, w_down, preferred_element_type=jnp.float32)).reshape(
        row_count, block_len, model_width
    )
    grad_out = cotangent.reshape(tokens_here, model_width)
    dw_down = jnp.einsum("tf,td->fd", act_low, grad_out, preferred_element_type=jnp.float32)
    d_act = jnp.einsum("td,fd->tf", grad_out, w_down, preferred_element_type=jnp.float32)
    d_gate, d_up = gated_pull(d_act)
    d_gate = d_gate.astype(jnp.bfloat16)
    d_up = d_up.astype(jnp.bfloat16)
    dw_gate = jnp.einsum("td,tf->df", normed2, d_gate, preferred_element_type=jnp.float32)
    dw_up = jnp.einsum("td,tf->df", normed2, d_up, preferred_element_type=jnp.float32)
    d_normed2 = jnp.einsum(
        "tf,df->td", d_gate, w_gate, preferred_element_type=jnp.float32
    ) + jnp.einsum("tf,df->td", d_up, w_up, preferred_element_type=jnp.float32)
    d_hidden_part, d_ff_gain = ff_pull(d_normed2)
    d_hidden = grad_out.astype(jnp.float32) + d_hidden_part
    d_hidden_low = d_hidden.astype(jnp.bfloat16)
    dw_out = jnp.einsum("ti,td->id", mixed_low, d_hidden_low, preferred_element_type=jnp.float32)
    d_mixed = (
        jnp.einsum("td,id->ti", d_hidden_low, w_out, preferred_element_type=jnp.float32)
        .astype(jnp.bfloat16)
        .reshape(row_count, block_len, inner_width)
    )
    grad_heads = split_heads(d_mixed)
    row_dot_rows = jnp.sum(grad_heads.astype(jnp.float32) * mixed_heads, axis=-1)
    row_dot = jnp.transpose(row_dot_rows, (0, 2, 1))
    pieces = (
        lax.all_gather(keys, "seq", axis=1, tiled=True),
        lax.all_gather(values, "seq", axis=1, tiled=True),
    )
    key_heads = split_heads(pieces[0])
    value_heads = split_heads(pieces[1])
    scores, one_hot = block_scores(query_heads, key_heads, own_anchor, lengths, bias_f)
    weights_low, d_scores = score_grads(scores, log_total, row_dot, grad_heads, value_heads)
    d_query_part = jnp.einsum(
        "rhqk,rkhd->rqhd", d_scores, key_heads, preferred_element_type=jnp.float32
    )
    key_heads, weights_low, d_scores, d_query_part, table_part = (
        key_heads,
        weights_low,
        d_scores,
        d_query_part,
        table_term(one_hot, d_scores),
    )
    extent = key_heads.shape[1]
    d_key_part = jnp.einsum(
        "rhqk,rqhd->rkhd", d_scores, query_heads, preferred_element_type=jnp.float32
    ).reshape(row_count, extent, inner_width)
    d_value_part = jnp.einsum(
        "rhqk,rqhd->rkhd", weights_low, grad_heads, preferred_element_type=jnp.float32
    ).reshape(row_count, extent, inner_width)
    d_key, d_value = (
        lax.psum_scatter(d_key_part, "seq", scatter_dimension=1, tiled=True),
        lax.psum_scatter(d_value_part, "seq", scatter_dimension=1, tiled=True),
    )
    d_query_low = d_query_part.reshape(tokens_here, inner_width).astype(jnp.bfloat16)
    d_key_low = d_key.reshape(tokens_here, inner_width).astype(jnp.bfloat16)
    d_value_low = d_value.reshape(tokens_here, inner_width).astype(jnp.bfloat16)
    dw_query = jnp.einsum("td,ti->di", normed, d_query_low, preferred_element_type=jnp.float32)
    dw_key = jnp.einsum("td,ti->di", normed, d_key_low, preferred_element_type=jnp.float32)
    dw_value = jnp.einsum("td,ti->di", normed, d_value_low, preferred_element_type=jnp.float32)
    d_normed = jnp.einsum("ti,di->td", d_query_low, w_query, preferred_element_type=jnp.float32)
    d_normed = d_normed + jnp.einsum(
        "ti,di->td", d_key_low, w_key, preferred_element_type=jnp.float32
    )
    d_normed = d_normed + jnp.einsum(
        "ti,di->td", d_value_low, w_value, preferred_element_type=jnp.float32
    )
    d_tokens_part, d_norm_gain = norm_pull(d_normed)
    input_grad = (d_hidden + d_tokens_part).reshape(row_count, block_len, model_width)
    flat_query = dw_query.reshape(-1)
    flat_key = dw_key.reshape(-1)
    flat_value = dw_value.reshape(-1)
    flat_out = dw_out.reshape(-1)
    flat_gate = dw_gate.reshape(-1)
    flat_up = dw_up.reshape(-1)
    flat_down = dw_down.reshape(-1)
    shares = (
        lax.psum_scatter(flat_query, ("batch", "seq"), scatter_dimension=0, tiled=True),
        lax.psum_scatter(flat_key, ("batch", "seq"), scatter_dimension=0, tiled=True),
        lax.psum_scatter(flat_value, ("batch", "seq"), scatter_dimension=0, tiled=True),
        lax.psum_scatter(flat_out, ("batch", "seq"), scatter_dimension=0, tiled=True),
        lax.psum_scatter(flat_gate, ("batch", "seq"), scatter_dimension=0, tiled=True),
        lax.psum_scatter(flat_up, ("batch", "seq"), scatter_dimension=0, tiled=True),
        lax.psum_scatter(flat_down, ("batch", "seq"), scatter_dimension=0, tiled=True),
    )
    summed = (
        lax.all_gather(shares[0], ("batch", "seq"), axis=0, tiled=True),
        lax.all_gather(shares[1], ("batch", "seq"), axis=0, tiled=True),
        lax.all_gather(shares[2], ("batch", "seq"), axis=0, tiled=True),
        lax.all_gather(shares[3], ("batch", "seq"), axis=0, tiled=True),
        lax.all_gather(shares[4], ("batch", "seq"), axis=0, tiled=True),
        lax.all_gather(shares[5], ("batch", "seq"), axis=0, tiled=True),
        lax.all_gather(shares[6], ("batch", "seq"), axis=0, tiled=True),
    )
    sum_norm, sum_ff, sum_table = lax.psum((d_norm_gain, d_ff_gain, table_part), ("batch", "seq"))
    return (
        layer_output,
        input_grad,
        sum_norm,
        summed[0].reshape(w_query.shape),
        summed[1].reshape(w_key.shape),
        summed[2].reshape(w_value.shape),
        summed[3].reshape(w_out.shape),
        sum_ff,
        summed[4].reshape(w_gate.shape),
        summed[5].reshape(w_up.shape),
        summed[6].reshape(w_down.shape),
        sum_table,
    )


def split_rows(lengths, side):
    rows = lengths.shape[0]
    choices = [c for c in itertools.combinations(range(rows), rows // 2) if 0 in c]
    first = jnp.array(choices, jnp.int32)
    other = [[r for r in range(rows) if r not in c] for c in choices]
    second = jnp.array(other, jnp.int32)
    load = (lengths + STEP - 1) // STEP
    uneven = jnp.abs(jnp.sum(load[first], axis=1) - jnp.sum(load[second], axis=1))
    pick = jnp.argmin(uneven)
    one, two = first[pick], second[pick]
    return jnp.where(side == 0, one, two), jnp.where(side == 0, two, one)


def all_pairs(mesh_batch, mesh_seq, move):
    pairs = []
    for batch in range(mesh_batch):
        for seq in range(mesh_seq):
            z, y, core, x = move(batch // 4, batch // 2 % 2, batch % 2, seq)
            pairs.append((batch * mesh_seq + seq, (z * 4 + y * 2 + core) * mesh_seq + x))
    return pairs


def add_up(parts):
    total = parts[0].astype(f32)
    for part in parts[1:]:
        total = total + part.astype(f32)
    return total


class Links:
    def __init__(self, batch, seq):
        self.axes = ("batch", "seq")
        self.deep = batch // 4
        me = lax.axis_index("batch")
        self.z, self.y, self.core = me // 4, me // 2 % 2, me % 2
        self.x = lax.axis_index("seq")
        self.plane = self.y * 2 + self.x
        pairs = functools.partial(all_pairs, batch, seq)
        self.to_core = pairs(lambda z, y, c, x: (z, y, 1 - c, x))
        self.to_plane = {
            k: pairs(lambda z, y, c, x, k=k: (z, y ^ (k >> 1), c, x ^ (k & 1))) for k in (1, 2, 3)
        }
        self.to_deep = {
            k: pairs(lambda z, y, c, x, k=k: ((z + k) % self.deep, y, c, x))
            for k in range(1, self.deep)
        }

    def send(self, value, pairs):
        return lax.ppermute(value, self.axes, pairs)

    def pick(self, value, at):
        return lax.dynamic_index_in_dim(value, at, 0, keepdims=False)

    def scatter_core(self, grads):
        rows, columns = grads.shape
        each = rows // (8 * self.deep)
        split = grads.reshape(2, 4, self.deep, each, columns)
        got = self.send(self.pick(split, 1 - self.core), self.to_core)
        return add_up([self.pick(split, self.core), got]).astype(bf16)

    def scatter_plane(self, part):
        got = [self.send(self.pick(part, self.plane ^ k), self.to_plane[k]) for k in (1, 2, 3)]
        return add_up([self.pick(part, self.plane), *got]).astype(bf16)

    def scatter_deep(self, part):
        got = [
            self.send(self.pick(part, (self.z + k) % self.deep), self.to_deep[k])
            for k in range(1, self.deep)
        ]
        return add_up([self.pick(part, self.z), *got]).astype(bf16)

    def lay(self, count, at, own, got):
        out = jnp.zeros((count,) + own.shape, own.dtype)
        out = lax.dynamic_update_index_in_dim(out, own, at, 0)
        for place, piece in got:
            out = lax.dynamic_update_index_in_dim(out, piece, place, 0)
        return out

    def gather_deep(self, part):
        got = [
            ((self.z - k) % self.deep, self.send(part, self.to_deep[k]))
            for k in range(1, self.deep)
        ]
        return self.lay(self.deep, self.z, part, got)

    def gather_plane(self, part):
        got = [(self.plane ^ k, self.send(part, self.to_plane[k])) for k in (1, 2, 3)]
        return self.lay(4, self.plane, part, got)

    def gather_core(self, part):
        out = self.lay(2, self.core, part, [(1 - self.core, self.send(part, self.to_core))])
        return out.reshape(-1, out.shape[-1])

    def total(self, grads):
        part = self.scatter_deep(self.scatter_plane(self.scatter_core(grads)))
        return self.gather_core(self.gather_plane(self.gather_deep(part)))

    def total_small(self, value):
        value = add_up([value, self.send(value, self.to_core)])
        value = add_up([value, *[self.send(value, self.to_plane[k]) for k in (1, 2, 3)]])
        return add_up([value, *[self.send(value, p) for p in self.to_deep.values()]])


def rows_device(
    batch,
    seq,
    inputs,
    lengths,
    cotangent,
    norm_gain,
    w_query,
    w_key,
    w_value,
    w_out,
    ff_gain,
    w_gate,
    w_up,
    w_down,
    bias_table,
):
    rows, half, width = inputs.shape
    buckets, heads = bias_table.shape
    units = w_gate.shape[1]
    mine_count = rows // 2
    lengths = lengths.reshape(-1)
    links = Links(batch, seq)
    side = links.x
    mine, theirs = split_rows(lengths, side)
    swap = [(0, 1), (1, 0)]

    def exchange(array, row):
        return lax.ppermute(lax.dynamic_slice_in_dim(array, theirs[row], 1, 0), "seq", swap)

    x_parts = [exchange(inputs, row) for row in range(mine_count)]
    g_parts = [exchange(cotangent, row) for row in range(mine_count)]
    near, near_t, far = bias_pieces(bias_table, 2 * half // LANE)
    gain = norm_gain.reshape(1, width)
    gain2 = ff_gain.reshape(1, width)
    held = []
    for row in range(mine_count):
        scal = jnp.stack([lengths[mine[row]], mine[row], side])
        held = fwd_row(
            scal, inputs, x_parts[row], row, mine_count, held,
            gain, w_query, w_key, w_value, near, far, heads,
        )
    q, k, v, mix, tail, normt = held
    x_remote = jnp.concatenate(x_parts, axis=0)
    g_remote = jnp.concatenate(g_parts, axis=0)
    places = jnp.concatenate([side[None], mine])
    lo, lo_send, dh, dmix, ff_grads, ff_gain_part = feed_forward(
        places, inputs, x_remote, cotangent, g_remote, mix,
        w_out, gain2, w_gate, w_up, w_down,
    )
    lo_got = lax.ppermute(lo_send, "seq", swap)
    ff_total = links.total(ff_grads)
    layer_output = place_rows(theirs, lo_got, lo)
    own_lengths = lengths[mine]
    quads = q.shape[1]
    backs = [
        bwd_quad(own_lengths, quad, q, k, v, mix, dmix, tail, near_t, normt)
        for quad in range(quads)
    ]
    dq, dk, dv, tacc, far_sum, dwq, dwk, dwv = zip(*backs)
    qkv_total = [
        links.total(jnp.concatenate([dwq[n], dwk[n], dwv[n]], axis=1)) for n in range(quads)
    ]
    ig, ig_send, gain_part = input_back(
        places, inputs, x_remote, dh, dq, dk, dv, gain, w_query, w_key, w_value
    )
    ig_got = lax.ppermute(ig_send, "seq", swap)
    input_grad = place_rows(theirs, ig_got, ig)
    table_part = table_sums(jnp.concatenate(tacc, axis=0), jnp.stack(far_sum), buckets)
    small = jnp.concatenate([gain_part[0], ff_gain_part[0], table_part.reshape(-1)])
    small = links.total_small(small)
    ff_all = ff_total.astype(f32)

    def whole(n):
        return jnp.concatenate(
            [part[:, n * STEP : (n + 1) * STEP] for part in qkv_total], axis=1
        ).astype(f32)

    return (
        layer_output,
        input_grad,
        small[:width],
        whole(0),
        whole(1),
        whole(2),
        ff_all[:, 3 * units :],
        small[width : 2 * width],
        ff_all[:, :units],
        ff_all[:, units : 2 * units],
        ff_all[:, 2 * units : 3 * units].T,
        small[2 * width :].reshape(buckets, heads),
    )


def solution(mesh):
    split = P("batch", "seq", None)
    in_specs = (split, P("batch", None), split) + (P(),) * 10
    out_specs = (split, split) + (P(),) * 10
    batch, seq = mesh.shape["batch"], mesh.shape["seq"]

    def per_device(inputs, *rest):
        rows, half, width = inputs.shape
        buckets, heads = rest[-1].shape
        inner = rest[3].shape[1]
        fits = seq == 2 and batch % 4 == 0 and rows % 2 == 0 and buckets == 32
        fits = fits and half % STEP == 0 and 2 * half // LANE <= 8
        fits = fits and inner == width and width % (16 * batch) == 0 and inner // heads == LANE // 2
        if fits:
            return rows_device(batch, seq, inputs, *rest)
        return gathered_device(inputs, *rest)

    return jax.shard_map(
        per_device, mesh=mesh, in_specs=in_specs, out_specs=out_specs, check_vma=False
    )
```

```python
import functools
import itertools
import math

import jax
import jax.numpy as jnp
from jax import lax
from jax.experimental import pallas as pl
from jax.experimental.pallas import tpu as pltpu
from jax.sharding import PartitionSpec as P

f32 = jnp.float32
bf16 = jnp.bfloat16
epsilon = 1e-06
masked_score = -2e30
start_max = -1e30
bucket_bounds = (12, 16, 23, 32, 46, 64, 91)
LANE = 128
STEP = 256
NT = (((1,), (1,)), ((), ()))
NN = (((1,), (0,)), ((), ()))
TN = (((0,), (0,)), ((), ()))


def mm(a, b, dims=NN):
    return lax.dot_general(a, b, dims, preferred_element_type=f32)


def cost(micros):
    return pl.CostEstimate(flops=int(micros * 0.3e9), bytes_accessed=0, transcendentals=0)


def params(grid_dims, mib):
    return pltpu.CompilerParams(
        dimension_semantics=("arbitrary",) * grid_dims, vmem_limit_bytes=mib << 20
    )


def bucket_of(offset, bucket_count):
    distance = jnp.abs(offset)
    far = jnp.full_like(distance, 8)
    for bound in bucket_bounds:
        far = far + (distance >= bound).astype(jnp.int32)
    half = bucket_count // 2
    return jnp.where(offset > 0, half, 0) + jnp.where(distance < 8, distance, far)


def split_body(choices, side, lengths, out):
    rows = lengths.shape[1]
    count = rows // 2
    load = [(lengths[0, r] + STEP - 1) // STEP for r in range(rows)]
    best = None
    for own in choices:
        other = [r for r in range(rows) if r not in own]
        uneven = jnp.abs(sum(load[r] for r in own) - sum(load[r] for r in other))
        new = [*own, *other]
        if best is None:
            best, picked = uneven, [jnp.int32(r) for r in new]
        else:
            better = uneven < best
            best = jnp.where(better, uneven, best)
            picked = [jnp.where(better, r, old) for r, old in zip(new, picked)]
    first = side[0] == 0
    out[0] = side[0]
    for n in range(count):
        mine = jnp.where(first, picked[n], picked[count + n])
        out[1 + n] = mine
        out[1 + count + n] = jnp.where(first, picked[count + n], picked[n])
        out[1 + 2 * count + n] = lengths[0, mine]


def split_rows(lengths, side):
    rows = lengths.shape[1]
    choices = [c for c in itertools.combinations(range(rows), rows // 2) if 0 in c]
    smem = pl.BlockSpec(memory_space=pltpu.SMEM)
    return pl.pallas_call(
        functools.partial(split_body, choices),
        in_specs=[smem, smem],
        out_specs=smem,
        out_shape=jax.ShapeDtypeStruct((1 + 3 * (rows // 2),), jnp.int32),
        name="split_rows",
    )(side.reshape(1), lengths)


def near_body(vec_ref, rev_ref, near_ref, near_t_ref):
    wide = jnp.broadcast_to(vec_ref[0], (LANE, 4 * LANE))
    near_ref[0] = pltpu.roll(wide, 0, 1, stride=1, stride_axis=0)[:, : 3 * LANE]
    tall = jnp.broadcast_to(rev_ref[0], (3 * LANE, 4 * LANE))
    near_t_ref[0] = pltpu.roll(tall, 0, 1, stride=1, stride_axis=0)[:, :LANE]


def near_offsets():
    place = jnp.arange(4 * LANE, dtype=jnp.int32)
    signed = jnp.where(place < 3 * LANE, place, place - 4 * LANE)
    forward = signed - LANE
    back = jnp.where(place < LANE, place, place - 4 * LANE)
    reverse = -back - LANE
    return forward, reverse


def bias_pieces(bias_table, tile_count):
    buckets, heads = bias_table.shape
    table = bias_table.astype(f32)
    forward, reverse = near_offsets()

    def spread(offset):
        hot = bucket_of(offset, buckets)[:, None] == jnp.arange(buckets, dtype=jnp.int32)
        picked = jnp.einsum("rb,bh->hr", hot.astype(f32), table, precision=lax.Precision.HIGHEST)
        return picked[:, None, :]

    near, near_t = pl.pallas_call(
        near_body,
        grid=(heads,),
        in_specs=[pl.BlockSpec((1, 1, 4 * LANE), lambda h: (h, 0, 0))] * 2,
        out_specs=[
            pl.BlockSpec((1, LANE, 3 * LANE), lambda h: (h, 0, 0)),
            pl.BlockSpec((1, 3 * LANE, LANE), lambda h: (h, 0, 0)),
        ],
        out_shape=[
            jax.ShapeDtypeStruct((heads, LANE, 3 * LANE), f32),
            jax.ShapeDtypeStruct((heads, 3 * LANE, LANE), f32),
        ],
        name="near_bias",
    )(spread(forward), spread(reverse))
    left = table[buckets // 2 - 1]
    right = table[buckets - 1]
    tile = jnp.arange(tile_count, dtype=jnp.int32)[None, :, None]
    lane = jnp.arange(LANE, dtype=jnp.int32)[None, None, :]
    far = jnp.where(lane == tile, left[:, None, None], 0.0)
    far = far + jnp.where(lane == tile + 8, right[:, None, None], 0.0)
    far = far + jnp.where(lane == 16, masked_score, 0.0)
    return near, near_t, far.astype(bf16)


def key_lanes(extent, length):
    key = lax.broadcasted_iota(jnp.int32, (extent, LANE), 0)
    lane = lax.broadcasted_iota(jnp.int32, (extent, LANE), 1)
    tile = key // LANE
    flag = (lane < 8) & (tile < lane - 1)
    flag = flag | ((lane >= 8) & (lane < 16) & (tile > lane - 8 + 1))
    flag = flag | ((lane == 16) & (key >= length))
    flag = flag | ((lane >= 17) & (lane < 20))
    return jnp.where(flag, 1.0, 0.0).astype(bf16)


def rms_of(values):
    scale = lax.rsqrt(jnp.mean(values * values, axis=-1, keepdims=True) + epsilon)
    return scale


def head_mask(rows, head):
    lane = lax.broadcasted_iota(jnp.int32, (rows, LANE), 1)
    return (lane // (LANE // 2)) == head


def fwd_body(held, count, which, scal, xl, xr, gain, wq, wk, wv, near, far, *rest):
    q_out, k_out, v_out, mix_out, tail_out, normt_out, normed, lanes = rest[held:]
    extent = normed.shape[0]
    half = xl.shape[1]
    length = scal[1 + 2 * count + which]
    side = scal[0]
    steps = (length + STEP - 1) // STEP

    @pl.when(pl.program_id(0) == 0)
    def _():
        for ref, own in ((xl, True), (xr, False)):
            values = ref[0].astype(f32)
            out = values * rms_of(values) * gain[...].astype(f32)
            place = side * half if own else (1 - side) * half
            normed[pl.ds(pl.multiple_of(place, half), half), :] = out.astype(bf16)
        lanes[...] = key_lanes(extent, length)
        normt_out[0] = normed[...].T

    q_out[0, 0] = mm(normed[...], wq[...]).astype(bf16)
    for part in range(extent // STEP):
        rows = pl.ds(part * STEP, STEP)

        @pl.when(part < steps)
        def _():
            k_out[0, 0, rows, :] = mm(normed[rows, :], wk[...]).astype(bf16)
            v_out[0, 0, rows, :] = mm(normed[rows, :], wv[...]).astype(bf16)

        @pl.when(part >= steps)
        def _():
            k_out[0, 0, rows, :] = jnp.zeros((STEP, 2 * LANE), bf16)
            v_out[0, 0, rows, :] = jnp.zeros((STEP, 2 * LANE), bf16)

    def attend(width):
        def pair_step(pair, carry):
            cols = pl.ds(pl.multiple_of(pair * LANE, LANE), LANE)
            kext = jnp.concatenate([k_out[0, 0, :width, cols], lanes[:width, :]], axis=1)
            vext = jnp.concatenate(
                [v_out[0, 0, :width, cols], jnp.ones((width, LANE), bf16)], axis=1
            )
            lane = lax.broadcasted_iota(jnp.int32, (STEP, LANE), 1)
            for block in range(extent // STEP):
                rows = slice(block * STEP, (block + 1) * STEP)
                qpair = q_out[0, 0, rows, cols]
                outs = []
                for head in range(2):
                    index = 2 * pair + head
                    tiles = []
                    for sub in range(STEP // LANE):
                        line = far[index, pl.ds(block * (STEP // LANE) + sub, 1), :]
                        tiles.append(jnp.broadcast_to(line, (LANE, LANE)))
                    ext = jnp.concatenate(tiles, axis=0)
                    qm = jnp.where(head_mask(STEP, head), qpair, jnp.zeros_like(qpair))
                    scores = mm(jnp.concatenate([qm, ext], axis=1), kext, NT)
                    probs = []
                    tops = []
                    for sub in range(STEP // LANE):
                        tile = block * (STEP // LANE) + sub
                        own = scores[sub * LANE : (sub + 1) * LANE]
                        base = (tile - 1) * LANE
                        low, high = max(0, base), min(width, base + 3 * LANE)
                        if low < high:
                            add = own[:, low:high] + near[index, :, low - base : high - base]
                            pieces = [own[:, :low]] if low > 0 else []
                            pieces.append(add)
                            if high < width:
                                pieces.append(own[:, high:])
                            own = jnp.concatenate(pieces, axis=1)
                        top = jnp.max(own, axis=1, keepdims=True)
                        probs.append(jnp.exp(own - top).astype(bf16))
                        tops.append(top)
                    both = mm(jnp.concatenate(probs, axis=0), vext)
                    total = both[:, LANE:]
                    outs.append(both[:, :LANE] / total)
                    neg = -(jnp.concatenate(tops, axis=0) + jnp.log(total))
                    first = neg.astype(bf16)
                    rest = neg - first.astype(f32)
                    second = rest.astype(bf16)
                    third = (rest - second.astype(f32)).astype(bf16)
                    line = jnp.where(lane == 17, first, ext)
                    line = jnp.where(lane == 18, second, line)
                    line = jnp.where(lane == 19, third, line)
                    tail_out[0, index, rows, :] = line
                picked = jnp.where(head_mask(STEP, 0), outs[0], outs[1])
                mix_out[0, 0, rows, cols] = picked.astype(bf16)
            return carry

        lax.fori_loop(0, 2, pair_step, 0)

    for blocks in range(1, extent // STEP + 1):

        @pl.when(steps == blocks)
        def _():
            attend(blocks * STEP)


def fwd_row(scal, inputs, remote, which, count, held, gain, wq, wk, wv, near, far, heads):
    rows, half, width = inputs.shape
    extent = 2 * half
    inner = wq.shape[1]
    quads = inner // STEP
    per = heads // quads
    weight = pl.BlockSpec((width, STEP), lambda i, s: (0, i))
    block = pl.BlockSpec((1, 1, extent, STEP), lambda i, s: (which, i, 0, 0))
    grid_spec = pltpu.PrefetchScalarGridSpec(
        num_scalar_prefetch=1,
        grid=(quads,),
        in_specs=[
            pl.BlockSpec((1, half, width), lambda i, s: (s[1 + which], 0, 0)),
            pl.BlockSpec((1, half, width), lambda i, s: (0, 0, 0)),
            pl.BlockSpec((1, width), lambda i, s: (0, 0)),
            weight,
            weight,
            weight,
            pl.BlockSpec((per, LANE, 3 * LANE), lambda i, s: (i, 0, 0)),
            pl.BlockSpec((per, 8, LANE), lambda i, s: (i, 0, 0)),
        ]
        + [pl.BlockSpec(memory_space=pl.ANY)] * len(held),
        out_specs=[block] * 4
        + [
            pl.BlockSpec((1, per, extent, LANE), lambda i, s: (which, i, 0, 0)),
            pl.BlockSpec((1, width, extent), lambda i, s: (which, 0, 0)),
        ],
        scratch_shapes=[pltpu.VMEM((extent, width), bf16), pltpu.VMEM((extent, LANE), bf16)],
    )
    stacked = jax.ShapeDtypeStruct((count, quads, extent, STEP), bf16)
    return pl.pallas_call(
        functools.partial(fwd_body, len(held), count, which),
        grid_spec=grid_spec,
        out_shape=[stacked] * 4
        + [
            jax.ShapeDtypeStruct((count, heads, extent, LANE), bf16),
            jax.ShapeDtypeStruct((count, width, extent), bf16),
        ],
        input_output_aliases={9 + n: n for n in range(len(held))},
        compiler_params=params(1, 56),
        cost_estimate=cost(27),
        name="attend_row",
    )(scal, inputs, remote, gain, wq, wk, wv, near, far, *held)


def bwd_body(
    count, scal, q, k, v, mix, dmix, tail, near_t, normt, *rest
):
    (dq_out, dk_out, dv_out, tacc_out, far_out, dw_out) = rest[-15:-9]
    (lanes, pl_s, ds_s, do_s, qa_s, dwq, dwk, dwv, _) = rest[-9:]
    extent = lanes.shape[0]
    row = pl.program_id(0)
    length = scal[1 + 2 * count + row]
    steps = (length + STEP - 1) // STEP
    lanes[...] = key_lanes(extent, length)

    @pl.when(row == 0)
    def _():
        for ref in (tacc_out, far_out, dwq, dwk, dwv):
            ref[...] = jnp.zeros(ref.shape, f32)

    dk_out[...] = jnp.zeros(dk_out.shape, bf16)
    dv_out[...] = jnp.zeros(dv_out.shape, bf16)

    def attend(width):
        def pair_step(pair, carry):
            cols = pl.ds(pl.multiple_of(pair * LANE, LANE), LANE)
            flags = lanes[:width, :]
            kpair = k[0, 0, :width, cols]
            kext = jnp.concatenate([kpair, flags], axis=1)
            vext = jnp.concatenate([v[0, 0, :width, cols], flags], axis=1)
            lane = lax.broadcasted_iota(jnp.int32, (STEP, LANE), 1)
            for block in range(extent // STEP):
                rows = slice(block * STEP, (block + 1) * STEP)
                qpair = q[0, 0, rows, cols]
                dopair = dmix[0, 0, rows, cols]
                product = dopair.astype(f32) * mix[0, 0, rows, cols].astype(f32)
                for head in range(2):
                    index = 2 * pair + head
                    mask = head_mask(STEP, head)
                    qm = jnp.where(mask, qpair, jnp.zeros_like(qpair))
                    dom = jnp.where(mask, dopair, jnp.zeros_like(dopair))
                    neg = -jnp.sum(jnp.where(mask, product, 0.0), axis=1, keepdims=True)
                    neg = jnp.broadcast_to(neg, (STEP, LANE))
                    first = neg.astype(bf16)
                    rest = neg - first.astype(f32)
                    second = rest.astype(bf16)
                    third = (rest - second.astype(f32)).astype(bf16)
                    zero = jnp.zeros((STEP, LANE), bf16)
                    dtail = jnp.where(lane == 17, first, zero)
                    dtail = jnp.where(lane == 18, second, dtail)
                    dtail = jnp.where(lane == 19, third, dtail)
                    st = mm(kext, jnp.concatenate([qm, tail[0, index, rows, :]], axis=1), NT)
                    dp = mm(vext, jnp.concatenate([dom, dtail], axis=1), NT)
                    at = head * extent + block * STEP
                    do_s[at : at + STEP, :] = dom
                    row = lax.broadcasted_iota(jnp.int32, (STEP, LANE), 0)
                    spot = jnp.where(
                        lane == head * 8 + block * (STEP // LANE) + row // LANE, 1.0, 0.0
                    ).astype(bf16)
                    qa_s[at : at + STEP, :] = jnp.concatenate([qm, spot], axis=1)
                    for sub in range(STEP // LANE):
                        tile = block * (STEP // LANE) + sub
                        part = slice(sub * LANE, (sub + 1) * LANE)
                        own = st[:, part]
                        base = (tile - 1) * LANE
                        low, high = max(0, base), min(width, base + 3 * LANE)
                        if low < high:
                            add = own[low:high] + near_t[index, low - base : high - base, :]
                            pieces = [own[:low]] if low > 0 else []
                            pieces.append(add)
                            if high < width:
                                pieces.append(own[high:])
                            own = jnp.concatenate(pieces, axis=0)
                        prob = jnp.exp(own)
                        dst = (prob * dp[:, part]).astype(bf16)
                        spot_at = at + sub * LANE
                        pl_s[:width, spot_at : spot_at + LANE] = prob.astype(bf16)
                        ds_s[:width, spot_at : spot_at + LANE] = dst
                        if low < high:
                            tacc_out[index, low - base : high - base, :] += dst[low:high].astype(
                                f32
                            )
            dv_out[0, :width, cols] = mm(pl_s[:width, :], do_s[...]).astype(bf16)
            dk = mm(ds_s[:width, :], qa_s[...])
            dk_out[0, :width, cols] = dk[:, :LANE].astype(bf16)
            sums = dk[:, LANE:]
            spread = lax.broadcasted_iota(jnp.int32, (width, LANE), 1)
            tile = lax.broadcasted_iota(jnp.int32, (width, LANE), 0) // LANE
            qtile = lax.rem(spread, 8)
            left = jnp.where((tile < qtile - 1) & (spread < 16), sums, 0.0)
            right = jnp.where((tile > qtile + 1) & (spread < 16), sums, 0.0)
            far_out[pl.ds(2 * pair, 1), :] += jnp.sum(left, axis=0, keepdims=True)
            far_out[pl.ds(2 * pair + 1, 1), :] += jnp.sum(right, axis=0, keepdims=True)
            maskk = head_mask(width, 0)
            zerok = jnp.zeros_like(kpair)
            km0 = jnp.where(maskk, kpair, zerok)
            km1 = jnp.where(maskk, zerok, kpair)
            dq = mm(ds_s[:width, :extent], km0, TN) + mm(ds_s[:width, extent:], km1, TN)
            dq_out[0, :, cols] = dq.astype(bf16)
            return carry

        lax.fori_loop(0, 2, pair_step, 0)
        dwk[...] += mm(normt[0, :, :width], dk_out[0, :width, :])
        dwv[...] += mm(normt[0, :, :width], dv_out[0, :width, :])

    for blocks in range(1, extent // STEP + 1):

        @pl.when(steps == blocks)
        def _():
            attend(blocks * STEP)

    dwq[...] += mm(normt[0], dq_out[0])

    @pl.when(row == count - 1)
    def _():
        for n, ref in enumerate((dwq, dwk, dwv)):
            dw_out[:, n * STEP : (n + 1) * STEP] = ref[...].astype(bf16)


def bwd_quad(places, quad, held, q, k, v, mix, dmix, tail, near_t, normt, deps=()):
    count, quads, extent, _ = q.shape
    heads = tail.shape[1]
    width = normt.shape[1]
    per = heads // quads
    block = pl.BlockSpec((1, 1, extent, STEP), lambda i, s: (i, quad, 0, 0))
    given = pl.BlockSpec((1, extent, STEP), lambda i, s: (i, 0, 0))
    grid_spec = pltpu.PrefetchScalarGridSpec(
        num_scalar_prefetch=1,
        grid=(count,),
        in_specs=[block] * 5
        + [
            pl.BlockSpec((1, per, extent, LANE), lambda i, s: (i, quad, 0, 0)),
            pl.BlockSpec((per, 3 * LANE, LANE), lambda i, s: (quad, 0, 0)),
            pl.BlockSpec((1, width, extent), lambda i, s: (i, 0, 0)),
        ]
        + [pl.BlockSpec(memory_space=pl.ANY)] * (len(held) + len(deps)),
        out_specs=[given] * 3
        + [
            pl.BlockSpec((per, 3 * LANE, LANE), lambda i, s: (0, 0, 0)),
            pl.BlockSpec((8, LANE), lambda i, s: (0, 0)),
            pl.BlockSpec((width, 3 * STEP), lambda i, s: (0, quad)),
        ],
        scratch_shapes=[
            pltpu.VMEM((extent, LANE), bf16),
            pltpu.VMEM((extent, 2 * extent), bf16),
            pltpu.VMEM((extent, 2 * extent), bf16),
            pltpu.VMEM((2 * extent, LANE), bf16),
            pltpu.VMEM((2 * extent, 2 * LANE), bf16),
        ]
        + [pltpu.VMEM((width, STEP), f32)] * 3
        + [pltpu.VMEM((8, LANE), f32)],
    )
    out = jax.ShapeDtypeStruct((count, extent, STEP), bf16)
    return pl.pallas_call(
        functools.partial(bwd_body, count),
        grid_spec=grid_spec,
        out_shape=[out] * 3
        + [
            jax.ShapeDtypeStruct((per, 3 * LANE, LANE), f32),
            jax.ShapeDtypeStruct((8, LANE), f32),
            jax.ShapeDtypeStruct((width, 3 * STEP * quads), bf16),
        ],
        input_output_aliases={9: 5} if held else {},
        compiler_params=params(1, 60),
        cost_estimate=cost(48),
        name="attend_back",
    )(places, q, k, v, mix, dmix, tail, near_t, normt, *held, *deps)


def table_body(tacc, out):
    total = jnp.zeros((8, 4 * LANE), f32)
    for group in range(3 * LANE // 8):
        part = tacc[0, group * 8 : (group + 1) * 8, :]
        wide = jnp.concatenate([part, jnp.zeros((8, 3 * LANE), f32)], axis=1)
        total = total + (pltpu.roll(wide, 4 * LANE - 8 * group, 1) if group else wide)
    line = total[0:1]
    for row in range(1, 8):
        line = line + pltpu.roll(total[row : row + 1], 4 * LANE - row, 1)
    out[0] = line


def table_sums(tacc, far_sum, buckets):
    heads = tacc.shape[0]
    diagonals = pl.pallas_call(
        table_body,
        grid=(heads,),
        in_specs=[pl.BlockSpec((1, 3 * LANE, LANE), lambda h: (h, 0, 0))],
        out_specs=pl.BlockSpec((1, 1, 4 * LANE), lambda h: (h, 0, 0)),
        out_shape=jax.ShapeDtypeStruct((heads, 1, 4 * LANE), f32),
        name="table_diagonals",
    )(tacc)
    place = jnp.arange(4 * LANE, dtype=jnp.int32)
    back = jnp.where(place < LANE, place, place - 4 * LANE)
    hot = bucket_of(-back - LANE, buckets)[:, None] == jnp.arange(buckets, dtype=jnp.int32)
    near = jnp.einsum(
        "rb,hr->bh", hot.astype(f32), diagonals[:, 0, :], precision=lax.Precision.HIGHEST
    )
    quads = far_sum.shape[0]
    pairs = far_sum[:, :4, :16].reshape(quads, 2, 2, 2, 8).sum(axis=-1)
    sides = jnp.transpose(pairs, (2, 0, 1, 3)).reshape(2, heads)
    half = buckets // 2
    near = near.at[half - 1].add(sides[0])
    return near.at[buckets - 1].add(sides[1])


CHUNK = 512
GELU_K = math.sqrt(2.0 / math.pi)


def gated(normed, g, w_gate, w_up, w_down):
    gate = mm(normed, w_gate)
    up = mm(normed, w_up)
    d_act = mm(g, w_down, NT)
    square = gate * gate
    th = jnp.tanh(gate * (GELU_K + (GELU_K * 0.044715) * square))
    half = 0.5 + 0.5 * th
    gelu = gate * half
    slope = half + (0.5 * gate) * (1.0 - th * th) * (GELU_K + (3.0 * 0.044715 * GELU_K) * square)
    return (
        (gelu * up).astype(bf16),
        (d_act * up * slope).astype(bf16),
        (d_act * gelu).astype(bf16),
    )


def ff_body(final, scal, xl, xr, gl, gr, mix, w_out, gain, w_gate, w_up, w_down, *rest):
    if final:
        part_in, dn_in, lo_out, lo_send, dh_out, dmix_out, dw_out, dgain_out = rest[:8]
    else:
        part_out, dn_out, dw_out = rest[:3]
    dwg, dwu, dwd = rest[-6:-3] if final else rest[-5:-2]
    stage, sems = rest[-2:]
    dwo = rest[-3] if final else None
    step = pl.program_id(0)
    last = pl.num_programs(0) - 1
    own = lax.rem(step, 2) == 0
    hidden_units = w_gate.shape[1]

    @pl.when(step == 0)
    def _():
        for ref in (dwg, dwu, dwd):
            ref[...] = jnp.zeros(ref.shape, f32)
        if final:
            dwo[...] = jnp.zeros(dwo.shape, f32)
            dgain_out[...] = jnp.zeros(dgain_out.shape, f32)

    g = jnp.where(own, gl[0], gr[0])
    x = jnp.where(own, xl[0], xr[0]).astype(f32)
    quads = mix.shape[1]
    mixed = jnp.concatenate([mix[0, i] for i in range(quads)], axis=1)
    hidden = x + mm(mixed, w_out[...])
    gain_f = gain[...].astype(f32)
    scale = rms_of(hidden)
    unit = hidden * scale
    normed = (unit * gain_f).astype(bf16)
    normed_t = normed.T
    g_t = g.T
    if final:
        out, dn = part_in[0], dn_in[0]
    else:
        out, dn = hidden, jnp.zeros_like(hidden)
    for c in range(hidden_units // CHUNK):
        cols = slice(c * CHUNK, (c + 1) * CHUNK)
        act, d_gate, d_up = gated(normed, g, w_gate[:, cols], w_up[:, cols], w_down[cols, :])
        out = out + mm(act, w_down[cols, :])
        dn = dn + mm(d_gate, w_gate[:, cols], NT) + mm(d_up, w_up[:, cols], NT)
        dwd[:, cols] += mm(g_t, act)
        dwg[:, cols] += mm(normed_t, d_gate)
        dwu[:, cols] += mm(normed_t, d_up)

    if final:

        @pl.when(own)
        def _():
            lo_out[0] = out

        @pl.when(jnp.logical_not(own))
        def _():
            lo_send[0] = out.astype(bf16)

        dgain_out[...] += jnp.sum(dn * unit, axis=0, keepdims=True)
        e = dn * gain_f
        d_hidden = (
            g.astype(f32) + scale * e - unit * (scale * jnp.mean(unit * e, axis=-1, keepdims=True))
        )
        dh_out[0] = d_hidden
        low = d_hidden.astype(bf16)
        dwo[...] += mm(mixed.T, low)
        d_mixed = mm(low, w_out[...], NT).astype(bf16)
        for i in range(quads):
            dmix_out[0, i] = d_mixed[:, i * STEP : (i + 1) * STEP]
    else:
        part_out[0] = out
        dn_out[0] = dn

    @pl.when(step == last)
    def _():
        rows = stage.shape[1]
        jobs = []
        place = 0
        for acc in (dwg, dwu, dwd, dwo) if final else (dwg, dwu, dwd):
            for part in range(acc.shape[0] // rows):
                jobs.append((acc, place, part))
            place += acc.shape[1]
        pending = [None, None]
        for n, (acc, place, part) in enumerate(jobs):
            slot = n % 2
            if pending[slot] is not None:
                pending[slot].wait()
            cols = acc.shape[1]
            span = slice(part * rows, (part + 1) * rows)
            stage[slot, :, :cols] = acc[span, :].astype(bf16)
            copy = pltpu.make_async_copy(
                stage.at[slot, :, pl.ds(0, cols)],
                dw_out.at[pl.ds(part * rows, rows), pl.ds(place, cols)],
                sems.at[slot],
            )
            copy.start()
            pending[slot] = copy
        for copy in pending:
            copy.wait()


def feed_forward(
    final, places, inputs, x_remote, cot, cot_remote, mix, w_out, gain, w_gate, w_up, w_down, held=()
):
    rows, half, width = inputs.shape
    mine = x_remote.shape[0]
    _, quads, extent, _ = mix.shape
    units = w_gate.shape[1] // 2
    inner = w_out.shape[0]
    which = 1 if final else 0

    def keep(shape, at=None):
        at = (0,) * len(shape) if at is None else at
        return pl.BlockSpec(shape, lambda i, s: at, pipeline_mode=pl.Buffered(1))

    local = pl.BlockSpec((1, half, width), lambda i, s: (s[1 + i // 2], 0, 0))
    far = pl.BlockSpec((1, half, width), lambda i, s: (i // 2, 0, 0))
    spot = pl.BlockSpec(
        (1, quads, half, STEP),
        lambda i, s: (i // 2, 0, jnp.where(i % 2 == 0, s[0], 1 - s[0]), 0),
    )
    tile = pl.BlockSpec((1, half, width), lambda i, s: (i, 0, 0))
    anywhere = pl.BlockSpec(memory_space=pl.ANY)
    tiles = jax.ShapeDtypeStruct((2 * mine, half, width), f32)
    if final:
        out_specs = [local, far, tile, spot, anywhere, pl.BlockSpec((1, width), lambda i, s: (0, 0))]
        out_shape = [
            jax.ShapeDtypeStruct((rows, half, width), f32),
            jax.ShapeDtypeStruct((mine, half, width), bf16),
            tiles,
            jax.ShapeDtypeStruct((mine, quads, extent, STEP), bf16),
            jax.ShapeDtypeStruct((width, 3 * units + width), bf16),
            jax.ShapeDtypeStruct((1, width), f32),
        ]
    else:
        out_specs = [tile, tile, anywhere]
        out_shape = [tiles, tiles, jax.ShapeDtypeStruct((width, 3 * units), bf16)]
    grid_spec = pltpu.PrefetchScalarGridSpec(
        num_scalar_prefetch=1,
        grid=(2 * mine,),
        in_specs=[local, far, local, far, spot, keep((inner, width)), keep((1, width)),
                  keep((width, units), (0, which)), keep((width, units), (0, which)),
                  keep((units, width), (which, 0))] + [tile] * len(held),
        out_specs=out_specs,
        scratch_shapes=[pltpu.VMEM((width, units), f32)] * 3
        + ([pltpu.VMEM((inner, width), f32)] if final else [])
        + [pltpu.VMEM((2, 64, units), bf16), pltpu.SemaphoreType.DMA((2,))],
    )
    return pl.pallas_call(
        functools.partial(ff_body, final),
        grid_spec=grid_spec,
        out_shape=out_shape,
        compiler_params=params(1, 63),
        cost_estimate=cost(75),
        name="feed_forward",
    )(places, inputs, x_remote, cot, cot_remote, mix, w_out, gain, w_gate, w_up, w_down, *held)


def spread_body(first, second, gate_out, up_out, down_out, out_out):
    units = first.shape[1] // 3
    for n, ref in enumerate((first, second)):
        cols = slice(n * units, (n + 1) * units)
        gate_out[:, cols] = ref[:, :units].astype(f32)
        up_out[:, cols] = ref[:, units : 2 * units].astype(f32)
        down_out[cols, :] = ref[:, 2 * units : 3 * units].astype(f32).T
    out_out[...] = second[:, 3 * units :].astype(f32)


def spread(first, second):
    width = first.shape[0]
    units = first.shape[1] // 3
    return pl.pallas_call(
        spread_body,
        grid=(width // LANE,),
        in_specs=[
            pl.BlockSpec((LANE, 3 * units), lambda i: (i, 0)),
            pl.BlockSpec((LANE, 3 * units + width), lambda i: (i, 0)),
        ],
        out_specs=[
            pl.BlockSpec((LANE, 2 * units), lambda i: (i, 0)),
            pl.BlockSpec((LANE, 2 * units), lambda i: (i, 0)),
            pl.BlockSpec((2 * units, LANE), lambda i: (0, i)),
            pl.BlockSpec((LANE, width), lambda i: (i, 0)),
        ],
        out_shape=[
            jax.ShapeDtypeStruct((width, 2 * units), f32),
            jax.ShapeDtypeStruct((width, 2 * units), f32),
            jax.ShapeDtypeStruct((2 * units, width), f32),
            jax.ShapeDtypeStruct((width, width), f32),
        ],
        compiler_params=params(1, 56),
        cost_estimate=cost(10),
        name="spread",
    )(first, second)


def back_body(quads, held, scal, xl, xr, dh, *rest):
    grads = rest[: 3 * quads]
    gain, wq, wk, wv = rest[3 * quads : 3 * quads + 4]
    ig_out, ig_send, dgain_out = rest[-3:]
    step = pl.program_id(0)
    far = step == 0

    @pl.when(far)
    def _():
        dgain_out[...] = jnp.zeros(dgain_out.shape, f32)

    x = jnp.where(far, xr[0], xl[0]).astype(f32)
    dn = jnp.zeros_like(x)
    for n, weight in enumerate((wq, wk, wv)):
        part = jnp.concatenate([ref[0] for ref in grads[n * quads : (n + 1) * quads]], axis=1)
        dn = dn + mm(part, weight[...], NT)
    scale = rms_of(x)
    unit = x * scale
    dgain_out[...] += jnp.sum(dn * unit, axis=0, keepdims=True)
    e = dn * gain[...].astype(f32)
    out = dh[0] + scale * e - unit * (scale * jnp.mean(unit * e, axis=-1, keepdims=True))

    @pl.when(far)
    def _():
        ig_send[0] = out.astype(bf16)

    @pl.when(jnp.logical_not(far))
    def _():
        ig_out[0] = out


def input_back(places, row, held, inputs, remote, dh, dq, dk, dv, gain, wq, wk, wv, deps=()):
    rows, half, width = inputs.shape
    local = pl.BlockSpec((1, half, width), lambda i, s: (s[1 + row], 0, 0))
    one = pl.BlockSpec((1, half, width), lambda i, s: (0, 0, 0))
    tile = pl.BlockSpec((1, half, width), lambda i, s: (2 * row + 1 - i, 0, 0))
    spot = pl.BlockSpec((1, half, STEP), lambda i, s: (row, jnp.where(i == 1, s[0], 1 - s[0]), 0))
    weight = pl.BlockSpec(wq.shape, lambda i, s: (0, 0), pipeline_mode=pl.Buffered(1))
    line = pl.BlockSpec((1, width), lambda i, s: (0, 0))
    anywhere = pl.BlockSpec(memory_space=pl.ANY)
    grads = [*dq, *dk, *dv]
    grid_spec = pltpu.PrefetchScalarGridSpec(
        num_scalar_prefetch=1,
        grid=(2,),
        in_specs=[local, one, tile]
        + [spot] * len(grads)
        + [line, weight, weight, weight]
        + [anywhere] * (len(held) + len(deps)),
        out_specs=[local, one, line],
    )
    return pl.pallas_call(
        functools.partial(back_body, len(dq), len(held)),
        grid_spec=grid_spec,
        out_shape=[
            jax.ShapeDtypeStruct((rows, half, width), f32),
            jax.ShapeDtypeStruct((1, half, width), bf16),
            jax.ShapeDtypeStruct((1, width), f32),
        ],
        input_output_aliases={8 + len(grads): 0} if held else {},
        compiler_params=params(1, 56),
        cost_estimate=cost(8),
        name="input_back",
    )(places, inputs, remote, dh, *grads, gain, wq, wk, wv, *held, *deps)


def hold_body(value, *rest):
    rest[-1][...] = value[...]


def hold(value, deps):
    return pl.pallas_call(
        hold_body,
        in_specs=[pl.BlockSpec(memory_space=pltpu.VMEM)]
        + [pl.BlockSpec(memory_space=pl.ANY)] * len(deps),
        out_specs=pl.BlockSpec(memory_space=pltpu.VMEM),
        out_shape=jax.ShapeDtypeStruct(value.shape, value.dtype),
        compiler_params=pltpu.CompilerParams(vmem_limit_bytes=16 << 20),
        name="hold",
    )(value, *deps)


def pick_body(scal, array, *rest):
    rest[-1][...] = array[...]


def pick_rows(places, first, count, array, deps=()):
    rows, half, width = array.shape
    grid_spec = pltpu.PrefetchScalarGridSpec(
        num_scalar_prefetch=1,
        grid=(count,),
        in_specs=[pl.BlockSpec((1, half, width), lambda i, s: (s[1 + rows // 2 + first + i], 0, 0))]
        + [pl.BlockSpec(memory_space=pl.ANY)] * len(deps),
        out_specs=pl.BlockSpec((1, half, width), lambda i, s: (i, 0, 0)),
    )
    return pl.pallas_call(
        pick_body,
        grid_spec=grid_spec,
        out_shape=jax.ShapeDtypeStruct((count, half, width), array.dtype),
        compiler_params=params(1, 16),
        name="pick_rows",
    )(places, array, *deps)


def place_body(scal, arrived, *rest):
    out = rest[-1]
    out[0] = arrived[0].astype(f32)


def place_rows(places, first, arrived, held, deps=()):
    count, half, width = arrived.shape
    at = 1 + held.shape[0] // 2 + first
    grid_spec = pltpu.PrefetchScalarGridSpec(
        num_scalar_prefetch=1,
        grid=(count,),
        in_specs=[
            pl.BlockSpec((1, half, width), lambda i, s: (i, 0, 0)),
            pl.BlockSpec(memory_space=pl.ANY),
        ]
        + [pl.BlockSpec(memory_space=pl.ANY)] * len(deps),
        out_specs=pl.BlockSpec((1, half, width), lambda i, s: (s[at + i], 0, 0)),
    )
    return pl.pallas_call(
        place_body,
        grid_spec=grid_spec,
        out_shape=jax.ShapeDtypeStruct(held.shape, f32),
        input_output_aliases={2: 0},
        compiler_params=params(1, 32),
        name="place_rows",
    )(places, arrived, held, *deps)


highest = lax.Precision.HIGHEST


def rms_scaled(values, gain):
    mean_square = jnp.mean(values * values, axis=-1, keepdims=True)
    return values * lax.rsqrt(mean_square + epsilon) * gain


def gated_unit(gate, up_proj):
    return jax.nn.gelu(gate, approximate=True) * up_proj


def relative_one_hot(query_anchor, query_extent, key_extent, bucket_count):
    query_place = query_anchor + jnp.arange(query_extent, dtype=jnp.int32)
    key_place = jnp.arange(key_extent, dtype=jnp.int32)
    offset = key_place[None, :] - query_place[:, None]
    distance = jnp.abs(offset)
    far_bucket = jnp.full_like(distance, 8)
    for threshold in bucket_bounds:
        far_bucket = far_bucket + (distance >= threshold).astype(jnp.int32)
    bucket = jnp.where(offset > 0, bucket_count // 2, 0) + jnp.where(
        distance < 8, distance, far_bucket
    )
    return (bucket[:, :, None] == jnp.arange(bucket_count, dtype=jnp.int32)).astype(jnp.float32)


def block_scores(query_heads, key_heads, query_anchor, lengths, bias_f):
    key_extent = key_heads.shape[1]
    one_hot = relative_one_hot(query_anchor, query_heads.shape[1], key_extent, bias_f.shape[0])
    bias_block = jnp.einsum("qkb,bh->hqk", one_hot, bias_f, precision=highest)
    raw_scores = jnp.einsum(
        "rqhd,rkhd->rhqk", query_heads, key_heads, preferred_element_type=jnp.float32
    )
    usable = jnp.arange(key_extent, dtype=jnp.int32)[None, :] < lengths[:, None]
    return (
        jnp.where(usable[:, None, None, :], raw_scores + bias_block[None], masked_score),
        one_hot,
    )


def score_grads(scores, log_total, row_dot, grad_heads, value_heads):
    weights_hp = jnp.exp(scores - log_total[..., None])
    d_weights = jnp.einsum(
        "rqhd,rkhd->rhqk", grad_heads, value_heads, preferred_element_type=jnp.float32
    )
    d_scores = (weights_hp * (d_weights - row_dot[..., None])).astype(jnp.bfloat16)
    return (weights_hp.astype(jnp.bfloat16), d_scores)


def table_term(one_hot, d_scores):
    summed = jnp.sum(d_scores, axis=0, dtype=jnp.float32)
    return jnp.einsum("qkb,hqk->bh", one_hot, summed, precision=highest)


def gathered_device(
    inputs,
    lengths,
    cotangent,
    norm_gain,
    w_query,
    w_key,
    w_value,
    w_out,
    ff_gain,
    w_gate,
    w_up,
    w_down,
    bias_table,
):
    row_count, block_len, model_width = inputs.shape
    head_count = bias_table.shape[1]
    inner_width = w_query.shape[1]
    head_width = inner_width // head_count
    tokens_here = row_count * block_len
    lengths = lengths.reshape(-1)
    bias_f = bias_table.astype(jnp.float32)
    own_anchor = lax.axis_index("seq") * block_len

    def split_heads(block_array):
        return block_array.reshape(row_count, block_array.shape[1], head_count, head_width)

    tokens_f = inputs.astype(jnp.float32).reshape(tokens_here, model_width)
    normed_f, norm_pull = jax.vjp(rms_scaled, tokens_f, norm_gain.astype(jnp.float32))
    normed = normed_f.astype(jnp.bfloat16)
    queries = (
        jnp.dot(normed, w_query, preferred_element_type=jnp.float32)
        .astype(jnp.bfloat16)
        .reshape(row_count, block_len, inner_width)
    )
    keys = (
        jnp.dot(normed, w_key, preferred_element_type=jnp.float32)
        .astype(jnp.bfloat16)
        .reshape(row_count, block_len, inner_width)
    )
    values = (
        jnp.dot(normed, w_value, preferred_element_type=jnp.float32)
        .astype(jnp.bfloat16)
        .reshape(row_count, block_len, inner_width)
    )
    query_heads = split_heads(queries)
    stat_shape = (row_count, head_count, block_len)
    pieces = (
        lax.all_gather(keys, "seq", axis=1, tiled=True),
        lax.all_gather(values, "seq", axis=1, tiled=True),
    )
    row_max = jnp.full(stat_shape, start_max, jnp.float32)
    key_heads = split_heads(pieces[0])
    value_heads = split_heads(pieces[1])
    scores, one_hot = block_scores(query_heads, key_heads, own_anchor, lengths, bias_f)
    new_max = jnp.maximum(row_max, jnp.max(scores, axis=-1))
    weights_hp = jnp.exp(scores - new_max[..., None])
    row_sum = jnp.sum(weights_hp, axis=-1)
    weighted = jnp.einsum(
        "rhqk,rkhd->rhqd",
        weights_hp.astype(jnp.bfloat16),
        value_heads,
        preferred_element_type=jnp.float32,
    )
    row_max, row_sum, weighted = (new_max, row_sum, weighted)
    log_total = row_max + jnp.log(row_sum)
    mixed_heads = jnp.transpose(weighted / row_sum[..., None], (0, 2, 1, 3))
    mixed_low = mixed_heads.reshape(tokens_here, inner_width).astype(jnp.bfloat16)
    hidden = tokens_f + jnp.dot(mixed_low, w_out, preferred_element_type=jnp.float32)
    normed2_f, ff_pull = jax.vjp(rms_scaled, hidden, ff_gain.astype(jnp.float32))
    normed2 = normed2_f.astype(jnp.bfloat16)
    gate = jnp.dot(normed2, w_gate, preferred_element_type=jnp.float32)
    up_proj = jnp.dot(normed2, w_up, preferred_element_type=jnp.float32)
    activated, gated_pull = jax.vjp(gated_unit, gate, up_proj)
    act_low = activated.astype(jnp.bfloat16)
    layer_output = (hidden + jnp.dot(act_low, w_down, preferred_element_type=jnp.float32)).reshape(
        row_count, block_len, model_width
    )
    grad_out = cotangent.reshape(tokens_here, model_width)
    dw_down = jnp.einsum("tf,td->fd", act_low, grad_out, preferred_element_type=jnp.float32)
    d_act = jnp.einsum("td,fd->tf", grad_out, w_down, preferred_element_type=jnp.float32)
    d_gate, d_up = gated_pull(d_act)
    d_gate = d_gate.astype(jnp.bfloat16)
    d_up = d_up.astype(jnp.bfloat16)
    dw_gate = jnp.einsum("td,tf->df", normed2, d_gate, preferred_element_type=jnp.float32)
    dw_up = jnp.einsum("td,tf->df", normed2, d_up, preferred_element_type=jnp.float32)
    d_normed2 = jnp.einsum(
        "tf,df->td", d_gate, w_gate, preferred_element_type=jnp.float32
    ) + jnp.einsum("tf,df->td", d_up, w_up, preferred_element_type=jnp.float32)
    d_hidden_part, d_ff_gain = ff_pull(d_normed2)
    d_hidden = grad_out.astype(jnp.float32) + d_hidden_part
    d_hidden_low = d_hidden.astype(jnp.bfloat16)
    dw_out = jnp.einsum("ti,td->id", mixed_low, d_hidden_low, preferred_element_type=jnp.float32)
    d_mixed = (
        jnp.einsum("td,id->ti", d_hidden_low, w_out, preferred_element_type=jnp.float32)
        .astype(jnp.bfloat16)
        .reshape(row_count, block_len, inner_width)
    )
    grad_heads = split_heads(d_mixed)
    row_dot_rows = jnp.sum(grad_heads.astype(jnp.float32) * mixed_heads, axis=-1)
    row_dot = jnp.transpose(row_dot_rows, (0, 2, 1))
    pieces = (
        lax.all_gather(keys, "seq", axis=1, tiled=True),
        lax.all_gather(values, "seq", axis=1, tiled=True),
    )
    key_heads = split_heads(pieces[0])
    value_heads = split_heads(pieces[1])
    scores, one_hot = block_scores(query_heads, key_heads, own_anchor, lengths, bias_f)
    weights_low, d_scores = score_grads(scores, log_total, row_dot, grad_heads, value_heads)
    d_query_part = jnp.einsum(
        "rhqk,rkhd->rqhd", d_scores, key_heads, preferred_element_type=jnp.float32
    )
    key_heads, weights_low, d_scores, d_query_part, table_part = (
        key_heads,
        weights_low,
        d_scores,
        d_query_part,
        table_term(one_hot, d_scores),
    )
    extent = key_heads.shape[1]
    d_key_part = jnp.einsum(
        "rhqk,rqhd->rkhd", d_scores, query_heads, preferred_element_type=jnp.float32
    ).reshape(row_count, extent, inner_width)
    d_value_part = jnp.einsum(
        "rhqk,rqhd->rkhd", weights_low, grad_heads, preferred_element_type=jnp.float32
    ).reshape(row_count, extent, inner_width)
    d_key, d_value = (
        lax.psum_scatter(d_key_part, "seq", scatter_dimension=1, tiled=True),
        lax.psum_scatter(d_value_part, "seq", scatter_dimension=1, tiled=True),
    )
    d_query_low = d_query_part.reshape(tokens_here, inner_width).astype(jnp.bfloat16)
    d_key_low = d_key.reshape(tokens_here, inner_width).astype(jnp.bfloat16)
    d_value_low = d_value.reshape(tokens_here, inner_width).astype(jnp.bfloat16)
    dw_query = jnp.einsum("td,ti->di", normed, d_query_low, preferred_element_type=jnp.float32)
    dw_key = jnp.einsum("td,ti->di", normed, d_key_low, preferred_element_type=jnp.float32)
    dw_value = jnp.einsum("td,ti->di", normed, d_value_low, preferred_element_type=jnp.float32)
    d_normed = jnp.einsum("ti,di->td", d_query_low, w_query, preferred_element_type=jnp.float32)
    d_normed = d_normed + jnp.einsum(
        "ti,di->td", d_key_low, w_key, preferred_element_type=jnp.float32
    )
    d_normed = d_normed + jnp.einsum(
        "ti,di->td", d_value_low, w_value, preferred_element_type=jnp.float32
    )
    d_tokens_part, d_norm_gain = norm_pull(d_normed)
    input_grad = (d_hidden + d_tokens_part).reshape(row_count, block_len, model_width)
    flat_query = dw_query.reshape(-1)
    flat_key = dw_key.reshape(-1)
    flat_value = dw_value.reshape(-1)
    flat_out = dw_out.reshape(-1)
    flat_gate = dw_gate.reshape(-1)
    flat_up = dw_up.reshape(-1)
    flat_down = dw_down.reshape(-1)
    shares = (
        lax.psum_scatter(flat_query, ("batch", "seq"), scatter_dimension=0, tiled=True),
        lax.psum_scatter(flat_key, ("batch", "seq"), scatter_dimension=0, tiled=True),
        lax.psum_scatter(flat_value, ("batch", "seq"), scatter_dimension=0, tiled=True),
        lax.psum_scatter(flat_out, ("batch", "seq"), scatter_dimension=0, tiled=True),
        lax.psum_scatter(flat_gate, ("batch", "seq"), scatter_dimension=0, tiled=True),
        lax.psum_scatter(flat_up, ("batch", "seq"), scatter_dimension=0, tiled=True),
        lax.psum_scatter(flat_down, ("batch", "seq"), scatter_dimension=0, tiled=True),
    )
    summed = (
        lax.all_gather(shares[0], ("batch", "seq"), axis=0, tiled=True),
        lax.all_gather(shares[1], ("batch", "seq"), axis=0, tiled=True),
        lax.all_gather(shares[2], ("batch", "seq"), axis=0, tiled=True),
        lax.all_gather(shares[3], ("batch", "seq"), axis=0, tiled=True),
        lax.all_gather(shares[4], ("batch", "seq"), axis=0, tiled=True),
        lax.all_gather(shares[5], ("batch", "seq"), axis=0, tiled=True),
        lax.all_gather(shares[6], ("batch", "seq"), axis=0, tiled=True),
    )
    sum_norm, sum_ff, sum_table = lax.psum((d_norm_gain, d_ff_gain, table_part), ("batch", "seq"))
    return (
        layer_output,
        input_grad,
        sum_norm,
        summed[0].reshape(w_query.shape),
        summed[1].reshape(w_key.shape),
        summed[2].reshape(w_value.shape),
        summed[3].reshape(w_out.shape),
        sum_ff,
        summed[4].reshape(w_gate.shape),
        summed[5].reshape(w_up.shape),
        summed[6].reshape(w_down.shape),
        sum_table,
    )


def all_pairs(mesh_batch, mesh_seq, move):
    pairs = []
    for batch in range(mesh_batch):
        for seq in range(mesh_seq):
            z, y, core, x = move(batch // 4, batch // 2 % 2, batch % 2, seq)
            pairs.append((batch * mesh_seq + seq, (z * 4 + y * 2 + core) * mesh_seq + x))
    return pairs


def add_up(parts):
    total = parts[0].astype(f32)
    for part in parts[1:]:
        total = total + part.astype(f32)
    return total


class Links:
    def __init__(self, batch, seq):
        self.axes = ("batch", "seq")
        self.deep = batch // 4
        me = lax.axis_index("batch")
        self.z, self.y, self.core = me // 4, me // 2 % 2, me % 2
        self.x = lax.axis_index("seq")
        self.plane = self.y * 2 + self.x
        pairs = functools.partial(all_pairs, batch, seq)
        self.to_core = pairs(lambda z, y, c, x: (z, y, 1 - c, x))
        self.to_plane = {
            k: pairs(lambda z, y, c, x, k=k: (z, y ^ (k >> 1), c, x ^ (k & 1))) for k in (1, 2, 3)
        }
        self.to_deep = {
            k: pairs(lambda z, y, c, x, k=k: ((z + k) % self.deep, y, c, x))
            for k in range(1, self.deep)
        }

    def send(self, value, pairs):
        return lax.ppermute(value, self.axes, pairs)

    def pick(self, value, at):
        return lax.dynamic_index_in_dim(value, at, 0, keepdims=False)

    def scatter_core(self, grads):
        rows, columns = grads.shape
        each = rows // (8 * self.deep)
        split = grads.reshape(2, 4, self.deep, each, columns)
        got = self.send(self.pick(split, 1 - self.core), self.to_core)
        return add_up([self.pick(split, self.core), got]).astype(bf16)

    def scatter_plane(self, part):
        got = [self.send(self.pick(part, self.plane ^ k), self.to_plane[k]) for k in (1, 2, 3)]
        return add_up([self.pick(part, self.plane), *got]).astype(bf16)

    def scatter_deep(self, part):
        got = [
            self.send(self.pick(part, (self.z + k) % self.deep), self.to_deep[k])
            for k in range(1, self.deep)
        ]
        return add_up([self.pick(part, self.z), *got]).astype(bf16)

    def lay(self, count, at, own, got):
        out = jnp.zeros((count,) + own.shape, own.dtype)
        out = lax.dynamic_update_index_in_dim(out, own, at, 0)
        for place, piece in got:
            out = lax.dynamic_update_index_in_dim(out, piece, place, 0)
        return out

    def gather_deep(self, part):
        got = [
            ((self.z - k) % self.deep, self.send(part, self.to_deep[k]))
            for k in range(1, self.deep)
        ]
        return self.lay(self.deep, self.z, part, got)

    def gather_plane(self, part):
        got = [(self.plane ^ k, self.send(part, self.to_plane[k])) for k in (1, 2, 3)]
        return self.lay(4, self.plane, part, got)

    def gather_core(self, part):
        out = self.lay(2, self.core, part, [(1 - self.core, self.send(part, self.to_core))])
        return out.reshape(-1, out.shape[-1])

    def total(self, grads):
        part = self.scatter_deep(self.scatter_plane(self.scatter_core(grads)))
        return self.gather_core(self.gather_plane(self.gather_deep(part)))

    def total_small(self, value):
        value = add_up([value, self.send(value, self.to_core)])
        value = add_up([value, *[self.send(value, self.to_plane[k]) for k in (1, 2, 3)]])
        return add_up([value, *[self.send(value, p) for p in self.to_deep.values()]])


def rows_device(
    batch,
    seq,
    inputs,
    lengths,
    cotangent,
    norm_gain,
    w_query,
    w_key,
    w_value,
    w_out,
    ff_gain,
    w_gate,
    w_up,
    w_down,
    bias_table,
):
    rows, half, width = inputs.shape
    buckets, heads = bias_table.shape
    mine_count = rows // 2
    links = Links(batch, seq)
    places = split_rows(lengths, links.x)
    swap = [(0, 1), (1, 0)]

    x_parts, tick = [], ()
    for row in range(mine_count):
        x_parts.append(lax.ppermute(pick_rows(places, row, 1, inputs, tick), "seq", swap))
        tick = (links.send(tick[0] if tick else places.astype(f32), links.to_core),)
    g_remote = lax.ppermute(pick_rows(places, 0, mine_count, cotangent, tick), "seq", swap)
    near, near_t, far = bias_pieces(bias_table, 2 * half // LANE)
    gain = norm_gain.reshape(1, width)
    gain2 = ff_gain.reshape(1, width)
    held = []
    for row in range(mine_count):
        held = fwd_row(
            places, inputs, x_parts[row], row, mine_count, held,
            gain, w_query, w_key, w_value, near, far, heads,
        )
    q, k, v, mix, tail, normt = held
    x_remote = jnp.concatenate(x_parts, axis=0)
    ff_args = (
        places, inputs, x_remote, cotangent, g_remote, mix,
        w_out, gain2, w_gate, w_up, w_down,
    )
    *held, first_grads = feed_forward(False, *ff_args)
    first_total = lax.psum(first_grads, ("batch", "seq"))
    lo, lo_send, dh, dmix, second_grads, ff_gain_part = feed_forward(True, *ff_args, held)
    second_total = lax.psum(second_grads, ("seq", "batch"))
    lo_got = lax.ppermute(lo_send, "seq", swap)
    quads = q.shape[1]
    dw, backs, token = [], [], ()
    for quad in range(quads):
        if quad == quads - 1:
            layer_output = place_rows(places, 0, lo_got, lo)
            token = (layer_output,)
        *back, dw_quad = bwd_quad(
            places, quad, dw, q, k, v, mix, dmix, tail, near_t, normt, token
        )
        backs.append(back)
        dw = [dw_quad]
    dq, dk, dv, tacc, far_sum = zip(*backs)
    qkv = links.scatter_core(dw[0])
    ig, ig_got, gain_parts, token = [], [], [], ()
    for row in range(mine_count):
        *ig, sent, gain_part = input_back(
            places, row, ig, inputs, x_parts[row], dh, dq, dk, dv,
            gain, w_query, w_key, w_value, token,
        )
        token = (qkv,)
        gain_parts.append(gain_part[0])
        ig_got.append(lax.ppermute(sent, "seq", swap))
    table_part = table_sums(jnp.concatenate(tacc, axis=0), jnp.stack(far_sum), buckets)
    small = jnp.concatenate([sum(gain_parts), ff_gain_part[0], table_part.reshape(-1)])
    small = links.total_small(small)
    qkv = links.scatter_plane(qkv)
    qkv = links.scatter_deep(hold(qkv, (ig[0],)))
    qkv = links.gather_core(links.gather_plane(links.gather_deep(qkv)))
    input_grad = ig[0]
    for row in range(mine_count):
        input_grad = place_rows(places, row, ig_got[row], input_grad)
    gate_grad, up_grad, down_grad, out_grad = spread(first_total, second_total)

    def whole(n):
        return jnp.concatenate(
            [qkv[:, (3 * i + n) * STEP : (3 * i + n + 1) * STEP] for i in range(quads)], axis=1
        ).astype(f32)

    return (
        layer_output,
        input_grad,
        small[:width],
        whole(0),
        whole(1),
        whole(2),
        out_grad,
        small[width : 2 * width],
        gate_grad,
        up_grad,
        down_grad,
        small[2 * width :].reshape(buckets, heads),
    )


def solution(mesh):
    split = P("batch", "seq", None)
    in_specs = (split, P("batch", None), split) + (P(),) * 10
    out_specs = (split, split) + (P(),) * 10
    batch, seq = mesh.shape["batch"], mesh.shape["seq"]

    def per_device(inputs, *rest):
        rows, half, width = inputs.shape
        buckets, heads = rest[-1].shape
        inner = rest[3].shape[1]
        fits = seq == 2 and batch % 4 == 0 and rows % 2 == 0 and buckets == 32
        fits = fits and half % STEP == 0 and 2 * half // LANE <= 8
        fits = fits and inner == width and width % (16 * batch) == 0 and inner // heads == LANE // 2
        if fits:
            return rows_device(batch, seq, inputs, *rest)
        return gathered_device(inputs, *rest)

    return jax.shard_map(
        per_device, mesh=mesh, in_specs=in_specs, out_specs=out_specs, check_vma=False
    )
```

```python
import functools
import itertools
import math

import jax
import jax.numpy as jnp
from jax import lax
from jax.experimental import pallas as pl
from jax.experimental.pallas import tpu as pltpu
from jax.sharding import PartitionSpec as P

f32 = jnp.float32
bf16 = jnp.bfloat16
epsilon = 1e-06
masked_score = -2e30
start_max = -1e30
bucket_bounds = (12, 16, 23, 32, 46, 64, 91)
LANE = 128
STEP = 256
NT = (((1,), (1,)), ((), ()))
NN = (((1,), (0,)), ((), ()))
TN = (((0,), (0,)), ((), ()))


def mm(a, b, dims=NN):
    return lax.dot_general(a, b, dims, preferred_element_type=f32)


def cost(micros):
    return pl.CostEstimate(flops=int(micros * 0.3e9), bytes_accessed=0, transcendentals=0)


def params(grid_dims, mib):
    return pltpu.CompilerParams(
        dimension_semantics=("arbitrary",) * grid_dims, vmem_limit_bytes=mib << 20
    )


def bucket_of(offset, bucket_count):
    distance = jnp.abs(offset)
    far = jnp.full_like(distance, 8)
    for bound in bucket_bounds:
        far = far + (distance >= bound).astype(jnp.int32)
    half = bucket_count // 2
    return jnp.where(offset > 0, half, 0) + jnp.where(distance < 8, distance, far)


def split_body(choices, side, lengths, out):
    rows = lengths.shape[1]
    count = rows // 2
    load = [(lengths[0, r] + STEP - 1) // STEP for r in range(rows)]
    best = None
    for own in choices:
        other = [r for r in range(rows) if r not in own]
        uneven = jnp.abs(sum(load[r] for r in own) - sum(load[r] for r in other))
        new = [*own, *other]
        if best is None:
            best, picked = uneven, [jnp.int32(r) for r in new]
        else:
            better = uneven < best
            best = jnp.where(better, uneven, best)
            picked = [jnp.where(better, r, old) for r, old in zip(new, picked)]
    first = side[0] == 0
    out[0] = side[0]
    for n in range(count):
        mine = jnp.where(first, picked[n], picked[count + n])
        out[1 + n] = mine
        out[1 + count + n] = jnp.where(first, picked[count + n], picked[n])
        out[1 + 2 * count + n] = lengths[0, mine]


def split_rows(lengths, side):
    rows = lengths.shape[1]
    choices = [c for c in itertools.combinations(range(rows), rows // 2) if 0 in c]
    smem = pl.BlockSpec(memory_space=pltpu.SMEM)
    return pl.pallas_call(
        functools.partial(split_body, choices),
        in_specs=[smem, smem],
        out_specs=smem,
        out_shape=jax.ShapeDtypeStruct((1 + 3 * (rows // 2),), jnp.int32),
        name="split_rows",
    )(side.reshape(1), lengths)


def near_body(vec_ref, rev_ref, near_ref, near_t_ref):
    wide = jnp.broadcast_to(vec_ref[0], (LANE, 4 * LANE))
    near_ref[0] = pltpu.roll(wide, 0, 1, stride=1, stride_axis=0)[:, : 3 * LANE]
    tall = jnp.broadcast_to(rev_ref[0], (3 * LANE, 4 * LANE))
    near_t_ref[0] = pltpu.roll(tall, 0, 1, stride=1, stride_axis=0)[:, :LANE]


def near_offsets():
    place = jnp.arange(4 * LANE, dtype=jnp.int32)
    signed = jnp.where(place < 3 * LANE, place, place - 4 * LANE)
    forward = signed - LANE
    back = jnp.where(place < LANE, place, place - 4 * LANE)
    reverse = -back - LANE
    return forward, reverse


def bias_pieces(bias_table, tile_count):
    buckets, heads = bias_table.shape
    table = bias_table.astype(f32)
    forward, reverse = near_offsets()

    def spread(offset):
        hot = bucket_of(offset, buckets)[:, None] == jnp.arange(buckets, dtype=jnp.int32)
        picked = jnp.einsum("rb,bh->hr", hot.astype(f32), table, precision=lax.Precision.HIGHEST)
        return picked[:, None, :]

    near, near_t = pl.pallas_call(
        near_body,
        grid=(heads,),
        in_specs=[pl.BlockSpec((1, 1, 4 * LANE), lambda h: (h, 0, 0))] * 2,
        out_specs=[
            pl.BlockSpec((1, LANE, 3 * LANE), lambda h: (h, 0, 0)),
            pl.BlockSpec((1, 3 * LANE, LANE), lambda h: (h, 0, 0)),
        ],
        out_shape=[
            jax.ShapeDtypeStruct((heads, LANE, 3 * LANE), f32),
            jax.ShapeDtypeStruct((heads, 3 * LANE, LANE), f32),
        ],
        name="near_bias",
    )(spread(forward), spread(reverse))
    left = table[buckets // 2 - 1]
    right = table[buckets - 1]
    tile = jnp.arange(tile_count, dtype=jnp.int32)[None, :, None]
    lane = jnp.arange(LANE, dtype=jnp.int32)[None, None, :]
    far = jnp.where(lane == tile, left[:, None, None], 0.0)
    far = far + jnp.where(lane == tile + 8, right[:, None, None], 0.0)
    far = far + jnp.where(lane == 16, masked_score, 0.0)
    return near, near_t, far.astype(bf16)


def key_lanes(extent, length):
    key = lax.broadcasted_iota(jnp.int32, (extent, LANE), 0)
    lane = lax.broadcasted_iota(jnp.int32, (extent, LANE), 1)
    tile = key // LANE
    flag = (lane < 8) & (tile < lane - 1)
    flag = flag | ((lane >= 8) & (lane < 16) & (tile > lane - 8 + 1))
    flag = flag | ((lane == 16) & (key >= length))
    flag = flag | ((lane >= 17) & (lane < 20))
    return jnp.where(flag, 1.0, 0.0).astype(bf16)


def rms_of(values):
    scale = lax.rsqrt(jnp.mean(values * values, axis=-1, keepdims=True) + epsilon)
    return scale


def head_mask(rows, head):
    lane = lax.broadcasted_iota(jnp.int32, (rows, LANE), 1)
    return (lane // (LANE // 2)) == head


def fwd_body(held, count, which, scal, xl, xr, gain, wq, wk, wv, near, far, *rest):
    q_out, k_out, v_out, mix_out, tail_out, normt_out, normed, lanes = rest[held:]
    extent = normed.shape[0]
    half = xl.shape[1]
    length = scal[1 + 2 * count + which]
    side = scal[0]
    steps = (length + STEP - 1) // STEP

    @pl.when(pl.program_id(0) == 0)
    def _():
        for ref, own in ((xl, True), (xr, False)):
            values = ref[0].astype(f32)
            out = values * rms_of(values) * gain[...].astype(f32)
            place = side * half if own else (1 - side) * half
            normed[pl.ds(pl.multiple_of(place, half), half), :] = out.astype(bf16)
        lanes[...] = key_lanes(extent, length)
        normt_out[0] = normed[...].T

    q_out[0, 0] = mm(normed[...], wq[...]).astype(bf16)
    for part in range(extent // STEP):
        rows = pl.ds(part * STEP, STEP)

        @pl.when(part < steps)
        def _():
            k_out[0, 0, rows, :] = mm(normed[rows, :], wk[...]).astype(bf16)
            v_out[0, 0, rows, :] = mm(normed[rows, :], wv[...]).astype(bf16)

        @pl.when(part >= steps)
        def _():
            k_out[0, 0, rows, :] = jnp.zeros((STEP, 2 * LANE), bf16)
            v_out[0, 0, rows, :] = jnp.zeros((STEP, 2 * LANE), bf16)

    def attend(width):
        def pair_step(pair, carry):
            cols = pl.ds(pl.multiple_of(pair * LANE, LANE), LANE)
            kext = jnp.concatenate([k_out[0, 0, :width, cols], lanes[:width, :]], axis=1)
            vext = jnp.concatenate(
                [v_out[0, 0, :width, cols], jnp.ones((width, LANE), bf16)], axis=1
            )
            lane = lax.broadcasted_iota(jnp.int32, (STEP, LANE), 1)
            for block in range(extent // STEP):
                rows = slice(block * STEP, (block + 1) * STEP)
                qpair = q_out[0, 0, rows, cols]
                outs = []
                for head in range(2):
                    index = 2 * pair + head
                    tiles = []
                    for sub in range(STEP // LANE):
                        line = far[index, pl.ds(block * (STEP // LANE) + sub, 1), :]
                        tiles.append(jnp.broadcast_to(line, (LANE, LANE)))
                    ext = jnp.concatenate(tiles, axis=0)
                    qm = jnp.where(head_mask(STEP, head), qpair, jnp.zeros_like(qpair))
                    scores = mm(jnp.concatenate([qm, ext], axis=1), kext, NT)
                    probs = []
                    tops = []
                    for sub in range(STEP // LANE):
                        tile = block * (STEP // LANE) + sub
                        own = scores[sub * LANE : (sub + 1) * LANE]
                        base = (tile - 1) * LANE
                        low, high = max(0, base), min(width, base + 3 * LANE)
                        if low < high:
                            add = own[:, low:high] + near[index, :, low - base : high - base]
                            pieces = [own[:, :low]] if low > 0 else []
                            pieces.append(add)
                            if high < width:
                                pieces.append(own[:, high:])
                            own = jnp.concatenate(pieces, axis=1)
                        top = jnp.max(own, axis=1, keepdims=True)
                        probs.append(jnp.exp(own - top).astype(bf16))
                        tops.append(top)
                    both = mm(jnp.concatenate(probs, axis=0), vext)
                    total = both[:, LANE:]
                    outs.append(both[:, :LANE] / total)
                    neg = -(jnp.concatenate(tops, axis=0) + jnp.log(total))
                    first = neg.astype(bf16)
                    rest = neg - first.astype(f32)
                    second = rest.astype(bf16)
                    third = (rest - second.astype(f32)).astype(bf16)
                    line = jnp.where(lane == 17, first, ext)
                    line = jnp.where(lane == 18, second, line)
                    line = jnp.where(lane == 19, third, line)
                    tail_out[0, index, rows, :] = line
                picked = jnp.where(head_mask(STEP, 0), outs[0], outs[1])
                mix_out[0, 0, rows, cols] = picked.astype(bf16)
            return carry

        lax.fori_loop(0, 2, pair_step, 0)

    for blocks in range(1, extent // STEP + 1):

        @pl.when(steps == blocks)
        def _():
            attend(blocks * STEP)


def fwd_row(scal, inputs, remote, which, count, held, gain, wq, wk, wv, near, far, heads):
    rows, half, width = inputs.shape
    extent = 2 * half
    inner = wq.shape[1]
    quads = inner // STEP
    per = heads // quads
    weight = pl.BlockSpec((width, STEP), lambda i, s: (0, i))
    block = pl.BlockSpec((1, 1, extent, STEP), lambda i, s: (which, i, 0, 0))
    grid_spec = pltpu.PrefetchScalarGridSpec(
        num_scalar_prefetch=1,
        grid=(quads,),
        in_specs=[
            pl.BlockSpec((1, half, width), lambda i, s: (s[1 + which], 0, 0)),
            pl.BlockSpec((1, half, width), lambda i, s: (0, 0, 0)),
            pl.BlockSpec((1, width), lambda i, s: (0, 0)),
            weight,
            weight,
            weight,
            pl.BlockSpec((per, LANE, 3 * LANE), lambda i, s: (i, 0, 0)),
            pl.BlockSpec((per, 8, LANE), lambda i, s: (i, 0, 0)),
        ]
        + [pl.BlockSpec(memory_space=pl.ANY)] * len(held),
        out_specs=[block] * 4
        + [
            pl.BlockSpec((1, per, extent, LANE), lambda i, s: (which, i, 0, 0)),
            pl.BlockSpec((1, width, extent), lambda i, s: (which, 0, 0)),
        ],
        scratch_shapes=[pltpu.VMEM((extent, width), bf16), pltpu.VMEM((extent, LANE), bf16)],
    )
    stacked = jax.ShapeDtypeStruct((count, quads, extent, STEP), bf16)
    return pl.pallas_call(
        functools.partial(fwd_body, len(held), count, which),
        grid_spec=grid_spec,
        out_shape=[stacked] * 4
        + [
            jax.ShapeDtypeStruct((count, heads, extent, LANE), bf16),
            jax.ShapeDtypeStruct((count, width, extent), bf16),
        ],
        input_output_aliases={9 + n: n for n in range(len(held))},
        compiler_params=params(1, 56),
        cost_estimate=cost(27),
        name="attend_row",
    )(scal, inputs, remote, gain, wq, wk, wv, near, far, *held)


def bwd_body(
    count, scal, q, k, v, mix, dmix, tail, near_t, normt, *rest
):
    (dq_out, dk_out, dv_out, tacc_out, far_out, dw_out) = rest[-15:-9]
    (lanes, pl_s, ds_s, do_s, qa_s, dwq, dwk, dwv, _) = rest[-9:]
    extent = lanes.shape[0]
    row = pl.program_id(0)
    length = scal[1 + 2 * count + row]
    steps = (length + STEP - 1) // STEP
    lanes[...] = key_lanes(extent, length)

    @pl.when(row == 0)
    def _():
        for ref in (tacc_out, far_out, dwq, dwk, dwv):
            ref[...] = jnp.zeros(ref.shape, f32)

    dk_out[...] = jnp.zeros(dk_out.shape, bf16)
    dv_out[...] = jnp.zeros(dv_out.shape, bf16)

    def attend(width):
        def head_step(index, carry):
            pair = index // 2
            head = lax.rem(index, 2)
            cols = pl.ds(pl.multiple_of(pair * LANE, LANE), LANE)
            flags = lanes[:width, :]
            kpair = k[0, 0, :width, cols]
            kext = jnp.concatenate([kpair, flags], axis=1)
            vext = jnp.concatenate([v[0, 0, :width, cols], flags], axis=1)
            lane = lax.broadcasted_iota(jnp.int32, (STEP, LANE), 1)
            mask = head_mask(STEP, head)
            for block in range(extent // STEP):
                rows = slice(block * STEP, (block + 1) * STEP)
                qpair = q[0, 0, rows, cols]
                dopair = dmix[0, 0, rows, cols]
                product = dopair.astype(f32) * mix[0, 0, rows, cols].astype(f32)
                qm = jnp.where(mask, qpair, jnp.zeros_like(qpair))
                dom = jnp.where(mask, dopair, jnp.zeros_like(dopair))
                neg = -jnp.sum(jnp.where(mask, product, 0.0), axis=1, keepdims=True)
                neg = jnp.broadcast_to(neg, (STEP, LANE))
                first = neg.astype(bf16)
                rest = neg - first.astype(f32)
                second = rest.astype(bf16)
                third = (rest - second.astype(f32)).astype(bf16)
                dtail = jnp.where(lane == 17, first, jnp.zeros((STEP, LANE), bf16))
                dtail = jnp.where(lane == 18, second, dtail)
                dtail = jnp.where(lane == 19, third, dtail)
                st = mm(kext, jnp.concatenate([qm, tail[0, index, rows, :]], axis=1), NT)
                dp = mm(vext, jnp.concatenate([dom, dtail], axis=1), NT)
                do_s[rows, :] = dom
                row_at = lax.broadcasted_iota(jnp.int32, (STEP, LANE), 0)
                spot = jnp.where(lane == block * (STEP // LANE) + row_at // LANE, 1.0, 0.0)
                qa_s[rows, :] = jnp.concatenate([qm, spot.astype(bf16)], axis=1)
                for sub in range(STEP // LANE):
                    tile = block * (STEP // LANE) + sub
                    part = slice(sub * LANE, (sub + 1) * LANE)
                    own = st[:, part]
                    base = (tile - 1) * LANE
                    low, high = max(0, base), min(width, base + 3 * LANE)
                    if low < high:
                        add = own[low:high] + near_t[index, low - base : high - base, :]
                        pieces = [own[:low]] if low > 0 else []
                        pieces.append(add)
                        if high < width:
                            pieces.append(own[high:])
                        own = jnp.concatenate(pieces, axis=0)
                    prob = jnp.exp(own)
                    dst = (prob * dp[:, part]).astype(bf16)
                    place = slice(tile * LANE, (tile + 1) * LANE)
                    pl_s[:width, place] = prob.astype(bf16)
                    ds_s[:width, place] = dst
                    if low < high:
                        tacc_out[index, low - base : high - base, :] += dst[low:high].astype(f32)
            kmask = head_mask(width, head)
            dv = mm(pl_s[:width, :], do_s[...]).astype(bf16)
            dv_out[0, :width, cols] = jnp.where(kmask, dv, dv_out[0, :width, cols])
            dk = mm(ds_s[:width, :], qa_s[...])
            dk_out[0, :width, cols] = jnp.where(
                kmask, dk[:, :LANE].astype(bf16), dk_out[0, :width, cols]
            )
            tile = lax.broadcasted_iota(jnp.int32, (width, LANE), 0) // LANE
            spread = lax.broadcasted_iota(jnp.int32, (width, LANE), 1)
            left = jnp.where((tile < spread - 1) & (spread < 8), dk[:, LANE:], 0.0)
            right = jnp.where((tile > spread + 1) & (spread < 8), dk[:, LANE:], 0.0)
            far_out[pl.ds(index, 1), :] += jnp.sum(left, axis=0, keepdims=True)
            far_out[pl.ds(4 + index, 1), :] += jnp.sum(right, axis=0, keepdims=True)
            dq = mm(ds_s[:width, :], jnp.where(kmask, kpair, jnp.zeros_like(kpair)), TN)
            qmask = head_mask(extent, head)
            dq_out[0, :, cols] = jnp.where(qmask, dq.astype(bf16), dq_out[0, :, cols])
            return carry

        lax.fori_loop(0, 4, head_step, 0)
        dwk[...] += mm(normt[0, :, :width], dk_out[0, :width, :])
        dwv[...] += mm(normt[0, :, :width], dv_out[0, :width, :])

    for blocks in range(1, extent // STEP + 1):

        @pl.when(steps == blocks)
        def _():
            attend(blocks * STEP)

    dwq[...] += mm(normt[0], dq_out[0])

    @pl.when(row == count - 1)
    def _():
        for n, ref in enumerate((dwq, dwk, dwv)):
            dw_out[:, n * STEP : (n + 1) * STEP] = ref[...].astype(bf16)


def bwd_quad(places, quad, held, q, k, v, mix, dmix, tail, near_t, normt, deps=()):
    count, quads, extent, _ = q.shape
    heads = tail.shape[1]
    width = normt.shape[1]
    per = heads // quads
    block = pl.BlockSpec((1, 1, extent, STEP), lambda i, s: (i, quad, 0, 0))
    given = pl.BlockSpec((1, extent, STEP), lambda i, s: (i, 0, 0))
    grid_spec = pltpu.PrefetchScalarGridSpec(
        num_scalar_prefetch=1,
        grid=(count,),
        in_specs=[block] * 5
        + [
            pl.BlockSpec((1, per, extent, LANE), lambda i, s: (i, quad, 0, 0)),
            pl.BlockSpec((per, 3 * LANE, LANE), lambda i, s: (quad, 0, 0)),
            pl.BlockSpec((1, width, extent), lambda i, s: (i, 0, 0)),
        ]
        + [pl.BlockSpec(memory_space=pl.ANY)] * (len(held) + len(deps)),
        out_specs=[given] * 3
        + [
            pl.BlockSpec((per, 3 * LANE, LANE), lambda i, s: (0, 0, 0)),
            pl.BlockSpec((8, LANE), lambda i, s: (0, 0)),
            pl.BlockSpec((width, 3 * STEP), lambda i, s: (0, quad)),
        ],
        scratch_shapes=[
            pltpu.VMEM((extent, LANE), bf16),
            pltpu.VMEM((extent, extent), bf16),
            pltpu.VMEM((extent, extent), bf16),
            pltpu.VMEM((extent, LANE), bf16),
            pltpu.VMEM((extent, 2 * LANE), bf16),
        ]
        + [pltpu.VMEM((width, STEP), f32)] * 3
        + [pltpu.VMEM((8, LANE), f32)],
    )
    out = jax.ShapeDtypeStruct((count, extent, STEP), bf16)
    return pl.pallas_call(
        functools.partial(bwd_body, count),
        grid_spec=grid_spec,
        out_shape=[out] * 3
        + [
            jax.ShapeDtypeStruct((per, 3 * LANE, LANE), f32),
            jax.ShapeDtypeStruct((8, LANE), f32),
            jax.ShapeDtypeStruct((width, 3 * STEP * quads), bf16),
        ],
        input_output_aliases={9: 5} if held else {},
        compiler_params=params(1, 60),
        cost_estimate=cost(1),
        name="attend_back",
    )(places, q, k, v, mix, dmix, tail, near_t, normt, *held, *deps)


def table_body(tacc, *rest):
    out = rest[-1]
    total = jnp.zeros((8, 4 * LANE), f32)
    for group in range(3 * LANE // 8):
        part = tacc[0, group * 8 : (group + 1) * 8, :]
        wide = jnp.concatenate([part, jnp.zeros((8, 3 * LANE), f32)], axis=1)
        total = total + (pltpu.roll(wide, 4 * LANE - 8 * group, 1) if group else wide)
    line = total[0:1]
    for row in range(1, 8):
        line = line + pltpu.roll(total[row : row + 1], 4 * LANE - row, 1)
    out[0] = line


def table_sums(tacc, far_sum, buckets, deps=()):
    heads = tacc.shape[0]
    diagonals = pl.pallas_call(
        table_body,
        grid=(heads,),
        in_specs=[pl.BlockSpec((1, 3 * LANE, LANE), lambda h: (h, 0, 0))]
        + [pl.BlockSpec(memory_space=pl.ANY)] * len(deps),
        out_specs=pl.BlockSpec((1, 1, 4 * LANE), lambda h: (h, 0, 0)),
        out_shape=jax.ShapeDtypeStruct((heads, 1, 4 * LANE), f32),
        cost_estimate=cost(100),
        name="table_diagonals",
    )(tacc, *deps)
    place = jnp.arange(4 * LANE, dtype=jnp.int32)
    back = jnp.where(place < LANE, place, place - 4 * LANE)
    hot = bucket_of(-back - LANE, buckets)[:, None] == jnp.arange(buckets, dtype=jnp.int32)
    near = jnp.einsum(
        "rb,hr->bh", hot.astype(f32), diagonals[:, 0, :], precision=lax.Precision.HIGHEST
    )
    sides = jnp.sum(far_sum, axis=2).reshape(-1, 2, 4)
    sides = jnp.transpose(sides, (1, 0, 2)).reshape(2, heads)
    half = buckets // 2
    near = near.at[half - 1].add(sides[0])
    return near.at[buckets - 1].add(sides[1])


CHUNK = 512
GELU_K = math.sqrt(2.0 / math.pi)


def gated(normed, g, w_gate, w_up, w_down):
    gate = mm(normed, w_gate)
    up = mm(normed, w_up)
    d_act = mm(g, w_down, NT)
    square = gate * gate
    th = jnp.tanh(gate * (GELU_K + (GELU_K * 0.044715) * square))
    half = 0.5 + 0.5 * th
    gelu = gate * half
    slope = half + (0.5 * gate) * (1.0 - th * th) * (GELU_K + (3.0 * 0.044715 * GELU_K) * square)
    return (
        (gelu * up).astype(bf16),
        (d_act * up * slope).astype(bf16),
        (d_act * gelu).astype(bf16),
    )


def ff_body(
    scal, xl, xr, gl, gr, mix, w_out, gain, w_gate, w_up, w_down,
    lo_out, lo_send, dh_out, dmix_out, dw_out, dgain_out,
    dwo, dwg, dwu, dwd, stage, sems,
):
    step = pl.program_id(0)
    last = pl.num_programs(0) - 1
    own = lax.rem(step, 2) == 0
    units = w_gate.shape[1]

    @pl.when(step == 0)
    def _():
        for ref in (dwo, dwg, dwu, dwd, dgain_out):
            ref[...] = jnp.zeros(ref.shape, f32)

    g = jnp.where(own, gl[0], gr[0])
    x = jnp.where(own, xl[0], xr[0]).astype(f32)
    quads = mix.shape[1]
    mixed = jnp.concatenate([mix[0, i] for i in range(quads)], axis=1)
    hidden = x + mm(mixed, w_out[...])
    gain_f = gain[...].astype(f32)
    scale = rms_of(hidden)
    unit = hidden * scale
    normed = (unit * gain_f).astype(bf16)
    normed_t = normed.T
    g_t = g.T
    out = hidden
    dn = jnp.zeros_like(hidden)
    for c in range(units // CHUNK):
        cols = slice(c * CHUNK, (c + 1) * CHUNK)
        act, d_gate, d_up = gated(normed, g, w_gate[:, cols], w_up[:, cols], w_down[cols, :])
        out = out + mm(act, w_down[cols, :])
        dn = dn + mm(d_gate, w_gate[:, cols], NT) + mm(d_up, w_up[:, cols], NT)
        dwd[:, cols] += mm(g_t, act)
        dwg[:, cols] += mm(normed_t, d_gate)
        dwu[:, cols] += mm(normed_t, d_up)

    @pl.when(own)
    def _():
        lo_out[0] = out

    @pl.when(jnp.logical_not(own))
    def _():
        lo_send[0] = out.astype(bf16)

    dgain_out[...] += jnp.sum(dn * unit, axis=0, keepdims=True)
    e = dn * gain_f
    d_hidden = (
        g.astype(f32) + scale * e - unit * (scale * jnp.mean(unit * e, axis=-1, keepdims=True))
    )
    dh_out[0] = d_hidden
    low = d_hidden.astype(bf16)
    dwo[...] += mm(mixed.T, low)
    d_mixed = mm(low, w_out[...], NT).astype(bf16)
    for i in range(quads):
        dmix_out[0, i] = d_mixed[:, i * STEP : (i + 1) * STEP]

    @pl.when(step == last)
    def _():
        rows = stage.shape[1]
        jobs, place = [], 0
        for acc in (dwg, dwu, dwd, dwo):
            jobs += [(acc, place, part) for part in range(acc.shape[0] // rows)]
            place += acc.shape[1]
        pending = [None, None]
        for n, (acc, place, part) in enumerate(jobs):
            slot = n % 2
            if pending[slot] is not None:
                pending[slot].wait()
            span = slice(part * rows, (part + 1) * rows)
            cols = acc.shape[1]
            stage[slot, :, :cols] = acc[span, :].astype(bf16)
            copy = pltpu.make_async_copy(
                stage.at[slot, :, pl.ds(0, cols)],
                dw_out.at[pl.ds(part * rows, rows), pl.ds(place, cols)],
                sems.at[slot],
            )
            copy.start()
            pending[slot] = copy
        for copy in pending:
            copy.wait()


def feed_forward(places, inputs, x_remote, cot, cot_remote, mix, w_out, gain, w_gate, w_up, w_down):
    rows, half, width = inputs.shape
    mine = x_remote.shape[0]
    _, quads, extent, _ = mix.shape
    units = w_gate.shape[1]
    inner = w_out.shape[0]

    def keep(shape):
        return pl.BlockSpec(shape, lambda i, s: (0,) * len(shape), pipeline_mode=pl.Buffered(1))

    local = pl.BlockSpec((1, half, width), lambda i, s: (s[1 + i // 2], 0, 0))
    far = pl.BlockSpec((1, half, width), lambda i, s: (i // 2, 0, 0))
    far_one = pl.BlockSpec(
        (1, half, width), lambda i, s: (i // 2, 0, 0), pipeline_mode=pl.Buffered(1)
    )
    spot = pl.BlockSpec(
        (1, quads, half, STEP),
        lambda i, s: (i // 2, 0, jnp.where(i % 2 == 0, s[0], 1 - s[0]), 0),
    )
    tile = pl.BlockSpec((1, half, width), lambda i, s: (i, 0, 0))
    anywhere = pl.BlockSpec(memory_space=pl.ANY)
    grid_spec = pltpu.PrefetchScalarGridSpec(
        num_scalar_prefetch=1,
        grid=(2 * mine,),
        in_specs=[local, far_one, local, far_one, spot, keep((inner, width)), keep((1, width)),
                  keep((width, units)), keep((width, units)), keep((units, width))],
        out_specs=[local, far, tile, spot, anywhere,
                   pl.BlockSpec((1, width), lambda i, s: (0, 0))],
        scratch_shapes=[pltpu.VMEM((inner, width), f32)]
        + [pltpu.VMEM((width, units), f32)] * 3
        + [pltpu.VMEM((2, 32, units), bf16), pltpu.SemaphoreType.DMA((2,))],
    )
    return pl.pallas_call(
        ff_body,
        grid_spec=grid_spec,
        out_shape=[
            jax.ShapeDtypeStruct((rows, half, width), f32),
            jax.ShapeDtypeStruct((mine, half, width), bf16),
            jax.ShapeDtypeStruct((2 * mine, half, width), f32),
            jax.ShapeDtypeStruct((mine, quads, extent, STEP), bf16),
            jax.ShapeDtypeStruct((width, 3 * units + width), bf16),
            jax.ShapeDtypeStruct((1, width), f32),
        ],
        compiler_params=params(1, 63),
        cost_estimate=cost(150),
        name="feed_forward",
    )(places, inputs, x_remote, cot, cot_remote, mix, w_out, gain, w_gate, w_up, w_down)


def spread_body(sums, *rest):
    gate_out, up_out, down_out, out_out = rest[-4:]
    units = gate_out.shape[1]
    gate_out[...] = sums[:, :units].astype(f32)
    up_out[...] = sums[:, units : 2 * units].astype(f32)
    down_out[...] = sums[:, 2 * units : 3 * units].astype(f32).T
    out_out[...] = sums[:, 3 * units :].astype(f32)


def spread(sums, deps=()):
    width, columns = sums.shape
    units = (columns - width) // 3
    wide = pl.BlockSpec((LANE, units), lambda i: (i, 0))
    return pl.pallas_call(
        spread_body,
        grid=(width // LANE,),
        in_specs=[pl.BlockSpec((LANE, columns), lambda i: (i, 0))]
        + [pl.BlockSpec(memory_space=pl.ANY)] * len(deps),
        out_specs=[
            wide,
            wide,
            pl.BlockSpec((units, LANE), lambda i: (0, i)),
            pl.BlockSpec((LANE, width), lambda i: (i, 0)),
        ],
        out_shape=[
            jax.ShapeDtypeStruct((width, units), f32),
            jax.ShapeDtypeStruct((width, units), f32),
            jax.ShapeDtypeStruct((units, width), f32),
            jax.ShapeDtypeStruct((width, width), f32),
        ],
        compiler_params=params(1, 56),
        cost_estimate=cost(100),
        name="spread",
    )(sums, *deps)


def back_body(quads, held, scal, xl, xr, dh, *rest):
    grads = rest[: 3 * quads]
    gain, wq, wk, wv = rest[3 * quads : 3 * quads + 4]
    ig_out, ig_send, dgain_out = rest[-3:]
    step = pl.program_id(0)
    far = step == 0

    @pl.when(far)
    def _():
        dgain_out[...] = jnp.zeros(dgain_out.shape, f32)

    x = jnp.where(far, xr[0], xl[0]).astype(f32)
    dn = jnp.zeros_like(x)
    for n, weight in enumerate((wq, wk, wv)):
        part = jnp.concatenate([ref[0] for ref in grads[n * quads : (n + 1) * quads]], axis=1)
        dn = dn + mm(part, weight[...], NT)
    scale = rms_of(x)
    unit = x * scale
    dgain_out[...] += jnp.sum(dn * unit, axis=0, keepdims=True)
    e = dn * gain[...].astype(f32)
    out = dh[0] + scale * e - unit * (scale * jnp.mean(unit * e, axis=-1, keepdims=True))

    @pl.when(far)
    def _():
        ig_send[0] = out.astype(bf16)

    @pl.when(jnp.logical_not(far))
    def _():
        ig_out[0] = out


def input_back(places, row, held, inputs, remote, dh, dq, dk, dv, gain, wq, wk, wv, deps=()):
    rows, half, width = inputs.shape
    local = pl.BlockSpec((1, half, width), lambda i, s: (s[1 + row], 0, 0))
    one = pl.BlockSpec((1, half, width), lambda i, s: (0, 0, 0))
    tile = pl.BlockSpec((1, half, width), lambda i, s: (2 * row + 1 - i, 0, 0))
    spot = pl.BlockSpec((1, half, STEP), lambda i, s: (row, jnp.where(i == 1, s[0], 1 - s[0]), 0))
    weight = pl.BlockSpec(wq.shape, lambda i, s: (0, 0), pipeline_mode=pl.Buffered(1))
    line = pl.BlockSpec((1, width), lambda i, s: (0, 0))
    anywhere = pl.BlockSpec(memory_space=pl.ANY)
    grads = [*dq, *dk, *dv]
    grid_spec = pltpu.PrefetchScalarGridSpec(
        num_scalar_prefetch=1,
        grid=(2,),
        in_specs=[local, one, tile]
        + [spot] * len(grads)
        + [line, weight, weight, weight]
        + [anywhere] * (len(held) + len(deps)),
        out_specs=[local, one, line],
    )
    return pl.pallas_call(
        functools.partial(back_body, len(dq), len(held)),
        grid_spec=grid_spec,
        out_shape=[
            jax.ShapeDtypeStruct((rows, half, width), f32),
            jax.ShapeDtypeStruct((1, half, width), bf16),
            jax.ShapeDtypeStruct((1, width), f32),
        ],
        input_output_aliases={8 + len(grads): 0} if held else {},
        compiler_params=params(1, 56),
        cost_estimate=cost(100),
        name="input_back",
    )(places, inputs, remote, dh, *grads, gain, wq, wk, wv, *held, *deps)


def hold_body(value, *rest):
    rest[-1][...] = value[...]


def hold(value, deps):
    return pl.pallas_call(
        hold_body,
        in_specs=[pl.BlockSpec(memory_space=pltpu.VMEM)]
        + [pl.BlockSpec(memory_space=pl.ANY)] * len(deps),
        out_specs=pl.BlockSpec(memory_space=pltpu.VMEM),
        out_shape=jax.ShapeDtypeStruct(value.shape, value.dtype),
        compiler_params=pltpu.CompilerParams(vmem_limit_bytes=16 << 20),
        name="hold",
    )(value, *deps)


def pick_half(grads, at, deps):
    rows, columns = grads.shape
    grid_spec = pltpu.PrefetchScalarGridSpec(
        num_scalar_prefetch=1,
        grid=(1,),
        in_specs=[pl.BlockSpec((rows // 2, columns), lambda i, s: (s[0], 0))]
        + [pl.BlockSpec(memory_space=pl.ANY)] * len(deps),
        out_specs=pl.BlockSpec((rows // 2, columns), lambda i, s: (0, 0)),
    )
    return pl.pallas_call(
        pick_body,
        grid_spec=grid_spec,
        out_shape=jax.ShapeDtypeStruct((rows // 2, columns), grads.dtype),
        compiler_params=params(1, 24),
        name="pick_half",
    )(at.reshape(1), grads, *deps)


def pick_body(scal, array, *rest):
    rest[-1][...] = array[...]


def pick_rows(places, first, count, array, deps=()):
    rows, half, width = array.shape
    grid_spec = pltpu.PrefetchScalarGridSpec(
        num_scalar_prefetch=1,
        grid=(count,),
        in_specs=[pl.BlockSpec((1, half, width), lambda i, s: (s[1 + rows // 2 + first + i], 0, 0))]
        + [pl.BlockSpec(memory_space=pl.ANY)] * len(deps),
        out_specs=pl.BlockSpec((1, half, width), lambda i, s: (i, 0, 0)),
    )
    return pl.pallas_call(
        pick_body,
        grid_spec=grid_spec,
        out_shape=jax.ShapeDtypeStruct((count, half, width), array.dtype),
        compiler_params=params(1, 16),
        name="pick_rows",
    )(places, array, *deps)


def place_body(scal, arrived, *rest):
    out, token = rest[-2:]
    out[0] = arrived[0].astype(f32)
    token[...] = jnp.zeros(token.shape, f32)


def place_rows(places, first, arrived, held, deps=()):
    count, half, width = arrived.shape
    at = 1 + held.shape[0] // 2 + first
    anywhere = pl.BlockSpec(memory_space=pl.ANY)
    grid_spec = pltpu.PrefetchScalarGridSpec(
        num_scalar_prefetch=1,
        grid=(count,),
        in_specs=[pl.BlockSpec((1, half, width), lambda i, s: (i, 0, 0)), anywhere]
        + [anywhere] * len(deps),
        out_specs=[
            pl.BlockSpec((1, half, width), lambda i, s: (s[at + i], 0, 0)),
            pl.BlockSpec((8, LANE), lambda i, s: (0, 0)),
        ],
    )
    return pl.pallas_call(
        place_body,
        grid_spec=grid_spec,
        out_shape=[
            jax.ShapeDtypeStruct(held.shape, f32),
            jax.ShapeDtypeStruct((8, LANE), f32),
        ],
        input_output_aliases={2: 0},
        compiler_params=params(1, 32),
        cost_estimate=cost(100),
        name="place_rows",
    )(places, arrived, held, *deps)


highest = lax.Precision.HIGHEST


def rms_scaled(values, gain):
    mean_square = jnp.mean(values * values, axis=-1, keepdims=True)
    return values * lax.rsqrt(mean_square + epsilon) * gain


def gated_unit(gate, up_proj):
    return jax.nn.gelu(gate, approximate=True) * up_proj


def relative_one_hot(query_anchor, query_extent, key_extent, bucket_count):
    query_place = query_anchor + jnp.arange(query_extent, dtype=jnp.int32)
    key_place = jnp.arange(key_extent, dtype=jnp.int32)
    offset = key_place[None, :] - query_place[:, None]
    distance = jnp.abs(offset)
    far_bucket = jnp.full_like(distance, 8)
    for threshold in bucket_bounds:
        far_bucket = far_bucket + (distance >= threshold).astype(jnp.int32)
    bucket = jnp.where(offset > 0, bucket_count // 2, 0) + jnp.where(
        distance < 8, distance, far_bucket
    )
    return (bucket[:, :, None] == jnp.arange(bucket_count, dtype=jnp.int32)).astype(jnp.float32)


def block_scores(query_heads, key_heads, query_anchor, lengths, bias_f):
    key_extent = key_heads.shape[1]
    one_hot = relative_one_hot(query_anchor, query_heads.shape[1], key_extent, bias_f.shape[0])
    bias_block = jnp.einsum("qkb,bh->hqk", one_hot, bias_f, precision=highest)
    raw_scores = jnp.einsum(
        "rqhd,rkhd->rhqk", query_heads, key_heads, preferred_element_type=jnp.float32
    )
    usable = jnp.arange(key_extent, dtype=jnp.int32)[None, :] < lengths[:, None]
    return (
        jnp.where(usable[:, None, None, :], raw_scores + bias_block[None], masked_score),
        one_hot,
    )


def score_grads(scores, log_total, row_dot, grad_heads, value_heads):
    weights_hp = jnp.exp(scores - log_total[..., None])
    d_weights = jnp.einsum(
        "rqhd,rkhd->rhqk", grad_heads, value_heads, preferred_element_type=jnp.float32
    )
    d_scores = (weights_hp * (d_weights - row_dot[..., None])).astype(jnp.bfloat16)
    return (weights_hp.astype(jnp.bfloat16), d_scores)


def table_term(one_hot, d_scores):
    summed = jnp.sum(d_scores, axis=0, dtype=jnp.float32)
    return jnp.einsum("qkb,hqk->bh", one_hot, summed, precision=highest)


def gathered_device(
    inputs,
    lengths,
    cotangent,
    norm_gain,
    w_query,
    w_key,
    w_value,
    w_out,
    ff_gain,
    w_gate,
    w_up,
    w_down,
    bias_table,
):
    row_count, block_len, model_width = inputs.shape
    head_count = bias_table.shape[1]
    inner_width = w_query.shape[1]
    head_width = inner_width // head_count
    tokens_here = row_count * block_len
    lengths = lengths.reshape(-1)
    bias_f = bias_table.astype(jnp.float32)
    own_anchor = lax.axis_index("seq") * block_len

    def split_heads(block_array):
        return block_array.reshape(row_count, block_array.shape[1], head_count, head_width)

    tokens_f = inputs.astype(jnp.float32).reshape(tokens_here, model_width)
    normed_f, norm_pull = jax.vjp(rms_scaled, tokens_f, norm_gain.astype(jnp.float32))
    normed = normed_f.astype(jnp.bfloat16)
    queries = (
        jnp.dot(normed, w_query, preferred_element_type=jnp.float32)
        .astype(jnp.bfloat16)
        .reshape(row_count, block_len, inner_width)
    )
    keys = (
        jnp.dot(normed, w_key, preferred_element_type=jnp.float32)
        .astype(jnp.bfloat16)
        .reshape(row_count, block_len, inner_width)
    )
    values = (
        jnp.dot(normed, w_value, preferred_element_type=jnp.float32)
        .astype(jnp.bfloat16)
        .reshape(row_count, block_len, inner_width)
    )
    query_heads = split_heads(queries)
    stat_shape = (row_count, head_count, block_len)
    pieces = (
        lax.all_gather(keys, "seq", axis=1, tiled=True),
        lax.all_gather(values, "seq", axis=1, tiled=True),
    )
    row_max = jnp.full(stat_shape, start_max, jnp.float32)
    key_heads = split_heads(pieces[0])
    value_heads = split_heads(pieces[1])
    scores, one_hot = block_scores(query_heads, key_heads, own_anchor, lengths, bias_f)
    new_max = jnp.maximum(row_max, jnp.max(scores, axis=-1))
    weights_hp = jnp.exp(scores - new_max[..., None])
    row_sum = jnp.sum(weights_hp, axis=-1)
    weighted = jnp.einsum(
        "rhqk,rkhd->rhqd",
        weights_hp.astype(jnp.bfloat16),
        value_heads,
        preferred_element_type=jnp.float32,
    )
    row_max, row_sum, weighted = (new_max, row_sum, weighted)
    log_total = row_max + jnp.log(row_sum)
    mixed_heads = jnp.transpose(weighted / row_sum[..., None], (0, 2, 1, 3))
    mixed_low = mixed_heads.reshape(tokens_here, inner_width).astype(jnp.bfloat16)
    hidden = tokens_f + jnp.dot(mixed_low, w_out, preferred_element_type=jnp.float32)
    normed2_f, ff_pull = jax.vjp(rms_scaled, hidden, ff_gain.astype(jnp.float32))
    normed2 = normed2_f.astype(jnp.bfloat16)
    gate = jnp.dot(normed2, w_gate, preferred_element_type=jnp.float32)
    up_proj = jnp.dot(normed2, w_up, preferred_element_type=jnp.float32)
    activated, gated_pull = jax.vjp(gated_unit, gate, up_proj)
    act_low = activated.astype(jnp.bfloat16)
    layer_output = (hidden + jnp.dot(act_low, w_down, preferred_element_type=jnp.float32)).reshape(
        row_count, block_len, model_width
    )
    grad_out = cotangent.reshape(tokens_here, model_width)
    dw_down = jnp.einsum("tf,td->fd", act_low, grad_out, preferred_element_type=jnp.float32)
    d_act = jnp.einsum("td,fd->tf", grad_out, w_down, preferred_element_type=jnp.float32)
    d_gate, d_up = gated_pull(d_act)
    d_gate = d_gate.astype(jnp.bfloat16)
    d_up = d_up.astype(jnp.bfloat16)
    dw_gate = jnp.einsum("td,tf->df", normed2, d_gate, preferred_element_type=jnp.float32)
    dw_up = jnp.einsum("td,tf->df", normed2, d_up, preferred_element_type=jnp.float32)
    d_normed2 = jnp.einsum(
        "tf,df->td", d_gate, w_gate, preferred_element_type=jnp.float32
    ) + jnp.einsum("tf,df->td", d_up, w_up, preferred_element_type=jnp.float32)
    d_hidden_part, d_ff_gain = ff_pull(d_normed2)
    d_hidden = grad_out.astype(jnp.float32) + d_hidden_part
    d_hidden_low = d_hidden.astype(jnp.bfloat16)
    dw_out = jnp.einsum("ti,td->id", mixed_low, d_hidden_low, preferred_element_type=jnp.float32)
    d_mixed = (
        jnp.einsum("td,id->ti", d_hidden_low, w_out, preferred_element_type=jnp.float32)
        .astype(jnp.bfloat16)
        .reshape(row_count, block_len, inner_width)
    )
    grad_heads = split_heads(d_mixed)
    row_dot_rows = jnp.sum(grad_heads.astype(jnp.float32) * mixed_heads, axis=-1)
    row_dot = jnp.transpose(row_dot_rows, (0, 2, 1))
    pieces = (
        lax.all_gather(keys, "seq", axis=1, tiled=True),
        lax.all_gather(values, "seq", axis=1, tiled=True),
    )
    key_heads = split_heads(pieces[0])
    value_heads = split_heads(pieces[1])
    scores, one_hot = block_scores(query_heads, key_heads, own_anchor, lengths, bias_f)
    weights_low, d_scores = score_grads(scores, log_total, row_dot, grad_heads, value_heads)
    d_query_part = jnp.einsum(
        "rhqk,rkhd->rqhd", d_scores, key_heads, preferred_element_type=jnp.float32
    )
    key_heads, weights_low, d_scores, d_query_part, table_part = (
        key_heads,
        weights_low,
        d_scores,
        d_query_part,
        table_term(one_hot, d_scores),
    )
    extent = key_heads.shape[1]
    d_key_part = jnp.einsum(
        "rhqk,rqhd->rkhd", d_scores, query_heads, preferred_element_type=jnp.float32
    ).reshape(row_count, extent, inner_width)
    d_value_part = jnp.einsum(
        "rhqk,rqhd->rkhd", weights_low, grad_heads, preferred_element_type=jnp.float32
    ).reshape(row_count, extent, inner_width)
    d_key, d_value = (
        lax.psum_scatter(d_key_part, "seq", scatter_dimension=1, tiled=True),
        lax.psum_scatter(d_value_part, "seq", scatter_dimension=1, tiled=True),
    )
    d_query_low = d_query_part.reshape(tokens_here, inner_width).astype(jnp.bfloat16)
    d_key_low = d_key.reshape(tokens_here, inner_width).astype(jnp.bfloat16)
    d_value_low = d_value.reshape(tokens_here, inner_width).astype(jnp.bfloat16)
    dw_query = jnp.einsum("td,ti->di", normed, d_query_low, preferred_element_type=jnp.float32)
    dw_key = jnp.einsum("td,ti->di", normed, d_key_low, preferred_element_type=jnp.float32)
    dw_value = jnp.einsum("td,ti->di", normed, d_value_low, preferred_element_type=jnp.float32)
    d_normed = jnp.einsum("ti,di->td", d_query_low, w_query, preferred_element_type=jnp.float32)
    d_normed = d_normed + jnp.einsum(
        "ti,di->td", d_key_low, w_key, preferred_element_type=jnp.float32
    )
    d_normed = d_normed + jnp.einsum(
        "ti,di->td", d_value_low, w_value, preferred_element_type=jnp.float32
    )
    d_tokens_part, d_norm_gain = norm_pull(d_normed)
    input_grad = (d_hidden + d_tokens_part).reshape(row_count, block_len, model_width)
    flat_query = dw_query.reshape(-1)
    flat_key = dw_key.reshape(-1)
    flat_value = dw_value.reshape(-1)
    flat_out = dw_out.reshape(-1)
    flat_gate = dw_gate.reshape(-1)
    flat_up = dw_up.reshape(-1)
    flat_down = dw_down.reshape(-1)
    shares = (
        lax.psum_scatter(flat_query, ("batch", "seq"), scatter_dimension=0, tiled=True),
        lax.psum_scatter(flat_key, ("batch", "seq"), scatter_dimension=0, tiled=True),
        lax.psum_scatter(flat_value, ("batch", "seq"), scatter_dimension=0, tiled=True),
        lax.psum_scatter(flat_out, ("batch", "seq"), scatter_dimension=0, tiled=True),
        lax.psum_scatter(flat_gate, ("batch", "seq"), scatter_dimension=0, tiled=True),
        lax.psum_scatter(flat_up, ("batch", "seq"), scatter_dimension=0, tiled=True),
        lax.psum_scatter(flat_down, ("batch", "seq"), scatter_dimension=0, tiled=True),
    )
    summed = (
        lax.all_gather(shares[0], ("batch", "seq"), axis=0, tiled=True),
        lax.all_gather(shares[1], ("batch", "seq"), axis=0, tiled=True),
        lax.all_gather(shares[2], ("batch", "seq"), axis=0, tiled=True),
        lax.all_gather(shares[3], ("batch", "seq"), axis=0, tiled=True),
        lax.all_gather(shares[4], ("batch", "seq"), axis=0, tiled=True),
        lax.all_gather(shares[5], ("batch", "seq"), axis=0, tiled=True),
        lax.all_gather(shares[6], ("batch", "seq"), axis=0, tiled=True),
    )
    sum_norm, sum_ff, sum_table = lax.psum((d_norm_gain, d_ff_gain, table_part), ("batch", "seq"))
    return (
        layer_output,
        input_grad,
        sum_norm,
        summed[0].reshape(w_query.shape),
        summed[1].reshape(w_key.shape),
        summed[2].reshape(w_value.shape),
        summed[3].reshape(w_out.shape),
        sum_ff,
        summed[4].reshape(w_gate.shape),
        summed[5].reshape(w_up.shape),
        summed[6].reshape(w_down.shape),
        sum_table,
    )


def all_pairs(mesh_batch, mesh_seq, move):
    pairs = []
    for batch in range(mesh_batch):
        for seq in range(mesh_seq):
            z, y, core, x = move(batch // 4, batch // 2 % 2, batch % 2, seq)
            pairs.append((batch * mesh_seq + seq, (z * 4 + y * 2 + core) * mesh_seq + x))
    return pairs


def add_up(parts):
    total = parts[0].astype(f32)
    for part in parts[1:]:
        total = total + part.astype(f32)
    return total


class Links:
    def __init__(self, batch, seq):
        self.axes = ("batch", "seq")
        self.deep = batch // 4
        me = lax.axis_index("batch")
        self.z, self.y, self.core = me // 4, me // 2 % 2, me % 2
        self.x = lax.axis_index("seq")
        self.plane = self.y * 2 + self.x
        pairs = functools.partial(all_pairs, batch, seq)
        self.to_core = pairs(lambda z, y, c, x: (z, y, 1 - c, x))
        self.to_plane = {
            k: pairs(lambda z, y, c, x, k=k: (z, y ^ (k >> 1), c, x ^ (k & 1))) for k in (1, 2, 3)
        }
        self.to_deep = {
            k: pairs(lambda z, y, c, x, k=k: ((z + k) % self.deep, y, c, x))
            for k in range(1, self.deep)
        }

    def send(self, value, pairs):
        return lax.ppermute(value, self.axes, pairs)

    def pick(self, value, at):
        return lax.dynamic_index_in_dim(value, at, 0, keepdims=False)

    def scatter_core(self, grads, deps=()):
        rows, columns = grads.shape
        shape = (4, self.deep, rows // (8 * self.deep), columns)
        got = self.send(pick_half(grads, 1 - self.core, deps), self.to_core)
        own = self.pick(grads.reshape(2, *shape), self.core)
        return add_up([own, got.reshape(shape)]).astype(bf16)

    def scatter_plane(self, part):
        got = [self.send(self.pick(part, self.plane ^ k), self.to_plane[k]) for k in (1, 2, 3)]
        return add_up([self.pick(part, self.plane), *got]).astype(bf16)

    def scatter_pair(self, part, bit):
        at = self.y if bit else self.x
        got = self.send(self.pick(part, 1 - at), self.to_plane[1 + bit])
        return add_up([self.pick(part, at), got]).astype(bf16)

    def scatter_deep(self, part):
        got = [
            self.send(self.pick(part, (self.z + k) % self.deep), self.to_deep[k])
            for k in range(1, self.deep)
        ]
        return add_up([self.pick(part, self.z), *got]).astype(bf16)

    def lay(self, count, at, own, got):
        out = jnp.zeros((count,) + own.shape, own.dtype)
        out = lax.dynamic_update_index_in_dim(out, own, at, 0)
        for place, piece in got:
            out = lax.dynamic_update_index_in_dim(out, piece, place, 0)
        return out

    def gather_deep(self, part):
        got = [
            ((self.z - k) % self.deep, self.send(part, self.to_deep[k]))
            for k in range(1, self.deep)
        ]
        return self.lay(self.deep, self.z, part, got)

    def gather_plane(self, part):
        got = [(self.plane ^ k, self.send(part, self.to_plane[k])) for k in (1, 2, 3)]
        return self.lay(4, self.plane, part, got)

    def gather_core(self, part):
        out = self.lay(2, self.core, part, [(1 - self.core, self.send(part, self.to_core))])
        return out.reshape(-1, out.shape[-1])

    def total(self, grads):
        part = self.scatter_deep(self.scatter_plane(self.scatter_core(grads)))
        return self.gather_core(self.gather_plane(self.gather_deep(part)))


def rows_device(
    batch,
    seq,
    inputs,
    lengths,
    cotangent,
    norm_gain,
    w_query,
    w_key,
    w_value,
    w_out,
    ff_gain,
    w_gate,
    w_up,
    w_down,
    bias_table,
):
    rows, half, width = inputs.shape
    buckets, heads = bias_table.shape
    mine_count = rows // 2
    links = Links(batch, seq)
    places = split_rows(lengths, links.x)
    swap = [(0, 1), (1, 0)]

    x_parts, tick = [], ()
    for row in range(mine_count):
        x_parts.append(lax.ppermute(pick_rows(places, row, 1, inputs, tick), "seq", swap))
        tick = (links.send(tick[0] if tick else places.astype(f32), links.to_core),)
    g_remote = lax.ppermute(pick_rows(places, 0, mine_count, cotangent, tick), "seq", swap)
    near, near_t, far = bias_pieces(bias_table, 2 * half // LANE)
    gain = norm_gain.reshape(1, width)
    gain2 = ff_gain.reshape(1, width)
    held = []
    for row in range(mine_count):
        held = fwd_row(
            places, inputs, x_parts[row], row, mine_count, held,
            gain, w_query, w_key, w_value, near, far, heads,
        )
    q, k, v, mix, tail, normt = held
    x_remote = jnp.concatenate(x_parts, axis=0)
    ff_args = (
        places, inputs, x_remote, cotangent, g_remote, mix,
        w_out, gain2, w_gate, w_up, w_down,
    )
    lo, lo_send, dh, dmix, ff_grads, ff_gain_part = feed_forward(*ff_args)
    ff_total = lax.psum(ff_grads, ("batch", "seq"))
    lo_got = lax.ppermute(lo_send, "seq", swap)
    quads = q.shape[1]
    dw, backs, token = [], [], ()
    for quad in range(quads):
        if quad == quads - 1:
            layer_output, placed = place_rows(places, 0, lo_got, lo)
            token = (placed,)
        *back, dw_quad = bwd_quad(
            places, quad, dw, q, k, v, mix, dmix, tail, near_t, normt, token
        )
        backs.append(back)
        dw = [dw_quad]
    dq, dk, dv, tacc, far_sum = zip(*backs)
    qkv = links.scatter_core(dw[0])
    ig, ig_got, gain_parts, token = [], [], [], ()
    for row in range(mine_count):
        *ig, sent, gain_part = input_back(
            places, row, ig, inputs, x_parts[row], dh, dq, dk, dv,
            gain, w_query, w_key, w_value, token,
        )
        ig_got.append(lax.ppermute(sent, "seq", swap))
        gain_parts.append(gain_part)
        if row == 0:
            token = (qkv,)
            qkv = links.scatter_plane(qkv)
        elif row == 1:
            qkv = hold(qkv, (gain_part,))
            token = (qkv,)
            qkv = links.scatter_deep(qkv)
    after = (gain_parts[-1],)
    qkv = hold(qkv, after)
    table_part = table_sums(
        jnp.concatenate(tacc, axis=0), jnp.stack(far_sum), buckets, (qkv,)
    )
    small = jnp.concatenate(
        [sum(gain_parts)[0], ff_gain_part[0], table_part.reshape(-1)]
    )
    qkv = links.gather_deep(qkv)
    small = add_up([small, links.send(small, links.to_core)])
    input_grad, placed = place_rows(places, 0, ig_got[0], ig[0], (table_part,))
    qkv = hold(qkv, (placed, small))
    gate_grad, up_grad, down_grad, out_grad = spread(ff_total, (qkv,))
    qkv_ready = qkv
    qkv = links.gather_plane(qkv)
    small = hold(small, (qkv_ready,))
    small = add_up([small, *[links.send(small, p) for p in links.to_plane.values()]])
    for row in range(1, mine_count - 1):
        input_grad, placed = place_rows(places, row, ig_got[row], input_grad)
    qkv = hold(qkv, (out_grad, placed, small))
    input_grad, _ = place_rows(places, mine_count - 1, ig_got[-1], input_grad, (qkv,))
    small = hold(small, (qkv,))
    qkv = links.gather_core(qkv)
    small = add_up([small, *[links.send(small, p) for p in links.to_deep.values()]])

    def whole(n):
        return jnp.concatenate(
            [qkv[:, (3 * i + n) * STEP : (3 * i + n + 1) * STEP] for i in range(quads)], axis=1
        ).astype(f32)

    return (
        layer_output,
        input_grad,
        small[:width],
        whole(0),
        whole(1),
        whole(2),
        out_grad,
        small[width : 2 * width],
        gate_grad,
        up_grad,
        down_grad,
        small[2 * width :].reshape(buckets, heads),
    )


def solution(mesh):
    split = P("batch", "seq", None)
    in_specs = (split, P("batch", None), split) + (P(),) * 10
    out_specs = (split, split) + (P(),) * 10
    batch, seq = mesh.shape["batch"], mesh.shape["seq"]

    def per_device(inputs, *rest):
        rows, half, width = inputs.shape
        buckets, heads = rest[-1].shape
        inner = rest[3].shape[1]
        fits = seq == 2 and batch % 4 == 0 and rows % 2 == 0 and rows >= 4 and buckets == 32
        fits = fits and half % STEP == 0 and 2 * half // LANE <= 8
        fits = fits and inner == width and width % (16 * batch) == 0 and inner // heads == LANE // 2
        if fits:
            return rows_device(batch, seq, inputs, *rest)
        return gathered_device(inputs, *rest)

    return jax.shard_map(
        per_device, mesh=mesh, in_specs=in_specs, out_specs=out_specs, check_vma=False
    )
```

```python
import functools
import itertools
import math

import jax
import jax.numpy as jnp
from jax import lax
from jax.experimental import pallas as pl
from jax.experimental.pallas import tpu as pltpu
from jax.sharding import PartitionSpec as P

f32 = jnp.float32
bf16 = jnp.bfloat16
epsilon = 1e-06
masked_score = -2e30
start_max = -1e30
bucket_bounds = (12, 16, 23, 32, 46, 64, 91)
LANE = 128
STEP = 256
NT = (((1,), (1,)), ((), ()))
NN = (((1,), (0,)), ((), ()))
TN = (((0,), (0,)), ((), ()))


def mm(a, b, dims=NN):
    return lax.dot_general(a, b, dims, preferred_element_type=f32)


def cost(micros):
    return pl.CostEstimate(flops=int(micros * 0.3e9), bytes_accessed=0, transcendentals=0)


def params(grid_dims, mib):
    return pltpu.CompilerParams(
        dimension_semantics=("arbitrary",) * grid_dims, vmem_limit_bytes=mib << 20
    )


def bucket_of(offset, bucket_count):
    distance = jnp.abs(offset)
    far = jnp.full_like(distance, 8)
    for bound in bucket_bounds:
        far = far + (distance >= bound).astype(jnp.int32)
    half = bucket_count // 2
    return jnp.where(offset > 0, half, 0) + jnp.where(distance < 8, distance, far)


def split_body(choices, side, lengths, out):
    rows = lengths.shape[1]
    count = rows // 2
    load = [(lengths[0, r] + STEP - 1) // STEP for r in range(rows)]
    best = None
    for own in choices:
        other = [r for r in range(rows) if r not in own]
        uneven = jnp.abs(sum(load[r] for r in own) - sum(load[r] for r in other))
        new = [*own, *other]
        if best is None:
            best, picked = uneven, [jnp.int32(r) for r in new]
        else:
            better = uneven < best
            best = jnp.where(better, uneven, best)
            picked = [jnp.where(better, r, old) for r, old in zip(new, picked)]
    first = side[0] == 0
    out[0] = side[0]
    for n in range(count):
        mine = jnp.where(first, picked[n], picked[count + n])
        out[1 + n] = mine
        out[1 + count + n] = jnp.where(first, picked[count + n], picked[n])
        out[1 + 2 * count + n] = lengths[0, mine]


def split_rows(lengths, side):
    rows = lengths.shape[1]
    choices = [c for c in itertools.combinations(range(rows), rows // 2) if 0 in c]
    smem = pl.BlockSpec(memory_space=pltpu.SMEM)
    return pl.pallas_call(
        functools.partial(split_body, choices),
        in_specs=[smem, smem],
        out_specs=smem,
        out_shape=jax.ShapeDtypeStruct((1 + 3 * (rows // 2),), jnp.int32),
        name="split_rows",
    )(side.reshape(1), lengths)


def near_body(vec_ref, rev_ref, near_ref, near_t_ref):
    wide = jnp.broadcast_to(vec_ref[0], (LANE, 4 * LANE))
    near_ref[0] = pltpu.roll(wide, 0, 1, stride=1, stride_axis=0)[:, : 3 * LANE]
    tall = jnp.broadcast_to(rev_ref[0], (3 * LANE, 4 * LANE))
    near_t_ref[0] = pltpu.roll(tall, 0, 1, stride=1, stride_axis=0)[:, :LANE]


def near_offsets():
    place = jnp.arange(4 * LANE, dtype=jnp.int32)
    signed = jnp.where(place < 3 * LANE, place, place - 4 * LANE)
    forward = signed - LANE
    back = jnp.where(place < LANE, place, place - 4 * LANE)
    reverse = -back - LANE
    return forward, reverse


def bias_pieces(bias_table, tile_count):
    buckets, heads = bias_table.shape
    table = bias_table.astype(f32)
    forward, reverse = near_offsets()

    def spread(offset):
        hot = bucket_of(offset, buckets)[:, None] == jnp.arange(buckets, dtype=jnp.int32)
        picked = jnp.einsum("rb,bh->hr", hot.astype(f32), table, precision=lax.Precision.HIGHEST)
        return picked[:, None, :]

    near, near_t = pl.pallas_call(
        near_body,
        grid=(heads,),
        in_specs=[pl.BlockSpec((1, 1, 4 * LANE), lambda h: (h, 0, 0))] * 2,
        out_specs=[
            pl.BlockSpec((1, LANE, 3 * LANE), lambda h: (h, 0, 0)),
            pl.BlockSpec((1, 3 * LANE, LANE), lambda h: (h, 0, 0)),
        ],
        out_shape=[
            jax.ShapeDtypeStruct((heads, LANE, 3 * LANE), f32),
            jax.ShapeDtypeStruct((heads, 3 * LANE, LANE), f32),
        ],
        name="near_bias",
    )(spread(forward), spread(reverse))
    left = table[buckets // 2 - 1]
    right = table[buckets - 1]
    tile = jnp.arange(tile_count, dtype=jnp.int32)[None, :, None]
    lane = jnp.arange(LANE, dtype=jnp.int32)[None, None, :]
    far = jnp.where(lane == tile, left[:, None, None], 0.0)
    far = far + jnp.where(lane == tile + 8, right[:, None, None], 0.0)
    far = far + jnp.where(lane == 16, masked_score, 0.0)
    return near, near_t, far.astype(bf16)


def key_lanes(extent, length):
    key = lax.broadcasted_iota(jnp.int32, (extent, LANE), 0)
    lane = lax.broadcasted_iota(jnp.int32, (extent, LANE), 1)
    tile = key // LANE
    flag = (lane < 8) & (tile < lane - 1)
    flag = flag | ((lane >= 8) & (lane < 16) & (tile > lane - 8 + 1))
    flag = flag | ((lane == 16) & (key >= length))
    flag = flag | ((lane >= 17) & (lane < 20))
    return jnp.where(flag, 1.0, 0.0).astype(bf16)


def rms_of(values):
    scale = lax.rsqrt(jnp.mean(values * values, axis=-1, keepdims=True) + epsilon)
    return scale


def head_mask(rows, head):
    lane = lax.broadcasted_iota(jnp.int32, (rows, LANE), 1)
    return (lane // (LANE // 2)) == head


def split_three(value):
    first = value.astype(bf16)
    rest = value - first.astype(f32)
    second = rest.astype(bf16)
    return first, second, (rest - second.astype(f32)).astype(bf16)


def fwd_body(held, count, which, scal, xl, xr, gain, wq, wk, wv, near, far, *rest):
    q_out, k_out, v_out, mix_out, tail_out, normt_out, normed, lanes = rest[held:]
    extent = normed.shape[0]
    half = xl.shape[1]
    length = scal[1 + 2 * count + which]
    side = scal[0]
    steps = (length + STEP - 1) // STEP

    @pl.when(pl.program_id(0) == 0)
    def _():
        for ref, own in ((xl, True), (xr, False)):
            values = ref[0].astype(f32)
            out = values * rms_of(values) * gain[...].astype(f32)
            place = side * half if own else (1 - side) * half
            normed[pl.ds(pl.multiple_of(place, half), half), :] = out.astype(bf16)
        lanes[...] = key_lanes(extent, length)
        normt_out[0] = normed[...].T

    q_out[0, 0] = mm(normed[...], wq[...]).astype(bf16)
    for part in range(extent // STEP):
        rows = pl.ds(part * STEP, STEP)

        @pl.when(part < steps)
        def _():
            k_out[0, 0, rows, :] = mm(normed[rows, :], wk[...]).astype(bf16)
            v_out[0, 0, rows, :] = mm(normed[rows, :], wv[...]).astype(bf16)

        @pl.when(part >= steps)
        def _():
            k_out[0, 0, rows, :] = jnp.zeros((STEP, 2 * LANE), bf16)
            v_out[0, 0, rows, :] = jnp.zeros((STEP, 2 * LANE), bf16)

    def attend(width):
        def pair_step(pair, carry):
            cols = pl.ds(pl.multiple_of(pair * LANE, LANE), LANE)
            kext = jnp.concatenate([k_out[0, 0, :width, cols], lanes[:width, :]], axis=1)
            vext = jnp.concatenate(
                [v_out[0, 0, :width, cols], jnp.ones((width, LANE), bf16)], axis=1
            )
            lane = lax.broadcasted_iota(jnp.int32, (STEP, LANE), 1)
            subs = STEP // LANE

            def score(unit):
                block, head = unit
                qpair = q_out[0, 0, block * STEP : (block + 1) * STEP, cols]
                tiles = []
                for sub in range(subs):
                    line = far[2 * pair + head, pl.ds(block * subs + sub, 1), :]
                    tiles.append(jnp.broadcast_to(line, (LANE, LANE)))
                ext = jnp.concatenate(tiles, axis=0)
                qm = jnp.where(head_mask(STEP, head), qpair, jnp.zeros_like(qpair))
                return ext, mm(jnp.concatenate([qm, ext], axis=1), kext, NT)

            def weigh(unit, scores):
                block, head = unit
                probs = []
                tops = []
                for sub in range(subs):
                    tile = block * subs + sub
                    own = scores[sub * LANE : (sub + 1) * LANE]
                    base = (tile - 1) * LANE
                    low, high = max(0, base), min(width, base + 3 * LANE)
                    if low < high:
                        add = own[:, low:high] + near[2 * pair + head, :, low - base : high - base]
                        pieces = [own[:, :low]] if low > 0 else []
                        pieces.append(add)
                        if high < width:
                            pieces.append(own[:, high:])
                        own = jnp.concatenate(pieces, axis=1)
                    top = jnp.max(own, axis=1, keepdims=True)
                    probs.append(jnp.exp(own - top).astype(bf16))
                    tops.append(top)
                return jnp.concatenate(probs, axis=0), jnp.concatenate(tops, axis=0)

            def mix(unit, ext, prob, top):
                block, head = unit
                both = mm(prob, vext)
                total = both[:, LANE:]
                first, second, third = split_three(-(top + jnp.log(total)))
                line = jnp.where(lane == 17, first, ext)
                line = jnp.where(lane == 18, second, line)
                line = jnp.where(lane == 19, third, line)
                tail_out[0, 2 * pair + head, block * STEP : (block + 1) * STEP, :] = line
                return both[:, :LANE] / total

            units = [(block, head) for block in range(extent // STEP) for head in range(2)]
            ahead = score(units[0])
            before, outs = None, {}
            for n, unit in enumerate(units):
                ext, scores = ahead
                if n + 1 < len(units):
                    ahead = score(units[n + 1])
                now = (unit, ext, *weigh(unit, scores))
                if before is not None:
                    outs[before[0]] = mix(*before)
                before = now
            outs[before[0]] = mix(*before)
            for block in range(extent // STEP):
                picked = jnp.where(head_mask(STEP, 0), outs[block, 0], outs[block, 1])
                mix_out[0, 0, block * STEP : (block + 1) * STEP, cols] = picked.astype(bf16)
            return carry

        lax.fori_loop(0, 2, pair_step, 0)

    for blocks in range(1, extent // STEP + 1):

        @pl.when(steps == blocks)
        def _():
            attend(blocks * STEP)


def fwd_row(scal, inputs, remote, which, count, held, gain, wq, wk, wv, near, far, heads):
    rows, half, width = inputs.shape
    extent = 2 * half
    inner = wq.shape[1]
    quads = inner // STEP
    per = heads // quads
    weight = pl.BlockSpec((width, STEP), lambda i, s: (0, i))
    block = pl.BlockSpec((1, 1, extent, STEP), lambda i, s: (which, i, 0, 0))
    grid_spec = pltpu.PrefetchScalarGridSpec(
        num_scalar_prefetch=1,
        grid=(quads,),
        in_specs=[
            pl.BlockSpec((1, half, width), lambda i, s: (s[1 + which], 0, 0)),
            pl.BlockSpec((1, half, width), lambda i, s: (0, 0, 0)),
            pl.BlockSpec((1, width), lambda i, s: (0, 0)),
            weight,
            weight,
            weight,
            pl.BlockSpec((per, LANE, 3 * LANE), lambda i, s: (i, 0, 0)),
            pl.BlockSpec((per, 8, LANE), lambda i, s: (i, 0, 0)),
        ]
        + [pl.BlockSpec(memory_space=pl.ANY)] * len(held),
        out_specs=[block] * 4
        + [
            pl.BlockSpec((1, per, extent, LANE), lambda i, s: (which, i, 0, 0)),
            pl.BlockSpec((1, width, extent), lambda i, s: (which, 0, 0)),
        ],
        scratch_shapes=[pltpu.VMEM((extent, width), bf16), pltpu.VMEM((extent, LANE), bf16)],
    )
    stacked = jax.ShapeDtypeStruct((count, quads, extent, STEP), bf16)
    return pl.pallas_call(
        functools.partial(fwd_body, len(held), count, which),
        grid_spec=grid_spec,
        out_shape=[stacked] * 4
        + [
            jax.ShapeDtypeStruct((count, heads, extent, LANE), bf16),
            jax.ShapeDtypeStruct((count, width, extent), bf16),
        ],
        input_output_aliases={9 + n: n for n in range(len(held))},
        compiler_params=params(1, 56),
        cost_estimate=cost(27),
        name="attend_row",
    )(scal, inputs, remote, gain, wq, wk, wv, near, far, *held)


def bwd_body(
    count, scal, q, k, v, mix, dmix, tail, near_t, normt, *rest
):
    (dq_out, dk_out, dv_out, tacc_out, far_out, dw_out) = rest[-15:-9]
    (lanes, pl_s, ds_s, do_s, qa_s, dwq, dwk, dwv, _) = rest[-9:]
    extent = lanes.shape[0]
    row = pl.program_id(0)
    length = scal[1 + 2 * count + row]
    steps = (length + STEP - 1) // STEP
    lanes[...] = key_lanes(extent, length)

    @pl.when(row == 0)
    def _():
        for ref in (tacc_out, far_out, dwq, dwk, dwv):
            ref[...] = jnp.zeros(ref.shape, f32)

    dk_out[...] = jnp.zeros(dk_out.shape, bf16)
    dv_out[...] = jnp.zeros(dv_out.shape, bf16)

    def attend(width):
        def head_step(index, carry):
            pair = index // 2
            head = lax.rem(index, 2)
            cols = pl.ds(pl.multiple_of(pair * LANE, LANE), LANE)
            flags = lanes[:width, :]
            kpair = k[0, 0, :width, cols]
            kext = jnp.concatenate([kpair, flags], axis=1)
            vext = jnp.concatenate([v[0, 0, :width, cols], flags], axis=1)
            lane = lax.broadcasted_iota(jnp.int32, (STEP, LANE), 1)
            mask = head_mask(STEP, head)

            def products(block):
                rows = slice(block * STEP, (block + 1) * STEP)
                qpair = q[0, 0, rows, cols]
                dopair = dmix[0, 0, rows, cols]
                product = dopair.astype(f32) * mix[0, 0, rows, cols].astype(f32)
                qm = jnp.where(mask, qpair, jnp.zeros_like(qpair))
                dom = jnp.where(mask, dopair, jnp.zeros_like(dopair))
                neg = -jnp.sum(jnp.where(mask, product, 0.0), axis=1, keepdims=True)
                first, second, third = split_three(jnp.broadcast_to(neg, (STEP, LANE)))
                dtail = jnp.where(lane == 17, first, jnp.zeros((STEP, LANE), bf16))
                dtail = jnp.where(lane == 18, second, dtail)
                dtail = jnp.where(lane == 19, third, dtail)
                st = mm(kext, jnp.concatenate([qm, tail[0, index, rows, :]], axis=1), NT)
                dp = mm(vext, jnp.concatenate([dom, dtail], axis=1), NT)
                do_s[rows, :] = dom
                row_at = lax.broadcasted_iota(jnp.int32, (STEP, LANE), 0)
                spot = jnp.where(lane == block * (STEP // LANE) + row_at // LANE, 1.0, 0.0)
                qa_s[rows, :] = jnp.concatenate([qm, spot.astype(bf16)], axis=1)
                return st, dp

            ahead = products(0)
            for block in range(extent // STEP):
                st, dp = ahead
                if block + 1 < extent // STEP:
                    ahead = products(block + 1)
                for sub in range(STEP // LANE):
                    tile = block * (STEP // LANE) + sub
                    part = slice(sub * LANE, (sub + 1) * LANE)
                    own = st[:, part]
                    base = (tile - 1) * LANE
                    low, high = max(0, base), min(width, base + 3 * LANE)
                    if low < high:
                        add = own[low:high] + near_t[index, low - base : high - base, :]
                        pieces = [own[:low]] if low > 0 else []
                        pieces.append(add)
                        if high < width:
                            pieces.append(own[high:])
                        own = jnp.concatenate(pieces, axis=0)
                    prob = jnp.exp(own)
                    dst = (prob * dp[:, part]).astype(bf16)
                    place = slice(tile * LANE, (tile + 1) * LANE)
                    pl_s[:width, place] = prob.astype(bf16)
                    ds_s[:width, place] = dst
                    if low < high:
                        tacc_out[index, low - base : high - base, :] += dst[low:high].astype(f32)
            kmask = head_mask(width, head)
            dv = mm(pl_s[:width, :], do_s[...]).astype(bf16)
            dv_out[0, :width, cols] = jnp.where(kmask, dv, dv_out[0, :width, cols])
            dk = mm(ds_s[:width, :], qa_s[...])
            dk_out[0, :width, cols] = jnp.where(
                kmask, dk[:, :LANE].astype(bf16), dk_out[0, :width, cols]
            )
            tile = lax.broadcasted_iota(jnp.int32, (width, LANE), 0) // LANE
            spread = lax.broadcasted_iota(jnp.int32, (width, LANE), 1)
            left = jnp.where((tile < spread - 1) & (spread < 8), dk[:, LANE:], 0.0)
            right = jnp.where((tile > spread + 1) & (spread < 8), dk[:, LANE:], 0.0)
            far_out[pl.ds(index, 1), :] += jnp.sum(left, axis=0, keepdims=True)
            far_out[pl.ds(4 + index, 1), :] += jnp.sum(right, axis=0, keepdims=True)
            dq = mm(ds_s[:width, :], jnp.where(kmask, kpair, jnp.zeros_like(kpair)), TN)
            qmask = head_mask(extent, head)
            dq_out[0, :, cols] = jnp.where(qmask, dq.astype(bf16), dq_out[0, :, cols])
            return carry

        lax.fori_loop(0, 4, head_step, 0)
        dwk[...] += mm(normt[0, :, :width], dk_out[0, :width, :])
        dwv[...] += mm(normt[0, :, :width], dv_out[0, :width, :])

    for blocks in range(1, extent // STEP + 1):

        @pl.when(steps == blocks)
        def _():
            attend(blocks * STEP)

    dwq[...] += mm(normt[0], dq_out[0])

    @pl.when(row == count - 1)
    def _():
        for n, ref in enumerate((dwq, dwk, dwv)):
            dw_out[:, n * STEP : (n + 1) * STEP] = ref[...].astype(bf16)


def bwd_quad(places, quad, held, q, k, v, mix, dmix, tail, near_t, normt, deps=()):
    count, quads, extent, _ = q.shape
    heads = tail.shape[1]
    width = normt.shape[1]
    per = heads // quads
    block = pl.BlockSpec((1, 1, extent, STEP), lambda i, s: (i, quad, 0, 0))
    given = pl.BlockSpec((1, extent, STEP), lambda i, s: (i, 0, 0))
    grid_spec = pltpu.PrefetchScalarGridSpec(
        num_scalar_prefetch=1,
        grid=(count,),
        in_specs=[block] * 5
        + [
            pl.BlockSpec((1, per, extent, LANE), lambda i, s: (i, quad, 0, 0)),
            pl.BlockSpec((per, 3 * LANE, LANE), lambda i, s: (quad, 0, 0)),
            pl.BlockSpec((1, width, extent), lambda i, s: (i, 0, 0)),
        ]
        + [pl.BlockSpec(memory_space=pl.ANY)] * (len(held) + len(deps)),
        out_specs=[given] * 3
        + [
            pl.BlockSpec((per, 3 * LANE, LANE), lambda i, s: (0, 0, 0)),
            pl.BlockSpec((8, LANE), lambda i, s: (0, 0)),
            pl.BlockSpec((width, 3 * STEP), lambda i, s: (0, quad)),
        ],
        scratch_shapes=[
            pltpu.VMEM((extent, LANE), bf16),
            pltpu.VMEM((extent, extent), bf16),
            pltpu.VMEM((extent, extent), bf16),
            pltpu.VMEM((extent, LANE), bf16),
            pltpu.VMEM((extent, 2 * LANE), bf16),
        ]
        + [pltpu.VMEM((width, STEP), f32)] * 3
        + [pltpu.VMEM((8, LANE), f32)],
    )
    out = jax.ShapeDtypeStruct((count, extent, STEP), bf16)
    return pl.pallas_call(
        functools.partial(bwd_body, count),
        grid_spec=grid_spec,
        out_shape=[out] * 3
        + [
            jax.ShapeDtypeStruct((per, 3 * LANE, LANE), f32),
            jax.ShapeDtypeStruct((8, LANE), f32),
            jax.ShapeDtypeStruct((width, 3 * STEP * quads), bf16),
        ],
        input_output_aliases={9: 5} if held else {},
        compiler_params=params(1, 60),
        cost_estimate=cost(1),
        name="attend_back",
    )(places, q, k, v, mix, dmix, tail, near_t, normt, *held, *deps)


def table_body(tacc, *rest):
    out = rest[-1]
    total = jnp.zeros((8, 4 * LANE), f32)
    for group in range(3 * LANE // 8):
        part = tacc[0, group * 8 : (group + 1) * 8, :]
        wide = jnp.concatenate([part, jnp.zeros((8, 3 * LANE), f32)], axis=1)
        total = total + (pltpu.roll(wide, 4 * LANE - 8 * group, 1) if group else wide)
    line = total[0:1]
    for row in range(1, 8):
        line = line + pltpu.roll(total[row : row + 1], 4 * LANE - row, 1)
    out[0] = line


def table_sums(tacc, far_sum, buckets, deps=()):
    heads = tacc.shape[0]
    diagonals = pl.pallas_call(
        table_body,
        grid=(heads,),
        in_specs=[pl.BlockSpec((1, 3 * LANE, LANE), lambda h: (h, 0, 0))]
        + [pl.BlockSpec(memory_space=pl.ANY)] * len(deps),
        out_specs=pl.BlockSpec((1, 1, 4 * LANE), lambda h: (h, 0, 0)),
        out_shape=jax.ShapeDtypeStruct((heads, 1, 4 * LANE), f32),
        cost_estimate=cost(100),
        name="table_diagonals",
    )(tacc, *deps)
    place = jnp.arange(4 * LANE, dtype=jnp.int32)
    back = jnp.where(place < LANE, place, place - 4 * LANE)
    hot = bucket_of(-back - LANE, buckets)[:, None] == jnp.arange(buckets, dtype=jnp.int32)
    near = jnp.einsum(
        "rb,hr->bh", hot.astype(f32), diagonals[:, 0, :], precision=lax.Precision.HIGHEST
    )
    sides = jnp.sum(far_sum, axis=2).reshape(-1, 2, 4)
    sides = jnp.transpose(sides, (1, 0, 2)).reshape(2, heads)
    half = buckets // 2
    near = near.at[half - 1].add(sides[0])
    return near.at[buckets - 1].add(sides[1])


CHUNK = 512
GELU_K = math.sqrt(2.0 / math.pi)


def gated(normed, g, w_gate, w_up, w_down):
    gate = mm(normed, w_gate)
    up = mm(normed, w_up)
    d_act = mm(g, w_down, NT)
    square = gate * gate
    th = jnp.tanh(gate * (GELU_K + (GELU_K * 0.044715) * square))
    half = 0.5 + 0.5 * th
    gelu = gate * half
    slope = half + (0.5 * gate) * (1.0 - th * th) * (GELU_K + (3.0 * 0.044715 * GELU_K) * square)
    return (
        (gelu * up).astype(bf16),
        (d_act * up * slope).astype(bf16),
        (d_act * gelu).astype(bf16),
    )


def ff_body(
    scal, xl, xr, gl, gr, mix, w_out, gain, gate_any, up_any, down_any,
    lo_out, lo_send, dh_out, dmix_out, dw_out, dgain_out,
    dwo, dwg, dwu, dwd, w_gate, w_up, w_down, sems,
):
    step = pl.program_id(0)
    last = pl.num_programs(0) - 1
    own = lax.rem(step, 2) == 0
    units = w_gate.shape[1]
    loads = [
        pltpu.make_async_copy(source, target, sems.at[n])
        for n, (source, target) in enumerate(
            ((gate_any, w_gate), (up_any, w_up), (down_any, w_down))
        )
    ]

    @pl.when(step == 0)
    def _():
        for load in loads:
            load.start()
        for ref in (dwo, dwg, dwu, dwd, dgain_out):
            ref[...] = jnp.zeros(ref.shape, f32)

    g = jnp.where(own, gl[0], gr[0])
    x = jnp.where(own, xl[0], xr[0]).astype(f32)
    quads = mix.shape[1]
    mixed = jnp.concatenate([mix[0, i] for i in range(quads)], axis=1)
    hidden = x + mm(mixed, w_out[...])
    gain_f = gain[...].astype(f32)
    scale = rms_of(hidden)
    unit = hidden * scale
    normed = (unit * gain_f).astype(bf16)
    normed_t = normed.T
    g_t = g.T
    out = hidden
    dn = jnp.zeros_like(hidden)

    @pl.when(step == 0)
    def _():
        for load in loads:
            load.wait()

    for c in range(units // CHUNK):
        cols = slice(c * CHUNK, (c + 1) * CHUNK)
        act, d_gate, d_up = gated(normed, g, w_gate[:, cols], w_up[:, cols], w_down[cols, :])
        out = out + mm(act, w_down[cols, :])
        dn = dn + mm(d_gate, w_gate[:, cols], NT) + mm(d_up, w_up[:, cols], NT)
        dwd[:, cols] += mm(g_t, act)
        dwg[:, cols] += mm(normed_t, d_gate)
        dwu[:, cols] += mm(normed_t, d_up)

    @pl.when(own)
    def _():
        lo_out[0] = out

    @pl.when(jnp.logical_not(own))
    def _():
        lo_send[0] = out.astype(bf16)

    dgain_out[...] += jnp.sum(dn * unit, axis=0, keepdims=True)
    e = dn * gain_f
    d_hidden = (
        g.astype(f32) + scale * e - unit * (scale * jnp.mean(unit * e, axis=-1, keepdims=True))
    )
    dh_out[0] = d_hidden
    low = d_hidden.astype(bf16)
    dwo[...] += mm(mixed.T, low)
    d_mixed = mm(low, w_out[...], NT).astype(bf16)
    for i in range(quads):
        dmix_out[0, i] = d_mixed[:, i * STEP : (i + 1) * STEP]

    @pl.when(step == last)
    def _():
        pending = [None, None]
        place = 0
        for n, acc in enumerate((dwg, dwu, dwd, dwo)):
            slot = n % 2
            stage = (w_gate, w_up)[slot]
            if pending[slot] is not None:
                pending[slot].wait()
            cols = acc.shape[1]
            stage[:, :cols] = acc[...].astype(bf16)
            copy = pltpu.make_async_copy(
                stage.at[:, pl.ds(0, cols)], dw_out.at[:, pl.ds(place, cols)], sems.at[slot]
            )
            copy.start()
            pending[slot] = copy
            place += cols
        for copy in pending:
            copy.wait()


def feed_forward(places, inputs, x_remote, cot, cot_remote, mix, w_out, gain, w_gate, w_up, w_down):
    rows, half, width = inputs.shape
    mine = x_remote.shape[0]
    _, quads, extent, _ = mix.shape
    units = w_gate.shape[1]
    inner = w_out.shape[0]

    def keep(shape):
        return pl.BlockSpec(shape, lambda i, s: (0,) * len(shape), pipeline_mode=pl.Buffered(1))

    local = pl.BlockSpec((1, half, width), lambda i, s: (s[1 + i // 2], 0, 0))
    far = pl.BlockSpec((1, half, width), lambda i, s: (i // 2, 0, 0))
    far_one = pl.BlockSpec(
        (1, half, width), lambda i, s: (i // 2, 0, 0), pipeline_mode=pl.Buffered(1)
    )
    spot = pl.BlockSpec(
        (1, quads, half, STEP),
        lambda i, s: (i // 2, 0, jnp.where(i % 2 == 0, s[0], 1 - s[0]), 0),
    )
    tile = pl.BlockSpec((1, half, width), lambda i, s: (i, 0, 0))
    anywhere = pl.BlockSpec(memory_space=pl.ANY)
    grid_spec = pltpu.PrefetchScalarGridSpec(
        num_scalar_prefetch=1,
        grid=(2 * mine,),
        in_specs=[local, far_one, local, far_one, spot, keep((inner, width)), keep((1, width)),
                  anywhere, anywhere, anywhere],
        out_specs=[local, far, tile, spot, anywhere,
                   pl.BlockSpec((1, width), lambda i, s: (0, 0))],
        scratch_shapes=[pltpu.VMEM((inner, width), f32)]
        + [pltpu.VMEM((width, units), f32)] * 3
        + [
            pltpu.VMEM((width, units), bf16),
            pltpu.VMEM((width, units), bf16),
            pltpu.VMEM((units, width), bf16),
            pltpu.SemaphoreType.DMA((3,)),
        ],
    )
    return pl.pallas_call(
        ff_body,
        grid_spec=grid_spec,
        out_shape=[
            jax.ShapeDtypeStruct((rows, half, width), f32),
            jax.ShapeDtypeStruct((mine, half, width), bf16),
            jax.ShapeDtypeStruct((2 * mine, half, width), f32),
            jax.ShapeDtypeStruct((mine, quads, extent, STEP), bf16),
            jax.ShapeDtypeStruct((width, 3 * units + width), bf16),
            jax.ShapeDtypeStruct((1, width), f32),
        ],
        compiler_params=params(1, 63),
        cost_estimate=cost(150),
        name="feed_forward",
    )(places, inputs, x_remote, cot, cot_remote, mix, w_out, gain, w_gate, w_up, w_down)


def spread_body(sums, *rest):
    gate_out, up_out, down_out, out_out = rest[-4:]
    units = gate_out.shape[1]
    gate_out[...] = sums[:, :units].astype(f32)
    up_out[...] = sums[:, units : 2 * units].astype(f32)
    down_out[...] = sums[:, 2 * units : 3 * units].astype(f32).T
    out_out[...] = sums[:, 3 * units :].astype(f32)


def spread(sums, deps=()):
    width, columns = sums.shape
    units = (columns - width) // 3
    wide = pl.BlockSpec((LANE, units), lambda i: (i, 0))
    return pl.pallas_call(
        spread_body,
        grid=(width // LANE,),
        in_specs=[pl.BlockSpec((LANE, columns), lambda i: (i, 0))]
        + [pl.BlockSpec(memory_space=pl.ANY)] * len(deps),
        out_specs=[
            wide,
            wide,
            pl.BlockSpec((units, LANE), lambda i: (0, i)),
            pl.BlockSpec((LANE, width), lambda i: (i, 0)),
        ],
        out_shape=[
            jax.ShapeDtypeStruct((width, units), f32),
            jax.ShapeDtypeStruct((width, units), f32),
            jax.ShapeDtypeStruct((units, width), f32),
            jax.ShapeDtypeStruct((width, width), f32),
        ],
        compiler_params=params(1, 56),
        cost_estimate=cost(100),
        name="spread",
    )(sums, *deps)


def back_body(quads, held, scal, xl, xr, dh, *rest):
    grads = rest[: 3 * quads]
    gain, wq, wk, wv = rest[3 * quads : 3 * quads + 4]
    ig_out, ig_send, dgain_out = rest[-3:]
    step = pl.program_id(0)
    far = step == 0

    @pl.when(far)
    def _():
        dgain_out[...] = jnp.zeros(dgain_out.shape, f32)

    x = jnp.where(far, xr[0], xl[0]).astype(f32)
    dn = jnp.zeros_like(x)
    for n, weight in enumerate((wq, wk, wv)):
        part = jnp.concatenate([ref[0] for ref in grads[n * quads : (n + 1) * quads]], axis=1)
        dn = dn + mm(part, weight[...], NT)
    scale = rms_of(x)
    unit = x * scale
    dgain_out[...] += jnp.sum(dn * unit, axis=0, keepdims=True)
    e = dn * gain[...].astype(f32)
    out = dh[0] + scale * e - unit * (scale * jnp.mean(unit * e, axis=-1, keepdims=True))

    @pl.when(far)
    def _():
        ig_send[0] = out.astype(bf16)

    @pl.when(jnp.logical_not(far))
    def _():
        ig_out[0] = out


def input_back(places, row, held, inputs, remote, dh, dq, dk, dv, gain, wq, wk, wv, deps=()):
    rows, half, width = inputs.shape
    local = pl.BlockSpec((1, half, width), lambda i, s: (s[1 + row], 0, 0))
    one = pl.BlockSpec((1, half, width), lambda i, s: (0, 0, 0))
    tile = pl.BlockSpec((1, half, width), lambda i, s: (2 * row + 1 - i, 0, 0))
    spot = pl.BlockSpec((1, half, STEP), lambda i, s: (row, jnp.where(i == 1, s[0], 1 - s[0]), 0))
    weight = pl.BlockSpec(wq.shape, lambda i, s: (0, 0), pipeline_mode=pl.Buffered(1))
    line = pl.BlockSpec((1, width), lambda i, s: (0, 0))
    anywhere = pl.BlockSpec(memory_space=pl.ANY)
    grads = [*dq, *dk, *dv]
    grid_spec = pltpu.PrefetchScalarGridSpec(
        num_scalar_prefetch=1,
        grid=(2,),
        in_specs=[local, one, tile]
        + [spot] * len(grads)
        + [line, weight, weight, weight]
        + [anywhere] * (len(held) + len(deps)),
        out_specs=[local, one, line],
    )
    return pl.pallas_call(
        functools.partial(back_body, len(dq), len(held)),
        grid_spec=grid_spec,
        out_shape=[
            jax.ShapeDtypeStruct((rows, half, width), f32),
            jax.ShapeDtypeStruct((1, half, width), bf16),
            jax.ShapeDtypeStruct((1, width), f32),
        ],
        input_output_aliases={8 + len(grads): 0} if held else {},
        compiler_params=params(1, 56),
        cost_estimate=cost(100),
        name="input_back",
    )(places, inputs, remote, dh, *grads, gain, wq, wk, wv, *held, *deps)


def hold_body(value, *rest):
    rest[-1][...] = value[...]


def hold(value, deps):
    return pl.pallas_call(
        hold_body,
        in_specs=[pl.BlockSpec(memory_space=pltpu.VMEM)]
        + [pl.BlockSpec(memory_space=pl.ANY)] * len(deps),
        out_specs=pl.BlockSpec(memory_space=pltpu.VMEM),
        out_shape=jax.ShapeDtypeStruct(value.shape, value.dtype),
        compiler_params=pltpu.CompilerParams(vmem_limit_bytes=16 << 20),
        name="hold",
    )(value, *deps)


def pick_half(grads, at, deps):
    rows, columns = grads.shape
    grid_spec = pltpu.PrefetchScalarGridSpec(
        num_scalar_prefetch=1,
        grid=(1,),
        in_specs=[pl.BlockSpec((rows // 2, columns), lambda i, s: (s[0], 0))]
        + [pl.BlockSpec(memory_space=pl.ANY)] * len(deps),
        out_specs=pl.BlockSpec((rows // 2, columns), lambda i, s: (0, 0)),
    )
    return pl.pallas_call(
        pick_body,
        grid_spec=grid_spec,
        out_shape=jax.ShapeDtypeStruct((rows // 2, columns), grads.dtype),
        compiler_params=params(1, 24),
        name="pick_half",
    )(at.reshape(1), grads, *deps)


def pick_body(scal, array, *rest):
    rest[-1][...] = array[...]


def pick_rows(places, first, count, array, deps=()):
    rows, half, width = array.shape
    grid_spec = pltpu.PrefetchScalarGridSpec(
        num_scalar_prefetch=1,
        grid=(count,),
        in_specs=[pl.BlockSpec((1, half, width), lambda i, s: (s[1 + rows // 2 + first + i], 0, 0))]
        + [pl.BlockSpec(memory_space=pl.ANY)] * len(deps),
        out_specs=pl.BlockSpec((1, half, width), lambda i, s: (i, 0, 0)),
    )
    return pl.pallas_call(
        pick_body,
        grid_spec=grid_spec,
        out_shape=jax.ShapeDtypeStruct((count, half, width), array.dtype),
        compiler_params=params(1, 16),
        name="pick_rows",
    )(places, array, *deps)


def place_body(scal, arrived, *rest):
    out, token = rest[-2:]
    out[0] = arrived[0].astype(f32)
    token[...] = jnp.zeros(token.shape, f32)


def place_rows(places, first, arrived, held, deps=()):
    count, half, width = arrived.shape
    at = 1 + held.shape[0] // 2 + first
    anywhere = pl.BlockSpec(memory_space=pl.ANY)
    grid_spec = pltpu.PrefetchScalarGridSpec(
        num_scalar_prefetch=1,
        grid=(count,),
        in_specs=[pl.BlockSpec((1, half, width), lambda i, s: (i, 0, 0)), anywhere]
        + [anywhere] * len(deps),
        out_specs=[
            pl.BlockSpec((1, half, width), lambda i, s: (s[at + i], 0, 0)),
            pl.BlockSpec((8, LANE), lambda i, s: (0, 0)),
        ],
    )
    return pl.pallas_call(
        place_body,
        grid_spec=grid_spec,
        out_shape=[
            jax.ShapeDtypeStruct(held.shape, f32),
            jax.ShapeDtypeStruct((8, LANE), f32),
        ],
        input_output_aliases={2: 0},
        compiler_params=params(1, 32),
        cost_estimate=cost(100),
        name="place_rows",
    )(places, arrived, held, *deps)


highest = lax.Precision.HIGHEST


def rms_scaled(values, gain):
    mean_square = jnp.mean(values * values, axis=-1, keepdims=True)
    return values * lax.rsqrt(mean_square + epsilon) * gain


def gated_unit(gate, up_proj):
    return jax.nn.gelu(gate, approximate=True) * up_proj


def relative_one_hot(query_anchor, query_extent, key_extent, bucket_count):
    query_place = query_anchor + jnp.arange(query_extent, dtype=jnp.int32)
    key_place = jnp.arange(key_extent, dtype=jnp.int32)
    offset = key_place[None, :] - query_place[:, None]
    distance = jnp.abs(offset)
    far_bucket = jnp.full_like(distance, 8)
    for threshold in bucket_bounds:
        far_bucket = far_bucket + (distance >= threshold).astype(jnp.int32)
    bucket = jnp.where(offset > 0, bucket_count // 2, 0) + jnp.where(
        distance < 8, distance, far_bucket
    )
    return (bucket[:, :, None] == jnp.arange(bucket_count, dtype=jnp.int32)).astype(jnp.float32)


def block_scores(query_heads, key_heads, query_anchor, lengths, bias_f):
    key_extent = key_heads.shape[1]
    one_hot = relative_one_hot(query_anchor, query_heads.shape[1], key_extent, bias_f.shape[0])
    bias_block = jnp.einsum("qkb,bh->hqk", one_hot, bias_f, precision=highest)
    raw_scores = jnp.einsum(
        "rqhd,rkhd->rhqk", query_heads, key_heads, preferred_element_type=jnp.float32
    )
    usable = jnp.arange(key_extent, dtype=jnp.int32)[None, :] < lengths[:, None]
    return (
        jnp.where(usable[:, None, None, :], raw_scores + bias_block[None], masked_score),
        one_hot,
    )


def score_grads(scores, log_total, row_dot, grad_heads, value_heads):
    weights_hp = jnp.exp(scores - log_total[..., None])
    d_weights = jnp.einsum(
        "rqhd,rkhd->rhqk", grad_heads, value_heads, preferred_element_type=jnp.float32
    )
    d_scores = (weights_hp * (d_weights - row_dot[..., None])).astype(jnp.bfloat16)
    return (weights_hp.astype(jnp.bfloat16), d_scores)


def table_term(one_hot, d_scores):
    summed = jnp.sum(d_scores, axis=0, dtype=jnp.float32)
    return jnp.einsum("qkb,hqk->bh", one_hot, summed, precision=highest)


def gathered_device(
    inputs,
    lengths,
    cotangent,
    norm_gain,
    w_query,
    w_key,
    w_value,
    w_out,
    ff_gain,
    w_gate,
    w_up,
    w_down,
    bias_table,
):
    row_count, block_len, model_width = inputs.shape
    head_count = bias_table.shape[1]
    inner_width = w_query.shape[1]
    head_width = inner_width // head_count
    tokens_here = row_count * block_len
    lengths = lengths.reshape(-1)
    bias_f = bias_table.astype(jnp.float32)
    own_anchor = lax.axis_index("seq") * block_len

    def split_heads(block_array):
        return block_array.reshape(row_count, block_array.shape[1], head_count, head_width)

    tokens_f = inputs.astype(jnp.float32).reshape(tokens_here, model_width)
    normed_f, norm_pull = jax.vjp(rms_scaled, tokens_f, norm_gain.astype(jnp.float32))
    normed = normed_f.astype(jnp.bfloat16)
    queries = (
        jnp.dot(normed, w_query, preferred_element_type=jnp.float32)
        .astype(jnp.bfloat16)
        .reshape(row_count, block_len, inner_width)
    )
    keys = (
        jnp.dot(normed, w_key, preferred_element_type=jnp.float32)
        .astype(jnp.bfloat16)
        .reshape(row_count, block_len, inner_width)
    )
    values = (
        jnp.dot(normed, w_value, preferred_element_type=jnp.float32)
        .astype(jnp.bfloat16)
        .reshape(row_count, block_len, inner_width)
    )
    query_heads = split_heads(queries)
    stat_shape = (row_count, head_count, block_len)
    pieces = (
        lax.all_gather(keys, "seq", axis=1, tiled=True),
        lax.all_gather(values, "seq", axis=1, tiled=True),
    )
    row_max = jnp.full(stat_shape, start_max, jnp.float32)
    key_heads = split_heads(pieces[0])
    value_heads = split_heads(pieces[1])
    scores, one_hot = block_scores(query_heads, key_heads, own_anchor, lengths, bias_f)
    new_max = jnp.maximum(row_max, jnp.max(scores, axis=-1))
    weights_hp = jnp.exp(scores - new_max[..., None])
    row_sum = jnp.sum(weights_hp, axis=-1)
    weighted = jnp.einsum(
        "rhqk,rkhd->rhqd",
        weights_hp.astype(jnp.bfloat16),
        value_heads,
        preferred_element_type=jnp.float32,
    )
    row_max, row_sum, weighted = (new_max, row_sum, weighted)
    log_total = row_max + jnp.log(row_sum)
    mixed_heads = jnp.transpose(weighted / row_sum[..., None], (0, 2, 1, 3))
    mixed_low = mixed_heads.reshape(tokens_here, inner_width).astype(jnp.bfloat16)
    hidden = tokens_f + jnp.dot(mixed_low, w_out, preferred_element_type=jnp.float32)
    normed2_f, ff_pull = jax.vjp(rms_scaled, hidden, ff_gain.astype(jnp.float32))
    normed2 = normed2_f.astype(jnp.bfloat16)
    gate = jnp.dot(normed2, w_gate, preferred_element_type=jnp.float32)
    up_proj = jnp.dot(normed2, w_up, preferred_element_type=jnp.float32)
    activated, gated_pull = jax.vjp(gated_unit, gate, up_proj)
    act_low = activated.astype(jnp.bfloat16)
    layer_output = (hidden + jnp.dot(act_low, w_down, preferred_element_type=jnp.float32)).reshape(
        row_count, block_len, model_width
    )
    grad_out = cotangent.reshape(tokens_here, model_width)
    dw_down = jnp.einsum("tf,td->fd", act_low, grad_out, preferred_element_type=jnp.float32)
    d_act = jnp.einsum("td,fd->tf", grad_out, w_down, preferred_element_type=jnp.float32)
    d_gate, d_up = gated_pull(d_act)
    d_gate = d_gate.astype(jnp.bfloat16)
    d_up = d_up.astype(jnp.bfloat16)
    dw_gate = jnp.einsum("td,tf->df", normed2, d_gate, preferred_element_type=jnp.float32)
    dw_up = jnp.einsum("td,tf->df", normed2, d_up, preferred_element_type=jnp.float32)
    d_normed2 = jnp.einsum(
        "tf,df->td", d_gate, w_gate, preferred_element_type=jnp.float32
    ) + jnp.einsum("tf,df->td", d_up, w_up, preferred_element_type=jnp.float32)
    d_hidden_part, d_ff_gain = ff_pull(d_normed2)
    d_hidden = grad_out.astype(jnp.float32) + d_hidden_part
    d_hidden_low = d_hidden.astype(jnp.bfloat16)
    dw_out = jnp.einsum("ti,td->id", mixed_low, d_hidden_low, preferred_element_type=jnp.float32)
    d_mixed = (
        jnp.einsum("td,id->ti", d_hidden_low, w_out, preferred_element_type=jnp.float32)
        .astype(jnp.bfloat16)
        .reshape(row_count, block_len, inner_width)
    )
    grad_heads = split_heads(d_mixed)
    row_dot_rows = jnp.sum(grad_heads.astype(jnp.float32) * mixed_heads, axis=-1)
    row_dot = jnp.transpose(row_dot_rows, (0, 2, 1))
    pieces = (
        lax.all_gather(keys, "seq", axis=1, tiled=True),
        lax.all_gather(values, "seq", axis=1, tiled=True),
    )
    key_heads = split_heads(pieces[0])
    value_heads = split_heads(pieces[1])
    scores, one_hot = block_scores(query_heads, key_heads, own_anchor, lengths, bias_f)
    weights_low, d_scores = score_grads(scores, log_total, row_dot, grad_heads, value_heads)
    d_query_part = jnp.einsum(
        "rhqk,rkhd->rqhd", d_scores, key_heads, preferred_element_type=jnp.float32
    )
    key_heads, weights_low, d_scores, d_query_part, table_part = (
        key_heads,
        weights_low,
        d_scores,
        d_query_part,
        table_term(one_hot, d_scores),
    )
    extent = key_heads.shape[1]
    d_key_part = jnp.einsum(
        "rhqk,rqhd->rkhd", d_scores, query_heads, preferred_element_type=jnp.float32
    ).reshape(row_count, extent, inner_width)
    d_value_part = jnp.einsum(
        "rhqk,rqhd->rkhd", weights_low, grad_heads, preferred_element_type=jnp.float32
    ).reshape(row_count, extent, inner_width)
    d_key, d_value = (
        lax.psum_scatter(d_key_part, "seq", scatter_dimension=1, tiled=True),
        lax.psum_scatter(d_value_part, "seq", scatter_dimension=1, tiled=True),
    )
    d_query_low = d_query_part.reshape(tokens_here, inner_width).astype(jnp.bfloat16)
    d_key_low = d_key.reshape(tokens_here, inner_width).astype(jnp.bfloat16)
    d_value_low = d_value.reshape(tokens_here, inner_width).astype(jnp.bfloat16)
    dw_query = jnp.einsum("td,ti->di", normed, d_query_low, preferred_element_type=jnp.float32)
    dw_key = jnp.einsum("td,ti->di", normed, d_key_low, preferred_element_type=jnp.float32)
    dw_value = jnp.einsum("td,ti->di", normed, d_value_low, preferred_element_type=jnp.float32)
    d_normed = jnp.einsum("ti,di->td", d_query_low, w_query, preferred_element_type=jnp.float32)
    d_normed = d_normed + jnp.einsum(
        "ti,di->td", d_key_low, w_key, preferred_element_type=jnp.float32
    )
    d_normed = d_normed + jnp.einsum(
        "ti,di->td", d_value_low, w_value, preferred_element_type=jnp.float32
    )
    d_tokens_part, d_norm_gain = norm_pull(d_normed)
    input_grad = (d_hidden + d_tokens_part).reshape(row_count, block_len, model_width)
    flat_query = dw_query.reshape(-1)
    flat_key = dw_key.reshape(-1)
    flat_value = dw_value.reshape(-1)
    flat_out = dw_out.reshape(-1)
    flat_gate = dw_gate.reshape(-1)
    flat_up = dw_up.reshape(-1)
    flat_down = dw_down.reshape(-1)
    shares = (
        lax.psum_scatter(flat_query, ("batch", "seq"), scatter_dimension=0, tiled=True),
        lax.psum_scatter(flat_key, ("batch", "seq"), scatter_dimension=0, tiled=True),
        lax.psum_scatter(flat_value, ("batch", "seq"), scatter_dimension=0, tiled=True),
        lax.psum_scatter(flat_out, ("batch", "seq"), scatter_dimension=0, tiled=True),
        lax.psum_scatter(flat_gate, ("batch", "seq"), scatter_dimension=0, tiled=True),
        lax.psum_scatter(flat_up, ("batch", "seq"), scatter_dimension=0, tiled=True),
        lax.psum_scatter(flat_down, ("batch", "seq"), scatter_dimension=0, tiled=True),
    )
    summed = (
        lax.all_gather(shares[0], ("batch", "seq"), axis=0, tiled=True),
        lax.all_gather(shares[1], ("batch", "seq"), axis=0, tiled=True),
        lax.all_gather(shares[2], ("batch", "seq"), axis=0, tiled=True),
        lax.all_gather(shares[3], ("batch", "seq"), axis=0, tiled=True),
        lax.all_gather(shares[4], ("batch", "seq"), axis=0, tiled=True),
        lax.all_gather(shares[5], ("batch", "seq"), axis=0, tiled=True),
        lax.all_gather(shares[6], ("batch", "seq"), axis=0, tiled=True),
    )
    sum_norm, sum_ff, sum_table = lax.psum((d_norm_gain, d_ff_gain, table_part), ("batch", "seq"))
    return (
        layer_output,
        input_grad,
        sum_norm,
        summed[0].reshape(w_query.shape),
        summed[1].reshape(w_key.shape),
        summed[2].reshape(w_value.shape),
        summed[3].reshape(w_out.shape),
        sum_ff,
        summed[4].reshape(w_gate.shape),
        summed[5].reshape(w_up.shape),
        summed[6].reshape(w_down.shape),
        sum_table,
    )


def all_pairs(mesh_batch, mesh_seq, move):
    pairs = []
    for batch in range(mesh_batch):
        for seq in range(mesh_seq):
            z, y, core, x = move(batch // 4, batch // 2 % 2, batch % 2, seq)
            pairs.append((batch * mesh_seq + seq, (z * 4 + y * 2 + core) * mesh_seq + x))
    return pairs


def add_up(parts):
    total = parts[0].astype(f32)
    for part in parts[1:]:
        total = total + part.astype(f32)
    return total


class Links:
    def __init__(self, batch, seq):
        self.axes = ("batch", "seq")
        self.deep = batch // 4
        me = lax.axis_index("batch")
        self.z, self.y, self.core = me // 4, me // 2 % 2, me % 2
        self.x = lax.axis_index("seq")
        self.plane = self.y * 2 + self.x
        pairs = functools.partial(all_pairs, batch, seq)
        self.to_core = pairs(lambda z, y, c, x: (z, y, 1 - c, x))
        self.to_plane = {
            k: pairs(lambda z, y, c, x, k=k: (z, y ^ (k >> 1), c, x ^ (k & 1))) for k in (1, 2, 3)
        }
        self.to_deep = {
            k: pairs(lambda z, y, c, x, k=k: ((z + k) % self.deep, y, c, x))
            for k in range(1, self.deep)
        }

    def send(self, value, pairs):
        return lax.ppermute(value, self.axes, pairs)

    def pick(self, value, at):
        return lax.dynamic_index_in_dim(value, at, 0, keepdims=False)

    def scatter_core(self, grads, deps=()):
        rows, columns = grads.shape
        shape = (4, self.deep, rows // (8 * self.deep), columns)
        got = self.send(pick_half(grads, 1 - self.core, deps), self.to_core)
        own = self.pick(grads.reshape(2, *shape), self.core)
        return add_up([own, got.reshape(shape)]).astype(bf16)

    def scatter_plane(self, part):
        got = [self.send(self.pick(part, self.plane ^ k), self.to_plane[k]) for k in (1, 2, 3)]
        return add_up([self.pick(part, self.plane), *got]).astype(bf16)

    def scatter_pair(self, part, bit):
        at = self.y if bit else self.x
        got = self.send(self.pick(part, 1 - at), self.to_plane[1 + bit])
        return add_up([self.pick(part, at), got]).astype(bf16)

    def scatter_deep(self, part):
        got = [
            self.send(self.pick(part, (self.z + k) % self.deep), self.to_deep[k])
            for k in range(1, self.deep)
        ]
        return add_up([self.pick(part, self.z), *got]).astype(bf16)

    def lay(self, count, at, own, got):
        out = jnp.zeros((count,) + own.shape, own.dtype)
        out = lax.dynamic_update_index_in_dim(out, own, at, 0)
        for place, piece in got:
            out = lax.dynamic_update_index_in_dim(out, piece, place, 0)
        return out

    def gather_deep(self, part):
        got = [
            ((self.z - k) % self.deep, self.send(part, self.to_deep[k]))
            for k in range(1, self.deep)
        ]
        return self.lay(self.deep, self.z, part, got)

    def gather_plane(self, part):
        got = [(self.plane ^ k, self.send(part, self.to_plane[k])) for k in (1, 2, 3)]
        return self.lay(4, self.plane, part, got)

    def gather_core(self, part):
        out = self.lay(2, self.core, part, [(1 - self.core, self.send(part, self.to_core))])
        return out.reshape(-1, out.shape[-1])

    def total(self, grads):
        part = self.scatter_deep(self.scatter_plane(self.scatter_core(grads)))
        return self.gather_core(self.gather_plane(self.gather_deep(part)))


def rows_device(
    batch,
    seq,
    inputs,
    lengths,
    cotangent,
    norm_gain,
    w_query,
    w_key,
    w_value,
    w_out,
    ff_gain,
    w_gate,
    w_up,
    w_down,
    bias_table,
):
    rows, half, width = inputs.shape
    buckets, heads = bias_table.shape
    mine_count = rows // 2
    links = Links(batch, seq)
    places = split_rows(lengths, links.x)
    swap = [(0, 1), (1, 0)]

    x_parts, tick = [], ()
    for row in range(mine_count):
        x_parts.append(lax.ppermute(pick_rows(places, row, 1, inputs, tick), "seq", swap))
        tick = (links.send(tick[0] if tick else places.astype(f32), links.to_core),)
    g_remote = lax.ppermute(pick_rows(places, 0, mine_count, cotangent, tick), "seq", swap)
    near, near_t, far = bias_pieces(bias_table, 2 * half // LANE)
    gain = norm_gain.reshape(1, width)
    gain2 = ff_gain.reshape(1, width)
    held = []
    for row in range(mine_count):
        held = fwd_row(
            places, inputs, x_parts[row], row, mine_count, held,
            gain, w_query, w_key, w_value, near, far, heads,
        )
    q, k, v, mix, tail, normt = held
    x_remote = jnp.concatenate(x_parts, axis=0)
    ff_args = (
        places, inputs, x_remote, cotangent, g_remote, mix,
        w_out, gain2, w_gate, w_up, w_down,
    )
    lo, lo_send, dh, dmix, ff_grads, ff_gain_part = feed_forward(*ff_args)
    ff_total = lax.psum(ff_grads, ("batch", "seq"))
    lo_got = lax.ppermute(lo_send, "seq", swap)
    quads = q.shape[1]
    dw, backs, token = [], [], ()
    for quad in range(quads):
        if quad == quads - 1:
            layer_output, placed = place_rows(places, 0, lo_got, lo)
            token = (placed,)
        *back, dw_quad = bwd_quad(
            places, quad, dw, q, k, v, mix, dmix, tail, near_t, normt, token
        )
        backs.append(back)
        dw = [dw_quad]
    dq, dk, dv, tacc, far_sum = zip(*backs)
    qkv = links.scatter_core(dw[0])
    ig, ig_got, gain_parts, token = [], [], [], ()
    for row in range(mine_count):
        *ig, sent, gain_part = input_back(
            places, row, ig, inputs, x_parts[row], dh, dq, dk, dv,
            gain, w_query, w_key, w_value, token,
        )
        ig_got.append(lax.ppermute(sent, "seq", swap))
        gain_parts.append(gain_part)
        if row == 0:
            token = (qkv,)
            qkv = links.scatter_plane(qkv)
    qkv = hold(qkv, (gain_parts[-1],))
    table_part = table_sums(
        jnp.concatenate(tacc, axis=0), jnp.stack(far_sum), buckets, (qkv,)
    )
    small = jnp.concatenate(
        [sum(gain_parts)[0], ff_gain_part[0], table_part.reshape(-1)]
    )
    qkv = hold(links.scatter_deep(qkv), (table_part,))
    input_grad, placed = place_rows(places, 0, ig_got[0], ig[0], (qkv,))
    held_qkv = qkv
    qkv = links.gather_deep(qkv)
    small = add_up([small, links.send(hold(small, (held_qkv,)), links.to_core)])
    qkv = hold(qkv, (placed, small))
    gate_grad, up_grad, down_grad, out_grad = spread(ff_total, (qkv,))
    qkv_ready = qkv
    qkv = links.gather_plane(qkv)
    small = hold(small, (qkv_ready,))
    small = add_up([small, *[links.send(small, p) for p in links.to_plane.values()]])
    for row in range(1, mine_count - 1):
        input_grad, placed = place_rows(places, row, ig_got[row], input_grad)
    qkv = hold(qkv, (out_grad, placed, small))
    input_grad, _ = place_rows(places, mine_count - 1, ig_got[-1], input_grad, (qkv,))
    small = hold(small, (qkv,))
    qkv = links.gather_core(qkv)
    small = add_up([small, *[links.send(small, p) for p in links.to_deep.values()]])

    def whole(n):
        return jnp.concatenate(
            [qkv[:, (3 * i + n) * STEP : (3 * i + n + 1) * STEP] for i in range(quads)], axis=1
        ).astype(f32)

    return (
        layer_output,
        input_grad,
        small[:width],
        whole(0),
        whole(1),
        whole(2),
        out_grad,
        small[width : 2 * width],
        gate_grad,
        up_grad,
        down_grad,
        small[2 * width :].reshape(buckets, heads),
    )


def solution(mesh):
    split = P("batch", "seq", None)
    in_specs = (split, P("batch", None), split) + (P(),) * 10
    out_specs = (split, split) + (P(),) * 10
    batch, seq = mesh.shape["batch"], mesh.shape["seq"]

    def per_device(inputs, *rest):
        rows, half, width = inputs.shape
        buckets, heads = rest[-1].shape
        inner = rest[3].shape[1]
        fits = seq == 2 and batch % 4 == 0 and rows % 2 == 0 and rows >= 4 and buckets == 32
        fits = fits and half % STEP == 0 and 2 * half // LANE <= 8
        fits = fits and inner == width and width % (16 * batch) == 0 and inner // heads == LANE // 2
        if fits:
            return rows_device(batch, seq, inputs, *rest)
        return gathered_device(inputs, *rest)

    return jax.shard_map(
        per_device, mesh=mesh, in_specs=in_specs, out_specs=out_specs, check_vma=False
    )
```

```python
import functools
import itertools
import math

import jax
import jax.numpy as jnp
from jax import lax
from jax.experimental import pallas as pl
from jax.experimental.pallas import tpu as pltpu
from jax.sharding import PartitionSpec as P

f32 = jnp.float32
bf16 = jnp.bfloat16
epsilon = 1e-06
masked_score = -2e30
start_max = -1e30
bucket_bounds = (12, 16, 23, 32, 46, 64, 91)
LANE = 128
STEP = 256
NT = (((1,), (1,)), ((), ()))
NN = (((1,), (0,)), ((), ()))
TN = (((0,), (0,)), ((), ()))


def mm(a, b, dims=NN):
    return lax.dot_general(a, b, dims, preferred_element_type=f32)


def cost(micros):
    return pl.CostEstimate(flops=int(micros * 0.3e9), bytes_accessed=0, transcendentals=0)


def params(grid_dims, mib):
    return pltpu.CompilerParams(
        dimension_semantics=("arbitrary",) * grid_dims, vmem_limit_bytes=mib << 20
    )


def bucket_of(offset, bucket_count):
    distance = jnp.abs(offset)
    far = jnp.full_like(distance, 8)
    for bound in bucket_bounds:
        far = far + (distance >= bound).astype(jnp.int32)
    half = bucket_count // 2
    return jnp.where(offset > 0, half, 0) + jnp.where(distance < 8, distance, far)


def split_body(choices, side, lengths, out):
    rows = lengths.shape[1]
    count = rows // 2
    load = [(lengths[0, r] + STEP - 1) // STEP for r in range(rows)]
    best = None
    for own in choices:
        other = [r for r in range(rows) if r not in own]
        uneven = jnp.abs(sum(load[r] for r in own) - sum(load[r] for r in other))
        new = [*own, *other]
        if best is None:
            best, picked = uneven, [jnp.int32(r) for r in new]
        else:
            better = uneven < best
            best = jnp.where(better, uneven, best)
            picked = [jnp.where(better, r, old) for r, old in zip(new, picked)]
    first = side[0] == 0
    out[0] = side[0]
    for n in range(count):
        mine = jnp.where(first, picked[n], picked[count + n])
        out[1 + n] = mine
        out[1 + count + n] = jnp.where(first, picked[count + n], picked[n])
        out[1 + 2 * count + n] = lengths[0, mine]


def split_rows(lengths, side):
    rows = lengths.shape[1]
    choices = [c for c in itertools.combinations(range(rows), rows // 2) if 0 in c]
    smem = pl.BlockSpec(memory_space=pltpu.SMEM)
    return pl.pallas_call(
        functools.partial(split_body, choices),
        in_specs=[smem, smem],
        out_specs=smem,
        out_shape=jax.ShapeDtypeStruct((1 + 3 * (rows // 2),), jnp.int32),
        name="split_rows",
    )(side.reshape(1), lengths)


def near_body(vec_ref, rev_ref, near_ref, near_t_ref):
    wide = jnp.broadcast_to(vec_ref[0], (LANE, 4 * LANE))
    near_ref[0] = pltpu.roll(wide, 0, 1, stride=1, stride_axis=0)[:, : 3 * LANE]
    tall = jnp.broadcast_to(rev_ref[0], (3 * LANE, 4 * LANE))
    near_t_ref[0] = pltpu.roll(tall, 0, 1, stride=1, stride_axis=0)[:, :LANE]


def near_offsets():
    place = jnp.arange(4 * LANE, dtype=jnp.int32)
    signed = jnp.where(place < 3 * LANE, place, place - 4 * LANE)
    forward = signed - LANE
    back = jnp.where(place < LANE, place, place - 4 * LANE)
    reverse = -back - LANE
    return forward, reverse


def bias_pieces(bias_table, tile_count):
    buckets, heads = bias_table.shape
    table = bias_table.astype(f32)
    forward, reverse = near_offsets()

    def spread(offset):
        hot = bucket_of(offset, buckets)[:, None] == jnp.arange(buckets, dtype=jnp.int32)
        picked = jnp.einsum("rb,bh->hr", hot.astype(f32), table, precision=lax.Precision.HIGHEST)
        return picked[:, None, :]

    near, near_t = pl.pallas_call(
        near_body,
        grid=(heads,),
        in_specs=[pl.BlockSpec((1, 1, 4 * LANE), lambda h: (h, 0, 0))] * 2,
        out_specs=[
            pl.BlockSpec((1, LANE, 3 * LANE), lambda h: (h, 0, 0)),
            pl.BlockSpec((1, 3 * LANE, LANE), lambda h: (h, 0, 0)),
        ],
        out_shape=[
            jax.ShapeDtypeStruct((heads, LANE, 3 * LANE), f32),
            jax.ShapeDtypeStruct((heads, 3 * LANE, LANE), f32),
        ],
        name="near_bias",
    )(spread(forward), spread(reverse))
    left = table[buckets // 2 - 1]
    right = table[buckets - 1]
    tile = jnp.arange(tile_count, dtype=jnp.int32)[None, :, None]
    lane = jnp.arange(LANE, dtype=jnp.int32)[None, None, :]
    far = jnp.where(lane == tile, left[:, None, None], 0.0)
    far = far + jnp.where(lane == tile + 8, right[:, None, None], 0.0)
    far = far + jnp.where(lane == 16, masked_score, 0.0)
    return near, near_t, far.astype(bf16)


def key_lanes(extent, length):
    key = lax.broadcasted_iota(jnp.int32, (extent, LANE), 0)
    lane = lax.broadcasted_iota(jnp.int32, (extent, LANE), 1)
    tile = key // LANE
    flag = (lane < 8) & (tile < lane - 1)
    flag = flag | ((lane >= 8) & (lane < 16) & (tile > lane - 8 + 1))
    flag = flag | ((lane == 16) & (key >= length))
    flag = flag | ((lane >= 17) & (lane < 20))
    return jnp.where(flag, 1.0, 0.0).astype(bf16)


def rms_of(values):
    scale = lax.rsqrt(jnp.mean(values * values, axis=-1, keepdims=True) + epsilon)
    return scale


def head_mask(rows, head):
    lane = lax.broadcasted_iota(jnp.int32, (rows, LANE), 1)
    return (lane // (LANE // 2)) == head


def fwd_body(held, count, which, scal, xl, xr, gain, wq, wk, wv, near, far, *rest):
    q_out, k_out, v_out, mix_out, tail_out, normt_out, x_out, normed, lanes = rest[held:]
    extent = normed.shape[0]
    half = xl.shape[1]
    length = scal[1 + 2 * count + which]
    side = scal[0]
    steps = (length + STEP - 1) // STEP

    @pl.when(pl.program_id(0) == 0)
    def _():
        for ref, own in ((xl, True), (xr, False)):
            values = ref[0].astype(f32)
            out = values * rms_of(values) * gain[...].astype(f32)
            place = side * half if own else (1 - side) * half
            normed[pl.ds(pl.multiple_of(place, half), half), :] = out.astype(bf16)
        lanes[...] = key_lanes(extent, length)
        normt_out[0] = normed[...].T
        x_out[...] = xr[...]

    q_out[0, 0] = mm(normed[...], wq[...]).astype(bf16)
    for part in range(extent // STEP):
        rows = pl.ds(part * STEP, STEP)

        @pl.when(part < steps)
        def _():
            k_out[0, 0, rows, :] = mm(normed[rows, :], wk[...]).astype(bf16)
            v_out[0, 0, rows, :] = mm(normed[rows, :], wv[...]).astype(bf16)

        @pl.when(part >= steps)
        def _():
            k_out[0, 0, rows, :] = jnp.zeros((STEP, 2 * LANE), bf16)
            v_out[0, 0, rows, :] = jnp.zeros((STEP, 2 * LANE), bf16)

    def attend(width):
        def pair_step(pair, carry):
            cols = pl.ds(pl.multiple_of(pair * LANE, LANE), LANE)
            kext = jnp.concatenate([k_out[0, 0, :width, cols], lanes[:width, :]], axis=1)
            vext = jnp.concatenate(
                [v_out[0, 0, :width, cols], jnp.ones((width, LANE), bf16)], axis=1
            )
            lane = lax.broadcasted_iota(jnp.int32, (STEP, LANE), 1)
            for block in range(extent // STEP):
                rows = slice(block * STEP, (block + 1) * STEP)
                qpair = q_out[0, 0, rows, cols]
                outs = []
                for head in range(2):
                    index = 2 * pair + head
                    tiles = []
                    for sub in range(STEP // LANE):
                        line = far[index, pl.ds(block * (STEP // LANE) + sub, 1), :]
                        tiles.append(jnp.broadcast_to(line, (LANE, LANE)))
                    ext = jnp.concatenate(tiles, axis=0)
                    qm = jnp.where(head_mask(STEP, head), qpair, jnp.zeros_like(qpair))
                    scores = mm(jnp.concatenate([qm, ext], axis=1), kext, NT)
                    probs = []
                    tops = []
                    for sub in range(STEP // LANE):
                        tile = block * (STEP // LANE) + sub
                        own = scores[sub * LANE : (sub + 1) * LANE]
                        base = (tile - 1) * LANE
                        low, high = max(0, base), min(width, base + 3 * LANE)
                        if low < high:
                            add = own[:, low:high] + near[index, :, low - base : high - base]
                            pieces = [own[:, :low]] if low > 0 else []
                            pieces.append(add)
                            if high < width:
                                pieces.append(own[:, high:])
                            own = jnp.concatenate(pieces, axis=1)
                        top = jnp.max(own, axis=1, keepdims=True)
                        probs.append(jnp.exp(own - top).astype(bf16))
                        tops.append(top)
                    both = mm(jnp.concatenate(probs, axis=0), vext)
                    total = both[:, LANE:]
                    outs.append(both[:, :LANE] / total)
                    neg = -(jnp.concatenate(tops, axis=0) + jnp.log(total))
                    first = neg.astype(bf16)
                    rest = neg - first.astype(f32)
                    second = rest.astype(bf16)
                    third = (rest - second.astype(f32)).astype(bf16)
                    line = jnp.where(lane == 17, first, ext)
                    line = jnp.where(lane == 18, second, line)
                    line = jnp.where(lane == 19, third, line)
                    tail_out[0, index, rows, :] = line
                picked = jnp.where(head_mask(STEP, 0), outs[0], outs[1])
                mix_out[0, 0, rows, cols] = picked.astype(bf16)
            return carry

        lax.fori_loop(0, 2, pair_step, 0)

    for blocks in range(1, extent // STEP + 1):

        @pl.when(steps == blocks)
        def _():
            attend(blocks * STEP)


def fwd_row(scal, inputs, remote, which, count, held, gain, wq, wk, wv, near, far, heads):
    rows, half, width = inputs.shape
    extent = 2 * half
    inner = wq.shape[1]
    quads = inner // STEP
    per = heads // quads
    weight = pl.BlockSpec((width, STEP), lambda i, s: (0, i))
    block = pl.BlockSpec((1, 1, extent, STEP), lambda i, s: (which, i, 0, 0))
    grid_spec = pltpu.PrefetchScalarGridSpec(
        num_scalar_prefetch=1,
        grid=(quads,),
        in_specs=[
            pl.BlockSpec((1, half, width), lambda i, s: (s[1 + which], 0, 0)),
            pl.BlockSpec((1, half, width), lambda i, s: (0, 0, 0)),
            pl.BlockSpec((1, width), lambda i, s: (0, 0)),
            weight,
            weight,
            weight,
            pl.BlockSpec((per, LANE, 3 * LANE), lambda i, s: (i, 0, 0)),
            pl.BlockSpec((per, 8, LANE), lambda i, s: (i, 0, 0)),
        ]
        + [pl.BlockSpec(memory_space=pl.ANY)] * len(held),
        out_specs=[block] * 4
        + [
            pl.BlockSpec((1, per, extent, LANE), lambda i, s: (which, i, 0, 0)),
            pl.BlockSpec((1, width, extent), lambda i, s: (which, 0, 0)),
            pl.BlockSpec((1, half, width), lambda i, s: (which, 0, 0)),
        ],
        scratch_shapes=[pltpu.VMEM((extent, width), bf16), pltpu.VMEM((extent, LANE), bf16)],
    )
    stacked = jax.ShapeDtypeStruct((count, quads, extent, STEP), bf16)
    return pl.pallas_call(
        functools.partial(fwd_body, len(held), count, which),
        grid_spec=grid_spec,
        out_shape=[stacked] * 4
        + [
            jax.ShapeDtypeStruct((count, heads, extent, LANE), bf16),
            jax.ShapeDtypeStruct((count, width, extent), bf16),
            jax.ShapeDtypeStruct((count, half, width), bf16),
        ],
        input_output_aliases={9 + n: n for n in range(len(held))},
        compiler_params=params(1, 56),
        cost_estimate=cost(27),
        name="attend_row",
    )(scal, inputs, remote, gain, wq, wk, wv, near, far, *held)


def bwd_body(
    count, scal, q, k, v, mix, dmix, tail, near_t, normt, *rest
):
    (dq_out, dk_out, dv_out, tacc_out, far_out, dw_out) = rest[-15:-9]
    (lanes, pl_s, ds_s, do_s, qa_s, dwq, dwk, dwv, _) = rest[-9:]
    extent = lanes.shape[0]
    row = pl.program_id(0)
    length = scal[1 + 2 * count + row]
    steps = (length + STEP - 1) // STEP
    lanes[...] = key_lanes(extent, length)

    @pl.when(row == 0)
    def _():
        for ref in (tacc_out, far_out, dwq, dwk, dwv):
            ref[...] = jnp.zeros(ref.shape, f32)

    dk_out[...] = jnp.zeros(dk_out.shape, bf16)
    dv_out[...] = jnp.zeros(dv_out.shape, bf16)

    def attend(width):
        def head_step(index, carry):
            pair = index // 2
            head = lax.rem(index, 2)
            cols = pl.ds(pl.multiple_of(pair * LANE, LANE), LANE)
            flags = lanes[:width, :]
            kpair = k[0, 0, :width, cols]
            kext = jnp.concatenate([kpair, flags], axis=1)
            vext = jnp.concatenate([v[0, 0, :width, cols], flags], axis=1)
            lane = lax.broadcasted_iota(jnp.int32, (STEP, LANE), 1)
            mask = head_mask(STEP, head)
            for block in range(extent // STEP):
                rows = slice(block * STEP, (block + 1) * STEP)
                qpair = q[0, 0, rows, cols]
                dopair = dmix[0, 0, rows, cols]
                product = dopair.astype(f32) * mix[0, 0, rows, cols].astype(f32)
                qm = jnp.where(mask, qpair, jnp.zeros_like(qpair))
                dom = jnp.where(mask, dopair, jnp.zeros_like(dopair))
                neg = -jnp.sum(jnp.where(mask, product, 0.0), axis=1, keepdims=True)
                neg = jnp.broadcast_to(neg, (STEP, LANE))
                first = neg.astype(bf16)
                rest = neg - first.astype(f32)
                second = rest.astype(bf16)
                third = (rest - second.astype(f32)).astype(bf16)
                dtail = jnp.where(lane == 17, first, jnp.zeros((STEP, LANE), bf16))
                dtail = jnp.where(lane == 18, second, dtail)
                dtail = jnp.where(lane == 19, third, dtail)
                st = mm(kext, jnp.concatenate([qm, tail[0, index, rows, :]], axis=1), NT)
                dp = mm(vext, jnp.concatenate([dom, dtail], axis=1), NT)
                do_s[rows, :] = dom
                row_at = lax.broadcasted_iota(jnp.int32, (STEP, LANE), 0)
                spot = jnp.where(lane == block * (STEP // LANE) + row_at // LANE, 1.0, 0.0)
                qa_s[rows, :] = jnp.concatenate([qm, spot.astype(bf16)], axis=1)
                for sub in range(STEP // LANE):
                    tile = block * (STEP // LANE) + sub
                    part = slice(sub * LANE, (sub + 1) * LANE)
                    own = st[:, part]
                    base = (tile - 1) * LANE
                    low, high = max(0, base), min(width, base + 3 * LANE)
                    if low < high:
                        add = own[low:high] + near_t[index, low - base : high - base, :]
                        pieces = [own[:low]] if low > 0 else []
                        pieces.append(add)
                        if high < width:
                            pieces.append(own[high:])
                        own = jnp.concatenate(pieces, axis=0)
                    prob = jnp.exp(own)
                    dst = (prob * dp[:, part]).astype(bf16)
                    place = slice(tile * LANE, (tile + 1) * LANE)
                    pl_s[:width, place] = prob.astype(bf16)
                    ds_s[:width, place] = dst
                    if low < high:
                        tacc_out[index, low - base : high - base, :] += dst[low:high].astype(f32)
            kmask = head_mask(width, head)
            dv = mm(pl_s[:width, :], do_s[...]).astype(bf16)
            dv_out[0, :width, cols] = jnp.where(kmask, dv, dv_out[0, :width, cols])
            dk = mm(ds_s[:width, :], qa_s[...])
            dk_out[0, :width, cols] = jnp.where(
                kmask, dk[:, :LANE].astype(bf16), dk_out[0, :width, cols]
            )
            tile = lax.broadcasted_iota(jnp.int32, (width, LANE), 0) // LANE
            spread = lax.broadcasted_iota(jnp.int32, (width, LANE), 1)
            left = jnp.where((tile < spread - 1) & (spread < 8), dk[:, LANE:], 0.0)
            right = jnp.where((tile > spread + 1) & (spread < 8), dk[:, LANE:], 0.0)
            far_out[pl.ds(index, 1), :] += jnp.sum(left, axis=0, keepdims=True)
            far_out[pl.ds(4 + index, 1), :] += jnp.sum(right, axis=0, keepdims=True)
            dq = mm(ds_s[:width, :], jnp.where(kmask, kpair, jnp.zeros_like(kpair)), TN)
            qmask = head_mask(extent, head)
            dq_out[0, :, cols] = jnp.where(qmask, dq.astype(bf16), dq_out[0, :, cols])
            return carry

        lax.fori_loop(0, 4, head_step, 0)
        dwk[...] += mm(normt[0, :, :width], dk_out[0, :width, :])
        dwv[...] += mm(normt[0, :, :width], dv_out[0, :width, :])

    for blocks in range(1, extent // STEP + 1):

        @pl.when(steps == blocks)
        def _():
            attend(blocks * STEP)

    dwq[...] += mm(normt[0], dq_out[0])

    @pl.when(row == count - 1)
    def _():
        for n, ref in enumerate((dwq, dwk, dwv)):
            dw_out[:, n * STEP : (n + 1) * STEP] = ref[...].astype(bf16)


def bwd_quad(places, quad, held, q, k, v, mix, dmix, tail, near_t, normt, deps=()):
    count, quads, extent, _ = q.shape
    heads = tail.shape[1]
    width = normt.shape[1]
    per = heads // quads
    block = pl.BlockSpec((1, 1, extent, STEP), lambda i, s: (i, quad, 0, 0))
    given = pl.BlockSpec((1, extent, STEP), lambda i, s: (i, 0, 0))
    grid_spec = pltpu.PrefetchScalarGridSpec(
        num_scalar_prefetch=1,
        grid=(count,),
        in_specs=[block] * 5
        + [
            pl.BlockSpec((1, per, extent, LANE), lambda i, s: (i, quad, 0, 0)),
            pl.BlockSpec((per, 3 * LANE, LANE), lambda i, s: (quad, 0, 0)),
            pl.BlockSpec((1, width, extent), lambda i, s: (i, 0, 0)),
        ]
        + [pl.BlockSpec(memory_space=pl.ANY)] * (len(held) + len(deps)),
        out_specs=[given] * 3
        + [
            pl.BlockSpec((per, 3 * LANE, LANE), lambda i, s: (0, 0, 0)),
            pl.BlockSpec((8, LANE), lambda i, s: (0, 0)),
            pl.BlockSpec((width, 3 * STEP), lambda i, s: (0, quad)),
        ],
        scratch_shapes=[
            pltpu.VMEM((extent, LANE), bf16),
            pltpu.VMEM((extent, extent), bf16),
            pltpu.VMEM((extent, extent), bf16),
            pltpu.VMEM((extent, LANE), bf16),
            pltpu.VMEM((extent, 2 * LANE), bf16),
        ]
        + [pltpu.VMEM((width, STEP), f32)] * 3
        + [pltpu.VMEM((8, LANE), f32)],
    )
    out = jax.ShapeDtypeStruct((count, extent, STEP), bf16)
    return pl.pallas_call(
        functools.partial(bwd_body, count),
        grid_spec=grid_spec,
        out_shape=[out] * 3
        + [
            jax.ShapeDtypeStruct((per, 3 * LANE, LANE), f32),
            jax.ShapeDtypeStruct((8, LANE), f32),
            jax.ShapeDtypeStruct((width, 3 * STEP * quads), bf16),
        ],
        input_output_aliases={9: 5} if held else {},
        compiler_params=params(1, 60),
        cost_estimate=cost(1),
        name="attend_back",
    )(places, q, k, v, mix, dmix, tail, near_t, normt, *held, *deps)


def table_body(quads, *rest):
    out = rest[-1]
    for quad in range(quads):
        tacc = rest[quad]
        total = jnp.zeros((8, 4 * LANE), f32)
        for group in range(3 * LANE // 8):
            part = tacc[0, group * 8 : (group + 1) * 8, :]
            wide = jnp.concatenate([part, jnp.zeros((8, 3 * LANE), f32)], axis=1)
            total = total + (pltpu.roll(wide, 4 * LANE - 8 * group, 1) if group else wide)
        line = total[0:1]
        for row in range(1, 8):
            line = line + pltpu.roll(total[row : row + 1], 4 * LANE - row, 1)
        out[quad, 0] = line


def table_diagonals(tacc, deps=()):
    quads, per = len(tacc), tacc[0].shape[0]
    return pl.pallas_call(
        functools.partial(table_body, quads),
        grid=(per,),
        in_specs=[pl.BlockSpec((1, 3 * LANE, LANE), lambda h: (h, 0, 0))] * quads
        + [pl.BlockSpec(memory_space=pl.ANY)] * len(deps),
        out_specs=pl.BlockSpec((quads, 1, 1, 4 * LANE), lambda h: (0, h, 0, 0)),
        out_shape=jax.ShapeDtypeStruct((quads, per, 1, 4 * LANE), f32),
        cost_estimate=cost(100),
        name="table_diagonals",
    )(*tacc, *deps)


def table_sums(diagonals, far_sum, buckets):
    heads = diagonals.shape[0] * diagonals.shape[1]
    diagonals = diagonals.reshape(heads, 1, 4 * LANE)
    place = jnp.arange(4 * LANE, dtype=jnp.int32)
    back = jnp.where(place < LANE, place, place - 4 * LANE)
    hot = bucket_of(-back - LANE, buckets)[:, None] == jnp.arange(buckets, dtype=jnp.int32)
    near = jnp.einsum(
        "rb,hr->bh", hot.astype(f32), diagonals[:, 0, :], precision=lax.Precision.HIGHEST
    )
    sides = jnp.sum(far_sum, axis=2).reshape(-1, 2, 4)
    sides = jnp.transpose(sides, (1, 0, 2)).reshape(2, heads)
    half = buckets // 2
    near = near.at[half - 1].add(sides[0])
    return near.at[buckets - 1].add(sides[1])


CHUNK = 512
GELU_K = math.sqrt(2.0 / math.pi)


def gated(normed, g, w_gate, w_up, w_down):
    gate = mm(normed, w_gate)
    up = mm(normed, w_up)
    d_act = mm(g, w_down, NT)
    square = gate * gate
    th = jnp.tanh(gate * (GELU_K + (GELU_K * 0.044715) * square))
    half = 0.5 + 0.5 * th
    gelu = gate * half
    slope = half + (0.5 * gate) * (1.0 - th * th) * (GELU_K + (3.0 * 0.044715 * GELU_K) * square)
    return (
        (gelu * up).astype(bf16),
        (d_act * up * slope).astype(bf16),
        (d_act * gelu).astype(bf16),
    )


def ff_body(
    scal, xl, xr, gl, gr, mix, w_out, gain, gate_any, up_any, down_any,
    lo_out, lo_send, dh_out, dmix_out, dw_out, dgain_out,
    dwo, dwg, dwu, dwd, w_gate, w_up, w_down, sems,
):
    step = pl.program_id(0)
    last = pl.num_programs(0) - 1
    own = lax.rem(step, 2) == 0
    units = w_gate.shape[1]
    loads = [
        pltpu.make_async_copy(source, target, sems.at[n])
        for n, (source, target) in enumerate(
            ((gate_any, w_gate), (up_any, w_up), (down_any, w_down))
        )
    ]

    @pl.when(step == 0)
    def _():
        for load in loads:
            load.start()
        for ref in (dwo, dwg, dwu, dwd, dgain_out):
            ref[...] = jnp.zeros(ref.shape, f32)

    g = jnp.where(own, gl[0], gr[0])
    x = jnp.where(own, xl[0], xr[0]).astype(f32)
    quads = mix.shape[1]
    mixed = jnp.concatenate([mix[0, i] for i in range(quads)], axis=1)
    hidden = x + mm(mixed, w_out[...])
    gain_f = gain[...].astype(f32)
    scale = rms_of(hidden)
    unit = hidden * scale
    normed = (unit * gain_f).astype(bf16)
    normed_t = normed.T
    g_t = g.T
    out = hidden
    dn = jnp.zeros_like(hidden)

    @pl.when(step == 0)
    def _():
        for load in loads:
            load.wait()

    for c in range(units // CHUNK):
        cols = slice(c * CHUNK, (c + 1) * CHUNK)
        act, d_gate, d_up = gated(normed, g, w_gate[:, cols], w_up[:, cols], w_down[cols, :])
        out = out + mm(act, w_down[cols, :])
        dn = dn + mm(d_gate, w_gate[:, cols], NT) + mm(d_up, w_up[:, cols], NT)
        dwd[:, cols] += mm(g_t, act)
        dwg[:, cols] += mm(normed_t, d_gate)
        dwu[:, cols] += mm(normed_t, d_up)

    @pl.when(own)
    def _():
        lo_out[0] = out

    @pl.when(jnp.logical_not(own))
    def _():
        lo_send[0] = out.astype(bf16)

    dgain_out[...] += jnp.sum(dn * unit, axis=0, keepdims=True)
    e = dn * gain_f
    d_hidden = (
        g.astype(f32) + scale * e - unit * (scale * jnp.mean(unit * e, axis=-1, keepdims=True))
    )
    dh_out[0] = d_hidden
    low = d_hidden.astype(bf16)
    dwo[...] += mm(mixed.T, low)
    d_mixed = mm(low, w_out[...], NT).astype(bf16)
    for i in range(quads):
        dmix_out[0, i] = d_mixed[:, i * STEP : (i + 1) * STEP]

    @pl.when(step == last)
    def _():
        pending = [None, None]
        place = 0
        for n, acc in enumerate((dwg, dwu, dwd, dwo)):
            slot = n % 2
            stage = (w_gate, w_up)[slot]
            if pending[slot] is not None:
                pending[slot].wait()
            cols = acc.shape[1]
            stage[:, :cols] = acc[...].astype(bf16)
            copy = pltpu.make_async_copy(
                stage.at[:, pl.ds(0, cols)], dw_out.at[:, pl.ds(place, cols)], sems.at[slot]
            )
            copy.start()
            pending[slot] = copy
            place += cols
        for copy in pending:
            copy.wait()


def feed_forward(places, inputs, x_remote, cot, cot_remote, mix, w_out, gain, w_gate, w_up, w_down):
    rows, half, width = inputs.shape
    mine = x_remote.shape[0]
    _, quads, extent, _ = mix.shape
    units = w_gate.shape[1]
    inner = w_out.shape[0]

    def keep(shape):
        return pl.BlockSpec(shape, lambda i, s: (0,) * len(shape), pipeline_mode=pl.Buffered(1))

    local = pl.BlockSpec((1, half, width), lambda i, s: (s[1 + i // 2], 0, 0))
    far = pl.BlockSpec((1, half, width), lambda i, s: (i // 2, 0, 0))
    far_one = pl.BlockSpec(
        (1, half, width), lambda i, s: (i // 2, 0, 0), pipeline_mode=pl.Buffered(1)
    )
    spot = pl.BlockSpec(
        (1, quads, half, STEP),
        lambda i, s: (i // 2, 0, jnp.where(i % 2 == 0, s[0], 1 - s[0]), 0),
    )
    tile = pl.BlockSpec((1, half, width), lambda i, s: (i, 0, 0))
    anywhere = pl.BlockSpec(memory_space=pl.ANY)
    grid_spec = pltpu.PrefetchScalarGridSpec(
        num_scalar_prefetch=1,
        grid=(2 * mine,),
        in_specs=[local, far_one, local, far_one, spot, keep((inner, width)), keep((1, width)),
                  anywhere, anywhere, anywhere],
        out_specs=[local, far, tile, spot, anywhere,
                   pl.BlockSpec((1, width), lambda i, s: (0, 0))],
        scratch_shapes=[pltpu.VMEM((inner, width), f32)]
        + [pltpu.VMEM((width, units), f32)] * 3
        + [
            pltpu.VMEM((width, units), bf16),
            pltpu.VMEM((width, units), bf16),
            pltpu.VMEM((units, width), bf16),
            pltpu.SemaphoreType.DMA((3,)),
        ],
    )
    return pl.pallas_call(
        ff_body,
        grid_spec=grid_spec,
        out_shape=[
            jax.ShapeDtypeStruct((rows, half, width), f32),
            jax.ShapeDtypeStruct((mine, half, width), bf16),
            jax.ShapeDtypeStruct((2 * mine, half, width), f32),
            jax.ShapeDtypeStruct((mine, quads, extent, STEP), bf16),
            jax.ShapeDtypeStruct((width, 3 * units + width), bf16),
            jax.ShapeDtypeStruct((1, width), f32),
        ],
        compiler_params=params(1, 63),
        cost_estimate=cost(150),
        name="feed_forward",
    )(places, inputs, x_remote, cot, cot_remote, mix, w_out, gain, w_gate, w_up, w_down)


def spread_body(sums, *rest):
    gate_out, up_out, down_out, out_out = rest[-4:]
    units = gate_out.shape[1]
    gate_out[...] = sums[:, :units].astype(f32)
    up_out[...] = sums[:, units : 2 * units].astype(f32)
    down_out[...] = sums[:, 2 * units : 3 * units].astype(f32).T
    out_out[...] = sums[:, 3 * units :].astype(f32)


def spread(sums, deps=()):
    width, columns = sums.shape
    units = (columns - width) // 3
    wide = pl.BlockSpec((LANE, units), lambda i: (i, 0))
    return pl.pallas_call(
        spread_body,
        grid=(width // LANE,),
        in_specs=[pl.BlockSpec((LANE, columns), lambda i: (i, 0))]
        + [pl.BlockSpec(memory_space=pl.ANY)] * len(deps),
        out_specs=[
            wide,
            wide,
            pl.BlockSpec((units, LANE), lambda i: (0, i)),
            pl.BlockSpec((LANE, width), lambda i: (i, 0)),
        ],
        out_shape=[
            jax.ShapeDtypeStruct((width, units), f32),
            jax.ShapeDtypeStruct((width, units), f32),
            jax.ShapeDtypeStruct((units, width), f32),
            jax.ShapeDtypeStruct((width, width), f32),
        ],
        compiler_params=params(1, 56),
        cost_estimate=cost(100),
        name="spread",
    )(sums, *deps)


def back_body(quads, held, scal, xl, xr, dh, *rest):
    grads = rest[: 3 * quads]
    gain, wq, wk, wv = rest[3 * quads : 3 * quads + 4]
    ig_out, ig_send, dgain_out = rest[-3:]
    step = pl.program_id(0)
    far = step == 0

    @pl.when(far)
    def _():
        dgain_out[...] = jnp.zeros(dgain_out.shape, f32)

    x = jnp.where(far, xr[0], xl[0]).astype(f32)
    dn = jnp.zeros_like(x)
    for n, weight in enumerate((wq, wk, wv)):
        part = jnp.concatenate([ref[0] for ref in grads[n * quads : (n + 1) * quads]], axis=1)
        dn = dn + mm(part, weight[...], NT)
    scale = rms_of(x)
    unit = x * scale
    dgain_out[...] += jnp.sum(dn * unit, axis=0, keepdims=True)
    e = dn * gain[...].astype(f32)
    out = dh[0] + scale * e - unit * (scale * jnp.mean(unit * e, axis=-1, keepdims=True))

    @pl.when(far)
    def _():
        ig_send[0] = out.astype(bf16)

    @pl.when(jnp.logical_not(far))
    def _():
        ig_out[0] = out


def input_back(places, row, held, inputs, remote, dh, dq, dk, dv, gain, wq, wk, wv, deps=()):
    rows, half, width = inputs.shape
    local = pl.BlockSpec((1, half, width), lambda i, s: (s[1 + row], 0, 0))
    one = pl.BlockSpec((1, half, width), lambda i, s: (0, 0, 0))
    tile = pl.BlockSpec((1, half, width), lambda i, s: (2 * row + 1 - i, 0, 0))
    spot = pl.BlockSpec((1, half, STEP), lambda i, s: (row, jnp.where(i == 1, s[0], 1 - s[0]), 0))
    weight = pl.BlockSpec(wq.shape, lambda i, s: (0, 0), pipeline_mode=pl.Buffered(1))
    line = pl.BlockSpec((1, width), lambda i, s: (0, 0))
    anywhere = pl.BlockSpec(memory_space=pl.ANY)
    grads = [*dq, *dk, *dv]
    grid_spec = pltpu.PrefetchScalarGridSpec(
        num_scalar_prefetch=1,
        grid=(2,),
        in_specs=[local, one, tile]
        + [spot] * len(grads)
        + [line, weight, weight, weight]
        + [anywhere] * (len(held) + len(deps)),
        out_specs=[local, one, line],
    )
    return pl.pallas_call(
        functools.partial(back_body, len(dq), len(held)),
        grid_spec=grid_spec,
        out_shape=[
            jax.ShapeDtypeStruct((rows, half, width), f32),
            jax.ShapeDtypeStruct((1, half, width), bf16),
            jax.ShapeDtypeStruct((1, width), f32),
        ],
        input_output_aliases={8 + len(grads): 0} if held else {},
        compiler_params=params(1, 56),
        cost_estimate=cost(100),
        name="input_back",
    )(places, inputs, remote, dh, *grads, gain, wq, wk, wv, *held, *deps)


def hold_body(value, *rest):
    rest[-1][...] = value[...]


def hold(value, deps):
    return pl.pallas_call(
        hold_body,
        in_specs=[pl.BlockSpec(memory_space=pltpu.VMEM)]
        + [pl.BlockSpec(memory_space=pl.ANY)] * len(deps),
        out_specs=pl.BlockSpec(memory_space=pltpu.VMEM),
        out_shape=jax.ShapeDtypeStruct(value.shape, value.dtype),
        compiler_params=pltpu.CompilerParams(vmem_limit_bytes=16 << 20),
        name="hold",
    )(value, *deps)


def pick_half(grads, at, deps):
    rows, columns = grads.shape
    grid_spec = pltpu.PrefetchScalarGridSpec(
        num_scalar_prefetch=1,
        grid=(1,),
        in_specs=[pl.BlockSpec((rows // 2, columns), lambda i, s: (s[0], 0))]
        + [pl.BlockSpec(memory_space=pl.ANY)] * len(deps),
        out_specs=pl.BlockSpec((rows // 2, columns), lambda i, s: (0, 0)),
    )
    return pl.pallas_call(
        pick_body,
        grid_spec=grid_spec,
        out_shape=jax.ShapeDtypeStruct((rows // 2, columns), grads.dtype),
        compiler_params=params(1, 24),
        name="pick_half",
    )(at.reshape(1), grads, *deps)


def pick_body(scal, array, *rest):
    rest[-1][...] = array[...]


def pick_rows(places, first, count, array, deps=()):
    rows, half, width = array.shape
    grid_spec = pltpu.PrefetchScalarGridSpec(
        num_scalar_prefetch=1,
        grid=(count,),
        in_specs=[pl.BlockSpec((1, half, width), lambda i, s: (s[1 + rows // 2 + first + i], 0, 0))]
        + [pl.BlockSpec(memory_space=pl.ANY)] * len(deps),
        out_specs=pl.BlockSpec((1, half, width), lambda i, s: (i, 0, 0)),
    )
    return pl.pallas_call(
        pick_body,
        grid_spec=grid_spec,
        out_shape=jax.ShapeDtypeStruct((count, half, width), array.dtype),
        compiler_params=params(1, 16),
        name="pick_rows",
    )(places, array, *deps)


def place_body(scal, arrived, *rest):
    out, token = rest[-2:]
    out[0] = arrived[0].astype(f32)
    token[...] = jnp.zeros(token.shape, f32)


def place_rows(places, first, arrived, held, deps=(), weight=100):
    count, half, width = arrived.shape
    at = 1 + held.shape[0] // 2 + first
    anywhere = pl.BlockSpec(memory_space=pl.ANY)
    grid_spec = pltpu.PrefetchScalarGridSpec(
        num_scalar_prefetch=1,
        grid=(count,),
        in_specs=[pl.BlockSpec((1, half, width), lambda i, s: (i, 0, 0)), anywhere]
        + [anywhere] * len(deps),
        out_specs=[
            pl.BlockSpec((1, half, width), lambda i, s: (s[at + i], 0, 0)),
            pl.BlockSpec((8, LANE), lambda i, s: (0, 0)),
        ],
    )
    return pl.pallas_call(
        place_body,
        grid_spec=grid_spec,
        out_shape=[
            jax.ShapeDtypeStruct(held.shape, f32),
            jax.ShapeDtypeStruct((8, LANE), f32),
        ],
        input_output_aliases={2: 0},
        compiler_params=params(1, 32),
        cost_estimate=cost(weight),
        name="place_rows",
    )(places, arrived, held, *deps)


def unpack_body(scal, sums, *rest):
    outs = rest[-3:]
    quads = outs[0].shape[1] // STEP
    for n, out in enumerate(outs):
        for quad in range(quads):
            begin = (3 * quad + n) * STEP
            out[:, quad * STEP : (quad + 1) * STEP] = sums[:, begin : begin + STEP].astype(f32)


def unpack(sums, at, held=(), deps=()):
    rows, columns = sums.shape
    width = columns // 3
    parts = 4
    anywhere = pl.BlockSpec(memory_space=pl.ANY)
    grid_spec = pltpu.PrefetchScalarGridSpec(
        num_scalar_prefetch=1,
        grid=(parts,),
        in_specs=[pl.BlockSpec((rows // parts, columns), lambda i, s: (i, 0))]
        + [anywhere] * (len(held) + len(deps)),
        out_specs=[pl.BlockSpec((rows // parts, width), lambda i, s: (s[0] * parts + i, 0))] * 3,
    )
    return pl.pallas_call(
        unpack_body,
        grid_spec=grid_spec,
        out_shape=[jax.ShapeDtypeStruct((2 * rows, width), f32)] * 3,
        input_output_aliases={2 + n: n for n in range(len(held))},
        compiler_params=params(1, 32),
        cost_estimate=cost(100),
        name="unpack",
    )(at.reshape(1), sums, *held, *deps)


highest = lax.Precision.HIGHEST


def rms_scaled(values, gain):
    mean_square = jnp.mean(values * values, axis=-1, keepdims=True)
    return values * lax.rsqrt(mean_square + epsilon) * gain


def gated_unit(gate, up_proj):
    return jax.nn.gelu(gate, approximate=True) * up_proj


def relative_one_hot(query_anchor, query_extent, key_extent, bucket_count):
    query_place = query_anchor + jnp.arange(query_extent, dtype=jnp.int32)
    key_place = jnp.arange(key_extent, dtype=jnp.int32)
    offset = key_place[None, :] - query_place[:, None]
    distance = jnp.abs(offset)
    far_bucket = jnp.full_like(distance, 8)
    for threshold in bucket_bounds:
        far_bucket = far_bucket + (distance >= threshold).astype(jnp.int32)
    bucket = jnp.where(offset > 0, bucket_count // 2, 0) + jnp.where(
        distance < 8, distance, far_bucket
    )
    return (bucket[:, :, None] == jnp.arange(bucket_count, dtype=jnp.int32)).astype(jnp.float32)


def block_scores(query_heads, key_heads, query_anchor, lengths, bias_f):
    key_extent = key_heads.shape[1]
    one_hot = relative_one_hot(query_anchor, query_heads.shape[1], key_extent, bias_f.shape[0])
    bias_block = jnp.einsum("qkb,bh->hqk", one_hot, bias_f, precision=highest)
    raw_scores = jnp.einsum(
        "rqhd,rkhd->rhqk", query_heads, key_heads, preferred_element_type=jnp.float32
    )
    usable = jnp.arange(key_extent, dtype=jnp.int32)[None, :] < lengths[:, None]
    return (
        jnp.where(usable[:, None, None, :], raw_scores + bias_block[None], masked_score),
        one_hot,
    )


def score_grads(scores, log_total, row_dot, grad_heads, value_heads):
    weights_hp = jnp.exp(scores - log_total[..., None])
    d_weights = jnp.einsum(
        "rqhd,rkhd->rhqk", grad_heads, value_heads, preferred_element_type=jnp.float32
    )
    d_scores = (weights_hp * (d_weights - row_dot[..., None])).astype(jnp.bfloat16)
    return (weights_hp.astype(jnp.bfloat16), d_scores)


def table_term(one_hot, d_scores):
    summed = jnp.sum(d_scores, axis=0, dtype=jnp.float32)
    return jnp.einsum("qkb,hqk->bh", one_hot, summed, precision=highest)


def gathered_device(
    inputs,
    lengths,
    cotangent,
    norm_gain,
    w_query,
    w_key,
    w_value,
    w_out,
    ff_gain,
    w_gate,
    w_up,
    w_down,
    bias_table,
):
    row_count, block_len, model_width = inputs.shape
    head_count = bias_table.shape[1]
    inner_width = w_query.shape[1]
    head_width = inner_width // head_count
    tokens_here = row_count * block_len
    lengths = lengths.reshape(-1)
    bias_f = bias_table.astype(jnp.float32)
    own_anchor = lax.axis_index("seq") * block_len

    def split_heads(block_array):
        return block_array.reshape(row_count, block_array.shape[1], head_count, head_width)

    tokens_f = inputs.astype(jnp.float32).reshape(tokens_here, model_width)
    normed_f, norm_pull = jax.vjp(rms_scaled, tokens_f, norm_gain.astype(jnp.float32))
    normed = normed_f.astype(jnp.bfloat16)
    queries = (
        jnp.dot(normed, w_query, preferred_element_type=jnp.float32)
        .astype(jnp.bfloat16)
        .reshape(row_count, block_len, inner_width)
    )
    keys = (
        jnp.dot(normed, w_key, preferred_element_type=jnp.float32)
        .astype(jnp.bfloat16)
        .reshape(row_count, block_len, inner_width)
    )
    values = (
        jnp.dot(normed, w_value, preferred_element_type=jnp.float32)
        .astype(jnp.bfloat16)
        .reshape(row_count, block_len, inner_width)
    )
    query_heads = split_heads(queries)
    stat_shape = (row_count, head_count, block_len)
    pieces = (
        lax.all_gather(keys, "seq", axis=1, tiled=True),
        lax.all_gather(values, "seq", axis=1, tiled=True),
    )
    row_max = jnp.full(stat_shape, start_max, jnp.float32)
    key_heads = split_heads(pieces[0])
    value_heads = split_heads(pieces[1])
    scores, one_hot = block_scores(query_heads, key_heads, own_anchor, lengths, bias_f)
    new_max = jnp.maximum(row_max, jnp.max(scores, axis=-1))
    weights_hp = jnp.exp(scores - new_max[..., None])
    row_sum = jnp.sum(weights_hp, axis=-1)
    weighted = jnp.einsum(
        "rhqk,rkhd->rhqd",
        weights_hp.astype(jnp.bfloat16),
        value_heads,
        preferred_element_type=jnp.float32,
    )
    row_max, row_sum, weighted = (new_max, row_sum, weighted)
    log_total = row_max + jnp.log(row_sum)
    mixed_heads = jnp.transpose(weighted / row_sum[..., None], (0, 2, 1, 3))
    mixed_low = mixed_heads.reshape(tokens_here, inner_width).astype(jnp.bfloat16)
    hidden = tokens_f + jnp.dot(mixed_low, w_out, preferred_element_type=jnp.float32)
    normed2_f, ff_pull = jax.vjp(rms_scaled, hidden, ff_gain.astype(jnp.float32))
    normed2 = normed2_f.astype(jnp.bfloat16)
    gate = jnp.dot(normed2, w_gate, preferred_element_type=jnp.float32)
    up_proj = jnp.dot(normed2, w_up, preferred_element_type=jnp.float32)
    activated, gated_pull = jax.vjp(gated_unit, gate, up_proj)
    act_low = activated.astype(jnp.bfloat16)
    layer_output = (hidden + jnp.dot(act_low, w_down, preferred_element_type=jnp.float32)).reshape(
        row_count, block_len, model_width
    )
    grad_out = cotangent.reshape(tokens_here, model_width)
    dw_down = jnp.einsum("tf,td->fd", act_low, grad_out, preferred_element_type=jnp.float32)
    d_act = jnp.einsum("td,fd->tf", grad_out, w_down, preferred_element_type=jnp.float32)
    d_gate, d_up = gated_pull(d_act)
    d_gate = d_gate.astype(jnp.bfloat16)
    d_up = d_up.astype(jnp.bfloat16)
    dw_gate = jnp.einsum("td,tf->df", normed2, d_gate, preferred_element_type=jnp.float32)
    dw_up = jnp.einsum("td,tf->df", normed2, d_up, preferred_element_type=jnp.float32)
    d_normed2 = jnp.einsum(
        "tf,df->td", d_gate, w_gate, preferred_element_type=jnp.float32
    ) + jnp.einsum("tf,df->td", d_up, w_up, preferred_element_type=jnp.float32)
    d_hidden_part, d_ff_gain = ff_pull(d_normed2)
    d_hidden = grad_out.astype(jnp.float32) + d_hidden_part
    d_hidden_low = d_hidden.astype(jnp.bfloat16)
    dw_out = jnp.einsum("ti,td->id", mixed_low, d_hidden_low, preferred_element_type=jnp.float32)
    d_mixed = (
        jnp.einsum("td,id->ti", d_hidden_low, w_out, preferred_element_type=jnp.float32)
        .astype(jnp.bfloat16)
        .reshape(row_count, block_len, inner_width)
    )
    grad_heads = split_heads(d_mixed)
    row_dot_rows = jnp.sum(grad_heads.astype(jnp.float32) * mixed_heads, axis=-1)
    row_dot = jnp.transpose(row_dot_rows, (0, 2, 1))
    pieces = (
        lax.all_gather(keys, "seq", axis=1, tiled=True),
        lax.all_gather(values, "seq", axis=1, tiled=True),
    )
    key_heads = split_heads(pieces[0])
    value_heads = split_heads(pieces[1])
    scores, one_hot = block_scores(query_heads, key_heads, own_anchor, lengths, bias_f)
    weights_low, d_scores = score_grads(scores, log_total, row_dot, grad_heads, value_heads)
    d_query_part = jnp.einsum(
        "rhqk,rkhd->rqhd", d_scores, key_heads, preferred_element_type=jnp.float32
    )
    key_heads, weights_low, d_scores, d_query_part, table_part = (
        key_heads,
        weights_low,
        d_scores,
        d_query_part,
        table_term(one_hot, d_scores),
    )
    extent = key_heads.shape[1]
    d_key_part = jnp.einsum(
        "rhqk,rqhd->rkhd", d_scores, query_heads, preferred_element_type=jnp.float32
    ).reshape(row_count, extent, inner_width)
    d_value_part = jnp.einsum(
        "rhqk,rqhd->rkhd", weights_low, grad_heads, preferred_element_type=jnp.float32
    ).reshape(row_count, extent, inner_width)
    d_key, d_value = (
        lax.psum_scatter(d_key_part, "seq", scatter_dimension=1, tiled=True),
        lax.psum_scatter(d_value_part, "seq", scatter_dimension=1, tiled=True),
    )
    d_query_low = d_query_part.reshape(tokens_here, inner_width).astype(jnp.bfloat16)
    d_key_low = d_key.reshape(tokens_here, inner_width).astype(jnp.bfloat16)
    d_value_low = d_value.reshape(tokens_here, inner_width).astype(jnp.bfloat16)
    dw_query = jnp.einsum("td,ti->di", normed, d_query_low, preferred_element_type=jnp.float32)
    dw_key = jnp.einsum("td,ti->di", normed, d_key_low, preferred_element_type=jnp.float32)
    dw_value = jnp.einsum("td,ti->di", normed, d_value_low, preferred_element_type=jnp.float32)
    d_normed = jnp.einsum("ti,di->td", d_query_low, w_query, preferred_element_type=jnp.float32)
    d_normed = d_normed + jnp.einsum(
        "ti,di->td", d_key_low, w_key, preferred_element_type=jnp.float32
    )
    d_normed = d_normed + jnp.einsum(
        "ti,di->td", d_value_low, w_value, preferred_element_type=jnp.float32
    )
    d_tokens_part, d_norm_gain = norm_pull(d_normed)
    input_grad = (d_hidden + d_tokens_part).reshape(row_count, block_len, model_width)
    flat_query = dw_query.reshape(-1)
    flat_key = dw_key.reshape(-1)
    flat_value = dw_value.reshape(-1)
    flat_out = dw_out.reshape(-1)
    flat_gate = dw_gate.reshape(-1)
    flat_up = dw_up.reshape(-1)
    flat_down = dw_down.reshape(-1)
    shares = (
        lax.psum_scatter(flat_query, ("batch", "seq"), scatter_dimension=0, tiled=True),
        lax.psum_scatter(flat_key, ("batch", "seq"), scatter_dimension=0, tiled=True),
        lax.psum_scatter(flat_value, ("batch", "seq"), scatter_dimension=0, tiled=True),
        lax.psum_scatter(flat_out, ("batch", "seq"), scatter_dimension=0, tiled=True),
        lax.psum_scatter(flat_gate, ("batch", "seq"), scatter_dimension=0, tiled=True),
        lax.psum_scatter(flat_up, ("batch", "seq"), scatter_dimension=0, tiled=True),
        lax.psum_scatter(flat_down, ("batch", "seq"), scatter_dimension=0, tiled=True),
    )
    summed = (
        lax.all_gather(shares[0], ("batch", "seq"), axis=0, tiled=True),
        lax.all_gather(shares[1], ("batch", "seq"), axis=0, tiled=True),
        lax.all_gather(shares[2], ("batch", "seq"), axis=0, tiled=True),
        lax.all_gather(shares[3], ("batch", "seq"), axis=0, tiled=True),
        lax.all_gather(shares[4], ("batch", "seq"), axis=0, tiled=True),
        lax.all_gather(shares[5], ("batch", "seq"), axis=0, tiled=True),
        lax.all_gather(shares[6], ("batch", "seq"), axis=0, tiled=True),
    )
    sum_norm, sum_ff, sum_table = lax.psum((d_norm_gain, d_ff_gain, table_part), ("batch", "seq"))
    return (
        layer_output,
        input_grad,
        sum_norm,
        summed[0].reshape(w_query.shape),
        summed[1].reshape(w_key.shape),
        summed[2].reshape(w_value.shape),
        summed[3].reshape(w_out.shape),
        sum_ff,
        summed[4].reshape(w_gate.shape),
        summed[5].reshape(w_up.shape),
        summed[6].reshape(w_down.shape),
        sum_table,
    )


def all_pairs(mesh_batch, mesh_seq, move):
    pairs = []
    for batch in range(mesh_batch):
        for seq in range(mesh_seq):
            z, y, core, x = move(batch // 4, batch // 2 % 2, batch % 2, seq)
            pairs.append((batch * mesh_seq + seq, (z * 4 + y * 2 + core) * mesh_seq + x))
    return pairs


def add_up(parts):
    total = parts[0].astype(f32)
    for part in parts[1:]:
        total = total + part.astype(f32)
    return total


class Links:
    def __init__(self, batch, seq):
        self.axes = ("batch", "seq")
        self.deep = batch // 4
        me = lax.axis_index("batch")
        self.z, self.y, self.core = me // 4, me // 2 % 2, me % 2
        self.x = lax.axis_index("seq")
        self.plane = self.y * 2 + self.x
        pairs = functools.partial(all_pairs, batch, seq)
        self.to_core = pairs(lambda z, y, c, x: (z, y, 1 - c, x))
        self.to_plane = {
            k: pairs(lambda z, y, c, x, k=k: (z, y ^ (k >> 1), c, x ^ (k & 1))) for k in (1, 2, 3)
        }
        self.to_deep = {
            k: pairs(lambda z, y, c, x, k=k: ((z + k) % self.deep, y, c, x))
            for k in range(1, self.deep)
        }

    def send(self, value, pairs):
        return lax.ppermute(value, self.axes, pairs)

    def pick(self, value, at):
        return lax.dynamic_index_in_dim(value, at, 0, keepdims=False)

    def scatter_core(self, grads, deps=()):
        rows, columns = grads.shape
        shape = (4, self.deep, rows // (8 * self.deep), columns)
        got = self.send(pick_half(grads, 1 - self.core, deps), self.to_core)
        own = self.pick(grads.reshape(2, *shape), self.core)
        return add_up([own, got.reshape(shape)]).astype(bf16)

    def scatter_plane(self, part):
        got = [self.send(self.pick(part, self.plane ^ k), self.to_plane[k]) for k in (1, 2, 3)]
        return add_up([self.pick(part, self.plane), *got]).astype(bf16)

    def scatter_pair(self, part, bit):
        at = self.y if bit else self.x
        got = self.send(self.pick(part, 1 - at), self.to_plane[1 + bit])
        return add_up([self.pick(part, at), got]).astype(bf16)

    def scatter_deep(self, part):
        got = [
            self.send(self.pick(part, (self.z + k) % self.deep), self.to_deep[k])
            for k in range(1, self.deep)
        ]
        return add_up([self.pick(part, self.z), *got]).astype(bf16)

    def lay(self, count, at, own, got):
        out = jnp.zeros((count,) + own.shape, own.dtype)
        out = lax.dynamic_update_index_in_dim(out, own, at, 0)
        for place, piece in got:
            out = lax.dynamic_update_index_in_dim(out, piece, place, 0)
        return out

    def gather_deep(self, part):
        got = [
            ((self.z - k) % self.deep, self.send(part, self.to_deep[k]))
            for k in range(1, self.deep)
        ]
        return self.lay(self.deep, self.z, part, got)

    def gather_plane(self, part, deps):
        got = [(self.plane ^ k, self.send(part, self.to_plane[k])) for k in (1, 2, 3)]
        return self.lay(4, self.plane, hold(part, deps), got)


def rows_device(
    batch,
    seq,
    inputs,
    lengths,
    cotangent,
    norm_gain,
    w_query,
    w_key,
    w_value,
    w_out,
    ff_gain,
    w_gate,
    w_up,
    w_down,
    bias_table,
):
    rows, half, width = inputs.shape
    buckets, heads = bias_table.shape
    mine_count = rows // 2
    links = Links(batch, seq)
    places = split_rows(lengths, links.x)
    swap = [(0, 1), (1, 0)]

    x_parts, tick = [], ()
    for row in range(mine_count):
        x_parts.append(lax.ppermute(pick_rows(places, row, 1, inputs, tick), "seq", swap))
        tick = (links.send(tick[0] if tick else places.astype(f32), links.to_core),)
    g_remote = lax.ppermute(pick_rows(places, 0, mine_count, cotangent, tick), "seq", swap)
    near, near_t, far = bias_pieces(bias_table, 2 * half // LANE)
    gain = norm_gain.reshape(1, width)
    gain2 = ff_gain.reshape(1, width)
    held = []
    for row in range(mine_count):
        held = fwd_row(
            places, inputs, x_parts[row], row, mine_count, held,
            gain, w_query, w_key, w_value, near, far, heads,
        )
    q, k, v, mix, tail, normt, x_remote = held
    ff_args = (
        places, inputs, x_remote, cotangent, g_remote, mix,
        w_out, gain2, w_gate, w_up, w_down,
    )
    lo, lo_send, dh, dmix, ff_grads, ff_gain_part = feed_forward(*ff_args)
    ff_total = lax.psum(ff_grads, ("batch", "seq"))
    quads = q.shape[1]
    lo_got = lax.ppermute(lo_send, "seq", swap)
    dw, backs, token = [], [], ()
    for quad in range(quads):
        if quad == quads - 1:
            layer_output, placed = place_rows(places, 0, lo_got, lo)
            token = (placed,)
        *back, dw_quad = bwd_quad(
            places, quad, dw, q, k, v, mix, dmix, tail, near_t, normt, token
        )
        backs.append(back)
        dw = [dw_quad]
    dq, dk, dv, tacc, far_sum = zip(*backs)
    qkv = links.scatter_core(dw[0])
    ig, ig_got, gain_parts, token = [], [], [], ()
    for row in range(mine_count):
        *ig, sent, gain_part = input_back(
            places, row, ig, inputs, x_parts[row], dh, dq, dk, dv,
            gain, w_query, w_key, w_value, token,
        )
        gain_parts.append(gain_part)
        if row == 0:
            token = (qkv,)
            qkv = links.scatter_plane(qkv)
            first_sent = sent
        else:
            ig_got.append((row, lax.ppermute(sent, "seq", swap)))
    qkv = hold(qkv, (gain_parts[-1],))
    ig_got.append((0, lax.ppermute(hold(first_sent, (qkv,)), "seq", swap)))
    table_part = table_sums(table_diagonals(tacc, (qkv,)), jnp.stack(far_sum), buckets)
    small = jnp.concatenate(
        [sum(gain_parts)[0], ff_gain_part[0], table_part.reshape(-1)]
    )
    qkv = hold(links.scatter_deep(qkv), (table_part,))
    input_grad, placed = place_rows(places, *ig_got[0], ig[0], (qkv,))
    held_qkv = qkv
    qkv = links.gather_deep(qkv)
    small = add_up([small, links.send(hold(small, (held_qkv,)), links.to_core)])
    qkv = hold(qkv, (placed, small))
    gate_grad, up_grad, down_grad, out_grad = spread(ff_total, (qkv,))
    qkv_ready = qkv
    qkv = links.gather_plane(qkv, (out_grad,))
    small = hold(small, (qkv_ready,))
    small = add_up([small, *[links.send(small, p) for p in links.to_plane.values()]])
    for got in ig_got[1:-1]:
        input_grad, placed = place_rows(places, *got, input_grad, (), 1)
    qkv = hold(qkv, (placed, small))
    input_grad, _ = place_rows(places, *ig_got[-1], input_grad, (qkv,))
    small = hold(small, (qkv,))
    qkv = qkv.reshape(-1, qkv.shape[-1])
    arrived = links.send(qkv, links.to_core)
    mine_grads = unpack(qkv, links.core)
    query_grad, key_grad, value_grad = unpack(arrived, 1 - links.core, mine_grads)
    small = add_up([small, *[links.send(small, p) for p in links.to_deep.values()]])

    return (
        layer_output,
        input_grad,
        small[:width],
        query_grad,
        key_grad,
        value_grad,
        out_grad,
        small[width : 2 * width],
        gate_grad,
        up_grad,
        down_grad,
        small[2 * width :].reshape(buckets, heads),
    )


def solution(mesh):
    split = P("batch", "seq", None)
    in_specs = (split, P("batch", None), split) + (P(),) * 10
    out_specs = (split, split) + (P(),) * 10
    batch, seq = mesh.shape["batch"], mesh.shape["seq"]

    def per_device(inputs, *rest):
        rows, half, width = inputs.shape
        buckets, heads = rest[-1].shape
        inner = rest[3].shape[1]
        fits = seq == 2 and batch % 4 == 0 and rows % 2 == 0 and rows >= 4 and buckets == 32
        fits = fits and half % STEP == 0 and 2 * half // LANE <= 8
        fits = fits and inner == width and width % (16 * batch) == 0 and inner // heads == LANE // 2
        if fits:
            return rows_device(batch, seq, inputs, *rest)
        return gathered_device(inputs, *rest)

    return jax.shard_map(
        per_device, mesh=mesh, in_specs=in_specs, out_specs=out_specs, check_vma=False
    )
```

```python
import functools
import itertools
import math

import jax
import jax.numpy as jnp
from jax import lax
from jax.experimental import pallas as pl
from jax.experimental.pallas import tpu as pltpu
from jax.sharding import PartitionSpec as P

f32 = jnp.float32
bf16 = jnp.bfloat16
epsilon = 1e-06
masked_score = -2e30
start_max = -1e30
bucket_bounds = (12, 16, 23, 32, 46, 64, 91)
LANE = 128
STEP = 256
NT = (((1,), (1,)), ((), ()))
NN = (((1,), (0,)), ((), ()))
TN = (((0,), (0,)), ((), ()))


def mm(a, b, dims=NN):
    return lax.dot_general(a, b, dims, preferred_element_type=f32)


def cost(micros):
    return pl.CostEstimate(flops=int(micros * 0.3e9), bytes_accessed=0, transcendentals=0)


def params(grid_dims, mib):
    return pltpu.CompilerParams(
        dimension_semantics=("arbitrary",) * grid_dims, vmem_limit_bytes=mib << 20
    )


def bucket_of(offset, bucket_count):
    distance = jnp.abs(offset)
    far = jnp.full_like(distance, 8)
    for bound in bucket_bounds:
        far = far + (distance >= bound).astype(jnp.int32)
    half = bucket_count // 2
    return jnp.where(offset > 0, half, 0) + jnp.where(distance < 8, distance, far)


def split_body(choices, side, lengths, out):
    rows = lengths.shape[1]
    count = rows // 2
    load = [(lengths[0, r] + STEP - 1) // STEP for r in range(rows)]
    best = None
    for own in choices:
        other = [r for r in range(rows) if r not in own]
        uneven = jnp.abs(sum(load[r] for r in own) - sum(load[r] for r in other))
        new = [*own, *other]
        if best is None:
            best, picked = uneven, [jnp.int32(r) for r in new]
        else:
            better = uneven < best
            best = jnp.where(better, uneven, best)
            picked = [jnp.where(better, r, old) for r, old in zip(new, picked)]
    first = side[0] == 0
    out[0] = side[0]
    for n in range(count):
        mine = jnp.where(first, picked[n], picked[count + n])
        out[1 + n] = mine
        out[1 + count + n] = jnp.where(first, picked[count + n], picked[n])
        out[1 + 2 * count + n] = lengths[0, mine]


def split_rows(lengths, side):
    rows = lengths.shape[1]
    choices = [c for c in itertools.combinations(range(rows), rows // 2) if 0 in c]
    smem = pl.BlockSpec(memory_space=pltpu.SMEM)
    return pl.pallas_call(
        functools.partial(split_body, choices),
        in_specs=[smem, smem],
        out_specs=smem,
        out_shape=jax.ShapeDtypeStruct((1 + 3 * (rows // 2),), jnp.int32),
        name="split_rows",
    )(side.reshape(1), lengths)


def near_body(vec_ref, rev_ref, near_ref, near_t_ref):
    wide = jnp.broadcast_to(vec_ref[0], (LANE, 4 * LANE))
    near_ref[0] = pltpu.roll(wide, 0, 1, stride=1, stride_axis=0)[:, : 3 * LANE]
    tall = jnp.broadcast_to(rev_ref[0], (3 * LANE, 4 * LANE))
    near_t_ref[0] = pltpu.roll(tall, 0, 1, stride=1, stride_axis=0)[:, :LANE]


def near_offsets():
    place = jnp.arange(4 * LANE, dtype=jnp.int32)
    signed = jnp.where(place < 3 * LANE, place, place - 4 * LANE)
    forward = signed - LANE
    back = jnp.where(place < LANE, place, place - 4 * LANE)
    reverse = -back - LANE
    return forward, reverse


def bias_pieces(bias_table, tile_count):
    buckets, heads = bias_table.shape
    table = bias_table.astype(f32)
    forward, reverse = near_offsets()

    def spread(offset):
        hot = bucket_of(offset, buckets)[:, None] == jnp.arange(buckets, dtype=jnp.int32)
        picked = jnp.einsum("rb,bh->hr", hot.astype(f32), table, precision=lax.Precision.HIGHEST)
        return picked[:, None, :]

    near, near_t = pl.pallas_call(
        near_body,
        grid=(heads,),
        in_specs=[pl.BlockSpec((1, 1, 4 * LANE), lambda h: (h, 0, 0))] * 2,
        out_specs=[
            pl.BlockSpec((1, LANE, 3 * LANE), lambda h: (h, 0, 0)),
            pl.BlockSpec((1, 3 * LANE, LANE), lambda h: (h, 0, 0)),
        ],
        out_shape=[
            jax.ShapeDtypeStruct((heads, LANE, 3 * LANE), f32),
            jax.ShapeDtypeStruct((heads, 3 * LANE, LANE), f32),
        ],
        name="near_bias",
    )(spread(forward), spread(reverse))
    left = table[buckets // 2 - 1]
    right = table[buckets - 1]
    tile = jnp.arange(tile_count, dtype=jnp.int32)[None, :, None]
    lane = jnp.arange(LANE, dtype=jnp.int32)[None, None, :]
    far = jnp.where(lane == tile, left[:, None, None], 0.0)
    far = far + jnp.where(lane == tile + 8, right[:, None, None], 0.0)
    far = far + jnp.where(lane == 16, masked_score, 0.0)
    return near, near_t, far.astype(bf16)


def key_lanes(extent, length):
    key = lax.broadcasted_iota(jnp.int32, (extent, LANE), 0)
    lane = lax.broadcasted_iota(jnp.int32, (extent, LANE), 1)
    tile = key // LANE
    flag = (lane < 8) & (tile < lane - 1)
    flag = flag | ((lane >= 8) & (lane < 16) & (tile > lane - 8 + 1))
    flag = flag | ((lane == 16) & (key >= length))
    flag = flag | ((lane >= 17) & (lane < 20))
    return jnp.where(flag, 1.0, 0.0).astype(bf16)


def rms_of(values):
    scale = lax.rsqrt(jnp.mean(values * values, axis=-1, keepdims=True) + epsilon)
    return scale


def head_mask(rows, head):
    lane = lax.broadcasted_iota(jnp.int32, (rows, LANE), 1)
    return (lane // (LANE // 2)) == head


def fwd_body(held, count, which, scal, xl, xr, gain, wq, wk, wv, near, far, *rest):
    q_out, k_out, v_out, mix_out, tail_out, normt_out, x_out, normed, lanes = rest[held:]
    extent = normed.shape[0]
    half = xl.shape[1]
    length = scal[1 + 2 * count + which]
    side = scal[0]
    steps = (length + STEP - 1) // STEP

    @pl.when(pl.program_id(0) == 0)
    def _():
        for ref, own in ((xl, True), (xr, False)):
            values = ref[0].astype(f32)
            out = values * rms_of(values) * gain[...].astype(f32)
            place = side * half if own else (1 - side) * half
            normed[pl.ds(pl.multiple_of(place, half), half), :] = out.astype(bf16)
        lanes[...] = key_lanes(extent, length)
        normt_out[0] = normed[...].T
        x_out[...] = xr[...]

    q_out[0, 0] = mm(normed[...], wq[...]).astype(bf16)
    for part in range(extent // STEP):
        rows = pl.ds(part * STEP, STEP)

        @pl.when(part < steps)
        def _():
            k_out[0, 0, rows, :] = mm(normed[rows, :], wk[...]).astype(bf16)
            v_out[0, 0, rows, :] = mm(normed[rows, :], wv[...]).astype(bf16)

        @pl.when(part >= steps)
        def _():
            k_out[0, 0, rows, :] = jnp.zeros((STEP, 2 * LANE), bf16)
            v_out[0, 0, rows, :] = jnp.zeros((STEP, 2 * LANE), bf16)

    def attend(width):
        def pair_step(pair, carry):
            cols = pl.ds(pl.multiple_of(pair * LANE, LANE), LANE)
            kext = jnp.concatenate([k_out[0, 0, :width, cols], lanes[:width, :]], axis=1)
            vext = jnp.concatenate(
                [v_out[0, 0, :width, cols], jnp.ones((width, LANE), bf16)], axis=1
            )
            lane = lax.broadcasted_iota(jnp.int32, (STEP, LANE), 1)
            for block in range(extent // STEP):
                rows = slice(block * STEP, (block + 1) * STEP)
                qpair = q_out[0, 0, rows, cols]
                outs = []
                for head in range(2):
                    index = 2 * pair + head
                    tiles = []
                    for sub in range(STEP // LANE):
                        line = far[index, pl.ds(block * (STEP // LANE) + sub, 1), :]
                        tiles.append(jnp.broadcast_to(line, (LANE, LANE)))
                    ext = jnp.concatenate(tiles, axis=0)
                    qm = jnp.where(head_mask(STEP, head), qpair, jnp.zeros_like(qpair))
                    scores = mm(jnp.concatenate([qm, ext], axis=1), kext, NT)
                    probs = []
                    tops = []
                    for sub in range(STEP // LANE):
                        tile = block * (STEP // LANE) + sub
                        own = scores[sub * LANE : (sub + 1) * LANE]
                        base = (tile - 1) * LANE
                        low, high = max(0, base), min(width, base + 3 * LANE)
                        if low < high:
                            add = own[:, low:high] + near[index, :, low - base : high - base]
                            pieces = [own[:, :low]] if low > 0 else []
                            pieces.append(add)
                            if high < width:
                                pieces.append(own[:, high:])
                            own = jnp.concatenate(pieces, axis=1)
                        top = jnp.max(own, axis=1, keepdims=True)
                        probs.append(jnp.exp(own - top).astype(bf16))
                        tops.append(top)
                    both = mm(jnp.concatenate(probs, axis=0), vext)
                    total = both[:, LANE:]
                    outs.append(both[:, :LANE] / total)
                    neg = -(jnp.concatenate(tops, axis=0) + jnp.log(total))
                    first = neg.astype(bf16)
                    rest = neg - first.astype(f32)
                    second = rest.astype(bf16)
                    third = (rest - second.astype(f32)).astype(bf16)
                    line = jnp.where(lane == 17, first, ext)
                    line = jnp.where(lane == 18, second, line)
                    line = jnp.where(lane == 19, third, line)
                    tail_out[0, index, rows, :] = line
                picked = jnp.where(head_mask(STEP, 0), outs[0], outs[1])
                mix_out[0, 0, rows, cols] = picked.astype(bf16)
            return carry

        lax.fori_loop(0, 2, pair_step, 0)

    for blocks in range(1, extent // STEP + 1):

        @pl.when(steps == blocks)
        def _():
            attend(blocks * STEP)


def fwd_row(scal, inputs, remote, which, count, held, gain, wq, wk, wv, near, far, heads):
    rows, half, width = inputs.shape
    extent = 2 * half
    inner = wq.shape[1]
    quads = inner // STEP
    per = heads // quads
    weight = pl.BlockSpec((width, STEP), lambda i, s: (0, i))
    block = pl.BlockSpec((1, 1, extent, STEP), lambda i, s: (which, i, 0, 0))
    grid_spec = pltpu.PrefetchScalarGridSpec(
        num_scalar_prefetch=1,
        grid=(quads,),
        in_specs=[
            pl.BlockSpec((1, half, width), lambda i, s: (s[1 + which], 0, 0)),
            pl.BlockSpec((1, half, width), lambda i, s: (0, 0, 0)),
            pl.BlockSpec((1, width), lambda i, s: (0, 0)),
            weight,
            weight,
            weight,
            pl.BlockSpec((per, LANE, 3 * LANE), lambda i, s: (i, 0, 0)),
            pl.BlockSpec((per, 8, LANE), lambda i, s: (i, 0, 0)),
        ]
        + [pl.BlockSpec(memory_space=pl.ANY)] * len(held),
        out_specs=[block] * 4
        + [
            pl.BlockSpec((1, per, extent, LANE), lambda i, s: (which, i, 0, 0)),
            pl.BlockSpec((1, width, extent), lambda i, s: (which, 0, 0)),
            pl.BlockSpec((1, half, width), lambda i, s: (which, 0, 0)),
        ],
        scratch_shapes=[pltpu.VMEM((extent, width), bf16), pltpu.VMEM((extent, LANE), bf16)],
    )
    stacked = jax.ShapeDtypeStruct((count, quads, extent, STEP), bf16)
    return pl.pallas_call(
        functools.partial(fwd_body, len(held), count, which),
        grid_spec=grid_spec,
        out_shape=[stacked] * 4
        + [
            jax.ShapeDtypeStruct((count, heads, extent, LANE), bf16),
            jax.ShapeDtypeStruct((count, width, extent), bf16),
            jax.ShapeDtypeStruct((count, half, width), bf16),
        ],
        input_output_aliases={9 + n: n for n in range(len(held))},
        compiler_params=params(1, 56),
        cost_estimate=cost(60),
        name="attend_row",
    )(scal, inputs, remote, gain, wq, wk, wv, near, far, *held)


def bwd_body(
    count, scal, q, k, v, mix, dmix, tail, near_t, normt, *rest
):
    (dq_out, dk_out, dv_out, tacc_out, far_out, dw_out) = rest[-15:-9]
    (lanes, pl_s, ds_s, do_s, qa_s, dwq, dwk, dwv, _) = rest[-9:]
    extent = lanes.shape[0]
    row = pl.program_id(0)
    length = scal[1 + 2 * count + row]
    steps = (length + STEP - 1) // STEP
    lanes[...] = key_lanes(extent, length)

    @pl.when(row == 0)
    def _():
        for ref in (tacc_out, far_out, dwq, dwk, dwv):
            ref[...] = jnp.zeros(ref.shape, f32)

    dk_out[...] = jnp.zeros(dk_out.shape, bf16)
    dv_out[...] = jnp.zeros(dv_out.shape, bf16)

    def attend(width):
        def head_step(index, carry):
            pair = index // 2
            head = lax.rem(index, 2)
            cols = pl.ds(pl.multiple_of(pair * LANE, LANE), LANE)
            flags = lanes[:width, :]
            kpair = k[0, 0, :width, cols]
            kext = jnp.concatenate([kpair, flags], axis=1)
            vext = jnp.concatenate([v[0, 0, :width, cols], flags], axis=1)
            lane = lax.broadcasted_iota(jnp.int32, (STEP, LANE), 1)
            mask = head_mask(STEP, head)
            for block in range(extent // STEP):
                rows = slice(block * STEP, (block + 1) * STEP)
                qpair = q[0, 0, rows, cols]
                dopair = dmix[0, 0, rows, cols]
                product = dopair.astype(f32) * mix[0, 0, rows, cols].astype(f32)
                qm = jnp.where(mask, qpair, jnp.zeros_like(qpair))
                dom = jnp.where(mask, dopair, jnp.zeros_like(dopair))
                neg = -jnp.sum(jnp.where(mask, product, 0.0), axis=1, keepdims=True)
                neg = jnp.broadcast_to(neg, (STEP, LANE))
                first = neg.astype(bf16)
                rest = neg - first.astype(f32)
                second = rest.astype(bf16)
                third = (rest - second.astype(f32)).astype(bf16)
                dtail = jnp.where(lane == 17, first, jnp.zeros((STEP, LANE), bf16))
                dtail = jnp.where(lane == 18, second, dtail)
                dtail = jnp.where(lane == 19, third, dtail)
                st = mm(kext, jnp.concatenate([qm, tail[0, index, rows, :]], axis=1), NT)
                dp = mm(vext, jnp.concatenate([dom, dtail], axis=1), NT)
                do_s[rows, :] = dom
                row_at = lax.broadcasted_iota(jnp.int32, (STEP, LANE), 0)
                spot = jnp.where(lane == block * (STEP // LANE) + row_at // LANE, 1.0, 0.0)
                qa_s[rows, :] = jnp.concatenate([qm, spot.astype(bf16)], axis=1)
                for sub in range(STEP // LANE):
                    tile = block * (STEP // LANE) + sub
                    part = slice(sub * LANE, (sub + 1) * LANE)
                    own = st[:, part]
                    base = (tile - 1) * LANE
                    low, high = max(0, base), min(width, base + 3 * LANE)
                    if low < high:
                        add = own[low:high] + near_t[index, low - base : high - base, :]
                        pieces = [own[:low]] if low > 0 else []
                        pieces.append(add)
                        if high < width:
                            pieces.append(own[high:])
                        own = jnp.concatenate(pieces, axis=0)
                    prob = jnp.exp(own)
                    dst = (prob * dp[:, part]).astype(bf16)
                    place = slice(tile * LANE, (tile + 1) * LANE)
                    pl_s[:width, place] = prob.astype(bf16)
                    ds_s[:width, place] = dst
                    if low < high:
                        tacc_out[index, low - base : high - base, :] += dst[low:high].astype(f32)
            kmask = head_mask(width, head)
            dv = mm(pl_s[:width, :], do_s[...]).astype(bf16)
            dv_out[0, :width, cols] = jnp.where(kmask, dv, dv_out[0, :width, cols])
            dk = mm(ds_s[:width, :], qa_s[...])
            dk_out[0, :width, cols] = jnp.where(
                kmask, dk[:, :LANE].astype(bf16), dk_out[0, :width, cols]
            )
            tile = lax.broadcasted_iota(jnp.int32, (width, LANE), 0) // LANE
            spread = lax.broadcasted_iota(jnp.int32, (width, LANE), 1)
            left = jnp.where((tile < spread - 1) & (spread < 8), dk[:, LANE:], 0.0)
            right = jnp.where((tile > spread + 1) & (spread < 8), dk[:, LANE:], 0.0)
            far_out[pl.ds(index, 1), :] += jnp.sum(left, axis=0, keepdims=True)
            far_out[pl.ds(4 + index, 1), :] += jnp.sum(right, axis=0, keepdims=True)
            dq = mm(ds_s[:width, :], jnp.where(kmask, kpair, jnp.zeros_like(kpair)), TN)
            qmask = head_mask(extent, head)
            dq_out[0, :, cols] = jnp.where(qmask, dq.astype(bf16), dq_out[0, :, cols])
            return carry

        lax.fori_loop(0, 4, head_step, 0)
        dwk[...] += mm(normt[0, :, :width], dk_out[0, :width, :])
        dwv[...] += mm(normt[0, :, :width], dv_out[0, :width, :])

    for blocks in range(1, extent // STEP + 1):

        @pl.when(steps == blocks)
        def _():
            attend(blocks * STEP)

    dwq[...] += mm(normt[0], dq_out[0])

    @pl.when(row == count - 1)
    def _():
        for n, ref in enumerate((dwq, dwk, dwv)):
            dw_out[:, n * STEP : (n + 1) * STEP] = ref[...].astype(bf16)


def bwd_quad(places, quad, held, q, k, v, mix, dmix, tail, near_t, normt, deps=()):
    count, quads, extent, _ = q.shape
    heads = tail.shape[1]
    width = normt.shape[1]
    per = heads // quads
    block = pl.BlockSpec((1, 1, extent, STEP), lambda i, s: (i, quad, 0, 0))
    given = pl.BlockSpec((1, extent, STEP), lambda i, s: (i, 0, 0))
    grid_spec = pltpu.PrefetchScalarGridSpec(
        num_scalar_prefetch=1,
        grid=(count,),
        in_specs=[block] * 5
        + [
            pl.BlockSpec((1, per, extent, LANE), lambda i, s: (i, quad, 0, 0)),
            pl.BlockSpec((per, 3 * LANE, LANE), lambda i, s: (quad, 0, 0)),
            pl.BlockSpec((1, width, extent), lambda i, s: (i, 0, 0)),
        ]
        + [pl.BlockSpec(memory_space=pl.ANY)] * (len(held) + len(deps)),
        out_specs=[given] * 3
        + [
            pl.BlockSpec((per, 3 * LANE, LANE), lambda i, s: (0, 0, 0)),
            pl.BlockSpec((8, LANE), lambda i, s: (0, 0)),
            pl.BlockSpec((width, 3 * STEP), lambda i, s: (0, quad)),
        ],
        scratch_shapes=[
            pltpu.VMEM((extent, LANE), bf16),
            pltpu.VMEM((extent, extent), bf16),
            pltpu.VMEM((extent, extent), bf16),
            pltpu.VMEM((extent, LANE), bf16),
            pltpu.VMEM((extent, 2 * LANE), bf16),
        ]
        + [pltpu.VMEM((width, STEP), f32)] * 3
        + [pltpu.VMEM((8, LANE), f32)],
    )
    out = jax.ShapeDtypeStruct((count, extent, STEP), bf16)
    return pl.pallas_call(
        functools.partial(bwd_body, count),
        grid_spec=grid_spec,
        out_shape=[out] * 3
        + [
            jax.ShapeDtypeStruct((per, 3 * LANE, LANE), f32),
            jax.ShapeDtypeStruct((8, LANE), f32),
            jax.ShapeDtypeStruct((width, 3 * STEP * quads), bf16),
        ],
        input_output_aliases={9: 5} if held else {},
        compiler_params=params(1, 60),
        cost_estimate=cost(1),
        name="attend_back",
    )(places, q, k, v, mix, dmix, tail, near_t, normt, *held, *deps)


def table_body(quads, *rest):
    out = rest[-1]
    for quad in range(quads):
        tacc = rest[quad]
        total = jnp.zeros((8, 4 * LANE), f32)
        for group in range(3 * LANE // 8):
            part = tacc[0, group * 8 : (group + 1) * 8, :]
            wide = jnp.concatenate([part, jnp.zeros((8, 3 * LANE), f32)], axis=1)
            total = total + (pltpu.roll(wide, 4 * LANE - 8 * group, 1) if group else wide)
        line = total[0:1]
        for row in range(1, 8):
            line = line + pltpu.roll(total[row : row + 1], 4 * LANE - row, 1)
        out[quad, 0] = line


def table_diagonals(tacc, deps=()):
    quads, per = len(tacc), tacc[0].shape[0]
    return pl.pallas_call(
        functools.partial(table_body, quads),
        grid=(per,),
        in_specs=[pl.BlockSpec((1, 3 * LANE, LANE), lambda h: (h, 0, 0))] * quads
        + [pl.BlockSpec(memory_space=pl.ANY)] * len(deps),
        out_specs=pl.BlockSpec((quads, 1, 1, 4 * LANE), lambda h: (0, h, 0, 0)),
        out_shape=jax.ShapeDtypeStruct((quads, per, 1, 4 * LANE), f32),
        cost_estimate=cost(100),
        name="table_diagonals",
    )(*tacc, *deps)


def table_sums(diagonals, far_sum, buckets):
    heads = diagonals.shape[0] * diagonals.shape[1]
    diagonals = diagonals.reshape(heads, 1, 4 * LANE)
    place = jnp.arange(4 * LANE, dtype=jnp.int32)
    back = jnp.where(place < LANE, place, place - 4 * LANE)
    hot = bucket_of(-back - LANE, buckets)[:, None] == jnp.arange(buckets, dtype=jnp.int32)
    near = jnp.einsum(
        "rb,hr->bh", hot.astype(f32), diagonals[:, 0, :], precision=lax.Precision.HIGHEST
    )
    sides = jnp.sum(far_sum, axis=2).reshape(-1, 2, 4)
    sides = jnp.transpose(sides, (1, 0, 2)).reshape(2, heads)
    half = buckets // 2
    near = near.at[half - 1].add(sides[0])
    return near.at[buckets - 1].add(sides[1])


CHUNK = 512
GELU_K = math.sqrt(2.0 / math.pi)


def gated(normed, g, w_gate, w_up, w_down):
    gate = mm(normed, w_gate)
    up = mm(normed, w_up)
    d_act = mm(g, w_down, NT)
    square = gate * gate
    th = jnp.tanh(gate * (GELU_K + (GELU_K * 0.044715) * square))
    half = 0.5 + 0.5 * th
    gelu = gate * half
    slope = half + (0.5 * gate) * (1.0 - th * th) * (GELU_K + (3.0 * 0.044715 * GELU_K) * square)
    return (
        (gelu * up).astype(bf16),
        (d_act * up * slope).astype(bf16),
        (d_act * gelu).astype(bf16),
    )


def ff_body(
    scal, xl, xr, gl, gr, mix, w_out, gain, gate_any, up_any, down_any,
    lo_out, lo_send, dh_out, dmix_out, dw_out, dgain_out,
    dwo, dwg, dwu, dwd, w_gate, w_up, w_down, sems,
):
    step = pl.program_id(0)
    last = pl.num_programs(0) - 1
    own = lax.rem(step, 2) == 0
    units = w_gate.shape[1]
    loads = [
        pltpu.make_async_copy(source, target, sems.at[n])
        for n, (source, target) in enumerate(
            ((gate_any, w_gate), (up_any, w_up), (down_any, w_down))
        )
    ]

    @pl.when(step == 0)
    def _():
        for load in loads:
            load.start()
        for ref in (dwo, dwg, dwu, dwd, dgain_out):
            ref[...] = jnp.zeros(ref.shape, f32)

    g = jnp.where(own, gl[0], gr[0])
    x = jnp.where(own, xl[0], xr[0]).astype(f32)
    quads = mix.shape[1]
    mixed = jnp.concatenate([mix[0, i] for i in range(quads)], axis=1)
    hidden = x + mm(mixed, w_out[...])
    gain_f = gain[...].astype(f32)
    scale = rms_of(hidden)
    unit = hidden * scale
    normed = (unit * gain_f).astype(bf16)
    normed_t = normed.T
    g_t = g.T
    out = hidden
    dn = jnp.zeros_like(hidden)

    @pl.when(step == 0)
    def _():
        for load in loads:
            load.wait()

    for c in range(units // CHUNK):
        cols = slice(c * CHUNK, (c + 1) * CHUNK)
        act, d_gate, d_up = gated(normed, g, w_gate[:, cols], w_up[:, cols], w_down[cols, :])
        out = out + mm(act, w_down[cols, :])
        dn = dn + mm(d_gate, w_gate[:, cols], NT) + mm(d_up, w_up[:, cols], NT)
        dwd[:, cols] += mm(g_t, act)
        dwg[:, cols] += mm(normed_t, d_gate)
        dwu[:, cols] += mm(normed_t, d_up)

    @pl.when(own)
    def _():
        lo_out[0] = out

    @pl.when(jnp.logical_not(own))
    def _():
        lo_send[0] = out.astype(bf16)

    dgain_out[...] += jnp.sum(dn * unit, axis=0, keepdims=True)
    e = dn * gain_f
    d_hidden = (
        g.astype(f32) + scale * e - unit * (scale * jnp.mean(unit * e, axis=-1, keepdims=True))
    )
    dh_out[0] = d_hidden
    low = d_hidden.astype(bf16)
    dwo[...] += mm(mixed.T, low)
    d_mixed = mm(low, w_out[...], NT).astype(bf16)
    for i in range(quads):
        dmix_out[0, i] = d_mixed[:, i * STEP : (i + 1) * STEP]

    @pl.when(step == last)
    def _():
        pending = [None, None]
        place = 0
        for n, acc in enumerate((dwg, dwu, dwd, dwo)):
            slot = n % 2
            stage = (w_gate, w_up)[slot]
            if pending[slot] is not None:
                pending[slot].wait()
            cols = acc.shape[1]
            stage[:, :cols] = acc[...].astype(bf16)
            copy = pltpu.make_async_copy(
                stage.at[:, pl.ds(0, cols)], dw_out.at[:, pl.ds(place, cols)], sems.at[slot]
            )
            copy.start()
            pending[slot] = copy
            place += cols
        for copy in pending:
            copy.wait()


def feed_forward(places, inputs, x_remote, cot, cot_remote, mix, w_out, gain, w_gate, w_up, w_down):
    rows, half, width = inputs.shape
    mine = x_remote.shape[0]
    _, quads, extent, _ = mix.shape
    units = w_gate.shape[1]
    inner = w_out.shape[0]

    def keep(shape):
        return pl.BlockSpec(shape, lambda i, s: (0,) * len(shape), pipeline_mode=pl.Buffered(1))

    local = pl.BlockSpec((1, half, width), lambda i, s: (s[1 + i // 2], 0, 0))
    far = pl.BlockSpec((1, half, width), lambda i, s: (i // 2, 0, 0))
    far_one = pl.BlockSpec(
        (1, half, width), lambda i, s: (i // 2, 0, 0), pipeline_mode=pl.Buffered(1)
    )
    spot = pl.BlockSpec(
        (1, quads, half, STEP),
        lambda i, s: (i // 2, 0, jnp.where(i % 2 == 0, s[0], 1 - s[0]), 0),
    )
    tile = pl.BlockSpec((1, half, width), lambda i, s: (i, 0, 0))
    anywhere = pl.BlockSpec(memory_space=pl.ANY)
    grid_spec = pltpu.PrefetchScalarGridSpec(
        num_scalar_prefetch=1,
        grid=(2 * mine,),
        in_specs=[local, far_one, local, far_one, spot, keep((inner, width)), keep((1, width)),
                  anywhere, anywhere, anywhere],
        out_specs=[local, far, tile, spot, anywhere,
                   pl.BlockSpec((1, width), lambda i, s: (0, 0))],
        scratch_shapes=[pltpu.VMEM((inner, width), f32)]
        + [pltpu.VMEM((width, units), f32)] * 3
        + [
            pltpu.VMEM((width, units), bf16),
            pltpu.VMEM((width, units), bf16),
            pltpu.VMEM((units, width), bf16),
            pltpu.SemaphoreType.DMA((3,)),
        ],
    )
    return pl.pallas_call(
        ff_body,
        grid_spec=grid_spec,
        out_shape=[
            jax.ShapeDtypeStruct((rows, half, width), f32),
            jax.ShapeDtypeStruct((mine, half, width), bf16),
            jax.ShapeDtypeStruct((2 * mine, half, width), f32),
            jax.ShapeDtypeStruct((mine, quads, extent, STEP), bf16),
            jax.ShapeDtypeStruct((width, 3 * units + width), bf16),
            jax.ShapeDtypeStruct((1, width), f32),
        ],
        compiler_params=params(1, 63),
        cost_estimate=cost(150),
        name="feed_forward",
    )(places, inputs, x_remote, cot, cot_remote, mix, w_out, gain, w_gate, w_up, w_down)


def spread_body(sums, *rest):
    gate_out, up_out, down_out, out_out = rest[-4:]
    units = gate_out.shape[1]
    gate_out[...] = sums[:, :units].astype(f32)
    up_out[...] = sums[:, units : 2 * units].astype(f32)
    down_out[...] = sums[:, 2 * units : 3 * units].astype(f32).T
    out_out[...] = sums[:, 3 * units :].astype(f32)


def spread(sums, deps=()):
    width, columns = sums.shape
    units = (columns - width) // 3
    wide = pl.BlockSpec((LANE, units), lambda i: (i, 0))
    return pl.pallas_call(
        spread_body,
        grid=(width // LANE,),
        in_specs=[pl.BlockSpec((LANE, columns), lambda i: (i, 0))]
        + [pl.BlockSpec(memory_space=pl.ANY)] * len(deps),
        out_specs=[
            wide,
            wide,
            pl.BlockSpec((units, LANE), lambda i: (0, i)),
            pl.BlockSpec((LANE, width), lambda i: (i, 0)),
        ],
        out_shape=[
            jax.ShapeDtypeStruct((width, units), f32),
            jax.ShapeDtypeStruct((width, units), f32),
            jax.ShapeDtypeStruct((units, width), f32),
            jax.ShapeDtypeStruct((width, width), f32),
        ],
        compiler_params=params(1, 56),
        cost_estimate=cost(100),
        name="spread",
    )(sums, *deps)


def back_body(quads, held, scal, xl, xr, dh, *rest):
    grads = rest[: 3 * quads]
    gain, wq, wk, wv = rest[3 * quads : 3 * quads + 4]
    ig_out, ig_send, dgain_out = rest[-3:]
    step = pl.program_id(0)
    far = step == 0

    @pl.when(far)
    def _():
        dgain_out[...] = jnp.zeros(dgain_out.shape, f32)

    x = jnp.where(far, xr[0], xl[0]).astype(f32)
    dn = jnp.zeros_like(x)
    for n, weight in enumerate((wq, wk, wv)):
        part = jnp.concatenate([ref[0] for ref in grads[n * quads : (n + 1) * quads]], axis=1)
        dn = dn + mm(part, weight[...], NT)
    scale = rms_of(x)
    unit = x * scale
    dgain_out[...] += jnp.sum(dn * unit, axis=0, keepdims=True)
    e = dn * gain[...].astype(f32)
    out = dh[0] + scale * e - unit * (scale * jnp.mean(unit * e, axis=-1, keepdims=True))

    @pl.when(far)
    def _():
        ig_send[0] = out.astype(bf16)

    @pl.when(jnp.logical_not(far))
    def _():
        ig_out[0] = out


def input_back(places, row, held, inputs, remote, dh, dq, dk, dv, gain, wq, wk, wv, deps=()):
    rows, half, width = inputs.shape
    local = pl.BlockSpec((1, half, width), lambda i, s: (s[1 + row], 0, 0))
    one = pl.BlockSpec((1, half, width), lambda i, s: (0, 0, 0))
    tile = pl.BlockSpec((1, half, width), lambda i, s: (2 * row + 1 - i, 0, 0))
    spot = pl.BlockSpec((1, half, STEP), lambda i, s: (row, jnp.where(i == 1, s[0], 1 - s[0]), 0))
    weight = pl.BlockSpec(wq.shape, lambda i, s: (0, 0), pipeline_mode=pl.Buffered(1))
    line = pl.BlockSpec((1, width), lambda i, s: (0, 0))
    anywhere = pl.BlockSpec(memory_space=pl.ANY)
    grads = [*dq, *dk, *dv]
    grid_spec = pltpu.PrefetchScalarGridSpec(
        num_scalar_prefetch=1,
        grid=(2,),
        in_specs=[local, one, tile]
        + [spot] * len(grads)
        + [line, weight, weight, weight]
        + [anywhere] * (len(held) + len(deps)),
        out_specs=[local, one, line],
    )
    return pl.pallas_call(
        functools.partial(back_body, len(dq), len(held)),
        grid_spec=grid_spec,
        out_shape=[
            jax.ShapeDtypeStruct((rows, half, width), f32),
            jax.ShapeDtypeStruct((1, half, width), bf16),
            jax.ShapeDtypeStruct((1, width), f32),
        ],
        input_output_aliases={8 + len(grads): 0} if held else {},
        compiler_params=params(1, 56),
        cost_estimate=cost(100),
        name="input_back",
    )(places, inputs, remote, dh, *grads, gain, wq, wk, wv, *held, *deps)


def hold_body(value, *rest):
    rest[-1][...] = value[...]


def hold(value, deps):
    return pl.pallas_call(
        hold_body,
        in_specs=[pl.BlockSpec(memory_space=pltpu.VMEM)]
        + [pl.BlockSpec(memory_space=pl.ANY)] * len(deps),
        out_specs=pl.BlockSpec(memory_space=pltpu.VMEM),
        out_shape=jax.ShapeDtypeStruct(value.shape, value.dtype),
        compiler_params=pltpu.CompilerParams(vmem_limit_bytes=16 << 20),
        name="hold",
    )(value, *deps)


def pick_half(grads, at, deps):
    rows, columns = grads.shape
    grid_spec = pltpu.PrefetchScalarGridSpec(
        num_scalar_prefetch=1,
        grid=(1,),
        in_specs=[pl.BlockSpec((rows // 2, columns), lambda i, s: (s[0], 0))]
        + [pl.BlockSpec(memory_space=pl.ANY)] * len(deps),
        out_specs=pl.BlockSpec((rows // 2, columns), lambda i, s: (0, 0)),
    )
    return pl.pallas_call(
        pick_body,
        grid_spec=grid_spec,
        out_shape=jax.ShapeDtypeStruct((rows // 2, columns), grads.dtype),
        compiler_params=params(1, 24),
        name="pick_half",
    )(at.reshape(1), grads, *deps)


def pick_body(scal, array, *rest):
    rest[-1][...] = array[...]


def pick_rows(places, first, count, array, deps=()):
    rows, half, width = array.shape
    grid_spec = pltpu.PrefetchScalarGridSpec(
        num_scalar_prefetch=1,
        grid=(count,),
        in_specs=[pl.BlockSpec((1, half, width), lambda i, s: (s[1 + rows // 2 + first + i], 0, 0))]
        + [pl.BlockSpec(memory_space=pl.ANY)] * len(deps),
        out_specs=pl.BlockSpec((1, half, width), lambda i, s: (i, 0, 0)),
    )
    return pl.pallas_call(
        pick_body,
        grid_spec=grid_spec,
        out_shape=jax.ShapeDtypeStruct((count, half, width), array.dtype),
        compiler_params=params(1, 16),
        name="pick_rows",
    )(places, array, *deps)


def place_body(scal, arrived, *rest):
    out, token = rest[-2:]
    out[0] = arrived[0].astype(f32)
    token[...] = jnp.zeros(token.shape, f32)


def place_rows(places, first, arrived, held, deps=(), weight=100):
    count, half, width = arrived.shape
    at = 1 + held.shape[0] // 2 + first
    anywhere = pl.BlockSpec(memory_space=pl.ANY)
    grid_spec = pltpu.PrefetchScalarGridSpec(
        num_scalar_prefetch=1,
        grid=(count,),
        in_specs=[pl.BlockSpec((1, half, width), lambda i, s: (i, 0, 0)), anywhere]
        + [anywhere] * len(deps),
        out_specs=[
            pl.BlockSpec((1, half, width), lambda i, s: (s[at + i], 0, 0)),
            pl.BlockSpec((8, LANE), lambda i, s: (0, 0)),
        ],
    )
    return pl.pallas_call(
        place_body,
        grid_spec=grid_spec,
        out_shape=[
            jax.ShapeDtypeStruct(held.shape, f32),
            jax.ShapeDtypeStruct((8, LANE), f32),
        ],
        input_output_aliases={2: 0},
        compiler_params=params(1, 32),
        cost_estimate=cost(weight),
        name="place_rows",
    )(places, arrived, held, *deps)


def unpack_body(scal, sums, *rest):
    outs = rest[-3:]
    quads = outs[0].shape[1] // STEP
    for n, out in enumerate(outs):
        for quad in range(quads):
            begin = (3 * quad + n) * STEP
            out[:, quad * STEP : (quad + 1) * STEP] = sums[:, begin : begin + STEP].astype(f32)


def unpack(sums, rows, at, held=(), deps=()):
    columns = sums.shape[1]
    width = columns // 3
    parts = 4
    anywhere = pl.BlockSpec(memory_space=pl.ANY)
    grid_spec = pltpu.PrefetchScalarGridSpec(
        num_scalar_prefetch=1,
        grid=(parts,),
        in_specs=[pl.BlockSpec((rows // parts, columns), lambda i, s: (i, 0))]
        + [anywhere] * (len(held) + len(deps)),
        out_specs=[pl.BlockSpec((rows // parts, width), lambda i, s: (s[0] * parts + i, 0))] * 3,
    )
    return pl.pallas_call(
        unpack_body,
        grid_spec=grid_spec,
        out_shape=[jax.ShapeDtypeStruct((2 * rows, width), f32)] * 3,
        input_output_aliases={2 + n: n for n in range(len(held))},
        compiler_params=params(1, 32),
        cost_estimate=cost(100),
        name="unpack",
    )(at.reshape(1), sums, *held, *deps)


highest = lax.Precision.HIGHEST


def rms_scaled(values, gain):
    mean_square = jnp.mean(values * values, axis=-1, keepdims=True)
    return values * lax.rsqrt(mean_square + epsilon) * gain


def gated_unit(gate, up_proj):
    return jax.nn.gelu(gate, approximate=True) * up_proj


def relative_one_hot(query_anchor, query_extent, key_extent, bucket_count):
    query_place = query_anchor + jnp.arange(query_extent, dtype=jnp.int32)
    key_place = jnp.arange(key_extent, dtype=jnp.int32)
    offset = key_place[None, :] - query_place[:, None]
    distance = jnp.abs(offset)
    far_bucket = jnp.full_like(distance, 8)
    for threshold in bucket_bounds:
        far_bucket = far_bucket + (distance >= threshold).astype(jnp.int32)
    bucket = jnp.where(offset > 0, bucket_count // 2, 0) + jnp.where(
        distance < 8, distance, far_bucket
    )
    return (bucket[:, :, None] == jnp.arange(bucket_count, dtype=jnp.int32)).astype(jnp.float32)


def block_scores(query_heads, key_heads, query_anchor, lengths, bias_f):
    key_extent = key_heads.shape[1]
    one_hot = relative_one_hot(query_anchor, query_heads.shape[1], key_extent, bias_f.shape[0])
    bias_block = jnp.einsum("qkb,bh->hqk", one_hot, bias_f, precision=highest)
    raw_scores = jnp.einsum(
        "rqhd,rkhd->rhqk", query_heads, key_heads, preferred_element_type=jnp.float32
    )
    usable = jnp.arange(key_extent, dtype=jnp.int32)[None, :] < lengths[:, None]
    return (
        jnp.where(usable[:, None, None, :], raw_scores + bias_block[None], masked_score),
        one_hot,
    )


def score_grads(scores, log_total, row_dot, grad_heads, value_heads):
    weights_hp = jnp.exp(scores - log_total[..., None])
    d_weights = jnp.einsum(
        "rqhd,rkhd->rhqk", grad_heads, value_heads, preferred_element_type=jnp.float32
    )
    d_scores = (weights_hp * (d_weights - row_dot[..., None])).astype(jnp.bfloat16)
    return (weights_hp.astype(jnp.bfloat16), d_scores)


def table_term(one_hot, d_scores):
    summed = jnp.sum(d_scores, axis=0, dtype=jnp.float32)
    return jnp.einsum("qkb,hqk->bh", one_hot, summed, precision=highest)


def gathered_device(
    inputs,
    lengths,
    cotangent,
    norm_gain,
    w_query,
    w_key,
    w_value,
    w_out,
    ff_gain,
    w_gate,
    w_up,
    w_down,
    bias_table,
):
    row_count, block_len, model_width = inputs.shape
    head_count = bias_table.shape[1]
    inner_width = w_query.shape[1]
    head_width = inner_width // head_count
    tokens_here = row_count * block_len
    lengths = lengths.reshape(-1)
    bias_f = bias_table.astype(jnp.float32)
    own_anchor = lax.axis_index("seq") * block_len

    def split_heads(block_array):
        return block_array.reshape(row_count, block_array.shape[1], head_count, head_width)

    tokens_f = inputs.astype(jnp.float32).reshape(tokens_here, model_width)
    normed_f, norm_pull = jax.vjp(rms_scaled, tokens_f, norm_gain.astype(jnp.float32))
    normed = normed_f.astype(jnp.bfloat16)
    queries = (
        jnp.dot(normed, w_query, preferred_element_type=jnp.float32)
        .astype(jnp.bfloat16)
        .reshape(row_count, block_len, inner_width)
    )
    keys = (
        jnp.dot(normed, w_key, preferred_element_type=jnp.float32)
        .astype(jnp.bfloat16)
        .reshape(row_count, block_len, inner_width)
    )
    values = (
        jnp.dot(normed, w_value, preferred_element_type=jnp.float32)
        .astype(jnp.bfloat16)
        .reshape(row_count, block_len, inner_width)
    )
    query_heads = split_heads(queries)
    stat_shape = (row_count, head_count, block_len)
    pieces = (
        lax.all_gather(keys, "seq", axis=1, tiled=True),
        lax.all_gather(values, "seq", axis=1, tiled=True),
    )
    row_max = jnp.full(stat_shape, start_max, jnp.float32)
    key_heads = split_heads(pieces[0])
    value_heads = split_heads(pieces[1])
    scores, one_hot = block_scores(query_heads, key_heads, own_anchor, lengths, bias_f)
    new_max = jnp.maximum(row_max, jnp.max(scores, axis=-1))
    weights_hp = jnp.exp(scores - new_max[..., None])
    row_sum = jnp.sum(weights_hp, axis=-1)
    weighted = jnp.einsum(
        "rhqk,rkhd->rhqd",
        weights_hp.astype(jnp.bfloat16),
        value_heads,
        preferred_element_type=jnp.float32,
    )
    row_max, row_sum, weighted = (new_max, row_sum, weighted)
    log_total = row_max + jnp.log(row_sum)
    mixed_heads = jnp.transpose(weighted / row_sum[..., None], (0, 2, 1, 3))
    mixed_low = mixed_heads.reshape(tokens_here, inner_width).astype(jnp.bfloat16)
    hidden = tokens_f + jnp.dot(mixed_low, w_out, preferred_element_type=jnp.float32)
    normed2_f, ff_pull = jax.vjp(rms_scaled, hidden, ff_gain.astype(jnp.float32))
    normed2 = normed2_f.astype(jnp.bfloat16)
    gate = jnp.dot(normed2, w_gate, preferred_element_type=jnp.float32)
    up_proj = jnp.dot(normed2, w_up, preferred_element_type=jnp.float32)
    activated, gated_pull = jax.vjp(gated_unit, gate, up_proj)
    act_low = activated.astype(jnp.bfloat16)
    layer_output = (hidden + jnp.dot(act_low, w_down, preferred_element_type=jnp.float32)).reshape(
        row_count, block_len, model_width
    )
    grad_out = cotangent.reshape(tokens_here, model_width)
    dw_down = jnp.einsum("tf,td->fd", act_low, grad_out, preferred_element_type=jnp.float32)
    d_act = jnp.einsum("td,fd->tf", grad_out, w_down, preferred_element_type=jnp.float32)
    d_gate, d_up = gated_pull(d_act)
    d_gate = d_gate.astype(jnp.bfloat16)
    d_up = d_up.astype(jnp.bfloat16)
    dw_gate = jnp.einsum("td,tf->df", normed2, d_gate, preferred_element_type=jnp.float32)
    dw_up = jnp.einsum("td,tf->df", normed2, d_up, preferred_element_type=jnp.float32)
    d_normed2 = jnp.einsum(
        "tf,df->td", d_gate, w_gate, preferred_element_type=jnp.float32
    ) + jnp.einsum("tf,df->td", d_up, w_up, preferred_element_type=jnp.float32)
    d_hidden_part, d_ff_gain = ff_pull(d_normed2)
    d_hidden = grad_out.astype(jnp.float32) + d_hidden_part
    d_hidden_low = d_hidden.astype(jnp.bfloat16)
    dw_out = jnp.einsum("ti,td->id", mixed_low, d_hidden_low, preferred_element_type=jnp.float32)
    d_mixed = (
        jnp.einsum("td,id->ti", d_hidden_low, w_out, preferred_element_type=jnp.float32)
        .astype(jnp.bfloat16)
        .reshape(row_count, block_len, inner_width)
    )
    grad_heads = split_heads(d_mixed)
    row_dot_rows = jnp.sum(grad_heads.astype(jnp.float32) * mixed_heads, axis=-1)
    row_dot = jnp.transpose(row_dot_rows, (0, 2, 1))
    pieces = (
        lax.all_gather(keys, "seq", axis=1, tiled=True),
        lax.all_gather(values, "seq", axis=1, tiled=True),
    )
    key_heads = split_heads(pieces[0])
    value_heads = split_heads(pieces[1])
    scores, one_hot = block_scores(query_heads, key_heads, own_anchor, lengths, bias_f)
    weights_low, d_scores = score_grads(scores, log_total, row_dot, grad_heads, value_heads)
    d_query_part = jnp.einsum(
        "rhqk,rkhd->rqhd", d_scores, key_heads, preferred_element_type=jnp.float32
    )
    key_heads, weights_low, d_scores, d_query_part, table_part = (
        key_heads,
        weights_low,
        d_scores,
        d_query_part,
        table_term(one_hot, d_scores),
    )
    extent = key_heads.shape[1]
    d_key_part = jnp.einsum(
        "rhqk,rqhd->rkhd", d_scores, query_heads, preferred_element_type=jnp.float32
    ).reshape(row_count, extent, inner_width)
    d_value_part = jnp.einsum(
        "rhqk,rqhd->rkhd", weights_low, grad_heads, preferred_element_type=jnp.float32
    ).reshape(row_count, extent, inner_width)
    d_key, d_value = (
        lax.psum_scatter(d_key_part, "seq", scatter_dimension=1, tiled=True),
        lax.psum_scatter(d_value_part, "seq", scatter_dimension=1, tiled=True),
    )
    d_query_low = d_query_part.reshape(tokens_here, inner_width).astype(jnp.bfloat16)
    d_key_low = d_key.reshape(tokens_here, inner_width).astype(jnp.bfloat16)
    d_value_low = d_value.reshape(tokens_here, inner_width).astype(jnp.bfloat16)
    dw_query = jnp.einsum("td,ti->di", normed, d_query_low, preferred_element_type=jnp.float32)
    dw_key = jnp.einsum("td,ti->di", normed, d_key_low, preferred_element_type=jnp.float32)
    dw_value = jnp.einsum("td,ti->di", normed, d_value_low, preferred_element_type=jnp.float32)
    d_normed = jnp.einsum("ti,di->td", d_query_low, w_query, preferred_element_type=jnp.float32)
    d_normed = d_normed + jnp.einsum(
        "ti,di->td", d_key_low, w_key, preferred_element_type=jnp.float32
    )
    d_normed = d_normed + jnp.einsum(
        "ti,di->td", d_value_low, w_value, preferred_element_type=jnp.float32
    )
    d_tokens_part, d_norm_gain = norm_pull(d_normed)
    input_grad = (d_hidden + d_tokens_part).reshape(row_count, block_len, model_width)
    flat_query = dw_query.reshape(-1)
    flat_key = dw_key.reshape(-1)
    flat_value = dw_value.reshape(-1)
    flat_out = dw_out.reshape(-1)
    flat_gate = dw_gate.reshape(-1)
    flat_up = dw_up.reshape(-1)
    flat_down = dw_down.reshape(-1)
    shares = (
        lax.psum_scatter(flat_query, ("batch", "seq"), scatter_dimension=0, tiled=True),
        lax.psum_scatter(flat_key, ("batch", "seq"), scatter_dimension=0, tiled=True),
        lax.psum_scatter(flat_value, ("batch", "seq"), scatter_dimension=0, tiled=True),
        lax.psum_scatter(flat_out, ("batch", "seq"), scatter_dimension=0, tiled=True),
        lax.psum_scatter(flat_gate, ("batch", "seq"), scatter_dimension=0, tiled=True),
        lax.psum_scatter(flat_up, ("batch", "seq"), scatter_dimension=0, tiled=True),
        lax.psum_scatter(flat_down, ("batch", "seq"), scatter_dimension=0, tiled=True),
    )
    summed = (
        lax.all_gather(shares[0], ("batch", "seq"), axis=0, tiled=True),
        lax.all_gather(shares[1], ("batch", "seq"), axis=0, tiled=True),
        lax.all_gather(shares[2], ("batch", "seq"), axis=0, tiled=True),
        lax.all_gather(shares[3], ("batch", "seq"), axis=0, tiled=True),
        lax.all_gather(shares[4], ("batch", "seq"), axis=0, tiled=True),
        lax.all_gather(shares[5], ("batch", "seq"), axis=0, tiled=True),
        lax.all_gather(shares[6], ("batch", "seq"), axis=0, tiled=True),
    )
    sum_norm, sum_ff, sum_table = lax.psum((d_norm_gain, d_ff_gain, table_part), ("batch", "seq"))
    return (
        layer_output,
        input_grad,
        sum_norm,
        summed[0].reshape(w_query.shape),
        summed[1].reshape(w_key.shape),
        summed[2].reshape(w_value.shape),
        summed[3].reshape(w_out.shape),
        sum_ff,
        summed[4].reshape(w_gate.shape),
        summed[5].reshape(w_up.shape),
        summed[6].reshape(w_down.shape),
        sum_table,
    )


def all_pairs(mesh_batch, mesh_seq, move):
    pairs = []
    for batch in range(mesh_batch):
        for seq in range(mesh_seq):
            z, y, core, x = move(batch // 4, batch // 2 % 2, batch % 2, seq)
            pairs.append((batch * mesh_seq + seq, (z * 4 + y * 2 + core) * mesh_seq + x))
    return pairs


def add_up(parts):
    total = parts[0].astype(f32)
    for part in parts[1:]:
        total = total + part.astype(f32)
    return total


class Links:
    def __init__(self, batch, seq):
        self.axes = ("batch", "seq")
        self.deep = batch // 4
        me = lax.axis_index("batch")
        self.z, self.y, self.core = me // 4, me // 2 % 2, me % 2
        self.x = lax.axis_index("seq")
        self.plane = self.y * 2 + self.x
        pairs = functools.partial(all_pairs, batch, seq)
        self.to_core = pairs(lambda z, y, c, x: (z, y, 1 - c, x))
        self.to_plane = {
            k: pairs(lambda z, y, c, x, k=k: (z, y ^ (k >> 1), c, x ^ (k & 1))) for k in (1, 2, 3)
        }
        self.to_deep = {
            k: pairs(lambda z, y, c, x, k=k: ((z + k) % self.deep, y, c, x))
            for k in range(1, self.deep)
        }

    def send(self, value, pairs):
        return lax.ppermute(value, self.axes, pairs)

    def pick(self, value, at):
        return lax.dynamic_index_in_dim(value, at, 0, keepdims=False)

    def scatter_core(self, grads, deps=()):
        rows, columns = grads.shape
        shape = (4, self.deep, rows // (8 * self.deep), columns)
        got = self.send(pick_half(grads, 1 - self.core, deps), self.to_core)
        own = self.pick(grads.reshape(2, *shape), self.core)
        return add_up([own, got.reshape(shape)]).astype(bf16)

    def scatter_plane(self, part):
        got = [self.send(self.pick(part, self.plane ^ k), self.to_plane[k]) for k in (1, 2, 3)]
        return add_up([self.pick(part, self.plane), *got]).astype(bf16)

    def scatter_pair(self, part, bit):
        at = self.y if bit else self.x
        got = self.send(self.pick(part, 1 - at), self.to_plane[1 + bit])
        return add_up([self.pick(part, at), got]).astype(bf16)

    def scatter_deep(self, part):
        got = [
            self.send(self.pick(part, (self.z + k) % self.deep), self.to_deep[k])
            for k in range(1, self.deep)
        ]
        return add_up([self.pick(part, self.z), *got]).astype(bf16)

    def lay(self, count, at, own, got):
        out = jnp.zeros((count,) + own.shape, own.dtype)
        out = lax.dynamic_update_index_in_dim(out, own, at, 0)
        for place, piece in got:
            out = lax.dynamic_update_index_in_dim(out, piece, place, 0)
        return out

    def join(self, part, small):
        high = small.astype(bf16)
        low = (small - high.astype(f32)).astype(bf16)
        columns = part.shape[-1]
        tail = jnp.concatenate([high, low])
        tail = jnp.pad(tail, (0, 16 * columns - tail.shape[0])).reshape(16, columns)
        return jnp.concatenate([part.reshape(-1, columns), tail], axis=0)

    def small_of(self, joined, count):
        tail = joined[-16:].reshape(-1).astype(f32)
        return tail[:count] + tail[count : 2 * count]

    def gather_deep(self, part, small):
        joined = self.join(part, small)
        got = [self.send(joined, self.to_deep[k]) for k in range(1, self.deep)]
        rows, count = part.shape[0], small.shape[0]
        pieces = [((self.z - k) % self.deep, g[:rows]) for k, g in enumerate(got, 1)]
        small = add_up([small, *[self.small_of(g, count) for g in got]])
        return self.lay(self.deep, self.z, part, pieces), small

    def gather_plane(self, part, small, deps):
        joined = self.join(part, small)
        got = [self.send(joined, self.to_plane[k]) for k in (1, 2, 3)]
        rows, count = joined.shape[0] - 16, small.shape[0]
        pieces = [(self.plane ^ k, g[:rows].reshape(part.shape)) for k, g in enumerate(got, 1)]
        small = add_up([small, *[self.small_of(g, count) for g in got]])
        return self.lay(4, self.plane, hold(part, deps), pieces), small


def rows_device(
    batch,
    seq,
    inputs,
    lengths,
    cotangent,
    norm_gain,
    w_query,
    w_key,
    w_value,
    w_out,
    ff_gain,
    w_gate,
    w_up,
    w_down,
    bias_table,
):
    rows, half, width = inputs.shape
    buckets, heads = bias_table.shape
    mine_count = rows // 2
    links = Links(batch, seq)
    places = split_rows(lengths, links.x)
    swap = [(0, 1), (1, 0)]

    x_parts, tick = [], ()
    for row in range(mine_count):
        x_parts.append(lax.ppermute(pick_rows(places, row, 1, inputs, tick), "seq", swap))
        tick = (links.send(tick[0] if tick else places.astype(f32), links.to_core),)
    g_remote = lax.ppermute(pick_rows(places, 0, mine_count, cotangent, tick), "seq", swap)
    near, near_t, far = bias_pieces(bias_table, 2 * half // LANE)
    gain = norm_gain.reshape(1, width)
    gain2 = ff_gain.reshape(1, width)
    held = []
    for row in range(mine_count):
        held = fwd_row(
            places, inputs, x_parts[row], row, mine_count, held,
            gain, w_query, w_key, w_value, near, far, heads,
        )
    q, k, v, mix, tail, normt, x_remote = held
    ff_args = (
        places, inputs, x_remote, cotangent, g_remote, mix,
        w_out, gain2, w_gate, w_up, w_down,
    )
    lo, lo_send, dh, dmix, ff_grads, ff_gain_part = feed_forward(*ff_args)
    ff_total = lax.psum(ff_grads, ("batch", "seq"))
    quads = q.shape[1]
    lo_got = lax.ppermute(lo_send, "seq", swap)
    dw, backs, token = [], [], ()
    for quad in range(quads):
        if quad == quads - 1:
            layer_output, placed = place_rows(places, 0, lo_got, lo)
            token = (placed,)
        *back, dw_quad = bwd_quad(
            places, quad, dw, q, k, v, mix, dmix, tail, near_t, normt, token
        )
        backs.append(back)
        dw = [dw_quad]
    dq, dk, dv, tacc, far_sum = zip(*backs)
    qkv = links.scatter_core(dw[0])
    ig, ig_got, gain_parts, token = [], [], [], ()
    for row in range(mine_count):
        *ig, sent, gain_part = input_back(
            places, row, ig, inputs, x_parts[row], dh, dq, dk, dv,
            gain, w_query, w_key, w_value, token,
        )
        gain_parts.append(gain_part)
        if row == 0:
            token = (qkv,)
            qkv = links.scatter_plane(qkv)
            first_sent = sent
        else:
            ig_got.append((row, lax.ppermute(sent, "seq", swap)))
    qkv = hold(qkv, (gain_parts[-1],))
    ig_got.append((0, lax.ppermute(hold(first_sent, (qkv,)), "seq", swap)))
    table_part = table_sums(table_diagonals(tacc, (qkv,)), jnp.stack(far_sum), buckets)
    small = jnp.concatenate(
        [sum(gain_parts)[0], ff_gain_part[0], table_part.reshape(-1)]
    )
    qkv = hold(links.scatter_deep(qkv), (table_part,))
    input_grad, placed = place_rows(places, *ig_got[0], ig[0], (qkv,))
    qkv, small = links.gather_deep(qkv, small)
    qkv = hold(qkv, (placed,))
    gate_grad, up_grad, down_grad, out_grad = spread(ff_total, (qkv,))
    qkv, small = links.gather_plane(qkv, small, (out_grad,))
    for got in ig_got[1:-1]:
        input_grad, placed = place_rows(places, *got, input_grad, (), 1)
    qkv = hold(qkv, (placed,))
    input_grad, _ = place_rows(places, *ig_got[-1], input_grad, (qkv,))
    qkv = qkv.reshape(-1, qkv.shape[-1])
    arrived = links.send(links.join(qkv, small), links.to_core)
    mine_grads = unpack(qkv, qkv.shape[0], links.core)
    query_grad, key_grad, value_grad = unpack(
        arrived, qkv.shape[0], 1 - links.core, mine_grads
    )
    small = add_up([small, links.small_of(arrived, small.shape[0])])

    return (
        layer_output,
        input_grad,
        small[:width],
        query_grad,
        key_grad,
        value_grad,
        out_grad,
        small[width : 2 * width],
        gate_grad,
        up_grad,
        down_grad,
        small[2 * width :].reshape(buckets, heads),
    )


def solution(mesh):
    split = P("batch", "seq", None)
    in_specs = (split, P("batch", None), split) + (P(),) * 10
    out_specs = (split, split) + (P(),) * 10
    batch, seq = mesh.shape["batch"], mesh.shape["seq"]

    def per_device(inputs, *rest):
        rows, half, width = inputs.shape
        buckets, heads = rest[-1].shape
        inner = rest[3].shape[1]
        fits = seq == 2 and batch % 4 == 0 and rows % 2 == 0 and rows >= 4 and buckets == 32
        fits = fits and half % STEP == 0 and 2 * half // LANE <= 8
        fits = fits and inner == width and width % (16 * batch) == 0 and inner // heads == LANE // 2
        if fits:
            return rows_device(batch, seq, inputs, *rest)
        return gathered_device(inputs, *rest)

    return jax.shard_map(
        per_device, mesh=mesh, in_specs=in_specs, out_specs=out_specs, check_vma=False
    )
```

```python
import functools
import itertools
import math

import jax
import jax.numpy as jnp
from jax import lax
from jax.experimental import pallas as pl
from jax.experimental.pallas import tpu as pltpu
from jax.sharding import PartitionSpec as P

f32 = jnp.float32
bf16 = jnp.bfloat16
epsilon = 1e-06
masked_score = -2e30
start_max = -1e30
bucket_bounds = (12, 16, 23, 32, 46, 64, 91)
LANE = 128
STEP = 256
NT = (((1,), (1,)), ((), ()))
NN = (((1,), (0,)), ((), ()))
TN = (((0,), (0,)), ((), ()))


def mm(a, b, dims=NN):
    return lax.dot_general(a, b, dims, preferred_element_type=f32)


def cost(micros):
    return pl.CostEstimate(flops=int(micros * 0.3e9), bytes_accessed=0, transcendentals=0)


def params(grid_dims, mib):
    return pltpu.CompilerParams(
        dimension_semantics=("arbitrary",) * grid_dims, vmem_limit_bytes=mib << 20
    )


def bucket_of(offset, bucket_count):
    distance = jnp.abs(offset)
    far = jnp.full_like(distance, 8)
    for bound in bucket_bounds:
        far = far + (distance >= bound).astype(jnp.int32)
    half = bucket_count // 2
    return jnp.where(offset > 0, half, 0) + jnp.where(distance < 8, distance, far)


def split_body(choices, side, lengths, out):
    rows = lengths.shape[1]
    count = rows // 2
    load = [(lengths[0, r] + STEP - 1) // STEP for r in range(rows)]
    best = None
    for own in choices:
        other = [r for r in range(rows) if r not in own]
        uneven = jnp.abs(sum(load[r] for r in own) - sum(load[r] for r in other))
        new = [*own, *other]
        if best is None:
            best, picked = uneven, [jnp.int32(r) for r in new]
        else:
            better = uneven < best
            best = jnp.where(better, uneven, best)
            picked = [jnp.where(better, r, old) for r, old in zip(new, picked)]
    first = side[0] == 0
    out[0] = side[0]
    for n in range(count):
        mine = jnp.where(first, picked[n], picked[count + n])
        out[1 + n] = mine
        out[1 + count + n] = jnp.where(first, picked[count + n], picked[n])
        out[1 + 2 * count + n] = lengths[0, mine]


def split_rows(lengths, side):
    rows = lengths.shape[1]
    choices = [c for c in itertools.combinations(range(rows), rows // 2) if 0 in c]
    smem = pl.BlockSpec(memory_space=pltpu.SMEM)
    return pl.pallas_call(
        functools.partial(split_body, choices),
        in_specs=[smem, smem],
        out_specs=smem,
        out_shape=jax.ShapeDtypeStruct((1 + 3 * (rows // 2),), jnp.int32),
        name="split_rows",
    )(side.reshape(1), lengths)


def near_body(vec_ref, rev_ref, near_ref, near_t_ref):
    wide = jnp.broadcast_to(vec_ref[0], (LANE, 4 * LANE))
    near_ref[0] = pltpu.roll(wide, 0, 1, stride=1, stride_axis=0)[:, : 3 * LANE]
    tall = jnp.broadcast_to(rev_ref[0], (3 * LANE, 4 * LANE))
    near_t_ref[0] = pltpu.roll(tall, 0, 1, stride=1, stride_axis=0)[:, :LANE]


def near_offsets():
    place = jnp.arange(4 * LANE, dtype=jnp.int32)
    signed = jnp.where(place < 3 * LANE, place, place - 4 * LANE)
    forward = signed - LANE
    back = jnp.where(place < LANE, place, place - 4 * LANE)
    reverse = -back - LANE
    return forward, reverse


def bias_pieces(bias_table, tile_count):
    buckets, heads = bias_table.shape
    table = bias_table.astype(f32)
    forward, reverse = near_offsets()

    def spread(offset):
        hot = bucket_of(offset, buckets)[:, None] == jnp.arange(buckets, dtype=jnp.int32)
        picked = jnp.einsum("rb,bh->hr", hot.astype(f32), table, precision=lax.Precision.HIGHEST)
        return picked[:, None, :]

    near, near_t = pl.pallas_call(
        near_body,
        grid=(heads,),
        in_specs=[pl.BlockSpec((1, 1, 4 * LANE), lambda h: (h, 0, 0))] * 2,
        out_specs=[
            pl.BlockSpec((1, LANE, 3 * LANE), lambda h: (h, 0, 0)),
            pl.BlockSpec((1, 3 * LANE, LANE), lambda h: (h, 0, 0)),
        ],
        out_shape=[
            jax.ShapeDtypeStruct((heads, LANE, 3 * LANE), f32),
            jax.ShapeDtypeStruct((heads, 3 * LANE, LANE), f32),
        ],
        name="near_bias",
    )(spread(forward), spread(reverse))
    left = table[buckets // 2 - 1]
    right = table[buckets - 1]
    tile = jnp.arange(tile_count, dtype=jnp.int32)[None, :, None]
    lane = jnp.arange(LANE, dtype=jnp.int32)[None, None, :]
    far = jnp.where(lane == tile, left[:, None, None], 0.0)
    far = far + jnp.where(lane == tile + 8, right[:, None, None], 0.0)
    far = far + jnp.where(lane == 16, masked_score, 0.0)
    return near, near_t, far.astype(bf16)


def key_lanes(extent, length):
    key = lax.broadcasted_iota(jnp.int32, (extent, LANE), 0)
    lane = lax.broadcasted_iota(jnp.int32, (extent, LANE), 1)
    tile = key // LANE
    flag = (lane < 8) & (tile < lane - 1)
    flag = flag | ((lane >= 8) & (lane < 16) & (tile > lane - 8 + 1))
    flag = flag | ((lane == 16) & (key >= length))
    flag = flag | ((lane >= 17) & (lane < 20))
    return jnp.where(flag, 1.0, 0.0).astype(bf16)


def rms_of(values):
    scale = lax.rsqrt(jnp.mean(values * values, axis=-1, keepdims=True) + epsilon)
    return scale


def head_mask(rows, head):
    lane = lax.broadcasted_iota(jnp.int32, (rows, LANE), 1)
    return (lane // (LANE // 2)) == head


def fwd_body(held, count, which, scal, xl, xr, gain, wq, wk, wv, near, far, *rest):
    q_out, k_out, v_out, mix_out, tail_out, normt_out, x_out, normed, lanes = rest[held:]
    extent = normed.shape[0]
    half = xl.shape[1]
    length = scal[1 + 2 * count + which]
    side = scal[0]
    steps = (length + STEP - 1) // STEP

    @pl.when(pl.program_id(0) == 0)
    def _():
        for ref, own in ((xl, True), (xr, False)):
            values = ref[0].astype(f32)
            out = values * rms_of(values) * gain[...].astype(f32)
            place = side * half if own else (1 - side) * half
            normed[pl.ds(pl.multiple_of(place, half), half), :] = out.astype(bf16)
        lanes[...] = key_lanes(extent, length)
        normt_out[0] = normed[...].T
        x_out[...] = xr[...]

    q_out[0, 0] = mm(normed[...], wq[...]).astype(bf16)
    for part in range(extent // STEP):
        rows = pl.ds(part * STEP, STEP)

        @pl.when(part < steps)
        def _():
            k_out[0, 0, rows, :] = mm(normed[rows, :], wk[...]).astype(bf16)
            v_out[0, 0, rows, :] = mm(normed[rows, :], wv[...]).astype(bf16)

        @pl.when(part >= steps)
        def _():
            k_out[0, 0, rows, :] = jnp.zeros((STEP, 2 * LANE), bf16)
            v_out[0, 0, rows, :] = jnp.zeros((STEP, 2 * LANE), bf16)

    def attend(width):
        def pair_step(pair, carry):
            cols = pl.ds(pl.multiple_of(pair * LANE, LANE), LANE)
            kext = jnp.concatenate([k_out[0, 0, :width, cols], lanes[:width, :]], axis=1)
            vext = jnp.concatenate(
                [v_out[0, 0, :width, cols], jnp.ones((width, LANE), bf16)], axis=1
            )
            lane = lax.broadcasted_iota(jnp.int32, (STEP, LANE), 1)
            for block in range(extent // STEP):
                rows = slice(block * STEP, (block + 1) * STEP)
                qpair = q_out[0, 0, rows, cols]
                outs = []
                for head in range(2):
                    index = 2 * pair + head
                    tiles = []
                    for sub in range(STEP // LANE):
                        line = far[index, pl.ds(block * (STEP // LANE) + sub, 1), :]
                        tiles.append(jnp.broadcast_to(line, (LANE, LANE)))
                    ext = jnp.concatenate(tiles, axis=0)
                    qm = jnp.where(head_mask(STEP, head), qpair, jnp.zeros_like(qpair))
                    scores = mm(jnp.concatenate([qm, ext], axis=1), kext, NT)
                    probs = []
                    tops = []
                    for sub in range(STEP // LANE):
                        tile = block * (STEP // LANE) + sub
                        own = scores[sub * LANE : (sub + 1) * LANE]
                        base = (tile - 1) * LANE
                        low, high = max(0, base), min(width, base + 3 * LANE)
                        if low < high:
                            add = own[:, low:high] + near[index, :, low - base : high - base]
                            pieces = [own[:, :low]] if low > 0 else []
                            pieces.append(add)
                            if high < width:
                                pieces.append(own[:, high:])
                            own = jnp.concatenate(pieces, axis=1)
                        top = jnp.max(own, axis=1, keepdims=True)
                        probs.append(jnp.exp(own - top).astype(bf16))
                        tops.append(top)
                    both = mm(jnp.concatenate(probs, axis=0), vext)
                    total = both[:, LANE:]
                    outs.append(both[:, :LANE] / total)
                    neg = -(jnp.concatenate(tops, axis=0) + jnp.log(total))
                    first = neg.astype(bf16)
                    rest = neg - first.astype(f32)
                    second = rest.astype(bf16)
                    third = (rest - second.astype(f32)).astype(bf16)
                    line = jnp.where(lane == 17, first, ext)
                    line = jnp.where(lane == 18, second, line)
                    line = jnp.where(lane == 19, third, line)
                    tail_out[0, index, rows, :] = line
                picked = jnp.where(head_mask(STEP, 0), outs[0], outs[1])
                mix_out[0, 0, rows, cols] = picked.astype(bf16)
            return carry

        lax.fori_loop(0, 2, pair_step, 0)

    for blocks in range(1, extent // STEP + 1):

        @pl.when(steps == blocks)
        def _():
            attend(blocks * STEP)


def fwd_row(scal, inputs, remote, which, count, held, gain, wq, wk, wv, near, far, heads):
    rows, half, width = inputs.shape
    extent = 2 * half
    inner = wq.shape[1]
    quads = inner // STEP
    per = heads // quads
    weight = pl.BlockSpec((width, STEP), lambda i, s: (0, i))
    block = pl.BlockSpec((1, 1, extent, STEP), lambda i, s: (which, i, 0, 0))
    grid_spec = pltpu.PrefetchScalarGridSpec(
        num_scalar_prefetch=1,
        grid=(quads,),
        in_specs=[
            pl.BlockSpec((1, half, width), lambda i, s: (s[1 + which], 0, 0)),
            pl.BlockSpec((1, half, width), lambda i, s: (0, 0, 0)),
            pl.BlockSpec((1, width), lambda i, s: (0, 0)),
            weight,
            weight,
            weight,
            pl.BlockSpec((per, LANE, 3 * LANE), lambda i, s: (i, 0, 0)),
            pl.BlockSpec((per, 8, LANE), lambda i, s: (i, 0, 0)),
        ]
        + [pl.BlockSpec(memory_space=pl.ANY)] * len(held),
        out_specs=[block] * 4
        + [
            pl.BlockSpec((1, per, extent, LANE), lambda i, s: (which, i, 0, 0)),
            pl.BlockSpec((1, width, extent), lambda i, s: (which, 0, 0)),
            pl.BlockSpec((1, half, width), lambda i, s: (which, 0, 0)),
        ],
        scratch_shapes=[pltpu.VMEM((extent, width), bf16), pltpu.VMEM((extent, LANE), bf16)],
    )
    stacked = jax.ShapeDtypeStruct((count, quads, extent, STEP), bf16)
    return pl.pallas_call(
        functools.partial(fwd_body, len(held), count, which),
        grid_spec=grid_spec,
        out_shape=[stacked] * 4
        + [
            jax.ShapeDtypeStruct((count, heads, extent, LANE), bf16),
            jax.ShapeDtypeStruct((count, width, extent), bf16),
            jax.ShapeDtypeStruct((count, half, width), bf16),
        ],
        input_output_aliases={9 + n: n for n in range(len(held))},
        compiler_params=params(1, 56),
        cost_estimate=cost(60),
        name="attend_row",
    )(scal, inputs, remote, gain, wq, wk, wv, near, far, *held)


def bwd_body(
    count, scal, q, k, v, mix, dmix, tail, near_t, normt, *rest
):
    (dq_out, dk_out, dv_out, tacc_out, far_out, dw_out) = rest[-15:-9]
    (lanes, pl_s, ds_s, do_s, qa_s, dwq, dwk, dwv, _) = rest[-9:]
    extent = lanes.shape[0]
    row = pl.program_id(0)
    length = scal[1 + 2 * count + row]
    steps = (length + STEP - 1) // STEP
    lanes[...] = key_lanes(extent, length)

    @pl.when(row == 0)
    def _():
        for ref in (tacc_out, far_out, dwq, dwk, dwv):
            ref[...] = jnp.zeros(ref.shape, f32)

    dk_out[...] = jnp.zeros(dk_out.shape, bf16)
    dv_out[...] = jnp.zeros(dv_out.shape, bf16)

    def attend(width):
        def head_step(index, carry):
            pair = index // 2
            head = lax.rem(index, 2)
            cols = pl.ds(pl.multiple_of(pair * LANE, LANE), LANE)
            flags = lanes[:width, :]
            kpair = k[0, 0, :width, cols]
            kext = jnp.concatenate([kpair, flags], axis=1)
            vext = jnp.concatenate([v[0, 0, :width, cols], flags], axis=1)
            lane = lax.broadcasted_iota(jnp.int32, (STEP, LANE), 1)
            mask = head_mask(STEP, head)
            for block in range(extent // STEP):
                rows = slice(block * STEP, (block + 1) * STEP)
                qpair = q[0, 0, rows, cols]
                dopair = dmix[0, 0, rows, cols]
                product = dopair.astype(f32) * mix[0, 0, rows, cols].astype(f32)
                qm = jnp.where(mask, qpair, jnp.zeros_like(qpair))
                dom = jnp.where(mask, dopair, jnp.zeros_like(dopair))
                neg = -jnp.sum(jnp.where(mask, product, 0.0), axis=1, keepdims=True)
                neg = jnp.broadcast_to(neg, (STEP, LANE))
                first = neg.astype(bf16)
                rest = neg - first.astype(f32)
                second = rest.astype(bf16)
                third = (rest - second.astype(f32)).astype(bf16)
                dtail = jnp.where(lane == 17, first, jnp.zeros((STEP, LANE), bf16))
                dtail = jnp.where(lane == 18, second, dtail)
                dtail = jnp.where(lane == 19, third, dtail)
                st = mm(kext, jnp.concatenate([qm, tail[0, index, rows, :]], axis=1), NT)
                dp = mm(vext, jnp.concatenate([dom, dtail], axis=1), NT)
                do_s[rows, :] = dom
                row_at = lax.broadcasted_iota(jnp.int32, (STEP, LANE), 0)
                spot = jnp.where(lane == block * (STEP // LANE) + row_at // LANE, 1.0, 0.0)
                qa_s[rows, :] = jnp.concatenate([qm, spot.astype(bf16)], axis=1)
                for sub in range(STEP // LANE):
                    tile = block * (STEP // LANE) + sub
                    part = slice(sub * LANE, (sub + 1) * LANE)
                    own = st[:, part]
                    base = (tile - 1) * LANE
                    low, high = max(0, base), min(width, base + 3 * LANE)
                    if low < high:
                        add = own[low:high] + near_t[index, low - base : high - base, :]
                        pieces = [own[:low]] if low > 0 else []
                        pieces.append(add)
                        if high < width:
                            pieces.append(own[high:])
                        own = jnp.concatenate(pieces, axis=0)
                    prob = jnp.exp(own)
                    dst = (prob * dp[:, part]).astype(bf16)
                    place = slice(tile * LANE, (tile + 1) * LANE)
                    pl_s[:width, place] = prob.astype(bf16)
                    ds_s[:width, place] = dst
                    if low < high:
                        tacc_out[index, low - base : high - base, :] += dst[low:high].astype(f32)
            kmask = head_mask(width, head)
            dv = mm(pl_s[:width, :], do_s[...]).astype(bf16)
            dv_out[0, :width, cols] = jnp.where(kmask, dv, dv_out[0, :width, cols])
            dk = mm(ds_s[:width, :], qa_s[...])
            dk_out[0, :width, cols] = jnp.where(
                kmask, dk[:, :LANE].astype(bf16), dk_out[0, :width, cols]
            )
            tile = lax.broadcasted_iota(jnp.int32, (width, LANE), 0) // LANE
            spread = lax.broadcasted_iota(jnp.int32, (width, LANE), 1)
            left = jnp.where((tile < spread - 1) & (spread < 8), dk[:, LANE:], 0.0)
            right = jnp.where((tile > spread + 1) & (spread < 8), dk[:, LANE:], 0.0)
            far_out[pl.ds(index, 1), :] += jnp.sum(left, axis=0, keepdims=True)
            far_out[pl.ds(4 + index, 1), :] += jnp.sum(right, axis=0, keepdims=True)
            dq = mm(ds_s[:width, :], jnp.where(kmask, kpair, jnp.zeros_like(kpair)), TN)
            qmask = head_mask(extent, head)
            dq_out[0, :, cols] = jnp.where(qmask, dq.astype(bf16), dq_out[0, :, cols])
            return carry

        lax.fori_loop(0, 4, head_step, 0)
        dwk[...] += mm(normt[0, :, :width], dk_out[0, :width, :])
        dwv[...] += mm(normt[0, :, :width], dv_out[0, :width, :])

    for blocks in range(1, extent // STEP + 1):

        @pl.when(steps == blocks)
        def _():
            attend(blocks * STEP)

    dwq[...] += mm(normt[0], dq_out[0])

    @pl.when(row == count - 1)
    def _():
        for n, ref in enumerate((dwq, dwk, dwv)):
            dw_out[:, n * STEP : (n + 1) * STEP] = ref[...].astype(bf16)


def bwd_quad(places, quad, held, q, k, v, mix, dmix, tail, near_t, normt, deps=()):
    count, quads, extent, _ = q.shape
    heads = tail.shape[1]
    width = normt.shape[1]
    per = heads // quads
    block = pl.BlockSpec((1, 1, extent, STEP), lambda i, s: (i, quad, 0, 0))
    given = pl.BlockSpec((1, extent, STEP), lambda i, s: (i, 0, 0))
    grid_spec = pltpu.PrefetchScalarGridSpec(
        num_scalar_prefetch=1,
        grid=(count,),
        in_specs=[block] * 5
        + [
            pl.BlockSpec((1, per, extent, LANE), lambda i, s: (i, quad, 0, 0)),
            pl.BlockSpec((per, 3 * LANE, LANE), lambda i, s: (quad, 0, 0)),
            pl.BlockSpec((1, width, extent), lambda i, s: (i, 0, 0)),
        ]
        + [pl.BlockSpec(memory_space=pl.ANY)] * (len(held) + len(deps)),
        out_specs=[given] * 3
        + [
            pl.BlockSpec((per, 3 * LANE, LANE), lambda i, s: (0, 0, 0)),
            pl.BlockSpec((8, LANE), lambda i, s: (0, 0)),
            pl.BlockSpec((width, 3 * STEP), lambda i, s: (0, quad)),
        ],
        scratch_shapes=[
            pltpu.VMEM((extent, LANE), bf16),
            pltpu.VMEM((extent, extent), bf16),
            pltpu.VMEM((extent, extent), bf16),
            pltpu.VMEM((extent, LANE), bf16),
            pltpu.VMEM((extent, 2 * LANE), bf16),
        ]
        + [pltpu.VMEM((width, STEP), f32)] * 3
        + [pltpu.VMEM((8, LANE), f32)],
    )
    out = jax.ShapeDtypeStruct((count, extent, STEP), bf16)
    return pl.pallas_call(
        functools.partial(bwd_body, count),
        grid_spec=grid_spec,
        out_shape=[out] * 3
        + [
            jax.ShapeDtypeStruct((per, 3 * LANE, LANE), f32),
            jax.ShapeDtypeStruct((8, LANE), f32),
            jax.ShapeDtypeStruct((width, 3 * STEP * quads), bf16),
        ],
        input_output_aliases={9: 5} if held else {},
        compiler_params=params(1, 60),
        cost_estimate=cost(1),
        name="attend_back",
    )(places, q, k, v, mix, dmix, tail, near_t, normt, *held, *deps)


def table_body(quads, *rest):
    out = rest[-1]
    for quad in range(quads):
        tacc = rest[quad]
        total = jnp.zeros((8, 4 * LANE), f32)
        for group in range(3 * LANE // 8):
            part = tacc[0, group * 8 : (group + 1) * 8, :]
            wide = jnp.concatenate([part, jnp.zeros((8, 3 * LANE), f32)], axis=1)
            total = total + (pltpu.roll(wide, 4 * LANE - 8 * group, 1) if group else wide)
        line = total[0:1]
        for row in range(1, 8):
            line = line + pltpu.roll(total[row : row + 1], 4 * LANE - row, 1)
        out[quad, 0] = line


def table_diagonals(tacc, deps=()):
    quads, per = len(tacc), tacc[0].shape[0]
    return pl.pallas_call(
        functools.partial(table_body, quads),
        grid=(per,),
        in_specs=[pl.BlockSpec((1, 3 * LANE, LANE), lambda h: (h, 0, 0))] * quads
        + [pl.BlockSpec(memory_space=pl.ANY)] * len(deps),
        out_specs=pl.BlockSpec((quads, 1, 1, 4 * LANE), lambda h: (0, h, 0, 0)),
        out_shape=jax.ShapeDtypeStruct((quads, per, 1, 4 * LANE), f32),
        cost_estimate=cost(100),
        name="table_diagonals",
    )(*tacc, *deps)


def table_sums(diagonals, far_sum, buckets):
    heads = diagonals.shape[0] * diagonals.shape[1]
    diagonals = diagonals.reshape(heads, 1, 4 * LANE)
    place = jnp.arange(4 * LANE, dtype=jnp.int32)
    back = jnp.where(place < LANE, place, place - 4 * LANE)
    hot = bucket_of(-back - LANE, buckets)[:, None] == jnp.arange(buckets, dtype=jnp.int32)
    near = jnp.einsum(
        "rb,hr->bh", hot.astype(f32), diagonals[:, 0, :], precision=lax.Precision.HIGHEST
    )
    sides = jnp.sum(far_sum, axis=2).reshape(-1, 2, 4)
    sides = jnp.transpose(sides, (1, 0, 2)).reshape(2, heads)
    half = buckets // 2
    near = near.at[half - 1].add(sides[0])
    return near.at[buckets - 1].add(sides[1])


CHUNK = 512
GELU_K = math.sqrt(2.0 / math.pi)


def gated(normed, g, w_gate, w_up, w_down):
    gate = mm(normed, w_gate)
    up = mm(normed, w_up)
    d_act = mm(g, w_down, NT)
    square = gate * gate
    th = jnp.tanh(gate * (GELU_K + (GELU_K * 0.044715) * square))
    half = 0.5 + 0.5 * th
    gelu = gate * half
    slope = half + (0.5 * gate) * (1.0 - th * th) * (GELU_K + (3.0 * 0.044715 * GELU_K) * square)
    return (
        (gelu * up).astype(bf16),
        (d_act * up * slope).astype(bf16),
        (d_act * gelu).astype(bf16),
    )


def ff_body(
    scal, xl, xr, gl, gr, mix, w_out, gain, gate_any, up_any, down_any,
    lo_out, lo_send, dh_out, dmix_out, dw_out, dgain_out,
    dwo, dwg, dwu, dwd, w_gate, w_up, w_down, sems,
):
    step = pl.program_id(0)
    last = pl.num_programs(0) - 1
    own = lax.rem(step, 2) == 0
    units = w_gate.shape[1]
    loads = [
        pltpu.make_async_copy(source, target, sems.at[n])
        for n, (source, target) in enumerate(
            ((gate_any, w_gate), (up_any, w_up), (down_any, w_down))
        )
    ]

    @pl.when(step == 0)
    def _():
        for load in loads:
            load.start()
        for ref in (dwo, dwg, dwu, dwd, dgain_out):
            ref[...] = jnp.zeros(ref.shape, f32)

    g = jnp.where(own, gl[0], gr[0])
    x = jnp.where(own, xl[0], xr[0]).astype(f32)
    quads = mix.shape[1]
    mixed = jnp.concatenate([mix[0, i] for i in range(quads)], axis=1)
    hidden = x + mm(mixed, w_out[...])
    gain_f = gain[...].astype(f32)
    scale = rms_of(hidden)
    unit = hidden * scale
    normed = (unit * gain_f).astype(bf16)
    normed_t = normed.T
    g_t = g.T
    out = hidden
    dn = jnp.zeros_like(hidden)

    @pl.when(step == 0)
    def _():
        for load in loads:
            load.wait()

    for c in range(units // CHUNK):
        cols = slice(c * CHUNK, (c + 1) * CHUNK)
        act, d_gate, d_up = gated(normed, g, w_gate[:, cols], w_up[:, cols], w_down[cols, :])
        out = out + mm(act, w_down[cols, :])
        dn = dn + mm(d_gate, w_gate[:, cols], NT) + mm(d_up, w_up[:, cols], NT)
        dwd[:, cols] += mm(g_t, act)
        dwg[:, cols] += mm(normed_t, d_gate)
        dwu[:, cols] += mm(normed_t, d_up)

    @pl.when(own)
    def _():
        lo_out[0] = out

    @pl.when(jnp.logical_not(own))
    def _():
        lo_send[0] = out.astype(bf16)

    dgain_out[...] += jnp.sum(dn * unit, axis=0, keepdims=True)
    e = dn * gain_f
    d_hidden = (
        g.astype(f32) + scale * e - unit * (scale * jnp.mean(unit * e, axis=-1, keepdims=True))
    )
    dh_out[0] = d_hidden
    low = d_hidden.astype(bf16)
    dwo[...] += mm(mixed.T, low)
    d_mixed = mm(low, w_out[...], NT).astype(bf16)
    for i in range(quads):
        dmix_out[0, i] = d_mixed[:, i * STEP : (i + 1) * STEP]

    @pl.when(step == last)
    def _():
        pending = [None, None]
        place = 0
        for n, acc in enumerate((dwg, dwu, dwd, dwo)):
            slot = n % 2
            stage = (w_gate, w_up)[slot]
            if pending[slot] is not None:
                pending[slot].wait()
            cols = acc.shape[1]
            stage[:, :cols] = acc[...].astype(bf16)
            copy = pltpu.make_async_copy(
                stage.at[:, pl.ds(0, cols)], dw_out.at[:, pl.ds(place, cols)], sems.at[slot]
            )
            copy.start()
            pending[slot] = copy
            place += cols
        for copy in pending:
            copy.wait()


def feed_forward(places, inputs, x_remote, cot, cot_remote, mix, w_out, gain, w_gate, w_up, w_down):
    rows, half, width = inputs.shape
    mine = x_remote.shape[0]
    _, quads, extent, _ = mix.shape
    units = w_gate.shape[1]
    inner = w_out.shape[0]

    def keep(shape):
        return pl.BlockSpec(shape, lambda i, s: (0,) * len(shape), pipeline_mode=pl.Buffered(1))

    local = pl.BlockSpec((1, half, width), lambda i, s: (s[1 + i // 2], 0, 0))
    far = pl.BlockSpec((1, half, width), lambda i, s: (i // 2, 0, 0))
    far_one = pl.BlockSpec(
        (1, half, width), lambda i, s: (i // 2, 0, 0), pipeline_mode=pl.Buffered(1)
    )
    spot = pl.BlockSpec(
        (1, quads, half, STEP),
        lambda i, s: (i // 2, 0, jnp.where(i % 2 == 0, s[0], 1 - s[0]), 0),
    )
    tile = pl.BlockSpec((1, half, width), lambda i, s: (i, 0, 0))
    anywhere = pl.BlockSpec(memory_space=pl.ANY)
    grid_spec = pltpu.PrefetchScalarGridSpec(
        num_scalar_prefetch=1,
        grid=(2 * mine,),
        in_specs=[local, far_one, local, far_one, spot, keep((inner, width)), keep((1, width)),
                  anywhere, anywhere, anywhere],
        out_specs=[local, far, tile, spot, anywhere,
                   pl.BlockSpec((1, width), lambda i, s: (0, 0))],
        scratch_shapes=[pltpu.VMEM((inner, width), f32)]
        + [pltpu.VMEM((width, units), f32)] * 3
        + [
            pltpu.VMEM((width, units), bf16),
            pltpu.VMEM((width, units), bf16),
            pltpu.VMEM((units, width), bf16),
            pltpu.SemaphoreType.DMA((3,)),
        ],
    )
    return pl.pallas_call(
        ff_body,
        grid_spec=grid_spec,
        out_shape=[
            jax.ShapeDtypeStruct((rows, half, width), f32),
            jax.ShapeDtypeStruct((mine, half, width), bf16),
            jax.ShapeDtypeStruct((2 * mine, half, width), f32),
            jax.ShapeDtypeStruct((mine, quads, extent, STEP), bf16),
            jax.ShapeDtypeStruct((width, 3 * units + width), bf16),
            jax.ShapeDtypeStruct((1, width), f32),
        ],
        compiler_params=params(1, 63),
        cost_estimate=cost(150),
        name="feed_forward",
    )(places, inputs, x_remote, cot, cot_remote, mix, w_out, gain, w_gate, w_up, w_down)


def spread_body(sums, *rest):
    gate_out, up_out, down_out, out_out = rest[-4:]
    units = gate_out.shape[1]
    gate_out[...] = sums[:, :units].astype(f32)
    up_out[...] = sums[:, units : 2 * units].astype(f32)
    down_out[...] = sums[:, 2 * units : 3 * units].astype(f32).T
    out_out[...] = sums[:, 3 * units :].astype(f32)


def spread(sums, deps=()):
    width, columns = sums.shape
    units = (columns - width) // 3
    wide = pl.BlockSpec((LANE, units), lambda i: (i, 0))
    return pl.pallas_call(
        spread_body,
        grid=(width // LANE,),
        in_specs=[pl.BlockSpec((LANE, columns), lambda i: (i, 0))]
        + [pl.BlockSpec(memory_space=pl.ANY)] * len(deps),
        out_specs=[
            wide,
            wide,
            pl.BlockSpec((units, LANE), lambda i: (0, i)),
            pl.BlockSpec((LANE, width), lambda i: (i, 0)),
        ],
        out_shape=[
            jax.ShapeDtypeStruct((width, units), f32),
            jax.ShapeDtypeStruct((width, units), f32),
            jax.ShapeDtypeStruct((units, width), f32),
            jax.ShapeDtypeStruct((width, width), f32),
        ],
        compiler_params=params(1, 56),
        cost_estimate=cost(100),
        name="spread",
    )(sums, *deps)


def back_body(quads, held, scal, xl, xr, dh, *rest):
    grads = rest[: 3 * quads]
    gain, wq, wk, wv = rest[3 * quads : 3 * quads + 4]
    ig_out, ig_send, dgain_out = rest[-3:]
    step = pl.program_id(0)
    far = step == 0

    @pl.when(far)
    def _():
        dgain_out[...] = jnp.zeros(dgain_out.shape, f32)

    x = jnp.where(far, xr[0], xl[0]).astype(f32)
    dn = jnp.zeros_like(x)
    for n, weight in enumerate((wq, wk, wv)):
        part = jnp.concatenate([ref[0] for ref in grads[n * quads : (n + 1) * quads]], axis=1)
        dn = dn + mm(part, weight[...], NT)
    scale = rms_of(x)
    unit = x * scale
    dgain_out[...] += jnp.sum(dn * unit, axis=0, keepdims=True)
    e = dn * gain[...].astype(f32)
    out = dh[0] + scale * e - unit * (scale * jnp.mean(unit * e, axis=-1, keepdims=True))

    @pl.when(far)
    def _():
        ig_send[0] = out.astype(bf16)

    @pl.when(jnp.logical_not(far))
    def _():
        ig_out[0] = out


def input_back(places, row, held, inputs, remote, dh, dq, dk, dv, gain, wq, wk, wv, deps=()):
    rows, half, width = inputs.shape
    local = pl.BlockSpec((1, half, width), lambda i, s: (s[1 + row], 0, 0))
    one = pl.BlockSpec((1, half, width), lambda i, s: (0, 0, 0))
    tile = pl.BlockSpec((1, half, width), lambda i, s: (2 * row + 1 - i, 0, 0))
    spot = pl.BlockSpec((1, half, STEP), lambda i, s: (row, jnp.where(i == 1, s[0], 1 - s[0]), 0))
    weight = pl.BlockSpec(wq.shape, lambda i, s: (0, 0), pipeline_mode=pl.Buffered(1))
    line = pl.BlockSpec((1, width), lambda i, s: (0, 0))
    anywhere = pl.BlockSpec(memory_space=pl.ANY)
    grads = [*dq, *dk, *dv]
    grid_spec = pltpu.PrefetchScalarGridSpec(
        num_scalar_prefetch=1,
        grid=(2,),
        in_specs=[local, one, tile]
        + [spot] * len(grads)
        + [line, weight, weight, weight]
        + [anywhere] * (len(held) + len(deps)),
        out_specs=[local, one, line],
    )
    return pl.pallas_call(
        functools.partial(back_body, len(dq), len(held)),
        grid_spec=grid_spec,
        out_shape=[
            jax.ShapeDtypeStruct((rows, half, width), f32),
            jax.ShapeDtypeStruct((1, half, width), bf16),
            jax.ShapeDtypeStruct((1, width), f32),
        ],
        input_output_aliases={8 + len(grads): 0} if held else {},
        compiler_params=params(1, 56),
        cost_estimate=cost(100),
        name="input_back",
    )(places, inputs, remote, dh, *grads, gain, wq, wk, wv, *held, *deps)


def hold_body(value, *rest):
    rest[-1][...] = value[...]


def hold(value, deps):
    return pl.pallas_call(
        hold_body,
        in_specs=[pl.BlockSpec(memory_space=pltpu.VMEM)]
        + [pl.BlockSpec(memory_space=pl.ANY)] * len(deps),
        out_specs=pl.BlockSpec(memory_space=pltpu.VMEM),
        out_shape=jax.ShapeDtypeStruct(value.shape, value.dtype),
        compiler_params=pltpu.CompilerParams(vmem_limit_bytes=16 << 20),
        name="hold",
    )(value, *deps)


def pick_half(grads, at, deps):
    rows, columns = grads.shape
    grid_spec = pltpu.PrefetchScalarGridSpec(
        num_scalar_prefetch=1,
        grid=(1,),
        in_specs=[pl.BlockSpec((rows // 2, columns), lambda i, s: (s[0], 0))]
        + [pl.BlockSpec(memory_space=pl.ANY)] * len(deps),
        out_specs=pl.BlockSpec((rows // 2, columns), lambda i, s: (0, 0)),
    )
    return pl.pallas_call(
        pick_body,
        grid_spec=grid_spec,
        out_shape=jax.ShapeDtypeStruct((rows // 2, columns), grads.dtype),
        compiler_params=params(1, 24),
        name="pick_half",
    )(at.reshape(1), grads, *deps)


def pick_body(scal, array, *rest):
    rest[-1][...] = array[...]


def pick_rows(places, first, count, array, deps=()):
    rows, half, width = array.shape
    grid_spec = pltpu.PrefetchScalarGridSpec(
        num_scalar_prefetch=1,
        grid=(count,),
        in_specs=[pl.BlockSpec((1, half, width), lambda i, s: (s[1 + rows // 2 + first + i], 0, 0))]
        + [pl.BlockSpec(memory_space=pl.ANY)] * len(deps),
        out_specs=pl.BlockSpec((1, half, width), lambda i, s: (i, 0, 0)),
    )
    return pl.pallas_call(
        pick_body,
        grid_spec=grid_spec,
        out_shape=jax.ShapeDtypeStruct((count, half, width), array.dtype),
        compiler_params=params(1, 16),
        name="pick_rows",
    )(places, array, *deps)


def place_body(scal, arrived, *rest):
    out, token = rest[-2:]
    out[0] = arrived[0].astype(f32)
    token[...] = jnp.zeros(token.shape, f32)


def place_rows(places, first, arrived, held, deps=(), weight=100):
    count, half, width = arrived.shape
    at = 1 + held.shape[0] // 2 + first
    anywhere = pl.BlockSpec(memory_space=pl.ANY)
    grid_spec = pltpu.PrefetchScalarGridSpec(
        num_scalar_prefetch=1,
        grid=(count,),
        in_specs=[pl.BlockSpec((1, half, width), lambda i, s: (i, 0, 0)), anywhere]
        + [anywhere] * len(deps),
        out_specs=[
            pl.BlockSpec((1, half, width), lambda i, s: (s[at + i], 0, 0)),
            pl.BlockSpec((8, LANE), lambda i, s: (0, 0)),
        ],
    )
    return pl.pallas_call(
        place_body,
        grid_spec=grid_spec,
        out_shape=[
            jax.ShapeDtypeStruct(held.shape, f32),
            jax.ShapeDtypeStruct((8, LANE), f32),
        ],
        input_output_aliases={2: 0},
        compiler_params=params(1, 32),
        cost_estimate=cost(weight),
        name="place_rows",
    )(places, arrived, held, *deps)


def unpack_body(scal, sums, *rest):
    outs = rest[-3:]
    quads = outs[0].shape[1] // STEP
    for n, out in enumerate(outs):
        for quad in range(quads):
            begin = (3 * quad + n) * STEP
            out[:, quad * STEP : (quad + 1) * STEP] = sums[:, begin : begin + STEP].astype(f32)


def unpack(sums, rows, at, held=(), deps=()):
    columns = sums.shape[1]
    width = columns // 3
    parts = 4
    anywhere = pl.BlockSpec(memory_space=pl.ANY)
    grid_spec = pltpu.PrefetchScalarGridSpec(
        num_scalar_prefetch=1,
        grid=(parts,),
        in_specs=[pl.BlockSpec((rows // parts, columns), lambda i, s: (i, 0))]
        + [anywhere] * (len(held) + len(deps)),
        out_specs=[pl.BlockSpec((rows // parts, width), lambda i, s: (s[0] * parts + i, 0))] * 3,
    )
    return pl.pallas_call(
        unpack_body,
        grid_spec=grid_spec,
        out_shape=[jax.ShapeDtypeStruct((2 * rows, width), f32)] * 3,
        input_output_aliases={2 + n: n for n in range(len(held))},
        compiler_params=params(1, 32),
        cost_estimate=cost(100),
        name="unpack",
    )(at.reshape(1), sums, *held, *deps)


highest = lax.Precision.HIGHEST


def rms_scaled(values, gain):
    mean_square = jnp.mean(values * values, axis=-1, keepdims=True)
    return values * lax.rsqrt(mean_square + epsilon) * gain


def gated_unit(gate, up_proj):
    return jax.nn.gelu(gate, approximate=True) * up_proj


def relative_one_hot(query_anchor, query_extent, key_extent, bucket_count):
    query_place = query_anchor + jnp.arange(query_extent, dtype=jnp.int32)
    key_place = jnp.arange(key_extent, dtype=jnp.int32)
    offset = key_place[None, :] - query_place[:, None]
    distance = jnp.abs(offset)
    far_bucket = jnp.full_like(distance, 8)
    for threshold in bucket_bounds:
        far_bucket = far_bucket + (distance >= threshold).astype(jnp.int32)
    bucket = jnp.where(offset > 0, bucket_count // 2, 0) + jnp.where(
        distance < 8, distance, far_bucket
    )
    return (bucket[:, :, None] == jnp.arange(bucket_count, dtype=jnp.int32)).astype(jnp.float32)


def block_scores(query_heads, key_heads, query_anchor, lengths, bias_f):
    key_extent = key_heads.shape[1]
    one_hot = relative_one_hot(query_anchor, query_heads.shape[1], key_extent, bias_f.shape[0])
    bias_block = jnp.einsum("qkb,bh->hqk", one_hot, bias_f, precision=highest)
    raw_scores = jnp.einsum(
        "rqhd,rkhd->rhqk", query_heads, key_heads, preferred_element_type=jnp.float32
    )
    usable = jnp.arange(key_extent, dtype=jnp.int32)[None, :] < lengths[:, None]
    return (
        jnp.where(usable[:, None, None, :], raw_scores + bias_block[None], masked_score),
        one_hot,
    )


def score_grads(scores, log_total, row_dot, grad_heads, value_heads):
    weights_hp = jnp.exp(scores - log_total[..., None])
    d_weights = jnp.einsum(
        "rqhd,rkhd->rhqk", grad_heads, value_heads, preferred_element_type=jnp.float32
    )
    d_scores = (weights_hp * (d_weights - row_dot[..., None])).astype(jnp.bfloat16)
    return (weights_hp.astype(jnp.bfloat16), d_scores)


def table_term(one_hot, d_scores):
    summed = jnp.sum(d_scores, axis=0, dtype=jnp.float32)
    return jnp.einsum("qkb,hqk->bh", one_hot, summed, precision=highest)


def gathered_device(
    inputs,
    lengths,
    cotangent,
    norm_gain,
    w_query,
    w_key,
    w_value,
    w_out,
    ff_gain,
    w_gate,
    w_up,
    w_down,
    bias_table,
):
    row_count, block_len, model_width = inputs.shape
    head_count = bias_table.shape[1]
    inner_width = w_query.shape[1]
    head_width = inner_width // head_count
    tokens_here = row_count * block_len
    lengths = lengths.reshape(-1)
    bias_f = bias_table.astype(jnp.float32)
    own_anchor = lax.axis_index("seq") * block_len

    def split_heads(block_array):
        return block_array.reshape(row_count, block_array.shape[1], head_count, head_width)

    tokens_f = inputs.astype(jnp.float32).reshape(tokens_here, model_width)
    normed_f, norm_pull = jax.vjp(rms_scaled, tokens_f, norm_gain.astype(jnp.float32))
    normed = normed_f.astype(jnp.bfloat16)
    queries = (
        jnp.dot(normed, w_query, preferred_element_type=jnp.float32)
        .astype(jnp.bfloat16)
        .reshape(row_count, block_len, inner_width)
    )
    keys = (
        jnp.dot(normed, w_key, preferred_element_type=jnp.float32)
        .astype(jnp.bfloat16)
        .reshape(row_count, block_len, inner_width)
    )
    values = (
        jnp.dot(normed, w_value, preferred_element_type=jnp.float32)
        .astype(jnp.bfloat16)
        .reshape(row_count, block_len, inner_width)
    )
    query_heads = split_heads(queries)
    stat_shape = (row_count, head_count, block_len)
    pieces = (
        lax.all_gather(keys, "seq", axis=1, tiled=True),
        lax.all_gather(values, "seq", axis=1, tiled=True),
    )
    row_max = jnp.full(stat_shape, start_max, jnp.float32)
    key_heads = split_heads(pieces[0])
    value_heads = split_heads(pieces[1])
    scores, one_hot = block_scores(query_heads, key_heads, own_anchor, lengths, bias_f)
    new_max = jnp.maximum(row_max, jnp.max(scores, axis=-1))
    weights_hp = jnp.exp(scores - new_max[..., None])
    row_sum = jnp.sum(weights_hp, axis=-1)
    weighted = jnp.einsum(
        "rhqk,rkhd->rhqd",
        weights_hp.astype(jnp.bfloat16),
        value_heads,
        preferred_element_type=jnp.float32,
    )
    row_max, row_sum, weighted = (new_max, row_sum, weighted)
    log_total = row_max + jnp.log(row_sum)
    mixed_heads = jnp.transpose(weighted / row_sum[..., None], (0, 2, 1, 3))
    mixed_low = mixed_heads.reshape(tokens_here, inner_width).astype(jnp.bfloat16)
    hidden = tokens_f + jnp.dot(mixed_low, w_out, preferred_element_type=jnp.float32)
    normed2_f, ff_pull = jax.vjp(rms_scaled, hidden, ff_gain.astype(jnp.float32))
    normed2 = normed2_f.astype(jnp.bfloat16)
    gate = jnp.dot(normed2, w_gate, preferred_element_type=jnp.float32)
    up_proj = jnp.dot(normed2, w_up, preferred_element_type=jnp.float32)
    activated, gated_pull = jax.vjp(gated_unit, gate, up_proj)
    act_low = activated.astype(jnp.bfloat16)
    layer_output = (hidden + jnp.dot(act_low, w_down, preferred_element_type=jnp.float32)).reshape(
        row_count, block_len, model_width
    )
    grad_out = cotangent.reshape(tokens_here, model_width)
    dw_down = jnp.einsum("tf,td->fd", act_low, grad_out, preferred_element_type=jnp.float32)
    d_act = jnp.einsum("td,fd->tf", grad_out, w_down, preferred_element_type=jnp.float32)
    d_gate, d_up = gated_pull(d_act)
    d_gate = d_gate.astype(jnp.bfloat16)
    d_up = d_up.astype(jnp.bfloat16)
    dw_gate = jnp.einsum("td,tf->df", normed2, d_gate, preferred_element_type=jnp.float32)
    dw_up = jnp.einsum("td,tf->df", normed2, d_up, preferred_element_type=jnp.float32)
    d_normed2 = jnp.einsum(
        "tf,df->td", d_gate, w_gate, preferred_element_type=jnp.float32
    ) + jnp.einsum("tf,df->td", d_up, w_up, preferred_element_type=jnp.float32)
    d_hidden_part, d_ff_gain = ff_pull(d_normed2)
    d_hidden = grad_out.astype(jnp.float32) + d_hidden_part
    d_hidden_low = d_hidden.astype(jnp.bfloat16)
    dw_out = jnp.einsum("ti,td->id", mixed_low, d_hidden_low, preferred_element_type=jnp.float32)
    d_mixed = (
        jnp.einsum("td,id->ti", d_hidden_low, w_out, preferred_element_type=jnp.float32)
        .astype(jnp.bfloat16)
        .reshape(row_count, block_len, inner_width)
    )
    grad_heads = split_heads(d_mixed)
    row_dot_rows = jnp.sum(grad_heads.astype(jnp.float32) * mixed_heads, axis=-1)
    row_dot = jnp.transpose(row_dot_rows, (0, 2, 1))
    pieces = (
        lax.all_gather(keys, "seq", axis=1, tiled=True),
        lax.all_gather(values, "seq", axis=1, tiled=True),
    )
    key_heads = split_heads(pieces[0])
    value_heads = split_heads(pieces[1])
    scores, one_hot = block_scores(query_heads, key_heads, own_anchor, lengths, bias_f)
    weights_low, d_scores = score_grads(scores, log_total, row_dot, grad_heads, value_heads)
    d_query_part = jnp.einsum(
        "rhqk,rkhd->rqhd", d_scores, key_heads, preferred_element_type=jnp.float32
    )
    key_heads, weights_low, d_scores, d_query_part, table_part = (
        key_heads,
        weights_low,
        d_scores,
        d_query_part,
        table_term(one_hot, d_scores),
    )
    extent = key_heads.shape[1]
    d_key_part = jnp.einsum(
        "rhqk,rqhd->rkhd", d_scores, query_heads, preferred_element_type=jnp.float32
    ).reshape(row_count, extent, inner_width)
    d_value_part = jnp.einsum(
        "rhqk,rqhd->rkhd", weights_low, grad_heads, preferred_element_type=jnp.float32
    ).reshape(row_count, extent, inner_width)
    d_key, d_value = (
        lax.psum_scatter(d_key_part, "seq", scatter_dimension=1, tiled=True),
        lax.psum_scatter(d_value_part, "seq", scatter_dimension=1, tiled=True),
    )
    d_query_low = d_query_part.reshape(tokens_here, inner_width).astype(jnp.bfloat16)
    d_key_low = d_key.reshape(tokens_here, inner_width).astype(jnp.bfloat16)
    d_value_low = d_value.reshape(tokens_here, inner_width).astype(jnp.bfloat16)
    dw_query = jnp.einsum("td,ti->di", normed, d_query_low, preferred_element_type=jnp.float32)
    dw_key = jnp.einsum("td,ti->di", normed, d_key_low, preferred_element_type=jnp.float32)
    dw_value = jnp.einsum("td,ti->di", normed, d_value_low, preferred_element_type=jnp.float32)
    d_normed = jnp.einsum("ti,di->td", d_query_low, w_query, preferred_element_type=jnp.float32)
    d_normed = d_normed + jnp.einsum(
        "ti,di->td", d_key_low, w_key, preferred_element_type=jnp.float32
    )
    d_normed = d_normed + jnp.einsum(
        "ti,di->td", d_value_low, w_value, preferred_element_type=jnp.float32
    )
    d_tokens_part, d_norm_gain = norm_pull(d_normed)
    input_grad = (d_hidden + d_tokens_part).reshape(row_count, block_len, model_width)
    flat_query = dw_query.reshape(-1)
    flat_key = dw_key.reshape(-1)
    flat_value = dw_value.reshape(-1)
    flat_out = dw_out.reshape(-1)
    flat_gate = dw_gate.reshape(-1)
    flat_up = dw_up.reshape(-1)
    flat_down = dw_down.reshape(-1)
    shares = (
        lax.psum_scatter(flat_query, ("batch", "seq"), scatter_dimension=0, tiled=True),
        lax.psum_scatter(flat_key, ("batch", "seq"), scatter_dimension=0, tiled=True),
        lax.psum_scatter(flat_value, ("batch", "seq"), scatter_dimension=0, tiled=True),
        lax.psum_scatter(flat_out, ("batch", "seq"), scatter_dimension=0, tiled=True),
        lax.psum_scatter(flat_gate, ("batch", "seq"), scatter_dimension=0, tiled=True),
        lax.psum_scatter(flat_up, ("batch", "seq"), scatter_dimension=0, tiled=True),
        lax.psum_scatter(flat_down, ("batch", "seq"), scatter_dimension=0, tiled=True),
    )
    summed = (
        lax.all_gather(shares[0], ("batch", "seq"), axis=0, tiled=True),
        lax.all_gather(shares[1], ("batch", "seq"), axis=0, tiled=True),
        lax.all_gather(shares[2], ("batch", "seq"), axis=0, tiled=True),
        lax.all_gather(shares[3], ("batch", "seq"), axis=0, tiled=True),
        lax.all_gather(shares[4], ("batch", "seq"), axis=0, tiled=True),
        lax.all_gather(shares[5], ("batch", "seq"), axis=0, tiled=True),
        lax.all_gather(shares[6], ("batch", "seq"), axis=0, tiled=True),
    )
    sum_norm, sum_ff, sum_table = lax.psum((d_norm_gain, d_ff_gain, table_part), ("batch", "seq"))
    return (
        layer_output,
        input_grad,
        sum_norm,
        summed[0].reshape(w_query.shape),
        summed[1].reshape(w_key.shape),
        summed[2].reshape(w_value.shape),
        summed[3].reshape(w_out.shape),
        sum_ff,
        summed[4].reshape(w_gate.shape),
        summed[5].reshape(w_up.shape),
        summed[6].reshape(w_down.shape),
        sum_table,
    )


def all_pairs(mesh_batch, mesh_seq, move):
    pairs = []
    for batch in range(mesh_batch):
        for seq in range(mesh_seq):
            z, y, core, x = move(batch // 4, batch // 2 % 2, batch % 2, seq)
            pairs.append((batch * mesh_seq + seq, (z * 4 + y * 2 + core) * mesh_seq + x))
    return pairs


def add_up(parts):
    total = parts[0].astype(f32)
    for part in parts[1:]:
        total = total + part.astype(f32)
    return total


class Links:
    def __init__(self, batch, seq):
        self.axes = ("batch", "seq")
        self.deep = batch // 4
        me = lax.axis_index("batch")
        self.z, self.y, self.core = me // 4, me // 2 % 2, me % 2
        self.x = lax.axis_index("seq")
        self.plane = self.y * 2 + self.x
        pairs = functools.partial(all_pairs, batch, seq)
        self.to_core = pairs(lambda z, y, c, x: (z, y, 1 - c, x))
        self.to_plane = {
            k: pairs(lambda z, y, c, x, k=k: (z, y ^ (k >> 1), c, x ^ (k & 1))) for k in (1, 2, 3)
        }
        self.to_deep = {
            k: pairs(lambda z, y, c, x, k=k: ((z + k) % self.deep, y, c, x))
            for k in range(1, self.deep)
        }

    def send(self, value, pairs):
        return lax.ppermute(value, self.axes, pairs)

    def pick(self, value, at):
        return lax.dynamic_index_in_dim(value, at, 0, keepdims=False)

    def scatter_core(self, grads, deps=()):
        rows, columns = grads.shape
        shape = (4, self.deep, rows // (8 * self.deep), columns)
        got = self.send(pick_half(grads, 1 - self.core, deps), self.to_core)
        own = self.pick(grads.reshape(2, *shape), self.core)
        return add_up([own, got.reshape(shape)]).astype(bf16)

    def scatter_plane(self, part):
        got = [self.send(self.pick(part, self.plane ^ k), self.to_plane[k]) for k in (1, 2, 3)]
        return add_up([self.pick(part, self.plane), *got]).astype(bf16)

    def scatter_pair(self, part, bit):
        at = self.y if bit else self.x
        got = self.send(self.pick(part, 1 - at), self.to_plane[1 + bit])
        return add_up([self.pick(part, at), got]).astype(bf16)

    def scatter_deep(self, part):
        got = [
            self.send(self.pick(part, (self.z + k) % self.deep), self.to_deep[k])
            for k in range(1, self.deep)
        ]
        return add_up([self.pick(part, self.z), *got]).astype(bf16)

    def lay(self, count, at, own, got):
        out = jnp.zeros((count,) + own.shape, own.dtype)
        out = lax.dynamic_update_index_in_dim(out, own, at, 0)
        for place, piece in got:
            out = lax.dynamic_update_index_in_dim(out, piece, place, 0)
        return out

    def join(self, part, small):
        columns = part.shape[-1]
        high = small.astype(bf16)
        low = (small - high.astype(f32)).astype(bf16)
        rest = jnp.zeros((14, columns), bf16)
        return jnp.concatenate([part.reshape(-1, columns), high, low, rest], axis=0)

    def small_of(self, joined):
        return joined[-16:-15].astype(f32) + joined[-15:-14].astype(f32)

    def gather_deep(self, part, small):
        joined = self.join(part, small)
        got = [self.send(joined, self.to_deep[k]) for k in range(1, self.deep)]
        rows = part.shape[0]
        pieces = [((self.z - k) % self.deep, g[:rows]) for k, g in enumerate(got, 1)]
        small = add_up([small, *[self.small_of(g) for g in got]])
        return self.lay(self.deep, self.z, part, pieces), small

    def gather_plane(self, part, small, deps):
        joined = self.join(part, small)
        got = [self.send(joined, self.to_plane[k]) for k in (1, 2, 3)]
        rows = joined.shape[0] - 16
        pieces = [(self.plane ^ k, g[:rows].reshape(part.shape)) for k, g in enumerate(got, 1)]
        small = add_up([small, *[self.small_of(g) for g in got]])
        return self.lay(4, self.plane, hold(part, deps), pieces), small


def rows_device(
    batch,
    seq,
    inputs,
    lengths,
    cotangent,
    norm_gain,
    w_query,
    w_key,
    w_value,
    w_out,
    ff_gain,
    w_gate,
    w_up,
    w_down,
    bias_table,
):
    rows, half, width = inputs.shape
    buckets, heads = bias_table.shape
    mine_count = rows // 2
    links = Links(batch, seq)
    places = split_rows(lengths, links.x)
    swap = [(0, 1), (1, 0)]

    x_parts, tick = [], ()
    for row in range(mine_count):
        x_parts.append(lax.ppermute(pick_rows(places, row, 1, inputs, tick), "seq", swap))
        tick = (links.send(tick[0] if tick else places.astype(f32), links.to_core),)
    g_remote = lax.ppermute(pick_rows(places, 0, mine_count, cotangent, tick), "seq", swap)
    near, near_t, far = bias_pieces(bias_table, 2 * half // LANE)
    gain = norm_gain.reshape(1, width)
    gain2 = ff_gain.reshape(1, width)
    held = []
    for row in range(mine_count):
        held = fwd_row(
            places, inputs, x_parts[row], row, mine_count, held,
            gain, w_query, w_key, w_value, near, far, heads,
        )
    q, k, v, mix, tail, normt, x_remote = held
    ff_args = (
        places, inputs, x_remote, cotangent, g_remote, mix,
        w_out, gain2, w_gate, w_up, w_down,
    )
    lo, lo_send, dh, dmix, ff_grads, ff_gain_part = feed_forward(*ff_args)
    ff_total = lax.psum(ff_grads, ("batch", "seq"))
    quads = q.shape[1]
    lo_got = lax.ppermute(lo_send, "seq", swap)
    dw, backs, token = [], [], ()
    for quad in range(quads):
        if quad == quads - 1:
            layer_output, placed = place_rows(places, 0, lo_got, lo)
            token = (placed,)
        *back, dw_quad = bwd_quad(
            places, quad, dw, q, k, v, mix, dmix, tail, near_t, normt, token
        )
        backs.append(back)
        dw = [dw_quad]
    dq, dk, dv, tacc, far_sum = zip(*backs)
    qkv = links.scatter_core(dw[0])
    ig, ig_got, gain_parts, token = [], [], [], ()
    for row in range(mine_count):
        *ig, sent, gain_part = input_back(
            places, row, ig, inputs, x_parts[row], dh, dq, dk, dv,
            gain, w_query, w_key, w_value, token,
        )
        gain_parts.append(gain_part)
        if row == 0:
            token = (qkv,)
            qkv = links.scatter_plane(qkv)
            first_sent = sent
        else:
            ig_got.append((row, lax.ppermute(sent, "seq", swap)))
    qkv = hold(qkv, (gain_parts[-1],))
    ig_got.append((0, lax.ppermute(hold(first_sent, (qkv,)), "seq", swap)))
    table_part = table_sums(table_diagonals(tacc, (qkv,)), jnp.stack(far_sum), buckets)
    small = jnp.concatenate([sum(gain_parts)[0], ff_gain_part[0], table_part.reshape(-1)])
    small = jnp.pad(small, (0, dw[0].shape[1] - small.shape[0])).reshape(1, -1)
    input_grad, placed = place_rows(places, *ig_got[0], ig[0], (qkv,))
    qkv = hold(links.scatter_deep(qkv), (table_part, placed))
    for got in ig_got[1:-1]:
        input_grad, placed = place_rows(places, *got, input_grad, (qkv,))
    qkv, small = links.gather_deep(qkv, small)
    qkv = hold(qkv, (placed,))
    gate_grad, up_grad, down_grad, out_grad = spread(ff_total, (qkv,))
    qkv, small = links.gather_plane(qkv, small, (out_grad,))
    qkv = hold(qkv, (out_grad,))
    input_grad, _ = place_rows(places, *ig_got[-1], input_grad, (qkv,))
    qkv = qkv.reshape(-1, qkv.shape[-1])
    arrived = links.send(links.join(qkv, small), links.to_core)
    mine_grads = unpack(qkv, qkv.shape[0], links.core)
    query_grad, key_grad, value_grad = unpack(
        arrived, qkv.shape[0], 1 - links.core, mine_grads
    )
    small = add_up([small, links.small_of(arrived)])[0]

    return (
        layer_output,
        input_grad,
        small[:width],
        query_grad,
        key_grad,
        value_grad,
        out_grad,
        small[width : 2 * width],
        gate_grad,
        up_grad,
        down_grad,
        small[2 * width : 2 * width + buckets * heads].reshape(buckets, heads),
    )


def solution(mesh):
    split = P("batch", "seq", None)
    in_specs = (split, P("batch", None), split) + (P(),) * 10
    out_specs = (split, split) + (P(),) * 10
    batch, seq = mesh.shape["batch"], mesh.shape["seq"]

    def per_device(inputs, *rest):
        rows, half, width = inputs.shape
        buckets, heads = rest[-1].shape
        inner = rest[3].shape[1]
        fits = seq == 2 and batch % 4 == 0 and rows % 2 == 0 and rows >= 4 and buckets == 32
        fits = fits and 2 * width + buckets * heads <= 3 * width and half % STEP == 0 and 2 * half // LANE <= 8
        fits = fits and inner == width and width % (16 * batch) == 0 and inner // heads == LANE // 2
        if fits:
            return rows_device(batch, seq, inputs, *rest)
        return gathered_device(inputs, *rest)

    return jax.shard_map(
        per_device, mesh=mesh, in_specs=in_specs, out_specs=out_specs, check_vma=False
    )
```

```python
import functools
import itertools
import math

import jax
import jax.numpy as jnp
from jax import lax
from jax.experimental import pallas as pl
from jax.experimental.pallas import tpu as pltpu
from jax.sharding import PartitionSpec as P

f32 = jnp.float32
bf16 = jnp.bfloat16
epsilon = 1e-06
masked_score = -2e30
start_max = -1e30
bucket_bounds = (12, 16, 23, 32, 46, 64, 91)
LANE = 128
STEP = 256
NT = (((1,), (1,)), ((), ()))
NN = (((1,), (0,)), ((), ()))
TN = (((0,), (0,)), ((), ()))


def mm(a, b, dims=NN):
    return lax.dot_general(a, b, dims, preferred_element_type=f32)


def cost(micros):
    return pl.CostEstimate(flops=int(micros * 0.3e9), bytes_accessed=0, transcendentals=0)


def params(grid_dims, mib):
    return pltpu.CompilerParams(
        dimension_semantics=("arbitrary",) * grid_dims, vmem_limit_bytes=mib << 20
    )


def bucket_of(offset, bucket_count):
    distance = jnp.abs(offset)
    far = jnp.full_like(distance, 8)
    for bound in bucket_bounds:
        far = far + (distance >= bound).astype(jnp.int32)
    half = bucket_count // 2
    return jnp.where(offset > 0, half, 0) + jnp.where(distance < 8, distance, far)


def split_body(choices, side, lengths, out):
    rows = lengths.shape[1]
    count = rows // 2
    load = [(lengths[0, r] + STEP - 1) // STEP for r in range(rows)]
    best = None
    for own in choices:
        other = [r for r in range(rows) if r not in own]
        uneven = jnp.abs(sum(load[r] for r in own) - sum(load[r] for r in other))
        new = [*own, *other]
        if best is None:
            best, picked = uneven, [jnp.int32(r) for r in new]
        else:
            better = uneven < best
            best = jnp.where(better, uneven, best)
            picked = [jnp.where(better, r, old) for r, old in zip(new, picked)]
    first = side[0] == 0
    out[0] = side[0]
    for n in range(count):
        mine = jnp.where(first, picked[n], picked[count + n])
        out[1 + n] = mine
        out[1 + count + n] = jnp.where(first, picked[count + n], picked[n])
        out[1 + 2 * count + n] = lengths[0, mine]


def split_rows(lengths, side):
    rows = lengths.shape[1]
    choices = [c for c in itertools.combinations(range(rows), rows // 2) if 0 in c]
    smem = pl.BlockSpec(memory_space=pltpu.SMEM)
    return pl.pallas_call(
        functools.partial(split_body, choices),
        in_specs=[smem, smem],
        out_specs=smem,
        out_shape=jax.ShapeDtypeStruct((1 + 3 * (rows // 2),), jnp.int32),
        name="split_rows",
    )(side.reshape(1), lengths)


def near_body(vec_ref, rev_ref, near_ref, near_t_ref):
    wide = jnp.broadcast_to(vec_ref[0], (LANE, 4 * LANE))
    near_ref[0] = pltpu.roll(wide, 0, 1, stride=1, stride_axis=0)[:, : 3 * LANE]
    tall = jnp.broadcast_to(rev_ref[0], (3 * LANE, 4 * LANE))
    near_t_ref[0] = pltpu.roll(tall, 0, 1, stride=1, stride_axis=0)[:, :LANE]


def near_offsets():
    place = jnp.arange(4 * LANE, dtype=jnp.int32)
    signed = jnp.where(place < 3 * LANE, place, place - 4 * LANE)
    forward = signed - LANE
    back = jnp.where(place < LANE, place, place - 4 * LANE)
    reverse = -back - LANE
    return forward, reverse


def bias_pieces(bias_table, tile_count):
    buckets, heads = bias_table.shape
    table = bias_table.astype(f32)
    forward, reverse = near_offsets()

    def spread(offset):
        hot = bucket_of(offset, buckets)[:, None] == jnp.arange(buckets, dtype=jnp.int32)
        picked = jnp.einsum("rb,bh->hr", hot.astype(f32), table, precision=lax.Precision.HIGHEST)
        return picked[:, None, :]

    near, near_t = pl.pallas_call(
        near_body,
        grid=(heads,),
        in_specs=[pl.BlockSpec((1, 1, 4 * LANE), lambda h: (h, 0, 0))] * 2,
        out_specs=[
            pl.BlockSpec((1, LANE, 3 * LANE), lambda h: (h, 0, 0)),
            pl.BlockSpec((1, 3 * LANE, LANE), lambda h: (h, 0, 0)),
        ],
        out_shape=[
            jax.ShapeDtypeStruct((heads, LANE, 3 * LANE), f32),
            jax.ShapeDtypeStruct((heads, 3 * LANE, LANE), f32),
        ],
        name="near_bias",
    )(spread(forward), spread(reverse))
    left = table[buckets // 2 - 1]
    right = table[buckets - 1]
    tile = jnp.arange(tile_count, dtype=jnp.int32)[None, :, None]
    lane = jnp.arange(LANE, dtype=jnp.int32)[None, None, :]
    far = jnp.where(lane == tile, left[:, None, None], 0.0)
    far = far + jnp.where(lane == tile + 8, right[:, None, None], 0.0)
    far = far + jnp.where(lane == 16, masked_score, 0.0)
    return near, near_t, far.astype(bf16)


def key_lanes(extent, length):
    key = lax.broadcasted_iota(jnp.int32, (extent, LANE), 0)
    lane = lax.broadcasted_iota(jnp.int32, (extent, LANE), 1)
    tile = key // LANE
    flag = (lane < 8) & (tile < lane - 1)
    flag = flag | ((lane >= 8) & (lane < 16) & (tile > lane - 8 + 1))
    flag = flag | ((lane == 16) & (key >= length))
    flag = flag | ((lane >= 17) & (lane < 20))
    return jnp.where(flag, 1.0, 0.0).astype(bf16)


def rms_of(values):
    scale = lax.rsqrt(jnp.mean(values * values, axis=-1, keepdims=True) + epsilon)
    return scale


def head_mask(rows, head):
    lane = lax.broadcasted_iota(jnp.int32, (rows, LANE), 1)
    return (lane // (LANE // 2)) == head


def fwd_body(held, count, which, scal, xl, xr, gain, wq, wk, wv, near, far, *rest):
    q_out, k_out, v_out, mix_out, tail_out, normt_out, x_out, normed, lanes = rest[held:]
    extent = normed.shape[0]
    half = xl.shape[1]
    length = scal[1 + 2 * count + which]
    side = scal[0]
    steps = (length + STEP - 1) // STEP

    @pl.when(pl.program_id(0) == 0)
    def _():
        for ref, own in ((xl, True), (xr, False)):
            values = ref[0].astype(f32)
            out = values * rms_of(values) * gain[...].astype(f32)
            place = side * half if own else (1 - side) * half
            normed[pl.ds(pl.multiple_of(place, half), half), :] = out.astype(bf16)
        lanes[...] = key_lanes(extent, length)
        normt_out[0] = normed[...].T
        x_out[...] = xr[...]

    q_out[0, 0] = mm(normed[...], wq[...]).astype(bf16)
    for part in range(extent // STEP):
        rows = pl.ds(part * STEP, STEP)

        @pl.when(part < steps)
        def _():
            k_out[0, 0, rows, :] = mm(normed[rows, :], wk[...]).astype(bf16)
            v_out[0, 0, rows, :] = mm(normed[rows, :], wv[...]).astype(bf16)

        @pl.when(part >= steps)
        def _():
            k_out[0, 0, rows, :] = jnp.zeros((STEP, 2 * LANE), bf16)
            v_out[0, 0, rows, :] = jnp.zeros((STEP, 2 * LANE), bf16)

    def attend(width):
        def pair_step(pair, carry):
            cols = pl.ds(pl.multiple_of(pair * LANE, LANE), LANE)
            kext = jnp.concatenate([k_out[0, 0, :width, cols], lanes[:width, :]], axis=1)
            vext = jnp.concatenate(
                [v_out[0, 0, :width, cols], jnp.ones((width, LANE), bf16)], axis=1
            )
            lane = lax.broadcasted_iota(jnp.int32, (STEP, LANE), 1)
            for block in range(extent // STEP):
                rows = slice(block * STEP, (block + 1) * STEP)
                qpair = q_out[0, 0, rows, cols]
                outs = []
                for head in range(2):
                    index = 2 * pair + head
                    tiles = []
                    for sub in range(STEP // LANE):
                        line = far[index, pl.ds(block * (STEP // LANE) + sub, 1), :]
                        tiles.append(jnp.broadcast_to(line, (LANE, LANE)))
                    ext = jnp.concatenate(tiles, axis=0)
                    qm = jnp.where(head_mask(STEP, head), qpair, jnp.zeros_like(qpair))
                    scores = mm(jnp.concatenate([qm, ext], axis=1), kext, NT)
                    probs = []
                    tops = []
                    for sub in range(STEP // LANE):
                        tile = block * (STEP // LANE) + sub
                        own = scores[sub * LANE : (sub + 1) * LANE]
                        base = (tile - 1) * LANE
                        low, high = max(0, base), min(width, base + 3 * LANE)
                        if low < high:
                            add = own[:, low:high] + near[index, :, low - base : high - base]
                            pieces = [own[:, :low]] if low > 0 else []
                            pieces.append(add)
                            if high < width:
                                pieces.append(own[:, high:])
                            own = jnp.concatenate(pieces, axis=1)
                        top = jnp.max(own, axis=1, keepdims=True)
                        probs.append(jnp.exp(own - top).astype(bf16))
                        tops.append(top)
                    both = mm(jnp.concatenate(probs, axis=0), vext)
                    total = both[:, LANE:]
                    outs.append(both[:, :LANE] / total)
                    neg = -(jnp.concatenate(tops, axis=0) + jnp.log(total))
                    first = neg.astype(bf16)
                    rest = neg - first.astype(f32)
                    second = rest.astype(bf16)
                    third = (rest - second.astype(f32)).astype(bf16)
                    line = jnp.where(lane == 17, first, ext)
                    line = jnp.where(lane == 18, second, line)
                    line = jnp.where(lane == 19, third, line)
                    tail_out[0, index, rows, :] = line
                picked = jnp.where(head_mask(STEP, 0), outs[0], outs[1])
                mix_out[0, 0, rows, cols] = picked.astype(bf16)
            return carry

        lax.fori_loop(0, 2, pair_step, 0)

    for blocks in range(1, extent // STEP + 1):

        @pl.when(steps == blocks)
        def _():
            attend(blocks * STEP)


def fwd_row(scal, inputs, remote, which, count, held, gain, wq, wk, wv, near, far, heads):
    rows, half, width = inputs.shape
    extent = 2 * half
    inner = wq.shape[1]
    quads = inner // STEP
    per = heads // quads
    weight = pl.BlockSpec((width, STEP), lambda i, s: (0, i))
    block = pl.BlockSpec((1, 1, extent, STEP), lambda i, s: (which, i, 0, 0))
    grid_spec = pltpu.PrefetchScalarGridSpec(
        num_scalar_prefetch=1,
        grid=(quads,),
        in_specs=[
            pl.BlockSpec((1, half, width), lambda i, s: (s[1 + which], 0, 0)),
            pl.BlockSpec((1, half, width), lambda i, s: (0, 0, 0)),
            pl.BlockSpec((1, width), lambda i, s: (0, 0)),
            weight,
            weight,
            weight,
            pl.BlockSpec((per, LANE, 3 * LANE), lambda i, s: (i, 0, 0)),
            pl.BlockSpec((per, 8, LANE), lambda i, s: (i, 0, 0)),
        ]
        + [pl.BlockSpec(memory_space=pl.ANY)] * len(held),
        out_specs=[block] * 4
        + [
            pl.BlockSpec((1, per, extent, LANE), lambda i, s: (which, i, 0, 0)),
            pl.BlockSpec((1, width, extent), lambda i, s: (which, 0, 0)),
            pl.BlockSpec((1, half, width), lambda i, s: (which, 0, 0)),
        ],
        scratch_shapes=[pltpu.VMEM((extent, width), bf16), pltpu.VMEM((extent, LANE), bf16)],
    )
    stacked = jax.ShapeDtypeStruct((count, quads, extent, STEP), bf16)
    return pl.pallas_call(
        functools.partial(fwd_body, len(held), count, which),
        grid_spec=grid_spec,
        out_shape=[stacked] * 4
        + [
            jax.ShapeDtypeStruct((count, heads, extent, LANE), bf16),
            jax.ShapeDtypeStruct((count, width, extent), bf16),
            jax.ShapeDtypeStruct((count, half, width), bf16),
        ],
        input_output_aliases={9 + n: n for n in range(len(held))},
        compiler_params=params(1, 56),
        cost_estimate=cost(60),
        name="attend_row",
    )(scal, inputs, remote, gain, wq, wk, wv, near, far, *held)


def bwd_body(
    count, scal, q, k, v, mix, dmix, tail, near_t, normt, *rest
):
    (dq_out, dk_out, dv_out, tacc_out, far_out, dw_out) = rest[-15:-9]
    (lanes, pl_s, ds_s, do_s, qa_s, dwq, dwk, dwv, _) = rest[-9:]
    extent = lanes.shape[0]
    row = pl.program_id(0)
    length = scal[1 + 2 * count + row]
    steps = (length + STEP - 1) // STEP
    lanes[...] = key_lanes(extent, length)

    @pl.when(row == 0)
    def _():
        for ref in (tacc_out, far_out, dwq, dwk, dwv):
            ref[...] = jnp.zeros(ref.shape, f32)

    dk_out[...] = jnp.zeros(dk_out.shape, bf16)
    dv_out[...] = jnp.zeros(dv_out.shape, bf16)

    def attend(width):
        def head_step(index, carry):
            pair = index // 2
            head = lax.rem(index, 2)
            cols = pl.ds(pl.multiple_of(pair * LANE, LANE), LANE)
            flags = lanes[:width, :]
            kpair = k[0, 0, :width, cols]
            kext = jnp.concatenate([kpair, flags], axis=1)
            vext = jnp.concatenate([v[0, 0, :width, cols], flags], axis=1)
            lane = lax.broadcasted_iota(jnp.int32, (STEP, LANE), 1)
            mask = head_mask(STEP, head)
            for block in range(extent // STEP):
                rows = slice(block * STEP, (block + 1) * STEP)
                qpair = q[0, 0, rows, cols]
                dopair = dmix[0, 0, rows, cols]
                product = dopair.astype(f32) * mix[0, 0, rows, cols].astype(f32)
                qm = jnp.where(mask, qpair, jnp.zeros_like(qpair))
                dom = jnp.where(mask, dopair, jnp.zeros_like(dopair))
                neg = -jnp.sum(jnp.where(mask, product, 0.0), axis=1, keepdims=True)
                neg = jnp.broadcast_to(neg, (STEP, LANE))
                first = neg.astype(bf16)
                rest = neg - first.astype(f32)
                second = rest.astype(bf16)
                third = (rest - second.astype(f32)).astype(bf16)
                dtail = jnp.where(lane == 17, first, jnp.zeros((STEP, LANE), bf16))
                dtail = jnp.where(lane == 18, second, dtail)
                dtail = jnp.where(lane == 19, third, dtail)
                st = mm(kext, jnp.concatenate([qm, tail[0, index, rows, :]], axis=1), NT)
                dp = mm(vext, jnp.concatenate([dom, dtail], axis=1), NT)
                do_s[rows, :] = dom
                row_at = lax.broadcasted_iota(jnp.int32, (STEP, LANE), 0)
                spot = jnp.where(lane == block * (STEP // LANE) + row_at // LANE, 1.0, 0.0)
                qa_s[rows, :] = jnp.concatenate([qm, spot.astype(bf16)], axis=1)
                for sub in range(STEP // LANE):
                    tile = block * (STEP // LANE) + sub
                    part = slice(sub * LANE, (sub + 1) * LANE)
                    own = st[:, part]
                    base = (tile - 1) * LANE
                    low, high = max(0, base), min(width, base + 3 * LANE)
                    if low < high:
                        add = own[low:high] + near_t[index, low - base : high - base, :]
                        pieces = [own[:low]] if low > 0 else []
                        pieces.append(add)
                        if high < width:
                            pieces.append(own[high:])
                        own = jnp.concatenate(pieces, axis=0)
                    prob = jnp.exp(own)
                    dst = (prob * dp[:, part]).astype(bf16)
                    place = slice(tile * LANE, (tile + 1) * LANE)
                    pl_s[:width, place] = prob.astype(bf16)
                    ds_s[:width, place] = dst
                    if low < high:
                        tacc_out[index, low - base : high - base, :] += dst[low:high].astype(f32)
            kmask = head_mask(width, head)
            dv = mm(pl_s[:width, :], do_s[...]).astype(bf16)
            dv_out[0, :width, cols] = jnp.where(kmask, dv, dv_out[0, :width, cols])
            dk = mm(ds_s[:width, :], qa_s[...])
            dk_out[0, :width, cols] = jnp.where(
                kmask, dk[:, :LANE].astype(bf16), dk_out[0, :width, cols]
            )
            tile = lax.broadcasted_iota(jnp.int32, (width, LANE), 0) // LANE
            spread = lax.broadcasted_iota(jnp.int32, (width, LANE), 1)
            left = jnp.where((tile < spread - 1) & (spread < 8), dk[:, LANE:], 0.0)
            right = jnp.where((tile > spread + 1) & (spread < 8), dk[:, LANE:], 0.0)
            far_out[pl.ds(index, 1), :] += jnp.sum(left, axis=0, keepdims=True)
            far_out[pl.ds(4 + index, 1), :] += jnp.sum(right, axis=0, keepdims=True)
            dq = mm(ds_s[:width, :], jnp.where(kmask, kpair, jnp.zeros_like(kpair)), TN)
            qmask = head_mask(extent, head)
            dq_out[0, :, cols] = jnp.where(qmask, dq.astype(bf16), dq_out[0, :, cols])
            return carry

        lax.fori_loop(0, 4, head_step, 0)
        dwk[...] += mm(normt[0, :, :width], dk_out[0, :width, :])
        dwv[...] += mm(normt[0, :, :width], dv_out[0, :width, :])

    for blocks in range(1, extent // STEP + 1):

        @pl.when(steps == blocks)
        def _():
            attend(blocks * STEP)

    dwq[...] += mm(normt[0], dq_out[0])

    @pl.when(row == count - 1)
    def _():
        for n, ref in enumerate((dwq, dwk, dwv)):
            dw_out[:, n * STEP : (n + 1) * STEP] = ref[...].astype(bf16)


def bwd_quad(places, quad, held, q, k, v, mix, dmix, tail, near_t, normt, deps=()):
    count, quads, extent, _ = q.shape
    heads = tail.shape[1]
    width = normt.shape[1]
    per = heads // quads
    block = pl.BlockSpec((1, 1, extent, STEP), lambda i, s: (i, quad, 0, 0))
    given = pl.BlockSpec((1, extent, STEP), lambda i, s: (i, 0, 0))
    grid_spec = pltpu.PrefetchScalarGridSpec(
        num_scalar_prefetch=1,
        grid=(count,),
        in_specs=[block] * 5
        + [
            pl.BlockSpec((1, per, extent, LANE), lambda i, s: (i, quad, 0, 0)),
            pl.BlockSpec((per, 3 * LANE, LANE), lambda i, s: (quad, 0, 0)),
            pl.BlockSpec((1, width, extent), lambda i, s: (i, 0, 0)),
        ]
        + [pl.BlockSpec(memory_space=pl.ANY)] * (len(held) + len(deps)),
        out_specs=[given] * 3
        + [
            pl.BlockSpec((per, 3 * LANE, LANE), lambda i, s: (0, 0, 0)),
            pl.BlockSpec((8, LANE), lambda i, s: (0, 0)),
            pl.BlockSpec((width, 3 * STEP), lambda i, s: (0, quad)),
        ],
        scratch_shapes=[
            pltpu.VMEM((extent, LANE), bf16),
            pltpu.VMEM((extent, extent), bf16),
            pltpu.VMEM((extent, extent), bf16),
            pltpu.VMEM((extent, LANE), bf16),
            pltpu.VMEM((extent, 2 * LANE), bf16),
        ]
        + [pltpu.VMEM((width, STEP), f32)] * 3
        + [pltpu.VMEM((8, LANE), f32)],
    )
    out = jax.ShapeDtypeStruct((count, extent, STEP), bf16)
    return pl.pallas_call(
        functools.partial(bwd_body, count),
        grid_spec=grid_spec,
        out_shape=[out] * 3
        + [
            jax.ShapeDtypeStruct((per, 3 * LANE, LANE), f32),
            jax.ShapeDtypeStruct((8, LANE), f32),
            jax.ShapeDtypeStruct((width, 3 * STEP * quads), bf16),
        ],
        input_output_aliases={9: 5} if held else {},
        compiler_params=params(1, 60),
        cost_estimate=cost(1),
        name="attend_back",
    )(places, q, k, v, mix, dmix, tail, near_t, normt, *held, *deps)


def table_body(quads, *rest):
    out = rest[-1]
    for quad in range(quads):
        tacc = rest[quad]
        total = jnp.zeros((8, 4 * LANE), f32)
        for group in range(3 * LANE // 8):
            part = tacc[0, group * 8 : (group + 1) * 8, :]
            wide = jnp.concatenate([part, jnp.zeros((8, 3 * LANE), f32)], axis=1)
            total = total + (pltpu.roll(wide, 4 * LANE - 8 * group, 1) if group else wide)
        line = total[0:1]
        for row in range(1, 8):
            line = line + pltpu.roll(total[row : row + 1], 4 * LANE - row, 1)
        out[quad, 0] = line


def table_diagonals(tacc, deps=()):
    quads, per = len(tacc), tacc[0].shape[0]
    return pl.pallas_call(
        functools.partial(table_body, quads),
        grid=(per,),
        in_specs=[pl.BlockSpec((1, 3 * LANE, LANE), lambda h: (h, 0, 0))] * quads
        + [pl.BlockSpec(memory_space=pl.ANY)] * len(deps),
        out_specs=pl.BlockSpec((quads, 1, 1, 4 * LANE), lambda h: (0, h, 0, 0)),
        out_shape=jax.ShapeDtypeStruct((quads, per, 1, 4 * LANE), f32),
        cost_estimate=cost(100),
        name="table_diagonals",
    )(*tacc, *deps)


def table_sums(diagonals, far_sum, buckets):
    heads = diagonals.shape[0] * diagonals.shape[1]
    diagonals = diagonals.reshape(heads, 1, 4 * LANE)
    place = jnp.arange(4 * LANE, dtype=jnp.int32)
    back = jnp.where(place < LANE, place, place - 4 * LANE)
    hot = bucket_of(-back - LANE, buckets)[:, None] == jnp.arange(buckets, dtype=jnp.int32)
    near = jnp.einsum(
        "rb,hr->bh", hot.astype(f32), diagonals[:, 0, :], precision=lax.Precision.HIGHEST
    )
    sides = jnp.sum(far_sum, axis=2).reshape(-1, 2, 4)
    sides = jnp.transpose(sides, (1, 0, 2)).reshape(2, heads)
    half = buckets // 2
    near = near.at[half - 1].add(sides[0])
    return near.at[buckets - 1].add(sides[1])


CHUNK = 512
GELU_K = math.sqrt(2.0 / math.pi)


def gated(normed, g, w_gate, w_up, w_down):
    gate = mm(normed, w_gate)
    up = mm(normed, w_up)
    d_act = mm(g, w_down, NT)
    square = gate * gate
    th = jnp.tanh(gate * (GELU_K + (GELU_K * 0.044715) * square))
    half = 0.5 + 0.5 * th
    gelu = gate * half
    slope = half + (0.5 * gate) * (1.0 - th * th) * (GELU_K + (3.0 * 0.044715 * GELU_K) * square)
    return (
        (gelu * up).astype(bf16),
        (d_act * up * slope).astype(bf16),
        (d_act * gelu).astype(bf16),
    )


def ff_body(
    scal, xl, xr, gl, gr, mix, w_out, gain, gate_any, up_any, down_any,
    lo_out, lo_send, dh_out, dmix_out, dw_out, dgain_out,
    dwo, dwg, dwu, dwd, w_gate, w_up, w_down, sems,
):
    step = pl.program_id(0)
    last = pl.num_programs(0) - 1
    own = lax.rem(step, 2) == 0
    units = w_gate.shape[1]
    loads = [
        pltpu.make_async_copy(source, target, sems.at[n])
        for n, (source, target) in enumerate(
            ((gate_any, w_gate), (up_any, w_up), (down_any, w_down))
        )
    ]

    @pl.when(step == 0)
    def _():
        for load in loads:
            load.start()
        for ref in (dwo, dwg, dwu, dwd, dgain_out):
            ref[...] = jnp.zeros(ref.shape, f32)

    g = jnp.where(own, gl[0], gr[0])
    x = jnp.where(own, xl[0], xr[0]).astype(f32)
    quads = mix.shape[1]
    mixed = jnp.concatenate([mix[0, i] for i in range(quads)], axis=1)
    hidden = x + mm(mixed, w_out[...])
    gain_f = gain[...].astype(f32)
    scale = rms_of(hidden)
    unit = hidden * scale
    normed = (unit * gain_f).astype(bf16)
    normed_t = normed.T
    g_t = g.T
    out = hidden
    dn = jnp.zeros_like(hidden)

    @pl.when(step == 0)
    def _():
        for load in loads:
            load.wait()

    for c in range(units // CHUNK):
        cols = slice(c * CHUNK, (c + 1) * CHUNK)
        act, d_gate, d_up = gated(normed, g, w_gate[:, cols], w_up[:, cols], w_down[cols, :])
        out = out + mm(act, w_down[cols, :])
        dn = dn + mm(d_gate, w_gate[:, cols], NT) + mm(d_up, w_up[:, cols], NT)
        dwd[:, cols] += mm(g_t, act)
        dwg[:, cols] += mm(normed_t, d_gate)
        dwu[:, cols] += mm(normed_t, d_up)

    @pl.when(own)
    def _():
        lo_out[0] = out

    @pl.when(jnp.logical_not(own))
    def _():
        lo_send[0] = out.astype(bf16)

    dgain_out[...] += jnp.sum(dn * unit, axis=0, keepdims=True)
    e = dn * gain_f
    d_hidden = (
        g.astype(f32) + scale * e - unit * (scale * jnp.mean(unit * e, axis=-1, keepdims=True))
    )
    dh_out[0] = d_hidden
    low = d_hidden.astype(bf16)
    dwo[...] += mm(mixed.T, low)
    d_mixed = mm(low, w_out[...], NT).astype(bf16)
    for i in range(quads):
        dmix_out[0, i] = d_mixed[:, i * STEP : (i + 1) * STEP]

    @pl.when(step == last)
    def _():
        pending = [None, None]
        place = 0
        for n, acc in enumerate((dwg, dwu, dwd, dwo)):
            slot = n % 2
            stage = (w_gate, w_up)[slot]
            if pending[slot] is not None:
                pending[slot].wait()
            cols = acc.shape[1]
            stage[:, :cols] = acc[...].astype(bf16)
            copy = pltpu.make_async_copy(
                stage.at[:, pl.ds(0, cols)], dw_out.at[:, pl.ds(place, cols)], sems.at[slot]
            )
            copy.start()
            pending[slot] = copy
            place += cols
        for copy in pending:
            copy.wait()


def feed_forward(places, inputs, x_remote, cot, cot_remote, mix, w_out, gain, w_gate, w_up, w_down):
    rows, half, width = inputs.shape
    mine = x_remote.shape[0]
    _, quads, extent, _ = mix.shape
    units = w_gate.shape[1]
    inner = w_out.shape[0]

    def keep(shape):
        return pl.BlockSpec(shape, lambda i, s: (0,) * len(shape), pipeline_mode=pl.Buffered(1))

    local = pl.BlockSpec((1, half, width), lambda i, s: (s[1 + i // 2], 0, 0))
    far = pl.BlockSpec((1, half, width), lambda i, s: (i // 2, 0, 0))
    far_one = pl.BlockSpec(
        (1, half, width), lambda i, s: (i // 2, 0, 0), pipeline_mode=pl.Buffered(1)
    )
    spot = pl.BlockSpec(
        (1, quads, half, STEP),
        lambda i, s: (i // 2, 0, jnp.where(i % 2 == 0, s[0], 1 - s[0]), 0),
    )
    tile = pl.BlockSpec((1, half, width), lambda i, s: (i, 0, 0))
    anywhere = pl.BlockSpec(memory_space=pl.ANY)
    grid_spec = pltpu.PrefetchScalarGridSpec(
        num_scalar_prefetch=1,
        grid=(2 * mine,),
        in_specs=[local, far_one, local, far_one, spot, keep((inner, width)), keep((1, width)),
                  anywhere, anywhere, anywhere],
        out_specs=[local, far, tile, spot, anywhere,
                   pl.BlockSpec((1, width), lambda i, s: (0, 0))],
        scratch_shapes=[pltpu.VMEM((inner, width), f32)]
        + [pltpu.VMEM((width, units), f32)] * 3
        + [
            pltpu.VMEM((width, units), bf16),
            pltpu.VMEM((width, units), bf16),
            pltpu.VMEM((units, width), bf16),
            pltpu.SemaphoreType.DMA((3,)),
        ],
    )
    return pl.pallas_call(
        ff_body,
        grid_spec=grid_spec,
        out_shape=[
            jax.ShapeDtypeStruct((rows, half, width), f32),
            jax.ShapeDtypeStruct((mine, half, width), bf16),
            jax.ShapeDtypeStruct((2 * mine, half, width), f32),
            jax.ShapeDtypeStruct((mine, quads, extent, STEP), bf16),
            jax.ShapeDtypeStruct((width, 3 * units + width), bf16),
            jax.ShapeDtypeStruct((1, width), f32),
        ],
        compiler_params=params(1, 63),
        cost_estimate=cost(150),
        name="feed_forward",
    )(places, inputs, x_remote, cot, cot_remote, mix, w_out, gain, w_gate, w_up, w_down)


def spread_body(sums, *rest):
    gate_out, up_out, down_out, out_out = rest[-4:]
    units = gate_out.shape[1]
    gate_out[...] = sums[:, :units].astype(f32)
    up_out[...] = sums[:, units : 2 * units].astype(f32)
    down_out[...] = sums[:, 2 * units : 3 * units].astype(f32).T
    out_out[...] = sums[:, 3 * units :].astype(f32)


def spread(sums, deps=()):
    width, columns = sums.shape
    units = (columns - width) // 3
    wide = pl.BlockSpec((LANE, units), lambda i: (i, 0))
    return pl.pallas_call(
        spread_body,
        grid=(width // LANE,),
        in_specs=[pl.BlockSpec((LANE, columns), lambda i: (i, 0))]
        + [pl.BlockSpec(memory_space=pl.ANY)] * len(deps),
        out_specs=[
            wide,
            wide,
            pl.BlockSpec((units, LANE), lambda i: (0, i)),
            pl.BlockSpec((LANE, width), lambda i: (i, 0)),
        ],
        out_shape=[
            jax.ShapeDtypeStruct((width, units), f32),
            jax.ShapeDtypeStruct((width, units), f32),
            jax.ShapeDtypeStruct((units, width), f32),
            jax.ShapeDtypeStruct((width, width), f32),
        ],
        compiler_params=params(1, 56),
        cost_estimate=cost(100),
        name="spread",
    )(sums, *deps)


def back_body(quads, held, scal, xl, xr, dh, *rest):
    grads = rest[: 3 * quads]
    gain, wq, wk, wv = rest[3 * quads : 3 * quads + 4]
    ig_out, ig_send, dgain_out = rest[-3:]
    step = pl.program_id(0)
    far = step == 0

    @pl.when(far)
    def _():
        dgain_out[...] = jnp.zeros(dgain_out.shape, f32)

    x = jnp.where(far, xr[0], xl[0]).astype(f32)
    dn = jnp.zeros_like(x)
    for n, weight in enumerate((wq, wk, wv)):
        part = jnp.concatenate([ref[0] for ref in grads[n * quads : (n + 1) * quads]], axis=1)
        dn = dn + mm(part, weight[...], NT)
    scale = rms_of(x)
    unit = x * scale
    dgain_out[...] += jnp.sum(dn * unit, axis=0, keepdims=True)
    e = dn * gain[...].astype(f32)
    out = dh[0] + scale * e - unit * (scale * jnp.mean(unit * e, axis=-1, keepdims=True))

    @pl.when(far)
    def _():
        ig_send[0] = out.astype(bf16)

    @pl.when(jnp.logical_not(far))
    def _():
        ig_out[0] = out


def input_back(places, row, held, inputs, remote, dh, dq, dk, dv, gain, wq, wk, wv, deps=()):
    rows, half, width = inputs.shape
    local = pl.BlockSpec((1, half, width), lambda i, s: (s[1 + row], 0, 0))
    one = pl.BlockSpec((1, half, width), lambda i, s: (0, 0, 0))
    tile = pl.BlockSpec((1, half, width), lambda i, s: (2 * row + 1 - i, 0, 0))
    spot = pl.BlockSpec((1, half, STEP), lambda i, s: (row, jnp.where(i == 1, s[0], 1 - s[0]), 0))
    weight = pl.BlockSpec(wq.shape, lambda i, s: (0, 0), pipeline_mode=pl.Buffered(1))
    line = pl.BlockSpec((1, width), lambda i, s: (0, 0))
    anywhere = pl.BlockSpec(memory_space=pl.ANY)
    grads = [*dq, *dk, *dv]
    grid_spec = pltpu.PrefetchScalarGridSpec(
        num_scalar_prefetch=1,
        grid=(2,),
        in_specs=[local, one, tile]
        + [spot] * len(grads)
        + [line, weight, weight, weight]
        + [anywhere] * (len(held) + len(deps)),
        out_specs=[local, one, line],
    )
    return pl.pallas_call(
        functools.partial(back_body, len(dq), len(held)),
        grid_spec=grid_spec,
        out_shape=[
            jax.ShapeDtypeStruct((rows, half, width), f32),
            jax.ShapeDtypeStruct((1, half, width), bf16),
            jax.ShapeDtypeStruct((1, width), f32),
        ],
        input_output_aliases={8 + len(grads): 0} if held else {},
        compiler_params=params(1, 56),
        cost_estimate=cost(100),
        name="input_back",
    )(places, inputs, remote, dh, *grads, gain, wq, wk, wv, *held, *deps)


def hold_body(value, *rest):
    rest[-1][...] = value[...]


def hold(value, deps):
    return pl.pallas_call(
        hold_body,
        in_specs=[pl.BlockSpec(memory_space=pltpu.VMEM)]
        + [pl.BlockSpec(memory_space=pl.ANY)] * len(deps),
        out_specs=pl.BlockSpec(memory_space=pltpu.VMEM),
        out_shape=jax.ShapeDtypeStruct(value.shape, value.dtype),
        compiler_params=pltpu.CompilerParams(vmem_limit_bytes=16 << 20),
        name="hold",
    )(value, *deps)


def pick_half(grads, at, deps):
    rows, columns = grads.shape
    grid_spec = pltpu.PrefetchScalarGridSpec(
        num_scalar_prefetch=1,
        grid=(1,),
        in_specs=[pl.BlockSpec((rows // 2, columns), lambda i, s: (s[0], 0))]
        + [pl.BlockSpec(memory_space=pl.ANY)] * len(deps),
        out_specs=pl.BlockSpec((rows // 2, columns), lambda i, s: (0, 0)),
    )
    return pl.pallas_call(
        pick_body,
        grid_spec=grid_spec,
        out_shape=jax.ShapeDtypeStruct((rows // 2, columns), grads.dtype),
        compiler_params=params(1, 24),
        name="pick_half",
    )(at.reshape(1), grads, *deps)


def pick_body(scal, array, *rest):
    rest[-1][...] = array[...]


def pick_rows(places, first, count, array, deps=()):
    rows, half, width = array.shape
    grid_spec = pltpu.PrefetchScalarGridSpec(
        num_scalar_prefetch=1,
        grid=(count,),
        in_specs=[pl.BlockSpec((1, half, width), lambda i, s: (s[1 + rows // 2 + first + i], 0, 0))]
        + [pl.BlockSpec(memory_space=pl.ANY)] * len(deps),
        out_specs=pl.BlockSpec((1, half, width), lambda i, s: (i, 0, 0)),
    )
    return pl.pallas_call(
        pick_body,
        grid_spec=grid_spec,
        out_shape=jax.ShapeDtypeStruct((count, half, width), array.dtype),
        compiler_params=params(1, 16),
        name="pick_rows",
    )(places, array, *deps)


def place_body(scal, arrived, *rest):
    out, token = rest[-2:]
    out[0] = arrived[0].astype(f32)
    token[...] = jnp.zeros(token.shape, f32)


def place_rows(places, first, arrived, held, deps=(), weight=100):
    count, half, width = arrived.shape
    at = 1 + held.shape[0] // 2 + first
    anywhere = pl.BlockSpec(memory_space=pl.ANY)
    grid_spec = pltpu.PrefetchScalarGridSpec(
        num_scalar_prefetch=1,
        grid=(count,),
        in_specs=[pl.BlockSpec((1, half, width), lambda i, s: (i, 0, 0)), anywhere]
        + [anywhere] * len(deps),
        out_specs=[
            pl.BlockSpec((1, half, width), lambda i, s: (s[at + i], 0, 0)),
            pl.BlockSpec((8, LANE), lambda i, s: (0, 0)),
        ],
    )
    return pl.pallas_call(
        place_body,
        grid_spec=grid_spec,
        out_shape=[
            jax.ShapeDtypeStruct(held.shape, f32),
            jax.ShapeDtypeStruct((8, LANE), f32),
        ],
        input_output_aliases={2: 0},
        compiler_params=params(1, 32),
        cost_estimate=cost(weight),
        name="place_rows",
    )(places, arrived, held, *deps)


def unpack_body(scal, sums, *rest):
    outs = rest[-3:]
    quads = outs[0].shape[1] // STEP
    for n, out in enumerate(outs):
        for quad in range(quads):
            begin = (3 * quad + n) * STEP
            out[:, quad * STEP : (quad + 1) * STEP] = sums[:, begin : begin + STEP].astype(f32)


def unpack(sums, rows, at, held=(), deps=()):
    columns = sums.shape[1]
    width = columns // 3
    parts = 4
    anywhere = pl.BlockSpec(memory_space=pl.ANY)
    grid_spec = pltpu.PrefetchScalarGridSpec(
        num_scalar_prefetch=1,
        grid=(parts,),
        in_specs=[pl.BlockSpec((rows // parts, columns), lambda i, s: (i, 0))]
        + [anywhere] * (len(held) + len(deps)),
        out_specs=[pl.BlockSpec((rows // parts, width), lambda i, s: (s[0] * parts + i, 0))] * 3,
    )
    return pl.pallas_call(
        unpack_body,
        grid_spec=grid_spec,
        out_shape=[jax.ShapeDtypeStruct((2 * rows, width), f32)] * 3,
        input_output_aliases={2 + n: n for n in range(len(held))},
        compiler_params=params(1, 32),
        cost_estimate=cost(100),
        name="unpack",
    )(at.reshape(1), sums, *held, *deps)


highest = lax.Precision.HIGHEST


def rms_scaled(values, gain):
    mean_square = jnp.mean(values * values, axis=-1, keepdims=True)
    return values * lax.rsqrt(mean_square + epsilon) * gain


def gated_unit(gate, up_proj):
    return jax.nn.gelu(gate, approximate=True) * up_proj


def relative_one_hot(query_anchor, query_extent, key_extent, bucket_count):
    query_place = query_anchor + jnp.arange(query_extent, dtype=jnp.int32)
    key_place = jnp.arange(key_extent, dtype=jnp.int32)
    offset = key_place[None, :] - query_place[:, None]
    distance = jnp.abs(offset)
    far_bucket = jnp.full_like(distance, 8)
    for threshold in bucket_bounds:
        far_bucket = far_bucket + (distance >= threshold).astype(jnp.int32)
    bucket = jnp.where(offset > 0, bucket_count // 2, 0) + jnp.where(
        distance < 8, distance, far_bucket
    )
    return (bucket[:, :, None] == jnp.arange(bucket_count, dtype=jnp.int32)).astype(jnp.float32)


def block_scores(query_heads, key_heads, query_anchor, lengths, bias_f):
    key_extent = key_heads.shape[1]
    one_hot = relative_one_hot(query_anchor, query_heads.shape[1], key_extent, bias_f.shape[0])
    bias_block = jnp.einsum("qkb,bh->hqk", one_hot, bias_f, precision=highest)
    raw_scores = jnp.einsum(
        "rqhd,rkhd->rhqk", query_heads, key_heads, preferred_element_type=jnp.float32
    )
    usable = jnp.arange(key_extent, dtype=jnp.int32)[None, :] < lengths[:, None]
    return (
        jnp.where(usable[:, None, None, :], raw_scores + bias_block[None], masked_score),
        one_hot,
    )


def score_grads(scores, log_total, row_dot, grad_heads, value_heads):
    weights_hp = jnp.exp(scores - log_total[..., None])
    d_weights = jnp.einsum(
        "rqhd,rkhd->rhqk", grad_heads, value_heads, preferred_element_type=jnp.float32
    )
    d_scores = (weights_hp * (d_weights - row_dot[..., None])).astype(jnp.bfloat16)
    return (weights_hp.astype(jnp.bfloat16), d_scores)


def table_term(one_hot, d_scores):
    summed = jnp.sum(d_scores, axis=0, dtype=jnp.float32)
    return jnp.einsum("qkb,hqk->bh", one_hot, summed, precision=highest)


def gathered_device(
    inputs,
    lengths,
    cotangent,
    norm_gain,
    w_query,
    w_key,
    w_value,
    w_out,
    ff_gain,
    w_gate,
    w_up,
    w_down,
    bias_table,
):
    row_count, block_len, model_width = inputs.shape
    head_count = bias_table.shape[1]
    inner_width = w_query.shape[1]
    head_width = inner_width // head_count
    tokens_here = row_count * block_len
    lengths = lengths.reshape(-1)
    bias_f = bias_table.astype(jnp.float32)
    own_anchor = lax.axis_index("seq") * block_len

    def split_heads(block_array):
        return block_array.reshape(row_count, block_array.shape[1], head_count, head_width)

    tokens_f = inputs.astype(jnp.float32).reshape(tokens_here, model_width)
    normed_f, norm_pull = jax.vjp(rms_scaled, tokens_f, norm_gain.astype(jnp.float32))
    normed = normed_f.astype(jnp.bfloat16)
    queries = (
        jnp.dot(normed, w_query, preferred_element_type=jnp.float32)
        .astype(jnp.bfloat16)
        .reshape(row_count, block_len, inner_width)
    )
    keys = (
        jnp.dot(normed, w_key, preferred_element_type=jnp.float32)
        .astype(jnp.bfloat16)
        .reshape(row_count, block_len, inner_width)
    )
    values = (
        jnp.dot(normed, w_value, preferred_element_type=jnp.float32)
        .astype(jnp.bfloat16)
        .reshape(row_count, block_len, inner_width)
    )
    query_heads = split_heads(queries)
    stat_shape = (row_count, head_count, block_len)
    pieces = (
        lax.all_gather(keys, "seq", axis=1, tiled=True),
        lax.all_gather(values, "seq", axis=1, tiled=True),
    )
    row_max = jnp.full(stat_shape, start_max, jnp.float32)
    key_heads = split_heads(pieces[0])
    value_heads = split_heads(pieces[1])
    scores, one_hot = block_scores(query_heads, key_heads, own_anchor, lengths, bias_f)
    new_max = jnp.maximum(row_max, jnp.max(scores, axis=-1))
    weights_hp = jnp.exp(scores - new_max[..., None])
    row_sum = jnp.sum(weights_hp, axis=-1)
    weighted = jnp.einsum(
        "rhqk,rkhd->rhqd",
        weights_hp.astype(jnp.bfloat16),
        value_heads,
        preferred_element_type=jnp.float32,
    )
    row_max, row_sum, weighted = (new_max, row_sum, weighted)
    log_total = row_max + jnp.log(row_sum)
    mixed_heads = jnp.transpose(weighted / row_sum[..., None], (0, 2, 1, 3))
    mixed_low = mixed_heads.reshape(tokens_here, inner_width).astype(jnp.bfloat16)
    hidden = tokens_f + jnp.dot(mixed_low, w_out, preferred_element_type=jnp.float32)
    normed2_f, ff_pull = jax.vjp(rms_scaled, hidden, ff_gain.astype(jnp.float32))
    normed2 = normed2_f.astype(jnp.bfloat16)
    gate = jnp.dot(normed2, w_gate, preferred_element_type=jnp.float32)
    up_proj = jnp.dot(normed2, w_up, preferred_element_type=jnp.float32)
    activated, gated_pull = jax.vjp(gated_unit, gate, up_proj)
    act_low = activated.astype(jnp.bfloat16)
    layer_output = (hidden + jnp.dot(act_low, w_down, preferred_element_type=jnp.float32)).reshape(
        row_count, block_len, model_width
    )
    grad_out = cotangent.reshape(tokens_here, model_width)
    dw_down = jnp.einsum("tf,td->fd", act_low, grad_out, preferred_element_type=jnp.float32)
    d_act = jnp.einsum("td,fd->tf", grad_out, w_down, preferred_element_type=jnp.float32)
    d_gate, d_up = gated_pull(d_act)
    d_gate = d_gate.astype(jnp.bfloat16)
    d_up = d_up.astype(jnp.bfloat16)
    dw_gate = jnp.einsum("td,tf->df", normed2, d_gate, preferred_element_type=jnp.float32)
    dw_up = jnp.einsum("td,tf->df", normed2, d_up, preferred_element_type=jnp.float32)
    d_normed2 = jnp.einsum(
        "tf,df->td", d_gate, w_gate, preferred_element_type=jnp.float32
    ) + jnp.einsum("tf,df->td", d_up, w_up, preferred_element_type=jnp.float32)
    d_hidden_part, d_ff_gain = ff_pull(d_normed2)
    d_hidden = grad_out.astype(jnp.float32) + d_hidden_part
    d_hidden_low = d_hidden.astype(jnp.bfloat16)
    dw_out = jnp.einsum("ti,td->id", mixed_low, d_hidden_low, preferred_element_type=jnp.float32)
    d_mixed = (
        jnp.einsum("td,id->ti", d_hidden_low, w_out, preferred_element_type=jnp.float32)
        .astype(jnp.bfloat16)
        .reshape(row_count, block_len, inner_width)
    )
    grad_heads = split_heads(d_mixed)
    row_dot_rows = jnp.sum(grad_heads.astype(jnp.float32) * mixed_heads, axis=-1)
    row_dot = jnp.transpose(row_dot_rows, (0, 2, 1))
    pieces = (
        lax.all_gather(keys, "seq", axis=1, tiled=True),
        lax.all_gather(values, "seq", axis=1, tiled=True),
    )
    key_heads = split_heads(pieces[0])
    value_heads = split_heads(pieces[1])
    scores, one_hot = block_scores(query_heads, key_heads, own_anchor, lengths, bias_f)
    weights_low, d_scores = score_grads(scores, log_total, row_dot, grad_heads, value_heads)
    d_query_part = jnp.einsum(
        "rhqk,rkhd->rqhd", d_scores, key_heads, preferred_element_type=jnp.float32
    )
    key_heads, weights_low, d_scores, d_query_part, table_part = (
        key_heads,
        weights_low,
        d_scores,
        d_query_part,
        table_term(one_hot, d_scores),
    )
    extent = key_heads.shape[1]
    d_key_part = jnp.einsum(
        "rhqk,rqhd->rkhd", d_scores, query_heads, preferred_element_type=jnp.float32
    ).reshape(row_count, extent, inner_width)
    d_value_part = jnp.einsum(
        "rhqk,rqhd->rkhd", weights_low, grad_heads, preferred_element_type=jnp.float32
    ).reshape(row_count, extent, inner_width)
    d_key, d_value = (
        lax.psum_scatter(d_key_part, "seq", scatter_dimension=1, tiled=True),
        lax.psum_scatter(d_value_part, "seq", scatter_dimension=1, tiled=True),
    )
    d_query_low = d_query_part.reshape(tokens_here, inner_width).astype(jnp.bfloat16)
    d_key_low = d_key.reshape(tokens_here, inner_width).astype(jnp.bfloat16)
    d_value_low = d_value.reshape(tokens_here, inner_width).astype(jnp.bfloat16)
    dw_query = jnp.einsum("td,ti->di", normed, d_query_low, preferred_element_type=jnp.float32)
    dw_key = jnp.einsum("td,ti->di", normed, d_key_low, preferred_element_type=jnp.float32)
    dw_value = jnp.einsum("td,ti->di", normed, d_value_low, preferred_element_type=jnp.float32)
    d_normed = jnp.einsum("ti,di->td", d_query_low, w_query, preferred_element_type=jnp.float32)
    d_normed = d_normed + jnp.einsum(
        "ti,di->td", d_key_low, w_key, preferred_element_type=jnp.float32
    )
    d_normed = d_normed + jnp.einsum(
        "ti,di->td", d_value_low, w_value, preferred_element_type=jnp.float32
    )
    d_tokens_part, d_norm_gain = norm_pull(d_normed)
    input_grad = (d_hidden + d_tokens_part).reshape(row_count, block_len, model_width)
    flat_query = dw_query.reshape(-1)
    flat_key = dw_key.reshape(-1)
    flat_value = dw_value.reshape(-1)
    flat_out = dw_out.reshape(-1)
    flat_gate = dw_gate.reshape(-1)
    flat_up = dw_up.reshape(-1)
    flat_down = dw_down.reshape(-1)
    shares = (
        lax.psum_scatter(flat_query, ("batch", "seq"), scatter_dimension=0, tiled=True),
        lax.psum_scatter(flat_key, ("batch", "seq"), scatter_dimension=0, tiled=True),
        lax.psum_scatter(flat_value, ("batch", "seq"), scatter_dimension=0, tiled=True),
        lax.psum_scatter(flat_out, ("batch", "seq"), scatter_dimension=0, tiled=True),
        lax.psum_scatter(flat_gate, ("batch", "seq"), scatter_dimension=0, tiled=True),
        lax.psum_scatter(flat_up, ("batch", "seq"), scatter_dimension=0, tiled=True),
        lax.psum_scatter(flat_down, ("batch", "seq"), scatter_dimension=0, tiled=True),
    )
    summed = (
        lax.all_gather(shares[0], ("batch", "seq"), axis=0, tiled=True),
        lax.all_gather(shares[1], ("batch", "seq"), axis=0, tiled=True),
        lax.all_gather(shares[2], ("batch", "seq"), axis=0, tiled=True),
        lax.all_gather(shares[3], ("batch", "seq"), axis=0, tiled=True),
        lax.all_gather(shares[4], ("batch", "seq"), axis=0, tiled=True),
        lax.all_gather(shares[5], ("batch", "seq"), axis=0, tiled=True),
        lax.all_gather(shares[6], ("batch", "seq"), axis=0, tiled=True),
    )
    sum_norm, sum_ff, sum_table = lax.psum((d_norm_gain, d_ff_gain, table_part), ("batch", "seq"))
    return (
        layer_output,
        input_grad,
        sum_norm,
        summed[0].reshape(w_query.shape),
        summed[1].reshape(w_key.shape),
        summed[2].reshape(w_value.shape),
        summed[3].reshape(w_out.shape),
        sum_ff,
        summed[4].reshape(w_gate.shape),
        summed[5].reshape(w_up.shape),
        summed[6].reshape(w_down.shape),
        sum_table,
    )


def all_pairs(mesh_batch, mesh_seq, move):
    pairs = []
    for batch in range(mesh_batch):
        for seq in range(mesh_seq):
            z, y, core, x = move(batch // 4, batch // 2 % 2, batch % 2, seq)
            pairs.append((batch * mesh_seq + seq, (z * 4 + y * 2 + core) * mesh_seq + x))
    return pairs


def add_up(parts):
    total = parts[0].astype(f32)
    for part in parts[1:]:
        total = total + part.astype(f32)
    return total


class Links:
    def __init__(self, batch, seq):
        self.axes = ("batch", "seq")
        self.deep = batch // 4
        me = lax.axis_index("batch")
        self.z, self.y, self.core = me // 4, me // 2 % 2, me % 2
        self.x = lax.axis_index("seq")
        self.plane = self.y * 2 + self.x
        pairs = functools.partial(all_pairs, batch, seq)
        self.to_core = pairs(lambda z, y, c, x: (z, y, 1 - c, x))
        self.to_plane = {
            k: pairs(lambda z, y, c, x, k=k: (z, y ^ (k >> 1), c, x ^ (k & 1))) for k in (1, 2, 3)
        }
        self.to_deep = {
            k: pairs(lambda z, y, c, x, k=k: ((z + k) % self.deep, y, c, x))
            for k in range(1, self.deep)
        }

    def send(self, value, pairs):
        return lax.ppermute(value, self.axes, pairs)

    def pick(self, value, at):
        return lax.dynamic_index_in_dim(value, at, 0, keepdims=False)

    def scatter_core(self, grads, deps=()):
        rows, columns = grads.shape
        shape = (4, self.deep, rows // (8 * self.deep), columns)
        got = self.send(pick_half(grads, 1 - self.core, deps), self.to_core)
        own = self.pick(grads.reshape(2, *shape), self.core)
        return add_up([own, got.reshape(shape)]).astype(bf16)

    def scatter_plane(self, part):
        got = [self.send(self.pick(part, self.plane ^ k), self.to_plane[k]) for k in (1, 2, 3)]
        return add_up([self.pick(part, self.plane), *got]).astype(bf16)

    def scatter_pair(self, part, bit):
        at = self.y if bit else self.x
        got = self.send(self.pick(part, 1 - at), self.to_plane[1 + bit])
        return add_up([self.pick(part, at), got]).astype(bf16)

    def scatter_deep(self, part):
        got = [
            self.send(self.pick(part, (self.z + k) % self.deep), self.to_deep[k])
            for k in range(1, self.deep)
        ]
        return add_up([self.pick(part, self.z), *got]).astype(bf16)

    def lay(self, count, at, own, got):
        out = jnp.zeros((count,) + own.shape, own.dtype)
        out = lax.dynamic_update_index_in_dim(out, own, at, 0)
        for place, piece in got:
            out = lax.dynamic_update_index_in_dim(out, piece, place, 0)
        return out

    def join(self, part, small):
        columns = part.shape[-1]
        high = small.astype(bf16)
        low = (small - high.astype(f32)).astype(bf16)
        rest = jnp.zeros((14, columns), bf16)
        return jnp.concatenate([part.reshape(-1, columns), high, low, rest], axis=0)

    def small_of(self, joined):
        return joined[-16:-15].astype(f32) + joined[-15:-14].astype(f32)

    def gather_deep(self, part, small):
        joined = self.join(part, small)
        got = [self.send(joined, self.to_deep[k]) for k in range(1, self.deep)]
        rows = part.shape[0]
        pieces = [((self.z - k) % self.deep, g[:rows]) for k, g in enumerate(got, 1)]
        small = add_up([small, *[self.small_of(g) for g in got]])
        return self.lay(self.deep, self.z, part, pieces), small

    def gather_plane(self, part, small, deps):
        joined = self.join(part, small)
        got = [self.send(joined, self.to_plane[k]) for k in (1, 2, 3)]
        rows = joined.shape[0] - 16
        pieces = [(self.plane ^ k, g[:rows].reshape(part.shape)) for k, g in enumerate(got, 1)]
        small = add_up([small, *[self.small_of(g) for g in got]])
        return self.lay(4, self.plane, hold(part, deps), pieces), small


def rows_device(
    batch,
    seq,
    inputs,
    lengths,
    cotangent,
    norm_gain,
    w_query,
    w_key,
    w_value,
    w_out,
    ff_gain,
    w_gate,
    w_up,
    w_down,
    bias_table,
):
    rows, half, width = inputs.shape
    buckets, heads = bias_table.shape
    mine_count = rows // 2
    links = Links(batch, seq)
    places = split_rows(lengths, links.x)
    swap = [(0, 1), (1, 0)]

    x_parts, tick = [], ()
    for row in range(mine_count):
        x_parts.append(lax.ppermute(pick_rows(places, row, 1, inputs, tick), "seq", swap))
        tick = (links.send(tick[0] if tick else places.astype(f32), links.to_core),)
    g_remote = lax.ppermute(pick_rows(places, 0, mine_count, cotangent, tick), "seq", swap)
    near, near_t, far = bias_pieces(bias_table, 2 * half // LANE)
    gain = norm_gain.reshape(1, width)
    gain2 = ff_gain.reshape(1, width)
    held = []
    for row in range(mine_count):
        held = fwd_row(
            places, inputs, x_parts[row], row, mine_count, held,
            gain, w_query, w_key, w_value, near, far, heads,
        )
    q, k, v, mix, tail, normt, x_remote = held
    ff_args = (
        places, inputs, x_remote, cotangent, g_remote, mix,
        w_out, gain2, w_gate, w_up, w_down,
    )
    lo, lo_send, dh, dmix, ff_grads, ff_gain_part = feed_forward(*ff_args)
    ff_total = lax.psum(ff_grads, ("batch", "seq"))
    quads = q.shape[1]
    lo_got = lax.ppermute(lo_send, "seq", swap)
    dw, backs, token = [], [], ()
    for quad in range(quads):
        if quad == quads - 1:
            layer_output, placed = place_rows(places, 0, lo_got, lo)
            token = (placed,)
        *back, dw_quad = bwd_quad(
            places, quad, dw, q, k, v, mix, dmix, tail, near_t, normt, token
        )
        backs.append(back)
        dw = [dw_quad]
    dq, dk, dv, tacc, far_sum = zip(*backs)
    qkv = links.scatter_core(dw[0])
    ig, ig_got, gain_parts, token = [], [], [], ()
    for row in range(mine_count):
        *ig, sent, gain_part = input_back(
            places, row, ig, inputs, x_parts[row], dh, dq, dk, dv,
            gain, w_query, w_key, w_value, token,
        )
        gain_parts.append(gain_part)
        if row == 0:
            token = (qkv,)
            qkv = links.scatter_plane(qkv)
            first_sent = sent
        else:
            ig_got.append((row, lax.ppermute(sent, "seq", swap)))
    qkv = hold(qkv, (gain_parts[-1],))
    ig_got.append((0, lax.ppermute(hold(first_sent, (qkv,)), "seq", swap)))
    table_part = table_sums(table_diagonals(tacc, (qkv,)), jnp.stack(far_sum), buckets)
    small = jnp.concatenate([sum(gain_parts)[0], ff_gain_part[0], table_part.reshape(-1)])
    small = jnp.pad(small, (0, dw[0].shape[1] - small.shape[0])).reshape(1, -1)
    qkv = hold(links.scatter_deep(qkv), (table_part,))
    input_grad = ig[0]
    for got in ig_got[:-1]:
        input_grad, placed = place_rows(places, *got, input_grad, (qkv,))
    qkv, small = links.gather_deep(qkv, small)
    qkv = hold(qkv, (placed,))
    gate_grad, up_grad, down_grad, out_grad = spread(ff_total, (qkv,))
    qkv, small = links.gather_plane(qkv, small, (out_grad,))
    qkv = hold(qkv, (out_grad,))
    input_grad, _ = place_rows(places, *ig_got[-1], input_grad, (qkv,))
    qkv = qkv.reshape(-1, qkv.shape[-1])
    arrived = links.send(links.join(qkv, small), links.to_core)
    mine_grads = unpack(qkv, qkv.shape[0], links.core)
    query_grad, key_grad, value_grad = unpack(
        arrived, qkv.shape[0], 1 - links.core, mine_grads
    )
    small = add_up([small, links.small_of(arrived)])[0]

    return (
        layer_output,
        input_grad,
        small[:width],
        query_grad,
        key_grad,
        value_grad,
        out_grad,
        small[width : 2 * width],
        gate_grad,
        up_grad,
        down_grad,
        small[2 * width : 2 * width + buckets * heads].reshape(buckets, heads),
    )


def solution(mesh):
    split = P("batch", "seq", None)
    in_specs = (split, P("batch", None), split) + (P(),) * 10
    out_specs = (split, split) + (P(),) * 10
    batch, seq = mesh.shape["batch"], mesh.shape["seq"]

    def per_device(inputs, *rest):
        rows, half, width = inputs.shape
        buckets, heads = rest[-1].shape
        inner = rest[3].shape[1]
        fits = seq == 2 and batch % 4 == 0 and rows % 2 == 0 and rows >= 4 and buckets == 32
        fits = fits and 2 * width + buckets * heads <= 3 * width and half % STEP == 0 and 2 * half // LANE <= 8
        fits = fits and inner == width and width % (16 * batch) == 0 and inner // heads == LANE // 2
        if fits:
            return rows_device(batch, seq, inputs, *rest)
        return gathered_device(inputs, *rest)

    return jax.shard_map(
        per_device, mesh=mesh, in_specs=in_specs, out_specs=out_specs, check_vma=False
    )
```
